32 devices in a mesh: row: 8 (over z, y), col: 4 (over x, core).
Axes of the slice: x: 2, y: 2, z: 4, core: 2. Of those that a mesh axis runs over, the one named last changes fastest.
Arguments:
- atom_feats: bfloat16 [2048, 128], P(('row', 'col')), may hold values from -6 to 6
- key_starts: int32 [64], P(('row', 'col')), may hold values from -64 to 1984, as said below
- atom_counts: int32 [128], replicated, may hold values from 8 to 24, as said below
- atom_gain: float32 [128], replicated, may hold values from 0.1 to 1.9
- w_query: bfloat16 [128, 128], replicated, may hold values from -0.5 to 0.5
- w_key: bfloat16 [128, 128], replicated, may hold values from -0.5 to 0.5
- w_value: bfloat16 [128, 128], replicated, may hold values from -0.5 to 0.5
- w_out: bfloat16 [128, 128], replicated, may hold values from -0.5 to 0.5
- w_pool: bfloat16 [128, 384], replicated, may hold values from -0.5 to 0.5
- w_back: bfloat16 [384, 128], replicated, may hold values from -0.3125 to 0.3125
- pair_state: bfloat16 [128, 128, 128], P('row', 'col'), may hold values from -6 to 6
- w_left: bfloat16 [384, 32], replicated, may hold values from -0.3125 to 0.3125
- w_right: bfloat16 [384, 32], replicated, may hold values from -0.3125 to 0.3125
- w_outer: bfloat16 [32, 32, 128], replicated, may hold values from -0.1875 to 0.1875
- pair_gain: float32 [128], replicated, may hold values from 0.1 to 1.9
- w_gate: bfloat16 [128, 512], replicated, may hold values from -0.5 to 0.5
- w_lift: bfloat16 [128, 512], replicated, may hold values from -0.5 to 0.5
- w_drop: bfloat16 [512, 128], replicated, may hold values from -0.25 to 0.25
Outputs:
- atom_out: bfloat16 [2048, 128], P(('row', 'col'))
- token_single: bfloat16 [128, 384], P(('row', 'col'))
- pair_out: bfloat16 [128, 128, 128], P('row', 'col')
The draws below stay inside these ranges and needn't reach their ends.
Inputs may be any that keep to these rules, and one draw needn't show every extreme that they name: key_starts[b] = 32 * b - 64 + offset, with offset a whole number from 0 to 32; the offset is 0 for the first block and 32 for the last. `atom_counts`: the counts sum to 2048.
All inputs are finite; a program needn't handle non-finite values.
Results may differ from the reference program's by a relative error of at most 0.007.
Values may be sent and summed in bfloat16 or wider, within the bound.
No kernel may reach another device: no remote copies, remote signals or barrier semaphores. Data moves between devices by JAX's collectives and lax.ppermute only.
A program may use at most 64 MiB of HBM per device.

```python
import math
import jax
import jax.numpy as jnp
from jax import lax

CA = 128
CS = 384
CZ = 128
HEADS = 4
QB = 32
KW = 128
OPM = 32
PT = 512
APT = 16
FEWEST = 8
ATOMS = 2048
TOKENS = 128
NBLK = 64


def draw_key_starts(key, part):
    block_index = jnp.arange(NBLK, dtype=jnp.int32)
    offset = jax.random.randint(key, (NBLK,), 0, QB + 1, dtype=jnp.int32)
    offset = offset.at[0].set(0).at[NBLK - 1].set(QB)
    return (QB * block_index - KW // 2 + offset).astype(jnp.int32)


def draw_atom_counts(key, part):
    order_key = jax.random.fold_in(key, 11)
    extra_key = jax.random.fold_in(key, 23)
    spread_top = 2 * (APT - FEWEST)
    order = jax.random.permutation(order_key, TOKENS).astype(jnp.int32)
    first_extra = jax.random.randint(extra_key, (TOKENS // 2,), 0, spread_top + 1, dtype=jnp.int32)
    first_extra = first_extra.at[0].set(spread_top)
    extras = jnp.zeros((TOKENS,), jnp.int32)
    extras = extras.at[order[0::2]].set(first_extra)
    extras = extras.at[order[1::2]].set(spread_top - first_extra)
    return (FEWEST + extras).astype(jnp.int32)


def level_of(key, extent, split, smallest, largest):
    def one(axis_at, blocks):
        heights = jax.random.uniform(jax.random.fold_in(jax.random.fold_in(key, 6), axis_at), (blocks,), jnp.float32, smallest / len(split), largest / len(split))
        return jnp.repeat(jnp.exp(heights), extent[axis_at] // blocks).reshape((-1,) + (1,) * (len(extent) - axis_at - 1))

    loudness = one(*split[0])
    for cut in split[1:]:
        loudness = loudness * one(*cut)
    return loudness


def noise(rng, extent, width, most, split=(), held_as=jnp.bfloat16):
    values = jax.random.normal(rng, extent, jnp.float32) * width
    if len(split) > 0:
        values = level_of(rng, extent, split, -0.22, 0.18) * values
    return jnp.clip(values, min=-most, max=most).astype(held_as)


def setup_inputs(seed: int = 0) -> dict:
    arg_keys = jax.random.split(jax.random.key(seed), 19)
    atom_feats = noise(arg_keys[0], (ATOMS, CA), 1.0, 6.0, ((0, 32),))
    key_starts = draw_key_starts(jax.random.fold_in(arg_keys[18], 71), 0)
    atom_counts = draw_atom_counts(jax.random.fold_in(arg_keys[18], 71), 0)
    atom_gain = jnp.clip(1.0 + 0.18 * jax.random.normal(arg_keys[3], (CA,), jnp.float32), 0.1, 1.9)
    w_query = noise(arg_keys[4], (CA, CA), CA ** -0.5, 0.5)
    w_key = noise(arg_keys[5], (CA, CA), CA ** -0.5, 0.5)
    w_value = noise(arg_keys[6], (CA, CA), CA ** -0.5, 0.5)
    w_out = noise(arg_keys[7], (CA, CA), CA ** -0.5, 0.5)
    w_pool = noise(arg_keys[8], (CA, CS), CA ** -0.5, 0.5)
    w_back = noise(arg_keys[9], (CS, CA), CS ** -0.5, 0.3125)
    pair_state = noise(arg_keys[10], (TOKENS, TOKENS, CZ), 1.0, 6.0, ((0, 8), (1, 4)))
    w_left = noise(arg_keys[11], (CS, OPM), CS ** -0.5, 0.3125)
    w_right = noise(arg_keys[12], (CS, OPM), CS ** -0.5, 0.3125)
    w_outer = noise(arg_keys[13], (OPM, OPM, CZ), (OPM * OPM) ** -0.5, 0.1875)
    pair_gain = jnp.clip(1.0 + 0.18 * jax.random.normal(arg_keys[14], (CZ,), jnp.float32), 0.1, 1.9)
    w_gate = noise(arg_keys[15], (CZ, PT), CZ ** -0.5, 0.5)
    w_lift = noise(arg_keys[16], (CZ, PT), CZ ** -0.5, 0.5)
    w_drop = noise(arg_keys[17], (PT, CZ), PT ** -0.5, 0.25)
    return {"atom_feats": atom_feats, "key_starts": key_starts, "atom_counts": atom_counts, "atom_gain": atom_gain, "w_query": w_query, "w_key": w_key, "w_value": w_value, "w_out": w_out, "w_pool": w_pool, "w_back": w_back, "pair_state": pair_state, "w_left": w_left, "w_right": w_right, "w_outer": w_outer, "pair_gain": pair_gain, "w_gate": w_gate, "w_lift": w_lift, "w_drop": w_drop}


EPSILON = 1e-05

def layer_norm(values, gain):
    mean_value = lax.optimization_barrier(jnp.mean(values, axis=-1, keepdims=True))
    centred = values - mean_value
    variance = lax.optimization_barrier(jnp.mean(centred * centred, axis=-1, keepdims=True))
    return centred * lax.rsqrt(variance + EPSILON) * gain

def pair_rows(left_block, pair_block, outer_table, pair_gain, w_gate, w_lift, w_drop):
    outer_term = jnp.einsum('ia,jac->ijc', left_block.astype(jnp.float32), outer_table.astype(jnp.float32))
    summed = pair_block.astype(jnp.float32) + outer_term
    normed_pair = layer_norm(summed, pair_gain).astype(jnp.bfloat16).astype(jnp.float32)
    gate_proj = jnp.einsum('ijc,cf->ijf', normed_pair, w_gate.astype(jnp.float32))
    lift_proj = jnp.einsum('ijc,cf->ijf', normed_pair, w_lift.astype(jnp.float32))
    hidden = (jax.nn.silu(gate_proj) * lift_proj).astype(jnp.bfloat16).astype(jnp.float32)
    return (summed + jnp.einsum('ijf,fc->ijc', hidden, w_drop.astype(jnp.float32))).astype(jnp.bfloat16)

def reference(atom_feats, key_starts, atom_counts, atom_gain, w_query, w_key, w_value, w_out, w_pool, w_back, pair_state, w_left, w_right, w_outer, pair_gain, w_gate, w_lift, w_drop):
    atom_float = atom_feats.astype(jnp.float32)
    normed = layer_norm(atom_float, atom_gain).astype(jnp.bfloat16)
    queries = jnp.dot(normed, w_query, preferred_element_type=jnp.float32).astype(jnp.bfloat16)
    keys_all = jnp.dot(normed, w_key, preferred_element_type=jnp.float32).astype(jnp.bfloat16)
    values_all = jnp.dot(normed, w_value, preferred_element_type=jnp.float32).astype(jnp.bfloat16)
    half_window = KW // 2
    padded_keys = jnp.pad(keys_all, ((half_window, half_window), (0, 0)))
    padded_values = jnp.pad(values_all, ((half_window, half_window), (0, 0)))
    shifted = (key_starts + half_window).astype(jnp.int32)

    def windows_of(table):
        return jax.vmap(lambda first_row: lax.dynamic_slice_in_dim(table, first_row, KW, 0))(shifted)
    head_size = CA // HEADS
    key_blocks = windows_of(padded_keys).reshape(NBLK, KW, HEADS, head_size).astype(jnp.float32)
    value_blocks = windows_of(padded_values).reshape(NBLK, KW, HEADS, head_size).astype(jnp.float32)
    query_blocks = queries.reshape(NBLK, QB, HEADS, head_size).astype(jnp.float32)
    key_index = key_starts[:, None] + jnp.arange(KW, dtype=jnp.int32)[None, :]
    in_range = (key_index >= 0) & (key_index < ATOMS)
    scores = jnp.einsum('bqhd,bkhd->bhqk', query_blocks, key_blocks) * head_size ** (-0.5)
    raised = jnp.where(in_range[:, None, None, :], jnp.exp(scores), 0.0)
    weights = (raised / lax.optimization_barrier(jnp.sum(raised, axis=-1, keepdims=True))).astype(jnp.bfloat16).astype(jnp.float32)
    attended = jnp.einsum('bhqk,bkhd->bqhd', weights, value_blocks).astype(jnp.bfloat16).reshape(ATOMS, CA)
    updated = (atom_float + jnp.dot(attended, w_out, preferred_element_type=jnp.float32)).astype(jnp.bfloat16)
    feature = jax.nn.relu(jnp.dot(updated, w_pool, preferred_element_type=jnp.float32)).astype(jnp.bfloat16)
    token_ends = jnp.cumsum(atom_counts, dtype=jnp.int32)
    token_of = jnp.searchsorted(token_ends, jnp.arange(ATOMS, dtype=jnp.int32), side='right').astype(jnp.int32)
    pooled = jax.ops.segment_sum(feature.astype(jnp.float32), token_of, num_segments=TOKENS)
    token_single = (pooled / atom_counts[:, None].astype(jnp.float32)).astype(jnp.bfloat16)
    back_all = jnp.dot(token_single, w_back, preferred_element_type=jnp.float32).astype(jnp.bfloat16)
    atom_out = (updated.astype(jnp.float32) + back_all[token_of].astype(jnp.float32)).astype(jnp.bfloat16)
    left_all = jnp.dot(token_single, w_left, preferred_element_type=jnp.float32).astype(jnp.bfloat16)
    right_all = jnp.dot(token_single, w_right, preferred_element_type=jnp.float32).astype(jnp.bfloat16)
    outer_table = jnp.einsum('jb,abc->jac', right_all.astype(jnp.float32), w_outer.astype(jnp.float32)).astype(jnp.bfloat16)
    step_rows = math.gcd(TOKENS, 8)

    def one_block(pieces):
        return pair_rows(pieces[0], pieces[1], outer_table, pair_gain, w_gate, w_lift, w_drop)
    pair_out = lax.map(one_block, (left_all.reshape(-1, step_rows, OPM), pair_state.reshape(-1, step_rows, TOKENS, CZ)))
    return (atom_out, token_single, pair_out.reshape(TOKENS, TOKENS, CZ))
```

```python
import math

import jax
import jax.numpy as jnp
from jax import lax
from jax.sharding import PartitionSpec as P

HEADS = 4
QB = 32
KW = 128
FEWEST = 8


EPSILON = 1e-05


def with_halo(block, sides, width):
    for axis, dim in sides:
        count = lax.axis_size(axis)
        forward = [(i, i + 1) for i in range(count - 1)]
        backward = [(target, source) for source, target in forward]
        low = lax.ppermute(
            lax.slice_in_dim(block, block.shape[dim] - width, None, axis=dim), axis, forward
        )
        high = lax.ppermute(lax.slice_in_dim(block, 0, width, axis=dim), axis, backward)
        block = jnp.concatenate([low, block, high], axis=dim)
    return block


def shifted(block, axis, distance):
    devices = range(lax.axis_size(axis))
    route = [(i - distance, i) for i in devices if i - distance in devices]
    return lax.ppermute(block, axis, route)


def layer_norm(values, gain):
    mean_value = jnp.mean(values, axis=-1, keepdims=True)
    centred = values - mean_value
    variance = jnp.mean(centred * centred, axis=-1, keepdims=True)
    return centred * lax.rsqrt(variance + EPSILON) * gain


def project(source, weight):
    return jnp.dot(source, weight, preferred_element_type=jnp.float32).astype(jnp.bfloat16)


def per_device(
    atom_feats,
    key_starts,
    atom_counts,
    atom_gain,
    w_query,
    w_key,
    w_value,
    w_out,
    w_pool,
    w_back,
    pair_state,
    w_left,
    w_right,
    w_outer,
    pair_gain,
    w_gate,
    w_lift,
    w_drop,
):
    atom_rows, atom_width = atom_feats.shape
    devices = lax.axis_size(("row", "col"))
    position = lax.axis_index(("row", "col"))
    total_atoms = atom_rows * devices
    total_tokens = atom_counts.shape[0]
    own_tokens = total_tokens // devices
    rim_width = KW // 2
    first_atom = position * atom_rows
    atom_float = atom_feats.astype(jnp.float32)
    normed = layer_norm(atom_float, atom_gain).astype(jnp.bfloat16)
    queries = project(normed, w_query)
    w_keyval = jnp.concatenate([w_key, w_value], axis=1)
    keyvals = project(normed, w_keyval)
    extended = with_halo(keyvals, ((("row", "col"), 0),), rim_width)
    local_starts = key_starts - first_atom + rim_width
    windows = jax.vmap(lambda first_row: lax.dynamic_slice_in_dim(extended, first_row, KW, 0))(
        local_starts
    )
    head_size = atom_width // HEADS
    blocks = atom_rows // QB
    query_blocks = queries.reshape(blocks, QB, HEADS, head_size)
    key_blocks = windows[:, :, :atom_width].reshape(blocks, KW, HEADS, head_size)
    value_blocks = windows[:, :, atom_width:].reshape(blocks, KW, HEADS, head_size)
    key_index = key_starts[:, None] + jnp.arange(KW, dtype=jnp.int32)[None, :]
    in_range = (key_index >= 0) & (key_index < total_atoms)
    scores = jnp.einsum(
        "bqhd,bkhd->bhqk", query_blocks, key_blocks, preferred_element_type=jnp.float32
    ) * head_size ** (-0.5)
    raised = jnp.where(in_range[:, None, None, :], jnp.exp(scores), 0.0)
    weights = (raised / jnp.sum(raised, axis=-1, keepdims=True)).astype(jnp.bfloat16)
    attended = (
        jnp.einsum("bhqk,bkhd->bqhd", weights, value_blocks, preferred_element_type=jnp.float32)
        .astype(jnp.bfloat16)
        .reshape(atom_rows, atom_width)
    )
    updated = (atom_float + jnp.dot(attended, w_out, preferred_element_type=jnp.float32)).astype(
        jnp.bfloat16
    )
    feature = jax.nn.relu(jnp.dot(updated, w_pool, preferred_element_type=jnp.float32)).astype(
        jnp.bfloat16
    )
    token_ends = jnp.cumsum(atom_counts, dtype=jnp.int32)
    atom_index = first_atom + jnp.arange(atom_rows, dtype=jnp.int32)
    token_of = jnp.sum((token_ends[None, :] <= atom_index[:, None]).astype(jnp.int32), axis=1)
    count_float = atom_counts.astype(jnp.float32)
    slots = atom_rows // FEWEST
    token_starts = token_ends - atom_counts
    base_token = jnp.sum((token_starts < first_atom).astype(jnp.int32))
    relative = token_of - base_token
    slot_range = jnp.arange(slots, dtype=jnp.int32)
    member = (relative[:, None] == slot_range[None, :]).astype(jnp.bfloat16)
    local_sums = jnp.einsum("as,ac->sc", member, feature, preferred_element_type=jnp.float32)
    carried = (relative < 0).astype(jnp.bfloat16)[None, :]
    edge_sum = jnp.dot(carried, feature, preferred_element_type=jnp.float32)
    from_next = shifted(edge_sum, ("row", "col"), -1)
    next_token = jnp.sum((token_ends <= first_atom + atom_rows).astype(jnp.int32))
    target = (slot_range == next_token - base_token).astype(jnp.float32)[:, None]
    pooled_slots = local_sums + target * from_next
    padded_counts = jnp.concatenate([count_float, jnp.ones((slots,), jnp.float32)])
    slot_counts = lax.dynamic_slice_in_dim(padded_counts, base_token, slots, 0)
    slot_single = (pooled_slots / slot_counts[:, None]).astype(jnp.bfloat16)
    owner = token_starts // atom_rows
    owner_first = jnp.sum(
        (token_starts[None, :] < owner[:, None] * atom_rows).astype(jnp.int32), axis=1
    )
    row_of = owner * slots + jnp.arange(total_tokens, dtype=jnp.int32) - owner_first
    copies = jnp.broadcast_to(slot_single[None], (devices,) + slot_single.shape)
    gathered = lax.all_to_all(copies, ("row", "col"), 0, 0).reshape(devices * slots, -1)
    full_single = jnp.take(gathered, row_of, axis=0)
    left_all = project(full_single, w_left)
    right_all = project(full_single, w_right)
    back_all = project(full_single, w_back)
    token_single = lax.dynamic_slice_in_dim(full_single, position * own_tokens, own_tokens, 0)
    member_all = (token_of[:, None] == jnp.arange(total_tokens, dtype=jnp.int32)[None, :]).astype(
        jnp.bfloat16
    )
    lifted = jnp.dot(member_all, back_all, preferred_element_type=jnp.float32)
    atom_out = (updated.astype(jnp.float32) + lifted).astype(jnp.bfloat16)
    row_tokens, col_tokens, pair_width = pair_state.shape
    left_rows = lax.dynamic_slice_in_dim(
        left_all, lax.axis_index("row") * row_tokens, row_tokens, 0
    )
    right_cols = lax.dynamic_slice_in_dim(
        right_all, lax.axis_index("col") * col_tokens, col_tokens, 0
    )
    outer_table = jnp.einsum(
        "jb,abc->jac", right_cols, w_outer, preferred_element_type=jnp.float32
    ).astype(jnp.bfloat16)
    step_rows = math.gcd(row_tokens, 8)

    def pair_block(pieces):
        left_block, pair_piece = pieces
        outer_term = jnp.einsum(
            "ia,jac->ijc", left_block, outer_table, preferred_element_type=jnp.float32
        )
        summed = pair_piece.astype(jnp.float32) + outer_term
        normed_pair = layer_norm(summed, pair_gain).astype(jnp.bfloat16)
        gate_proj = jnp.einsum(
            "ijc,cf->ijf", normed_pair, w_gate, preferred_element_type=jnp.float32
        )
        lift_proj = jnp.einsum(
            "ijc,cf->ijf", normed_pair, w_lift, preferred_element_type=jnp.float32
        )
        hidden = (jax.nn.silu(gate_proj) * lift_proj).astype(jnp.bfloat16)
        return (
            summed + jnp.einsum("ijf,fc->ijc", hidden, w_drop, preferred_element_type=jnp.float32)
        ).astype(jnp.bfloat16)

    pair_out = lax.map(
        pair_block,
        (
            left_rows.reshape(-1, step_rows, left_rows.shape[1]),
            pair_state.reshape(-1, step_rows, col_tokens, pair_width),
        ),
    )
    return (atom_out, token_single, pair_out.reshape(row_tokens, col_tokens, pair_width))


def solution(mesh):
    in_specs = (
        P(("row", "col"), None),
        P(("row", "col")),
        P(),
        P(),
        P(),
        P(),
        P(),
        P(),
        P(),
        P(),
        P("row", "col", None),
        P(),
        P(),
        P(),
        P(),
        P(),
        P(),
        P(),
    )
    out_specs = (P(("row", "col"), None), P(("row", "col"), None), P("row", "col", None))
    return jax.shard_map(
        per_device, mesh=mesh, in_specs=in_specs, out_specs=out_specs, check_vma=False
    )
```

```python
import math

import jax
import jax.numpy as jnp
from jax import lax
from jax.experimental import pallas as pl
from jax.experimental.pallas import tpu as pltpu
from jax.sharding import PartitionSpec as P

HEADS = 4
QB = 32
KW = 128
EPSILON = 1e-05
HALF = KW // 2
RIM = 8
GROUPS = 4
PAIR_ROWS = 8
MASKED = -1e30
SPARE = 10 << 20
MOST = 63 << 20
LOG2E = 1.4426950408889634
AXES = ("row", "col")
BF = jnp.bfloat16
F32 = jnp.float32


def layer_norm(values, gain):
    mean_value = jnp.mean(values, axis=-1, keepdims=True)
    centred = values - mean_value
    variance = jnp.mean(centred * centred, axis=-1, keepdims=True)
    return centred * lax.rsqrt(variance + EPSILON) * gain


def dot(a, b):
    return jnp.dot(a, b, preferred_element_type=F32)


def dot_t(a, b):
    return lax.dot_general(a, b, (((1,), (1,)), ((), ())), preferred_element_type=F32)


def iota(shape, axis):
    return lax.broadcasted_iota(jnp.int32, shape, axis)


def kernel(
    mine,
    other,
    starts,
    counts,
    atom_gain,
    w_query,
    w_key,
    w_value,
    w_out,
    w_pool,
    w_back,
    pair_state,
    w_left,
    w_right,
    w_outer,
    pair_gain,
    w_gate,
    w_lift,
    w_drop,
    atom_out,
    token_single,
    pair_out,
    queries,
    keys,
    values,
    offsets,
    updated,
    pooled,
    singles,
    left_wide,
    right_wide,
):
    half_blocks, block_rows, width = mine.shape
    rows = block_rows - RIM
    atoms = 2 * half_blocks * rows
    tokens, channels = pooled.shape
    row_tokens, col_tokens, pair_width = pair_state.shape
    opm = w_left.shape[0]
    row, col = lax.axis_index("row"), lax.axis_index("col")
    position = row * lax.axis_size("col") + col
    parity = position % 2
    window = rows + KW

    zeros = jnp.zeros((HALF, width), BF)
    for table in (keys, values):
        table[0:HALF, :] = zeros
        table[HALF + atoms : 2 * HALF + atoms, :] = zeros
    w_kv = jnp.concatenate([w_key[...], w_value[...]], axis=1)

    def project(source, which, step):
        pieces = source[pl.ds(step * GROUPS, GROUPS)]
        raw = pieces[:, :rows, :].reshape(GROUPS * rows, width)
        normed = layer_norm(raw.astype(F32), atom_gain[...]).astype(BF)
        query = dot(normed, w_query[...]).astype(BF)
        keyval = dot(normed, w_kv).astype(BF)
        for at in range(GROUPS):
            block = 2 * (step * GROUPS + at) + which
            first = pl.multiple_of(block * rows, rows)
            part = slice(at * rows, (at + 1) * rows)
            updated[pl.ds(first, rows), :] = raw[part]
            queries[pl.ds(first, rows), :] = query[part]
            keys[pl.ds(first + HALF, rows), :] = keyval[part, :width]
            values[pl.ds(first + HALF, rows), :] = keyval[part, width:]
            offsets[block] = pieces[at, rows:, :].astype(F32)

    def project_step(step, carry):
        project(mine, parity, step)
        project(other, 1 - parity, step)
        return carry

    lax.fori_loop(0, half_blocks // GROUPS, project_step, 0)

    pooled[...] = jnp.zeros_like(pooled)
    head_of = iota((1, width), 1) // (width // HEADS)
    head_mask = [(head_of == h).astype(F32) for h in range(HEADS)]
    head_mask_bf = [m.astype(BF) for m in head_mask]
    ones = jnp.ones((window, width), BF)
    key_lane = iota((1, window), 1)
    key_lane_float = key_lane.astype(F32)
    scale = (width // HEADS) ** (-0.5) * LOG2E
    chunk = GROUPS * rows
    chunk_lane = iota((tokens, chunk), 1)

    def attend_step(step, carry):
        attended = []
        for at in range(GROUPS):
            block = step * GROUPS + at
            first = pl.multiple_of(block * rows, rows)
            query = queries[pl.ds(first, rows), :]
            key_part = keys[pl.ds(first, window), :]
            value_part = values[pl.ds(first, window), :]
            in_range = (key_lane >= HALF - first) & (key_lane < atoms + HALF - first)
            offset = offsets[block]
            bias = []
            for e in range(rows // QB):
                low = offset[e : e + 1, :]
                low = jnp.concatenate([low, low], axis=1)[:, :window] + (QB * e)
                seen = in_range & (key_lane_float >= low) & (key_lane_float < low + KW)
                bias.append(
                    jnp.broadcast_to(jnp.where(seen, 0.0, MASKED), (QB, window))
                )
            bias = jnp.concatenate(bias, axis=0)
            stacked = jnp.concatenate([query * m for m in head_mask_bf], axis=0)
            scores = dot_t(stacked, key_part)
            scores = jnp.concatenate(
                [scores[h * rows : (h + 1) * rows] + bias for h in range(HEADS)], axis=0
            )
            top = jnp.max(scores, axis=-1, keepdims=True)
            raised = jnp.exp2((scores - top) * scale).astype(BF)
            mixed = dot(raised, jnp.concatenate([value_part, ones], axis=1))
            total = sum(
                mixed[h * rows : (h + 1) * rows, :width] * head_mask[h] for h in range(HEADS)
            )
            weight = sum(
                mixed[h * rows : (h + 1) * rows, width:] * head_mask[h] for h in range(HEADS)
            )
            attended.append((total / weight).astype(BF))
        attended = jnp.concatenate(attended, axis=0)
        here = pl.multiple_of(step * chunk, chunk)
        fresh = (updated[pl.ds(here, chunk), :].astype(F32) + dot(attended, w_out[...])).astype(BF)
        updated[pl.ds(here, chunk), :] = fresh
        feature = jnp.maximum(dot(fresh, w_pool[...]), 0.0).astype(BF)
        begin = starts[...] - here
        member = (chunk_lane >= begin) & (chunk_lane < begin + counts[...])
        pooled[...] += dot(member.astype(F32).astype(BF), feature)
        return carry

    lax.fori_loop(0, atoms // chunk, attend_step, 0)

    single = (pooled[...] / counts[...].astype(F32)).astype(BF)
    singles[...] = single
    own_tokens = token_single.shape[0]
    pick = iota((own_tokens, tokens), 1) == iota((own_tokens, tokens), 0) + position * own_tokens
    token_single[...] = dot(pick.astype(F32).astype(BF), single).astype(BF)

    first = pl.multiple_of(position * rows, rows)
    atom_lane = iota((tokens, rows), 1) + first
    owner = (atom_lane >= starts[...]) & (atom_lane < starts[...] + counts[...])
    back = dot(single, w_back[...]).astype(BF)
    lifted = lax.dot_general(
        owner.astype(F32).astype(BF), back, (((0,), (0,)), ((), ())), preferred_element_type=F32
    )
    atom_out[...] = (updated[pl.ds(first, rows), :].astype(F32) + lifted).astype(BF)

    row_single = singles[pl.ds(pl.multiple_of(row * row_tokens, row_tokens), row_tokens), :]
    col_single = singles[pl.ds(pl.multiple_of(col * col_tokens, col_tokens), col_tokens), :]
    left = dot_t(row_single, w_left[...]).astype(BF)
    right = dot_t(col_single, w_right[...]).astype(BF)
    product_lane = iota((opm, opm * opm), 1)
    unit = iota((opm, opm * opm), 0)
    left_wide[...] = dot(left, (product_lane // opm == unit).astype(F32).astype(BF))
    right_wide[...] = dot(right, (product_lane % opm == unit).astype(F32).astype(BF))

    def pair_step(step, carry):
        here = pl.multiple_of(step * PAIR_ROWS, PAIR_ROWS)
        lefts = left_wide[pl.ds(here, PAIR_ROWS), :]
        rights = right_wide[...]
        products = jnp.concatenate(
            [(lefts[i : i + 1, :] * rights).astype(BF) for i in range(PAIR_ROWS)], axis=0
        )
        flat = pair_state[pl.ds(here, PAIR_ROWS)].reshape(PAIR_ROWS * col_tokens, pair_width)
        summed = flat.astype(F32) + dot(products, w_outer[...])
        normed = layer_norm(summed, pair_gain[...]).astype(BF)
        gate = dot(normed, w_gate[...])
        lift = dot(normed, w_lift[...])
        hidden = (gate * (0.5 + 0.5 * jnp.tanh(0.5 * gate)) * lift).astype(BF)
        result = (summed + dot(hidden, w_drop[...])).astype(BF)
        pair_out[pl.ds(here, PAIR_ROWS)] = result.reshape(PAIR_ROWS, col_tokens, pair_width)
        return carry

    lax.fori_loop(0, row_tokens // PAIR_ROWS, pair_step, 0)


def gather_blocks(block):
    devices = lax.axis_size(AXES)
    groups = [[i for i in range(devices) if i % 2 == side] for side in (0, 1)]
    copies = jnp.broadcast_to(block[None], (devices // 2,) + block.shape)
    mine = lax.all_to_all(copies, AXES, 0, 0, axis_index_groups=groups)
    other = lax.ppermute(mine, AXES, [(i, i ^ 1) for i in range(devices)])
    return mine, other


def per_device(
    atom_feats,
    key_starts,
    atom_counts,
    atom_gain,
    w_query,
    w_key,
    w_value,
    w_out,
    w_pool,
    w_back,
    pair_state,
    w_left,
    w_right,
    w_outer,
    pair_gain,
    w_gate,
    w_lift,
    w_drop,
):
    rows, width = atom_feats.shape
    devices = lax.axis_size(AXES)
    position = lax.axis_index(AXES)
    atoms = rows * devices
    tokens = atom_counts.shape[0]
    channels = w_pool.shape[1]
    blocks = rows // QB
    first_block = position * blocks
    offset = key_starts + HALF - QB * (first_block + jnp.arange(blocks, dtype=jnp.int32))
    rim = jnp.zeros((RIM, width), BF).at[:blocks].set(
        jnp.broadcast_to(offset.astype(BF)[:, None], (blocks, width))
    )
    mine, other = gather_blocks(jnp.concatenate([atom_feats, rim], axis=0))
    starts = jnp.cumsum(atom_counts, dtype=jnp.int32) - atom_counts
    opm = w_left.shape[1]
    vmem = pl.BlockSpec(memory_space=pltpu.VMEM)
    operands = (
        mine,
        other,
        starts[:, None],
        atom_counts[:, None],
        atom_gain[None],
        w_query,
        w_key,
        w_value,
        w_out,
        w_pool,
        w_back,
        pair_state,
        w_left.T,
        w_right.T,
        w_outer.reshape(opm * opm, -1),
        pair_gain[None],
        w_gate,
        w_lift,
        w_drop,
    )
    outputs = (
        jax.ShapeDtypeStruct(atom_feats.shape, BF),
        jax.ShapeDtypeStruct((tokens // devices, channels), BF),
        jax.ShapeDtypeStruct(pair_state.shape, BF),
    )
    scratch = [
        pltpu.VMEM((atoms, width), BF),
        pltpu.VMEM((atoms + 2 * HALF, width), BF),
        pltpu.VMEM((atoms + 2 * HALF, width), BF),
        pltpu.VMEM((devices, RIM, width), F32),
        pltpu.VMEM((atoms, width), BF),
        pltpu.VMEM((tokens, channels), F32),
        pltpu.VMEM((tokens, channels), BF),
        pltpu.VMEM((pair_state.shape[0], opm * opm), F32),
        pltpu.VMEM((pair_state.shape[1], opm * opm), F32),
    ]
    held = sum(math.prod(a.shape) * a.dtype.itemsize for a in operands + outputs)
    held += sum(math.prod(a.shape) * jnp.dtype(a.dtype).itemsize for a in scratch)
    return pl.pallas_call(
        kernel,
        out_shape=outputs,
        in_specs=[vmem] * len(operands),
        out_specs=(vmem,) * 3,
        scratch_shapes=scratch,
        compiler_params=pltpu.CompilerParams(vmem_limit_bytes=min(held + SPARE, MOST)),
        name="trunk_window",
    )(*operands)


def solution(mesh):
    in_specs = (
        P(("row", "col"), None),
        P(("row", "col")),
        P(),
        P(),
        P(),
        P(),
        P(),
        P(),
        P(),
        P(),
        P("row", "col", None),
        P(),
        P(),
        P(),
        P(),
        P(),
        P(),
        P(),
    )
    out_specs = (P(("row", "col"), None), P(("row", "col"), None), P("row", "col", None))
    return jax.shard_map(
        per_device, mesh=mesh, in_specs=in_specs, out_specs=out_specs, check_vma=False
    )
```

```python
import math

import jax
import jax.numpy as jnp
from jax import lax
from jax.experimental import pallas as pl
from jax.experimental.pallas import tpu as pltpu
from jax.sharding import PartitionSpec as P

HEADS = 4
QB = 32
KW = 128
EPSILON = 1e-05
HALF = KW // 2
RIM = 8
GROUPS = 4
PAIR_ROWS = 8
MASKED = -1e30
SPARE = 10 << 20
MOST = 63 << 20
LOG2E = 1.4426950408889634
AXES = ("row", "col")
BF = jnp.bfloat16
F32 = jnp.float32


def layer_norm(values, gain):
    mean_value = jnp.mean(values, axis=-1, keepdims=True)
    centred = values - mean_value
    variance = jnp.mean(centred * centred, axis=-1, keepdims=True)
    return centred * lax.rsqrt(variance + EPSILON) * gain


def dot(a, b):
    return jnp.dot(a, b, preferred_element_type=F32)


def dot_t(a, b):
    return lax.dot_general(a, b, (((1,), (1,)), ((), ())), preferred_element_type=F32)


def iota(shape, axis):
    return lax.broadcasted_iota(jnp.int32, shape, axis)


def reversed_bits(index, size):
    result = 0
    bit = 1
    while bit < size // 2:
        result = result + jnp.where(index & bit != 0, size // (2 * bit), 0)
        bit *= 2
    return result


def kernel(
    mine,
    other,
    starts,
    counts,
    atom_gain,
    w_query,
    w_key,
    w_value,
    w_out,
    w_pool,
    w_back,
    pair_state,
    w_left,
    w_right,
    w_outer,
    pair_gain,
    w_gate,
    w_lift,
    w_drop,
    atom_out,
    token_single,
    pair_out,
    queries,
    keys,
    values,
    offsets,
    updated,
    pooled,
    singles,
    left_wide,
    right_wide,
):
    half_blocks, block_rows, width = mine.shape
    rows = block_rows - RIM
    atoms = 2 * half_blocks * rows
    tokens, channels = pooled.shape
    row_tokens, col_tokens, pair_width = pair_state.shape
    opm = w_left.shape[0]
    row, col = lax.axis_index("row"), lax.axis_index("col")
    position = row * lax.axis_size("col") + col
    window = rows + KW

    zeros = jnp.zeros((HALF, width), BF)
    for table in (keys, values):
        table[0:HALF, :] = zeros
        table[HALF + atoms : 2 * HALF + atoms, :] = zeros
    w_kv = jnp.concatenate([w_key[...], w_value[...]], axis=1)

    def project(source, which, step):
        pieces = source[pl.ds(step * GROUPS, GROUPS)]
        raw = pieces[:, :rows, :].reshape(GROUPS * rows, width)
        normed = layer_norm(raw.astype(F32), atom_gain[...]).astype(BF)
        query = dot(normed, w_query[...]).astype(BF)
        keyval = dot(normed, w_kv).astype(BF)
        for at in range(GROUPS):
            block = position ^ which ^ reversed_bits(step * GROUPS + at, 2 * half_blocks)
            first = pl.multiple_of(block * rows, rows)
            part = slice(at * rows, (at + 1) * rows)
            updated[pl.ds(first, rows), :] = raw[part]
            queries[pl.ds(first, rows), :] = query[part]
            keys[pl.ds(first + HALF, rows), :] = keyval[part, :width]
            values[pl.ds(first + HALF, rows), :] = keyval[part, width:]
            offsets[block] = pieces[at, rows:, :].astype(F32)

    def project_step(step, carry):
        project(mine, 0, step)
        project(other, 1, step)
        return carry

    lax.fori_loop(0, half_blocks // GROUPS, project_step, 0)

    pooled[...] = jnp.zeros_like(pooled)
    head_of = iota((1, width), 1) // (width // HEADS)
    head_mask = [(head_of == h).astype(F32) for h in range(HEADS)]
    head_mask_bf = [m.astype(BF) for m in head_mask]
    ones = jnp.ones((window, width), BF)
    key_lane = iota((1, window), 1)
    key_lane_float = key_lane.astype(F32)
    scale = (width // HEADS) ** (-0.5) * LOG2E
    chunk = GROUPS * rows
    chunk_lane = iota((tokens, chunk), 1)

    def attend_step(step, carry):
        attended = []
        for at in range(GROUPS):
            block = step * GROUPS + at
            first = pl.multiple_of(block * rows, rows)
            query = queries[pl.ds(first, rows), :]
            key_part = keys[pl.ds(first, window), :]
            value_part = values[pl.ds(first, window), :]
            in_range = (key_lane >= HALF - first) & (key_lane < atoms + HALF - first)
            offset = offsets[block]
            bias = []
            for e in range(rows // QB):
                low = offset[e : e + 1, :]
                low = jnp.concatenate([low, low], axis=1)[:, :window] + (QB * e)
                seen = in_range & (key_lane_float >= low) & (key_lane_float < low + KW)
                bias.append(
                    jnp.broadcast_to(jnp.where(seen, 0.0, MASKED), (QB, window))
                )
            bias = jnp.concatenate(bias, axis=0)
            stacked = jnp.concatenate([query * m for m in head_mask_bf], axis=0)
            scores = dot_t(stacked, key_part)
            scores = jnp.concatenate(
                [scores[h * rows : (h + 1) * rows] + bias for h in range(HEADS)], axis=0
            )
            top = jnp.max(scores, axis=-1, keepdims=True)
            raised = jnp.exp2((scores - top) * scale).astype(BF)
            mixed = dot(raised, jnp.concatenate([value_part, ones], axis=1))
            total = sum(
                mixed[h * rows : (h + 1) * rows, :width] * head_mask[h] for h in range(HEADS)
            )
            weight = sum(
                mixed[h * rows : (h + 1) * rows, width:] * head_mask[h] for h in range(HEADS)
            )
            attended.append((total / weight).astype(BF))
        attended = jnp.concatenate(attended, axis=0)
        here = pl.multiple_of(step * chunk, chunk)
        fresh = (updated[pl.ds(here, chunk), :].astype(F32) + dot(attended, w_out[...])).astype(BF)
        updated[pl.ds(here, chunk), :] = fresh
        feature = jnp.maximum(dot(fresh, w_pool[...]), 0.0).astype(BF)
        begin = starts[...] - here
        member = (chunk_lane >= begin) & (chunk_lane < begin + counts[...])
        pooled[...] += dot(member.astype(F32).astype(BF), feature)
        return carry

    lax.fori_loop(0, atoms // chunk, attend_step, 0)

    single = (pooled[...] / counts[...].astype(F32)).astype(BF)
    singles[...] = single
    own_tokens = token_single.shape[0]
    pick = iota((own_tokens, tokens), 1) == iota((own_tokens, tokens), 0) + position * own_tokens
    token_single[...] = dot(pick.astype(F32).astype(BF), single).astype(BF)

    first = pl.multiple_of(position * rows, rows)
    atom_lane = iota((tokens, rows), 1) + first
    owner = (atom_lane >= starts[...]) & (atom_lane < starts[...] + counts[...])
    back = dot(single, w_back[...]).astype(BF)
    lifted = lax.dot_general(
        owner.astype(F32).astype(BF), back, (((0,), (0,)), ((), ())), preferred_element_type=F32
    )
    atom_out[...] = (updated[pl.ds(first, rows), :].astype(F32) + lifted).astype(BF)

    row_single = singles[pl.ds(pl.multiple_of(row * row_tokens, row_tokens), row_tokens), :]
    col_single = singles[pl.ds(pl.multiple_of(col * col_tokens, col_tokens), col_tokens), :]
    left = dot_t(row_single, w_left[...]).astype(BF)
    right = dot_t(col_single, w_right[...]).astype(BF)
    product_lane = iota((opm, opm * opm), 1)
    unit = iota((opm, opm * opm), 0)
    left_wide[...] = dot(left, (product_lane // opm == unit).astype(F32).astype(BF))
    right_wide[...] = dot(right, (product_lane % opm == unit).astype(F32).astype(BF))

    def pair_step(step, carry):
        here = pl.multiple_of(step * PAIR_ROWS, PAIR_ROWS)
        lefts = left_wide[pl.ds(here, PAIR_ROWS), :]
        rights = right_wide[...]
        products = jnp.concatenate(
            [(lefts[i : i + 1, :] * rights).astype(BF) for i in range(PAIR_ROWS)], axis=0
        )
        flat = pair_state[pl.ds(here, PAIR_ROWS)].reshape(PAIR_ROWS * col_tokens, pair_width)
        summed = flat.astype(F32) + dot(products, w_outer[...])
        normed = layer_norm(summed, pair_gain[...]).astype(BF)
        gate = dot(normed, w_gate[...])
        lift = dot(normed, w_lift[...])
        hidden = (gate * (0.5 + 0.5 * jnp.tanh(0.5 * gate)) * lift).astype(BF)
        result = (summed + dot(hidden, w_drop[...])).astype(BF)
        pair_out[pl.ds(here, PAIR_ROWS)] = result.reshape(PAIR_ROWS, col_tokens, pair_width)
        return carry

    lax.fori_loop(0, row_tokens // PAIR_ROWS, pair_step, 0)


def gather_blocks(block):
    devices = lax.axis_size(AXES)
    held = block[None]
    bit = devices // 2
    while bit > 1:
        held = jnp.concatenate([held, exchanged(held, bit)], axis=0)
        bit //= 2
    return held, exchanged(held, 1)


def exchanged(held, bit):
    return lax.ppermute(held, AXES, [(i, i ^ bit) for i in range(lax.axis_size(AXES))])


def per_device(
    atom_feats,
    key_starts,
    atom_counts,
    atom_gain,
    w_query,
    w_key,
    w_value,
    w_out,
    w_pool,
    w_back,
    pair_state,
    w_left,
    w_right,
    w_outer,
    pair_gain,
    w_gate,
    w_lift,
    w_drop,
):
    rows, width = atom_feats.shape
    devices = lax.axis_size(AXES)
    position = lax.axis_index(AXES)
    atoms = rows * devices
    tokens = atom_counts.shape[0]
    channels = w_pool.shape[1]
    blocks = rows // QB
    first_block = position * blocks
    offset = key_starts + HALF - QB * (first_block + jnp.arange(blocks, dtype=jnp.int32))
    rim = jnp.zeros((RIM, width), BF).at[:blocks].set(
        jnp.broadcast_to(offset.astype(BF)[:, None], (blocks, width))
    )
    mine, other = gather_blocks(jnp.concatenate([atom_feats, rim], axis=0))
    starts = jnp.cumsum(atom_counts, dtype=jnp.int32) - atom_counts
    opm = w_left.shape[1]
    vmem = pl.BlockSpec(memory_space=pltpu.VMEM)
    operands = (
        mine,
        other,
        starts[:, None],
        atom_counts[:, None],
        atom_gain[None],
        w_query,
        w_key,
        w_value,
        w_out,
        w_pool,
        w_back,
        pair_state,
        w_left.T,
        w_right.T,
        w_outer.reshape(opm * opm, -1),
        pair_gain[None],
        w_gate,
        w_lift,
        w_drop,
    )
    outputs = (
        jax.ShapeDtypeStruct(atom_feats.shape, BF),
        jax.ShapeDtypeStruct((tokens // devices, channels), BF),
        jax.ShapeDtypeStruct(pair_state.shape, BF),
    )
    scratch = [
        pltpu.VMEM((atoms, width), BF),
        pltpu.VMEM((atoms + 2 * HALF, width), BF),
        pltpu.VMEM((atoms + 2 * HALF, width), BF),
        pltpu.VMEM((devices, RIM, width), F32),
        pltpu.VMEM((atoms, width), BF),
        pltpu.VMEM((tokens, channels), F32),
        pltpu.VMEM((tokens, channels), BF),
        pltpu.VMEM((pair_state.shape[0], opm * opm), F32),
        pltpu.VMEM((pair_state.shape[1], opm * opm), F32),
    ]
    held = sum(math.prod(a.shape) * a.dtype.itemsize for a in operands + outputs)
    held += sum(math.prod(a.shape) * jnp.dtype(a.dtype).itemsize for a in scratch)
    return pl.pallas_call(
        kernel,
        out_shape=outputs,
        in_specs=[vmem] * len(operands),
        out_specs=(vmem,) * 3,
        scratch_shapes=scratch,
        compiler_params=pltpu.CompilerParams(vmem_limit_bytes=min(held + SPARE, MOST)),
        name="trunk_window",
    )(*operands)


def solution(mesh):
    in_specs = (
        P(("row", "col"), None),
        P(("row", "col")),
        P(),
        P(),
        P(),
        P(),
        P(),
        P(),
        P(),
        P(),
        P("row", "col", None),
        P(),
        P(),
        P(),
        P(),
        P(),
        P(),
        P(),
    )
    out_specs = (P(("row", "col"), None), P(("row", "col"), None), P("row", "col", None))
    return jax.shard_map(
        per_device, mesh=mesh, in_specs=in_specs, out_specs=out_specs, check_vma=False
    )
```

```python
import math

import jax
import jax.numpy as jnp
from jax import lax
from jax.experimental import pallas as pl
from jax.experimental.pallas import tpu as pltpu
from jax.sharding import PartitionSpec as P

HEADS = 4
QB = 32
KW = 128
EPSILON = 1e-05
HALF = KW // 2
RIM = 8
GROUPS = 4
PAIR_ROWS = 8
MASKED = -1e30
SPARE = 10 << 20
MOST = 63 << 20
LOG2E = 1.4426950408889634
AXES = ("row", "col")
BF = jnp.bfloat16
F32 = jnp.float32


def layer_norm(values, gain):
    mean_value = jnp.mean(values, axis=-1, keepdims=True)
    centred = values - mean_value
    variance = jnp.mean(centred * centred, axis=-1, keepdims=True)
    return centred * lax.rsqrt(variance + EPSILON) * gain


def dot(a, b):
    return jnp.dot(a, b, preferred_element_type=F32)


def dot_t(a, b):
    return lax.dot_general(a, b, (((1,), (1,)), ((), ())), preferred_element_type=F32)


def iota(shape, axis):
    return lax.broadcasted_iota(jnp.int32, shape, axis)


def kernel(
    mine,
    other,
    starts,
    counts,
    atom_gain,
    w_query,
    w_key,
    w_value,
    w_out,
    w_pool,
    w_back,
    pair_state,
    w_left,
    w_right,
    w_outer,
    pair_gain,
    w_gate,
    w_lift,
    w_drop,
    atom_out,
    token_single,
    pair_out,
    queries,
    keys,
    values,
    offsets,
    updated,
    pooled,
    singles,
    left_wide,
    right_wide,
):
    half_blocks, block_rows, width = mine.shape
    rows = block_rows - RIM
    atoms = 2 * half_blocks * rows
    tokens, channels = pooled.shape
    row_tokens, col_tokens, pair_width = pair_state.shape
    opm = w_left.shape[0]
    row, col = lax.axis_index("row"), lax.axis_index("col")
    position = row * lax.axis_size("col") + col
    window = rows + KW

    zeros = jnp.zeros((HALF, width), BF)
    for table in (keys, values):
        table[0:HALF, :] = zeros
        table[HALF + atoms : 2 * HALF + atoms, :] = zeros
    w_kv = jnp.concatenate([w_key[...], w_value[...]], axis=1)

    def project(source, which, step):
        pieces = source[pl.ds(step * GROUPS, GROUPS)]
        raw = pieces[:, :rows, :].reshape(GROUPS * rows, width)
        normed = layer_norm(raw.astype(F32), atom_gain[...]).astype(BF)
        query = dot(normed, w_query[...]).astype(BF)
        keyval = dot(normed, w_kv).astype(BF)
        for at in range(GROUPS):
            block = which * half_blocks + step * GROUPS + at
            first = pl.multiple_of(block * rows, rows)
            part = slice(at * rows, (at + 1) * rows)
            updated[pl.ds(first, rows), :] = raw[part]
            queries[pl.ds(first, rows), :] = query[part]
            keys[pl.ds(first + HALF, rows), :] = keyval[part, :width]
            values[pl.ds(first + HALF, rows), :] = keyval[part, width:]
            offsets[block] = pieces[at, rows:, :].astype(F32)

    def project_step(step, carry):
        project(mine, 0, step)
        project(other, 1, step)
        return carry

    lax.fori_loop(0, half_blocks // GROUPS, project_step, 0)

    pooled[...] = jnp.zeros_like(pooled)
    head_of = iota((1, width), 1) // (width // HEADS)
    head_mask = [(head_of == h).astype(F32) for h in range(HEADS)]
    head_mask_bf = [m.astype(BF) for m in head_mask]
    ones = jnp.ones((window, width), BF)
    key_lane = iota((1, window), 1)
    key_lane_float = key_lane.astype(F32)
    scale = (width // HEADS) ** (-0.5) * LOG2E
    chunk = GROUPS * rows
    chunk_lane = iota((tokens, chunk), 1)

    def attend_step(step, carry):
        attended = []
        for at in range(GROUPS):
            block = step * GROUPS + at
            first = pl.multiple_of(block * rows, rows)
            query = queries[pl.ds(first, rows), :]
            key_part = keys[pl.ds(first, window), :]
            value_part = values[pl.ds(first, window), :]
            in_range = (key_lane >= HALF - first) & (key_lane < atoms + HALF - first)
            offset = offsets[block]
            bias = []
            for e in range(rows // QB):
                low = offset[e : e + 1, :]
                low = jnp.concatenate([low, low], axis=1)[:, :window] + (QB * e)
                seen = in_range & (key_lane_float >= low) & (key_lane_float < low + KW)
                bias.append(
                    jnp.broadcast_to(jnp.where(seen, 0.0, MASKED), (QB, window))
                )
            bias = jnp.concatenate(bias, axis=0)
            stacked = jnp.concatenate([query * m for m in head_mask_bf], axis=0)
            scores = dot_t(stacked, key_part)
            scores = jnp.concatenate(
                [scores[h * rows : (h + 1) * rows] + bias for h in range(HEADS)], axis=0
            )
            top = jnp.max(scores, axis=-1, keepdims=True)
            raised = jnp.exp2((scores - top) * scale).astype(BF)
            mixed = dot(raised, jnp.concatenate([value_part, ones], axis=1))
            total = sum(
                mixed[h * rows : (h + 1) * rows, :width] * head_mask[h] for h in range(HEADS)
            )
            weight = sum(
                mixed[h * rows : (h + 1) * rows, width:] * head_mask[h] for h in range(HEADS)
            )
            attended.append((total / weight).astype(BF))
        attended = jnp.concatenate(attended, axis=0)
        here = pl.multiple_of(step * chunk, chunk)
        fresh = (updated[pl.ds(here, chunk), :].astype(F32) + dot(attended, w_out[...])).astype(BF)
        updated[pl.ds(here, chunk), :] = fresh
        feature = jnp.maximum(dot(fresh, w_pool[...]), 0.0).astype(BF)
        begin = starts[...] - here
        member = (chunk_lane >= begin) & (chunk_lane < begin + counts[...])
        pooled[...] += dot(member.astype(F32).astype(BF), feature)
        return carry

    lax.fori_loop(0, atoms // chunk, attend_step, 0)

    single = (pooled[...] / counts[...].astype(F32)).astype(BF)
    singles[...] = single
    own_tokens = token_single.shape[0]
    pick = iota((own_tokens, tokens), 1) == iota((own_tokens, tokens), 0) + position * own_tokens
    token_single[...] = dot(pick.astype(F32).astype(BF), single).astype(BF)

    first = pl.multiple_of(position * rows, rows)
    atom_lane = iota((tokens, rows), 1) + first
    owner = (atom_lane >= starts[...]) & (atom_lane < starts[...] + counts[...])
    back = dot(single, w_back[...]).astype(BF)
    lifted = lax.dot_general(
        owner.astype(F32).astype(BF), back, (((0,), (0,)), ((), ())), preferred_element_type=F32
    )
    atom_out[...] = (updated[pl.ds(first, rows), :].astype(F32) + lifted).astype(BF)

    row_single = singles[pl.ds(pl.multiple_of(row * row_tokens, row_tokens), row_tokens), :]
    col_single = singles[pl.ds(pl.multiple_of(col * col_tokens, col_tokens), col_tokens), :]
    left = dot_t(row_single, w_left[...]).astype(BF)
    right = dot_t(col_single, w_right[...]).astype(BF)
    product_lane = iota((opm, opm * opm), 1)
    unit = iota((opm, opm * opm), 0)
    left_wide[...] = dot(left, (product_lane // opm == unit).astype(F32).astype(BF))
    right_wide[...] = dot(right, (product_lane % opm == unit).astype(F32).astype(BF))

    def pair_step(step, carry):
        here = pl.multiple_of(step * PAIR_ROWS, PAIR_ROWS)
        lefts = left_wide[pl.ds(here, PAIR_ROWS), :]
        rights = right_wide[...]
        products = jnp.concatenate(
            [(lefts[i : i + 1, :] * rights).astype(BF) for i in range(PAIR_ROWS)], axis=0
        )
        flat = pair_state[pl.ds(here, PAIR_ROWS)].reshape(PAIR_ROWS * col_tokens, pair_width)
        summed = flat.astype(F32) + dot(products, w_outer[...])
        normed = layer_norm(summed, pair_gain[...]).astype(BF)
        gate = dot(normed, w_gate[...])
        lift = dot(normed, w_lift[...])
        hidden = (gate * (0.5 + 0.5 * jnp.tanh(0.5 * gate)) * lift).astype(BF)
        result = (summed + dot(hidden, w_drop[...])).astype(BF)
        pair_out[pl.ds(here, PAIR_ROWS)] = result.reshape(PAIR_ROWS, col_tokens, pair_width)
        return carry

    lax.fori_loop(0, row_tokens // PAIR_ROWS, pair_step, 0)


def gather_blocks(block):
    gathered = lax.all_gather(block, AXES)
    half = gathered.shape[0] // 2
    return gathered[:half], gathered[half:]


def per_device(
    atom_feats,
    key_starts,
    atom_counts,
    atom_gain,
    w_query,
    w_key,
    w_value,
    w_out,
    w_pool,
    w_back,
    pair_state,
    w_left,
    w_right,
    w_outer,
    pair_gain,
    w_gate,
    w_lift,
    w_drop,
):
    rows, width = atom_feats.shape
    devices = lax.axis_size(AXES)
    position = lax.axis_index(AXES)
    atoms = rows * devices
    tokens = atom_counts.shape[0]
    channels = w_pool.shape[1]
    blocks = rows // QB
    first_block = position * blocks
    offset = key_starts + HALF - QB * (first_block + jnp.arange(blocks, dtype=jnp.int32))
    rim = jnp.zeros((RIM, width), BF).at[:blocks].set(
        jnp.broadcast_to(offset.astype(BF)[:, None], (blocks, width))
    )
    mine, other = gather_blocks(jnp.concatenate([atom_feats, rim], axis=0))
    starts = jnp.cumsum(atom_counts, dtype=jnp.int32) - atom_counts
    opm = w_left.shape[1]
    vmem = pl.BlockSpec(memory_space=pltpu.VMEM)
    operands = (
        mine,
        other,
        starts[:, None],
        atom_counts[:, None],
        atom_gain[None],
        w_query,
        w_key,
        w_value,
        w_out,
        w_pool,
        w_back,
        pair_state,
        w_left.T,
        w_right.T,
        w_outer.reshape(opm * opm, -1),
        pair_gain[None],
        w_gate,
        w_lift,
        w_drop,
    )
    outputs = (
        jax.ShapeDtypeStruct(atom_feats.shape, BF),
        jax.ShapeDtypeStruct((tokens // devices, channels), BF),
        jax.ShapeDtypeStruct(pair_state.shape, BF),
    )
    scratch = [
        pltpu.VMEM((atoms, width), BF),
        pltpu.VMEM((atoms + 2 * HALF, width), BF),
        pltpu.VMEM((atoms + 2 * HALF, width), BF),
        pltpu.VMEM((devices, RIM, width), F32),
        pltpu.VMEM((atoms, width), BF),
        pltpu.VMEM((tokens, channels), F32),
        pltpu.VMEM((tokens, channels), BF),
        pltpu.VMEM((pair_state.shape[0], opm * opm), F32),
        pltpu.VMEM((pair_state.shape[1], opm * opm), F32),
    ]
    held = sum(math.prod(a.shape) * a.dtype.itemsize for a in operands + outputs)
    held += sum(math.prod(a.shape) * jnp.dtype(a.dtype).itemsize for a in scratch)
    return pl.pallas_call(
        kernel,
        out_shape=outputs,
        in_specs=[vmem] * len(operands),
        out_specs=(vmem,) * 3,
        scratch_shapes=scratch,
        compiler_params=pltpu.CompilerParams(vmem_limit_bytes=min(held + SPARE, MOST)),
        name="trunk_window",
    )(*operands)


def solution(mesh):
    in_specs = (
        P(("row", "col"), None),
        P(("row", "col")),
        P(),
        P(),
        P(),
        P(),
        P(),
        P(),
        P(),
        P(),
        P("row", "col", None),
        P(),
        P(),
        P(),
        P(),
        P(),
        P(),
        P(),
    )
    out_specs = (P(("row", "col"), None), P(("row", "col"), None), P("row", "col", None))
    return jax.shard_map(
        per_device, mesh=mesh, in_specs=in_specs, out_specs=out_specs, check_vma=False
    )
```

```python
import math

import jax
import jax.numpy as jnp
from jax import lax
from jax.experimental import pallas as pl
from jax.experimental.pallas import tpu as pltpu
from jax.sharding import PartitionSpec as P

HEADS = 4
QB = 32
KW = 128
EPSILON = 1e-05
HALF = KW // 2
FEWEST = 8
LANES = 128
SLOTS = 16
BLOCK = 24
DESTS = 32
PAIR_ROWS = 8
MASKED = -1e30
SPARE = 12 << 20
MOST = 60 << 20
LOG2E = 1.4426950408889634
AXES = ("row", "col")
BF = jnp.bfloat16
F32 = jnp.float32


def layer_norm(values, gain):
    mean_value = jnp.mean(values, axis=-1, keepdims=True)
    centred = values - mean_value
    variance = jnp.mean(centred * centred, axis=-1, keepdims=True)
    return centred * lax.rsqrt(variance + EPSILON) * gain


def dot(a, b):
    return jnp.dot(a, b, preferred_element_type=F32)


def dot_t(a, b):
    return lax.dot_general(a, b, (((1,), (1,)), ((), ())), preferred_element_type=F32)


def iota(shape, axis):
    return lax.broadcasted_iota(jnp.int32, shape, axis)


def flag(mask):
    return jnp.where(mask, 1.0, 0.0).astype(BF)


def atom_kernel(
    own,
    sibling,
    neighbour,
    key_starts,
    counts,
    counts_folded,
    atom_gain,
    w_query,
    w_key,
    w_value,
    w_out,
    w_pool,
    w_back,
    w_left,
    w_right,
    payload,
    updated,
    slot_back,
    slot_last,
    slot_member,
):
    rows, width = own.shape
    tokens = counts.shape[1]
    channels = w_pool.shape[1]
    tiles = channels // LANES
    opm = w_left.shape[0]
    devices = payload.shape[0] // BLOCK
    atoms = rows * devices
    own_tokens = tokens // devices
    token_rows = own_tokens * tiles
    slots = rows // FEWEST + 1
    position = lax.axis_index("row") * lax.axis_size("col") + lax.axis_index("col")
    first = position * rows
    even = position % 2 == 0

    own_float = own[...].astype(F32)
    sibling_float = sibling[...].astype(F32)
    neighbour_float = neighbour[...].astype(F32)
    low = jnp.where(even, neighbour_float, sibling_float)
    high = jnp.where(even, sibling_float, neighbour_float)
    extended = jnp.concatenate([low, own_float, high], axis=0)
    normed = layer_norm(extended, atom_gain[...]).astype(BF)
    keyval = dot(normed, jnp.concatenate([w_key[...], w_value[...]], axis=1)).astype(BF)
    query = dot(normed[rows : 2 * rows], w_query[...]).astype(BF)
    window = rows + KW
    key_lane = iota((1, window), 1)
    key_index = key_lane + (first - HALF)
    in_range = (key_index >= 0) & (key_index < atoms)
    bias = []
    for e in range(rows // QB):
        low_key = key_starts[0:1, e : e + 1]
        seen = in_range & (key_index >= low_key) & (key_index < low_key + KW)
        bias.append(jnp.broadcast_to(jnp.where(seen, 0.0, MASKED), (QB, window)))
    bias = jnp.concatenate(bias, axis=0)
    head_of = iota((1, width), 1) // (width // HEADS)
    head_mask = [(head_of == h).astype(F32) for h in range(HEADS)]
    stacked = jnp.concatenate([query * m.astype(BF) for m in head_mask], axis=0)
    scores = dot_t(stacked, keyval[:, :width])
    scores = scores + jnp.concatenate([bias] * HEADS, axis=0)
    top = jnp.max(scores, axis=-1, keepdims=True)
    scale = (width // HEADS) ** (-0.5) * LOG2E
    raised = jnp.exp2((scores - top) * scale).astype(BF)
    ones = jnp.ones((window, width), BF)
    mixed = dot(raised, jnp.concatenate([keyval[:, width:], ones], axis=1))
    total = sum(mixed[h * rows : (h + 1) * rows, :width] * head_mask[h] for h in range(HEADS))
    weight = sum(mixed[h * rows : (h + 1) * rows, width:] * head_mask[h] for h in range(HEADS))
    attended = (total / weight).astype(BF)
    fresh = (own_float + dot(attended, w_out[...])).astype(BF)
    updated[...] = fresh
    feature = jnp.maximum(dot(fresh, w_pool[...]), 0.0).astype(BF)

    counts_wide = jnp.broadcast_to(counts[...].astype(F32), (tiles * rows, tokens)).astype(BF)
    counts_lane = counts_wide[:LANES]
    folded = counts_folded[...].astype(F32).astype(BF)
    folds = folded.shape[0]
    upper = flag(iota((LANES, LANES), 0) <= iota((LANES, LANES), 1))
    within = dot(folded, upper)
    whole = dot(folded, jnp.ones((LANES, LANES), BF))
    base = jnp.zeros((1, 1), F32)
    before = jnp.zeros((1, LANES), F32)
    first_float = first.astype(F32)
    for fold in range(folds):
        ended = within[fold : fold + 1] + before <= first_float
        base = base + jnp.sum(jnp.where(ended, 1.0, 0.0), axis=1, keepdims=True)
        before = before + whole[fold : fold + 1]

    token_lane = iota((SLOTS, tokens), 1).astype(F32)
    slot_token = iota((SLOTS, tokens), 0).astype(F32) + base
    slot_end = dot_t(flag(token_lane <= slot_token), counts_lane)
    slot_start = dot_t(flag(token_lane < slot_token), counts_lane)
    atom_lane = iota((SLOTS, rows), 1).astype(F32) + first_float
    member = flag((atom_lane >= slot_start[:, :rows]) & (atom_lane < slot_end[:, :rows]))
    slot_member[...] = member
    slot_count = jnp.maximum(slot_end - slot_start, 1.0)
    slot_single = (
        dot(member, feature) / jnp.concatenate([slot_count] * tiles, axis=1)
    ).astype(BF)
    w_sides = jnp.concatenate(
        [w_left[...], w_right[...], jnp.zeros((LANES - 2 * opm, channels), BF)], axis=0
    )
    sides = dot_t(slot_single, w_sides).astype(BF)
    backs = dot(slot_single, w_back[...])
    slot_back[...] = backs
    last_atom = first_float + (rows - 1)
    last = jnp.where((slot_start <= last_atom) & (slot_end > last_atom), 1.0, 0.0)
    slot_last[...] = last
    to_before = backs[0:1] * jnp.where(slot_start[0:1] < first_float, 1.0, 0.0)
    goes_on = last * jnp.where(slot_end > first_float + rows, 1.0, 0.0)
    to_after = jnp.sum(backs * goes_on, axis=0, keepdims=True)
    spot = iota((SLOTS, LANES), 0)
    edges = jnp.where(spot == 0, to_before, jnp.where(spot == 1, to_after, 0.0)).astype(BF)
    shared = jnp.concatenate([sides, edges], axis=0)
    feature_tiles = jnp.concatenate(
        [feature[:, k * LANES : (k + 1) * LANES] for k in range(tiles)], axis=0
    )

    def send_step(step, carry):
        def place(lanes, axis):
            return iota((DESTS, BLOCK, lanes), axis).reshape(DESTS * BLOCK, lanes)

        def token_of(lanes):
            return (place(lanes, 0) + step * DESTS) * own_tokens + place(lanes, 1) % own_tokens

        token_at = iota((DESTS * BLOCK, tokens), 1)
        row_token = token_of(tokens)
        row_end = dot_t(flag(token_at <= row_token), counts_wide)
        row_start = dot_t(flag(token_at < row_token), counts_wide)
        lanes = tiles * rows
        lane = iota((DESTS * BLOCK, lanes), 1)
        atom = (lane % rows + first).astype(F32)
        tile_fits = place(lanes, 1) // own_tokens == lane // rows
        picks = flag(tile_fits & (atom >= row_start) & (atom < row_end))
        row_count = jnp.maximum(row_end - row_start, 1.0)[:, :LANES]
        singles = dot(picks, feature_tiles) / row_count
        dest, spot = place(2 * SLOTS, 0) + step * DESTS, place(2 * SLOTS, 1)
        source = iota((DESTS * BLOCK, 2 * SLOTS), 1)
        is_slot = (source < slots) & (spot == token_rows + source)
        edge = spot == token_rows + slots
        is_before = (source == SLOTS) & edge & (dest == position - 1)
        is_after = (source == SLOTS + 1) & edge & (dest == position + 1)
        part = (singles + dot(flag(is_slot | is_before | is_after), shared)).astype(BF)
        if devices == DESTS:
            payload[...] = part
        else:
            here = pl.multiple_of(step * (DESTS * BLOCK), DESTS * BLOCK)
            payload[pl.ds(here, DESTS * BLOCK), :] = part
        return carry

    if devices == DESTS:
        send_step(0, 0)
    else:
        lax.fori_loop(0, devices // DESTS, send_step, 0)


def pair_kernel(
    arrived,
    adder,
    updated,
    slot_back,
    slot_last,
    slot_member,
    pair_state,
    w_outer,
    pair_gain,
    w_gate,
    w_lift,
    w_drop,
    atom_out,
    token_single,
    pair_out,
):
    row_tokens, col_tokens, pair_width = pair_state.shape
    own_tokens, channels = token_single.shape
    tiles = channels // LANES
    token_rows = own_tokens * tiles
    opm = math.isqrt(w_outer.shape[0])
    added = dot(adder[...], arrived[...])
    left = added[SLOTS : SLOTS + row_tokens, :opm].astype(BF)
    right = added[SLOTS + row_tokens :, opm : 2 * opm].astype(BF)
    product_lane = iota((opm, opm * opm), 1)
    unit = iota((opm, opm * opm), 0)
    left_wide = dot(left, flag(product_lane // opm == unit))
    right_wide = dot(right, flag(product_lane % opm == unit))

    def pair_rows(lefts, here):
        products = jnp.concatenate(
            [(lefts[i : i + 1, :] * right_wide).astype(BF) for i in range(PAIR_ROWS)], axis=0
        )
        flat = pair_state[pl.ds(here, PAIR_ROWS)].reshape(PAIR_ROWS * col_tokens, pair_width)
        summed = flat.astype(F32) + dot(products, w_outer[...])
        normed = layer_norm(summed, pair_gain[...]).astype(BF)
        gate = dot(normed, w_gate[...])
        lift = dot(normed, w_lift[...])
        hidden = (gate * (0.5 + 0.5 * jnp.tanh(0.5 * gate)) * lift).astype(BF)
        result = (summed + dot(hidden, w_drop[...])).astype(BF)
        pair_out[pl.ds(here, PAIR_ROWS)] = result.reshape(PAIR_ROWS, col_tokens, pair_width)

    for step in range(row_tokens // PAIR_ROWS):
        here = step * PAIR_ROWS
        pair_rows(left_wide[here : here + PAIR_ROWS], here)

    token_single[...] = jnp.concatenate(
        [added[k * own_tokens : (k + 1) * own_tokens] for k in range(tiles)], axis=1
    ).astype(BF)
    spot = iota((SLOTS, LANES), 0)
    from_before = jnp.where(spot == 0, added[token_rows : token_rows + 1], 0.0)
    from_after = slot_last[...] * added[token_rows + 1 : token_rows + 2]
    back = (slot_back[...] + from_before + from_after).astype(BF)
    lifted = lax.dot_general(
        slot_member[...], back, (((0,), (0,)), ((), ())), preferred_element_type=F32
    )
    atom_out[...] = (updated[...].astype(F32) + lifted).astype(BF)


def adder_matrix(atom_counts, devices, rows, token_rows, row_tokens, col_tokens):
    position = lax.axis_index(AXES)
    slots = rows // FEWEST + 1
    ends = jnp.cumsum(atom_counts, dtype=jnp.int32)
    block = jnp.arange(devices, dtype=jnp.int32)
    base = jnp.sum((ends[None, :] <= (block * rows)[:, None]).astype(jnp.int32), axis=1)
    spot = jnp.arange(BLOCK, dtype=jnp.int32)
    is_slot = (spot >= token_rows) & (spot < token_rows + slots)
    token = jnp.where(is_slot[None, :], base[:, None] + (spot - token_rows)[None, :], -1)
    token = token.reshape(1, -1)
    place = jnp.arange(devices * BLOCK, dtype=jnp.int32)[None, :]
    line = jnp.arange(SLOTS, dtype=jnp.int32)[:, None]
    side = jnp.where(line == token_rows, position - 1, position + 1)
    edge = (line >= token_rows) & (line < token_rows + 2)
    fixed = jnp.where(
        edge,
        place == side * BLOCK + token_rows + slots,
        (place % BLOCK == line) & (line < token_rows),
    )
    first_row = lax.axis_index("row") * row_tokens
    first_col = lax.axis_index("col") * col_tokens
    lefts = token == (first_row + jnp.arange(row_tokens, dtype=jnp.int32))[:, None]
    rights = token == (first_col + jnp.arange(col_tokens, dtype=jnp.int32))[:, None]
    return jnp.concatenate([fixed, lefts, rights], axis=0).astype(BF)


def call(kernel, name, operands, outputs):
    vmem = pl.BlockSpec(memory_space=pltpu.VMEM)
    held = sum(math.prod(a.shape) * a.dtype.itemsize for a in operands + outputs)
    return pl.pallas_call(
        kernel,
        out_shape=outputs,
        in_specs=[vmem] * len(operands),
        out_specs=(vmem,) * len(outputs),
        compiler_params=pltpu.CompilerParams(vmem_limit_bytes=min(2 * held + SPARE, MOST)),
        name=name,
    )(*operands)


def per_device(
    atom_feats,
    key_starts,
    atom_counts,
    atom_gain,
    w_query,
    w_key,
    w_value,
    w_out,
    w_pool,
    w_back,
    pair_state,
    w_left,
    w_right,
    w_outer,
    pair_gain,
    w_gate,
    w_lift,
    w_drop,
):
    rows, width = atom_feats.shape
    devices = lax.axis_size(AXES)
    tokens = atom_counts.shape[0]
    channels = w_pool.shape[1]
    opm = w_left.shape[1]
    own_tokens = tokens // devices
    row_tokens, col_tokens, _ = pair_state.shape
    token_rows = own_tokens * channels // LANES
    sibling = lax.ppermute(atom_feats, AXES, [(i, i ^ 1) for i in range(devices)])
    across = [(i, i + 1) for i in range(1, devices - 1, 2)]
    neighbour = lax.ppermute(atom_feats, AXES, across + [(j, i) for i, j in across])
    payload, updated, slot_back, slot_last, slot_member = call(
        atom_kernel,
        "atoms",
        (
            atom_feats,
            sibling,
            neighbour,
            key_starts[None],
            atom_counts[None],
            atom_counts.reshape(-1, LANES),
            atom_gain[None],
            w_query,
            w_key,
            w_value,
            w_out,
            w_pool,
            w_back,
            w_left.T,
            w_right.T,
        ),
        (
            jax.ShapeDtypeStruct((devices * BLOCK, LANES), BF),
            jax.ShapeDtypeStruct((rows, width), BF),
            jax.ShapeDtypeStruct((SLOTS, width), F32),
            jax.ShapeDtypeStruct((SLOTS, width), F32),
            jax.ShapeDtypeStruct((SLOTS, rows), BF),
        ),
    )
    arrived = lax.all_to_all(payload.reshape(devices, BLOCK, LANES), AXES, 0, 0)
    adder = adder_matrix(atom_counts, devices, rows, token_rows, row_tokens, col_tokens)
    return call(
        pair_kernel,
        "pairs",
        (
            arrived.reshape(devices * BLOCK, LANES),
            adder,
            updated,
            slot_back,
            slot_last,
            slot_member,
            pair_state,
            w_outer.reshape(opm * opm, -1),
            pair_gain[None],
            w_gate,
            w_lift,
            w_drop,
        ),
        (
            jax.ShapeDtypeStruct(atom_feats.shape, BF),
            jax.ShapeDtypeStruct((own_tokens, channels), BF),
            jax.ShapeDtypeStruct(pair_state.shape, BF),
        ),
    )


def solution(mesh):
    in_specs = (
        P(("row", "col"), None),
        P(("row", "col")),
        P(),
        P(),
        P(),
        P(),
        P(),
        P(),
        P(),
        P(),
        P("row", "col", None),
        P(),
        P(),
        P(),
        P(),
        P(),
        P(),
        P(),
    )
    out_specs = (P(("row", "col"), None), P(("row", "col"), None), P("row", "col", None))
    return jax.shard_map(
        per_device, mesh=mesh, in_specs=in_specs, out_specs=out_specs, check_vma=False
    )
```

```python
import math

import jax
import jax.numpy as jnp
from jax import lax
from jax.experimental import pallas as pl
from jax.experimental.pallas import tpu as pltpu
from jax.sharding import PartitionSpec as P

HEADS = 4
QB = 32
KW = 128
EPSILON = 1e-05
HALF = KW // 2
FEWEST = 8
LANES = 128
SLOTS = 16
BLOCK = 24
DESTS = 32
PAIR_ROWS = 8
MASKED = -1e30
SPARE = 12 << 20
MOST = 60 << 20
LOG2E = 1.4426950408889634
AXES = ("row", "col")
BF = jnp.bfloat16
F32 = jnp.float32


def layer_norm(values, gain):
    mean_value = jnp.mean(values, axis=-1, keepdims=True)
    centred = values - mean_value
    variance = jnp.mean(centred * centred, axis=-1, keepdims=True)
    return centred * lax.rsqrt(variance + EPSILON) * gain


def dot(a, b):
    return jnp.dot(a, b, preferred_element_type=F32)


def dot_t(a, b):
    return lax.dot_general(a, b, (((1,), (1,)), ((), ())), preferred_element_type=F32)


def iota(shape, axis):
    return lax.broadcasted_iota(jnp.int32, shape, axis)


def flag(mask):
    return jnp.where(mask, 1.0, 0.0).astype(BF)


def place():
    return lax.axis_index("row") * lax.axis_size("col") + lax.axis_index("col")


def each_part(devices, step):
    if devices == DESTS:
        step(0)
    else:

        def body(at, carry):
            step(at)
            return carry

        lax.fori_loop(0, devices // DESTS, body, 0)


def part_rows(devices, at):
    size = DESTS * BLOCK
    if devices == DESTS:
        return pl.ds(0, size)
    return pl.ds(pl.multiple_of(at * size, size), size)


def ready_kernel(
    own,
    sibling,
    key_starts,
    counts,
    counts_folded,
    atom_gain,
    pair_gain,
    w_query,
    w_key,
    w_value,
    own_float,
    keyval,
    stacked,
    scores,
    top,
    far_bias,
    picks,
    row_scale,
    selects,
    member,
    slot_scale,
    before,
    goes_on,
    last,
    atom_gain_kept,
    pair_gain_kept,
):
    rows, width = own.shape
    tokens = counts.shape[1]
    tiles = picks.shape[1] // rows
    devices = picks.shape[0] // BLOCK
    atoms = rows * devices
    own_tokens = tokens // devices
    token_rows = own_tokens * tiles
    slots = rows // FEWEST + 1
    position = place()
    first = position * rows
    even = position % 2 == 0

    atom_gain_kept[...] = atom_gain[...]
    pair_gain_kept[...] = pair_gain[...]
    raw = jnp.concatenate([own[...].astype(F32), sibling[...].astype(F32)], axis=0)
    own_float[...] = raw[:rows]
    normed = layer_norm(raw, atom_gain[...]).astype(BF)
    near = dot(normed, jnp.concatenate([w_key[...], w_value[...]], axis=1)).astype(BF)
    keyval[...] = near
    query = dot(normed[:rows], w_query[...]).astype(BF)
    head_of = iota((1, width), 1) // (width // HEADS)
    heads = jnp.concatenate([query * flag(head_of == h) for h in range(HEADS)], axis=0)
    stacked[...] = heads
    near_lane = iota((1, 2 * rows), 1)
    side = jnp.where(even, 0, -2 * rows)
    near_index = first + near_lane + jnp.where(near_lane < rows, 0, side)
    far_index = first + jnp.where(even, -rows, rows) + iota((1, rows), 1)
    near_bias, bias = [], []
    for e in range(rows // QB):
        low = key_starts[0:1, e : e + 1]
        seen = (near_index >= low) & (near_index < low + KW)
        near_bias.append(jnp.broadcast_to(jnp.where(seen, 0.0, MASKED), (QB, 2 * rows)))
        seen = (far_index >= low) & (far_index < low + KW)
        seen = seen & (far_index >= 0) & (far_index < atoms)
        bias.append(jnp.broadcast_to(jnp.where(seen, 0.0, MASKED), (QB, rows)))
    far_bias[...] = jnp.concatenate(bias, axis=0)
    raw_scores = dot_t(heads, near[:, :width]) + jnp.concatenate(near_bias * HEADS, axis=0)
    scores[...] = raw_scores
    top[...] = jnp.max(raw_scores, axis=-1, keepdims=True)

    counts_wide = jnp.broadcast_to(counts[...].astype(F32), (tiles * rows, tokens)).astype(BF)
    counts_lane = counts_wide[:LANES]
    folded = counts_folded[...].astype(F32).astype(BF)
    upper = flag(iota((LANES, LANES), 0) <= iota((LANES, LANES), 1))
    within = dot(folded, upper)
    whole = dot(folded, jnp.ones((LANES, LANES), BF))
    base = jnp.zeros((1, 1), F32)
    passed = jnp.zeros((1, LANES), F32)
    first_float = first.astype(F32)
    for fold in range(folded.shape[0]):
        ended = within[fold : fold + 1] + passed <= first_float
        base = base + jnp.sum(jnp.where(ended, 1.0, 0.0), axis=1, keepdims=True)
        passed = passed + whole[fold : fold + 1]

    token_lane = iota((SLOTS, tokens), 1).astype(F32)
    slot_token = iota((SLOTS, tokens), 0).astype(F32) + base
    slot_end = dot_t(flag(token_lane <= slot_token), counts_lane)
    slot_start = dot_t(flag(token_lane < slot_token), counts_lane)
    atom_lane = iota((SLOTS, rows), 1).astype(F32) + first_float
    member[...] = flag((atom_lane >= slot_start[:, :rows]) & (atom_lane < slot_end[:, :rows]))
    slot_scale[...] = 1.0 / jnp.maximum(slot_end - slot_start, 1.0)
    last_atom = first_float + (rows - 1)
    is_last = jnp.where((slot_start <= last_atom) & (slot_end > last_atom), 1.0, 0.0)
    last[...] = is_last
    goes_on[...] = is_last * jnp.where(slot_end > first_float + rows, 1.0, 0.0)
    is_first = iota((SLOTS, LANES), 0) == 0
    before[...] = jnp.where(is_first & (slot_start < first_float), 1.0, 0.0)

    def rows_step(at):
        def spread(lanes, axis):
            return iota((DESTS, BLOCK, lanes), axis).reshape(DESTS * BLOCK, lanes)

        here = part_rows(devices, at)
        token_at = iota((DESTS * BLOCK, tokens), 1)
        row_token = (spread(tokens, 0) + at * DESTS) * own_tokens + spread(tokens, 1) % own_tokens
        row_end = dot_t(flag(token_at <= row_token), counts_wide)
        row_start = dot_t(flag(token_at < row_token), counts_wide)
        lanes = tiles * rows
        lane = iota((DESTS * BLOCK, lanes), 1)
        atom = (lane % rows + first).astype(F32)
        tile_fits = spread(lanes, 1) // own_tokens == lane // rows
        picks[here, :] = flag(tile_fits & (atom >= row_start) & (atom < row_end))
        row_scale[here, :] = 1.0 / jnp.maximum(row_end - row_start, 1.0)[:, :LANES]
        dest, spot = spread(2 * SLOTS, 0) + at * DESTS, spread(2 * SLOTS, 1)
        source = iota((DESTS * BLOCK, 2 * SLOTS), 1)
        is_slot = (source < slots) & (spot == token_rows + source)
        edge = spot == token_rows + slots
        is_before = (source == SLOTS) & edge & (dest == position - 1)
        is_after = (source == SLOTS + 1) & edge & (dest == position + 1)
        selects[here, :] = flag(is_slot | is_before | is_after)

    each_part(devices, rows_step)


def atom_kernel(
    neighbour,
    own_float,
    keyval,
    stacked,
    scores,
    top,
    far_bias,
    picks,
    row_scale,
    selects,
    member,
    slot_scale,
    before,
    goes_on,
    atom_gain,
    w_key,
    w_value,
    w_out,
    w_pool,
    w_back,
    w_left,
    w_right,
    payload,
    updated,
    slot_back,
):
    rows, width = own_float.shape
    channels = w_pool.shape[1]
    tiles = channels // LANES
    opm = w_left.shape[0]
    devices = payload.shape[0] // BLOCK
    normed = layer_norm(neighbour[...].astype(F32), atom_gain[...]).astype(BF)
    far = dot(normed, jnp.concatenate([w_key[...], w_value[...]], axis=1)).astype(BF)
    far_scores = dot_t(stacked[...], far[:, :width])
    far_scores = far_scores + jnp.concatenate([far_bias[...]] * HEADS, axis=0)
    most = jnp.maximum(top[...], jnp.max(far_scores, axis=-1, keepdims=True))
    scale = (width // HEADS) ** (-0.5) * LOG2E
    raised = jnp.concatenate(
        [
            jnp.exp2((scores[...] - most) * scale).astype(BF),
            jnp.exp2((far_scores - most) * scale).astype(BF),
        ],
        axis=1,
    )
    values = jnp.concatenate([keyval[:, width:], far[:, width:]], axis=0)
    mixed = dot(raised, jnp.concatenate([values, jnp.ones((3 * rows, width), BF)], axis=1))
    head_of = iota((1, width), 1) // (width // HEADS)
    head_mask = [(head_of == h).astype(F32) for h in range(HEADS)]
    total = sum(mixed[h * rows : (h + 1) * rows, :width] * head_mask[h] for h in range(HEADS))
    weight = sum(mixed[h * rows : (h + 1) * rows, width:] * head_mask[h] for h in range(HEADS))
    attended = (total / weight).astype(BF)
    fresh = (own_float[...] + dot(attended, w_out[...])).astype(BF)
    updated[...] = fresh
    feature = jnp.maximum(dot(fresh, w_pool[...]), 0.0).astype(BF)
    feature_tiles = jnp.concatenate(
        [feature[:, k * LANES : (k + 1) * LANES] for k in range(tiles)], axis=0
    )
    slot_single = (
        dot(member[...], feature) * jnp.concatenate([slot_scale[...]] * tiles, axis=1)
    ).astype(BF)
    w_sides = jnp.concatenate(
        [w_left[...], w_right[...], jnp.zeros((LANES - 2 * opm, channels), BF)], axis=0
    )
    sides = dot_t(slot_single, w_sides).astype(BF)
    backs = dot(slot_single, w_back[...])
    slot_back[...] = backs
    to_before = jnp.sum(backs * before[...], axis=0, keepdims=True)
    to_after = jnp.sum(backs * goes_on[...], axis=0, keepdims=True)
    spot = iota((SLOTS, LANES), 0)
    edges = jnp.where(spot == 0, to_before, jnp.where(spot == 1, to_after, 0.0)).astype(BF)
    shared = jnp.concatenate([sides, edges], axis=0)

    def send_step(at):
        here = part_rows(devices, at)
        singles = dot(picks[here, :], feature_tiles) * row_scale[here, :]
        payload[here, :] = (singles + dot(selects[here, :], shared)).astype(BF)

    each_part(devices, send_step)


def pair_kernel(
    arrived,
    adder,
    updated,
    slot_back,
    slot_last,
    slot_member,
    pair_state,
    w_outer,
    pair_gain,
    w_gate,
    w_lift,
    w_drop,
    atom_out,
    token_single,
    pair_out,
):
    row_tokens, col_tokens, pair_width = pair_state.shape
    own_tokens, channels = token_single.shape
    tiles = channels // LANES
    token_rows = own_tokens * tiles
    opm = math.isqrt(w_outer.shape[0])
    added = dot(adder[...], arrived[...])
    half_gate = w_gate[...] * jnp.asarray(0.5, BF)
    left = added[SLOTS : SLOTS + row_tokens, :opm].astype(BF)
    right = added[SLOTS + row_tokens :, opm : 2 * opm].astype(BF)
    product_lane = iota((opm, opm * opm), 1)
    unit = iota((opm, opm * opm), 0)
    left_wide = dot(left, flag(product_lane // opm == unit))
    right_wide = dot(right, flag(product_lane % opm == unit))

    def pair_rows(lefts, here):
        products = jnp.concatenate(
            [(lefts[i : i + 1, :] * right_wide).astype(BF) for i in range(PAIR_ROWS)], axis=0
        )
        flat = pair_state[pl.ds(here, PAIR_ROWS)].reshape(PAIR_ROWS * col_tokens, pair_width)
        summed = flat.astype(F32) + dot(products, w_outer[...])
        normed = layer_norm(summed, pair_gain[...]).astype(BF)
        gate = dot(normed, half_gate)
        lift = dot(normed, w_lift[...])
        hidden = (gate * lift * (1.0 + jnp.tanh(gate))).astype(BF)
        result = (summed + dot(hidden, w_drop[...])).astype(BF)
        pair_out[pl.ds(here, PAIR_ROWS)] = result.reshape(PAIR_ROWS, col_tokens, pair_width)

    for step in range(row_tokens // PAIR_ROWS):
        here = step * PAIR_ROWS
        pair_rows(left_wide[here : here + PAIR_ROWS], here)

    token_single[...] = jnp.concatenate(
        [added[k * own_tokens : (k + 1) * own_tokens] for k in range(tiles)], axis=1
    ).astype(BF)
    spot = iota((SLOTS, LANES), 0)
    from_before = jnp.where(spot == 0, added[token_rows : token_rows + 1], 0.0)
    from_after = slot_last[...] * added[token_rows + 1 : token_rows + 2]
    back = (slot_back[...] + from_before + from_after).astype(BF)
    lifted = lax.dot_general(
        slot_member[...], back, (((0,), (0,)), ((), ())), preferred_element_type=F32
    )
    atom_out[...] = (updated[...].astype(F32) + lifted).astype(BF)


def adder_matrix(atom_counts, devices, rows, token_rows, row_tokens, col_tokens):
    position = lax.axis_index(AXES)
    slots = rows // FEWEST + 1
    ends = jnp.cumsum(atom_counts, dtype=jnp.int32)
    block = jnp.arange(devices, dtype=jnp.int32)
    base = jnp.sum((ends[None, :] <= (block * rows)[:, None]).astype(jnp.int32), axis=1)
    spot = jnp.arange(BLOCK, dtype=jnp.int32)
    is_slot = (spot >= token_rows) & (spot < token_rows + slots)
    token = jnp.where(is_slot[None, :], base[:, None] + (spot - token_rows)[None, :], -1)
    token = token.reshape(1, -1)
    place = jnp.arange(devices * BLOCK, dtype=jnp.int32)[None, :]
    line = jnp.arange(SLOTS, dtype=jnp.int32)[:, None]
    side = jnp.where(line == token_rows, position - 1, position + 1)
    edge = (line >= token_rows) & (line < token_rows + 2)
    fixed = jnp.where(
        edge,
        place == side * BLOCK + token_rows + slots,
        (place % BLOCK == line) & (line < token_rows),
    )
    first_row = lax.axis_index("row") * row_tokens
    first_col = lax.axis_index("col") * col_tokens
    lefts = token == (first_row + jnp.arange(row_tokens, dtype=jnp.int32))[:, None]
    rights = token == (first_col + jnp.arange(col_tokens, dtype=jnp.int32))[:, None]
    return jnp.concatenate([fixed, lefts, rights], axis=0).astype(BF)


def call(kernel, name, operands, outputs):
    vmem = pl.BlockSpec(memory_space=pltpu.VMEM)
    held = sum(math.prod(a.shape) * a.dtype.itemsize for a in operands + outputs)
    return pl.pallas_call(
        kernel,
        out_shape=outputs,
        in_specs=[vmem] * len(operands),
        out_specs=(vmem,) * len(outputs),
        compiler_params=pltpu.CompilerParams(vmem_limit_bytes=min(2 * held + SPARE, MOST)),
        name=name,
    )(*operands)


def per_device(
    atom_feats,
    key_starts,
    atom_counts,
    atom_gain,
    w_query,
    w_key,
    w_value,
    w_out,
    w_pool,
    w_back,
    pair_state,
    w_left,
    w_right,
    w_outer,
    pair_gain,
    w_gate,
    w_lift,
    w_drop,
):
    rows, width = atom_feats.shape
    devices = lax.axis_size(AXES)
    tokens = atom_counts.shape[0]
    channels = w_pool.shape[1]
    opm = w_left.shape[1]
    own_tokens = tokens // devices
    row_tokens, col_tokens, _ = pair_state.shape
    token_rows = own_tokens * channels // LANES
    across = [(i, i + 1) for i in range(1, devices - 1, 2)]
    neighbour = lax.ppermute(atom_feats, AXES, across + [(j, i) for i, j in across])
    sibling = lax.ppermute(atom_feats, AXES, [(i, i ^ 1) for i in range(devices)])
    tiles = channels // LANES

    def held(*shape, dtype=F32):
        return jax.ShapeDtypeStruct(shape, dtype)

    ready = call(
        ready_kernel,
        "ready",
        (
            atom_feats,
            sibling,
            key_starts[None],
            atom_counts[None],
            atom_counts.reshape(-1, LANES),
            atom_gain[None],
            pair_gain[None],
            w_query,
            w_key,
            w_value,
        ),
        (
            held(rows, width),
            held(2 * rows, 2 * width, dtype=BF),
            held(HEADS * rows, width, dtype=BF),
            held(HEADS * rows, 2 * rows),
            held(HEADS * rows, 1),
            held(rows, rows),
            held(devices * BLOCK, tiles * rows, dtype=BF),
            held(devices * BLOCK, LANES),
            held(devices * BLOCK, 2 * SLOTS, dtype=BF),
            held(SLOTS, rows, dtype=BF),
            held(SLOTS, LANES),
            held(SLOTS, LANES),
            held(SLOTS, LANES),
            held(SLOTS, LANES),
            held(1, width),
            held(1, LANES),
        ),
    )
    slot_member, slot_last, atom_gain_kept, pair_gain_kept = ready[9], ready[13], ready[14], ready[15]
    payload, updated, slot_back = call(
        atom_kernel,
        "atoms",
        (neighbour,)
        + tuple(ready[:13])
        + (atom_gain_kept, w_key, w_value, w_out, w_pool, w_back, w_left.T, w_right.T),
        (
            held(devices * BLOCK, LANES, dtype=BF),
            held(rows, width, dtype=BF),
            held(SLOTS, width),
        ),
    )
    counts_after, updated = lax.optimization_barrier((atom_counts, updated))
    arrived = lax.all_to_all(payload.reshape(devices, BLOCK, LANES), AXES, 0, 0)
    adder = adder_matrix(counts_after, devices, rows, token_rows, row_tokens, col_tokens)
    return call(
        pair_kernel,
        "pairs",
        (
            arrived.reshape(devices * BLOCK, LANES),
            adder,
            updated,
            slot_back,
            slot_last,
            slot_member,
            pair_state,
            w_outer.reshape(opm * opm, -1),
            pair_gain_kept,
            w_gate,
            w_lift,
            w_drop,
        ),
        (
            jax.ShapeDtypeStruct(atom_feats.shape, BF),
            jax.ShapeDtypeStruct((own_tokens, channels), BF),
            jax.ShapeDtypeStruct(pair_state.shape, BF),
        ),
    )


def solution(mesh):
    in_specs = (
        P(("row", "col"), None),
        P(("row", "col")),
        P(),
        P(),
        P(),
        P(),
        P(),
        P(),
        P(),
        P(),
        P("row", "col", None),
        P(),
        P(),
        P(),
        P(),
        P(),
        P(),
        P(),
    )
    out_specs = (P(("row", "col"), None), P(("row", "col"), None), P("row", "col", None))
    return jax.shard_map(
        per_device, mesh=mesh, in_specs=in_specs, out_specs=out_specs, check_vma=False
    )
```

```python
import math

import jax
import jax.numpy as jnp
from jax import lax
from jax.experimental import pallas as pl
from jax.experimental.pallas import tpu as pltpu
from jax.sharding import PartitionSpec as P

HEADS = 4
QB = 32
KW = 128
EPSILON = 1e-05
HALF = KW // 2
FEWEST = 8
LANES = 128
SLOTS = 16
BLOCK = 24
DESTS = 32
PAIR_ROWS = 8
MASKED = -1e30
SPARE = 12 << 20
MOST = 60 << 20
LOG2E = 1.4426950408889634
AXES = ("row", "col")
BF = jnp.bfloat16
F32 = jnp.float32


def layer_norm(values, gain):
    mean_value = jnp.mean(values, axis=-1, keepdims=True)
    centred = values - mean_value
    variance = jnp.mean(centred * centred, axis=-1, keepdims=True)
    return centred * lax.rsqrt(variance + EPSILON) * gain


def dot(a, b):
    return jnp.dot(a, b, preferred_element_type=F32)


def dot_t(a, b):
    return lax.dot_general(a, b, (((1,), (1,)), ((), ())), preferred_element_type=F32)


def iota(shape, axis):
    return lax.broadcasted_iota(jnp.int32, shape, axis)


def flag(mask):
    return jnp.where(mask, 1.0, 0.0).astype(BF)


def place():
    return lax.axis_index("row") * lax.axis_size("col") + lax.axis_index("col")


def repeat(count, step):
    if count <= 8:
        for at in range(count):
            step(at)
    else:

        def body(at, carry):
            step(at)
            return carry

        lax.fori_loop(0, count, body, 0)


def span(at, size):
    if isinstance(at, int):
        return pl.ds(at * size, size)
    return pl.ds(pl.multiple_of(at * size, size), size)


def ready_kernel(
    own_far,
    starts_far,
    counts_far,
    folded_far,
    atom_gain_far,
    pair_gain_far,
    w_query_far,
    w_key_far,
    w_value_far,
    w_out_far,
    w_pool_far,
    w_back_far,
    w_left_far,
    w_right_far,
    own_float,
    keyval,
    stacked,
    scores,
    top,
    far_bias,
    picks,
    row_scale,
    member,
    slot_scale,
    before,
    goes_on,
    last,
    adder,
    atom_gain,
    pair_gain,
    w_kv,
    w_out,
    w_pool,
    w_back,
    w_sides,
    own,
    key_starts,
    counts,
    counts_folded,
    w_query,
    ends,
    arrivals,
):
    rows, width = own.shape
    tokens = counts.shape[1]
    opm = w_left_far.shape[0]
    pairs = (
        (counts_far, counts),
        (folded_far, counts_folded),
        (own_far, own),
        (starts_far, key_starts),
        (atom_gain_far, atom_gain),
        (w_query_far, w_query),
        (w_key_far, w_kv.at[:, :width]),
        (w_value_far, w_kv.at[:, width:]),
        (pair_gain_far, pair_gain),
        (w_out_far, w_out),
        (w_pool_far, w_pool),
        (w_back_far, w_back),
        (w_left_far, w_sides.at[:opm]),
        (w_right_far, w_sides.at[opm : 2 * opm]),
    )
    copies = [pltpu.make_async_copy(a, b, arrivals.at[k]) for k, (a, b) in enumerate(pairs)]
    for copy in copies:
        copy.start()

    tiles = picks.shape[1] // rows
    devices = picks.shape[0] // BLOCK
    atoms = rows * devices
    own_tokens = tokens // devices
    token_rows = own_tokens * tiles
    lead = BLOCK - token_rows
    slots = rows // FEWEST + 1
    position = place()
    first = position * rows
    even = position % 2 == 0
    first_float = first.astype(F32)
    w_sides[2 * opm :, :] = jnp.zeros((LANES - 2 * opm, tiles * LANES), BF)

    for copy in copies[:2]:
        copy.wait()
    counts_wide = jnp.broadcast_to(counts[...].astype(F32), (tiles * rows, tokens)).astype(BF)
    counts_lane = counts_wide[:LANES]
    folded = counts_folded[...].astype(F32).astype(BF)
    upper = flag(iota((LANES, LANES), 0) <= iota((LANES, LANES), 1))
    lower = flag(iota((LANES, LANES), 1) <= iota((LANES, LANES), 0))
    within = dot(folded, upper)
    whole = dot(folded, jnp.ones((LANES, LANES), BF))
    base = jnp.zeros((1, 1), F32)
    passed = jnp.zeros((1, LANES), F32)
    for fold in range(folded.shape[0]):
        ended = within[fold : fold + 1] + passed <= first_float
        base = base + jnp.sum(jnp.where(ended, 1.0, 0.0), axis=1, keepdims=True)
        part = slice(fold * LANES, (fold + 1) * LANES)
        ends[part, :] = passed + dot_t(lower, counts_lane[:, part])
        passed = passed + whole[fold : fold + 1]

    token_lane = iota((SLOTS, tokens), 1).astype(F32)
    slot_token = iota((SLOTS, tokens), 0).astype(F32) + base
    slot_end = dot_t(flag(token_lane <= slot_token), counts_lane)
    slot_start = dot_t(flag(token_lane < slot_token), counts_lane)
    atom_lane = iota((SLOTS, rows), 1).astype(F32) + first_float
    member[...] = flag((atom_lane >= slot_start[:, :rows]) & (atom_lane < slot_end[:, :rows]))
    slot_scale[...] = 1.0 / jnp.maximum(slot_end - slot_start, 1.0)
    last_atom = first_float + (rows - 1)
    is_last = jnp.where((slot_start <= last_atom) & (slot_end > last_atom), 1.0, 0.0)
    last[...] = is_last
    goes_on[...] = is_last * jnp.where(slot_end > first_float + rows, 1.0, 0.0)
    is_first = iota((SLOTS, LANES), 0) == 0
    before[...] = jnp.where(is_first & (slot_start < first_float), 1.0, 0.0)

    def rows_step(at):
        def spread(lanes, axis):
            return iota((DESTS, BLOCK, lanes), axis).reshape(DESTS * BLOCK, lanes)

        here = span(at, DESTS * BLOCK)
        token_at = iota((DESTS * BLOCK, tokens), 1)
        turn = spread(tokens, 1) - lead
        row_token = (spread(tokens, 0) + at * DESTS) * own_tokens + turn % own_tokens
        row_end = dot_t(flag(token_at <= row_token), counts_wide)
        row_start = dot_t(flag(token_at < row_token), counts_wide)
        lanes = tiles * rows
        lane = iota((DESTS * BLOCK, lanes), 1)
        atom = (lane % rows + first).astype(F32)
        turn = spread(lanes, 1) - lead
        tile_fits = (turn >= 0) & (turn // own_tokens == lane // rows)
        picks[here, :] = flag(tile_fits & (atom >= row_start) & (atom < row_end))
        row_scale[here, :] = 1.0 / jnp.maximum(row_end - row_start, 1.0)[:, :LANES]

    repeat(devices // DESTS, rows_step)

    row_tokens = tokens // lax.axis_size("row")
    col_tokens = tokens // lax.axis_size("col")
    first_row = lax.axis_index("row") * row_tokens
    first_col = lax.axis_index("col") * col_tokens

    def adder_step(at):
        here = span(at, LANES)
        spot_lane = iota((1, LANES), 1) + at * LANES
        block = spot_lane // BLOCK
        spot = spot_lane % BLOCK
        edge = (block * rows).astype(F32)
        tally = jnp.zeros((1, LANES), F32)
        for fold in range(tokens // LANES):
            ended = jnp.where(ends[fold * LANES : (fold + 1) * LANES, :] <= edge, 1.0, 0.0)
            tally = tally + jnp.sum(ended, axis=0, keepdims=True)
        token = jnp.where(spot < slots, tally.astype(jnp.int32) + spot, -1)
        line = iota((SLOTS, LANES), 0)
        wanted = jnp.where(
            line == token_rows,
            (position - 1) * BLOCK + slots + 1,
            jnp.where(line == token_rows + 1, (position + 1) * BLOCK + slots, -1),
        )
        fixed = (spot_lane == wanted) | ((line < token_rows) & (spot == line + lead))
        lefts = token == iota((row_tokens, LANES), 0) + first_row
        rights = token == iota((col_tokens, LANES), 0) + first_col
        adder[:SLOTS, here] = flag(fixed)
        adder[SLOTS : SLOTS + row_tokens, here] = flag(lefts)
        adder[SLOTS + row_tokens :, here] = flag(rights)

    repeat(devices * BLOCK // LANES, adder_step)

    for copy in copies[2:8]:
        copy.wait()
    raw = own[...].astype(F32)
    own_float[...] = raw
    normed = layer_norm(raw, atom_gain[...]).astype(BF)
    near = dot(normed, w_kv[...]).astype(BF)
    keyval[...] = near
    query = dot(normed, w_query[...]).astype(BF)
    head_of = iota((1, width), 1) // (width // HEADS)
    heads = jnp.concatenate([query * flag(head_of == h) for h in range(HEADS)], axis=0)
    stacked[...] = heads
    near_index = first + iota((1, rows), 1)
    far_lane = iota((1, 2 * rows), 1)
    is_low = (far_lane < rows) != even
    far_index = first + far_lane % rows + jnp.where(is_low, -rows, rows)
    near_bias, bias = [], []
    for e in range(rows // QB):
        low = key_starts[0:1, e : e + 1]
        seen = (near_index >= low) & (near_index < low + KW)
        near_bias.append(jnp.broadcast_to(jnp.where(seen, 0.0, MASKED), (QB, rows)))
        seen = (far_index >= low) & (far_index < low + KW)
        seen = seen & (far_index >= 0) & (far_index < atoms)
        bias.append(jnp.broadcast_to(jnp.where(seen, 0.0, MASKED), (QB, 2 * rows)))
    far_bias[...] = jnp.concatenate(bias, axis=0)
    raw_scores = dot_t(heads, near[:, :width]) + jnp.concatenate(near_bias * HEADS, axis=0)
    scores[...] = raw_scores
    top[...] = jnp.max(raw_scores, axis=-1, keepdims=True)
    for copy in copies[8:]:
        copy.wait()


def atom_kernel(
    neighbour,
    sibling,
    own_float,
    keyval,
    stacked,
    scores,
    top,
    far_bias,
    picks,
    row_scale,
    member,
    slot_scale,
    before,
    goes_on,
    atom_gain,
    w_kv,
    w_out,
    w_pool,
    w_back,
    w_sides,
    payload,
    updated,
    slot_back,
):
    rows, width = own_float.shape
    tiles = w_pool.shape[1] // LANES
    devices = payload.shape[0] // BLOCK
    slots = rows // FEWEST + 1
    raw = jnp.concatenate([sibling[...], neighbour[...]], axis=0).astype(F32)
    normed = layer_norm(raw, atom_gain[...]).astype(BF)
    far = dot(normed, w_kv[...]).astype(BF)
    far_scores = dot_t(stacked[...], far[:, :width])
    far_scores = far_scores + jnp.concatenate([far_bias[...]] * HEADS, axis=0)
    most = jnp.maximum(top[...], jnp.max(far_scores, axis=-1, keepdims=True))
    scale = (width // HEADS) ** (-0.5) * LOG2E
    raised = jnp.concatenate(
        [
            jnp.exp2((far_scores - most) * scale).astype(BF),
            jnp.exp2((scores[...] - most) * scale).astype(BF),
        ],
        axis=1,
    )
    values = jnp.concatenate([far[:, width:], keyval[:, width:]], axis=0)
    mixed = dot(raised, jnp.concatenate([values, jnp.ones((3 * rows, width), BF)], axis=1))
    head_of = iota((1, width), 1) // (width // HEADS)
    head_mask = [(head_of == h).astype(F32) for h in range(HEADS)]
    total = sum(mixed[h * rows : (h + 1) * rows, :width] * head_mask[h] for h in range(HEADS))
    weight = sum(mixed[h * rows : (h + 1) * rows, width:] * head_mask[h] for h in range(HEADS))
    attended = (total / weight).astype(BF)
    fresh = (own_float[...] + dot(attended, w_out[...])).astype(BF)
    updated[...] = fresh
    feature = jnp.maximum(dot(fresh, w_pool[...]), 0.0).astype(BF)
    feature_tiles = jnp.concatenate(
        [feature[:, k * LANES : (k + 1) * LANES] for k in range(tiles)], axis=0
    )
    slot_single = (
        dot(member[...], feature) * jnp.concatenate([slot_scale[...]] * tiles, axis=1)
    ).astype(BF)
    sides = dot_t(slot_single, w_sides[...])
    backs = dot(slot_single, w_back[...])
    slot_back[...] = backs
    to_before = jnp.sum(backs * before[...], axis=0, keepdims=True)
    to_after = jnp.sum(backs * goes_on[...], axis=0, keepdims=True)
    spot = iota((SLOTS, LANES), 0)
    shared = jnp.where(
        spot < slots,
        sides,
        jnp.where(spot == slots, to_before, jnp.where(spot == slots + 1, to_after, 0.0)),
    )
    shared = jnp.concatenate([shared, jnp.zeros((BLOCK - SLOTS, LANES), F32)], axis=0)

    def send_step(at):
        here = span(at, DESTS * BLOCK)
        singles = dot(picks[here, :], feature_tiles) * row_scale[here, :]
        singles = singles.reshape(DESTS, BLOCK, LANES) + shared[None]
        payload[here, :] = singles.reshape(DESTS * BLOCK, LANES).astype(BF)

    repeat(devices // DESTS, send_step)


def pair_kernel(
    arrived,
    adder,
    updated,
    slot_back,
    slot_last,
    slot_member,
    pair_state,
    w_outer,
    pair_gain,
    w_gate,
    w_lift,
    w_drop,
    atom_out,
    token_single,
    pair_far,
    pair_out,
    leaving,
):
    row_tokens, col_tokens, pair_width = pair_state.shape
    own_tokens, channels = token_single.shape
    tiles = channels // LANES
    token_rows = own_tokens * tiles
    opm = math.isqrt(w_outer.shape[0])
    added = dot(adder[...], arrived[...])
    half_gate = w_gate[...] * jnp.asarray(0.5, BF)
    left = added[SLOTS : SLOTS + row_tokens, :opm].astype(BF)
    right = added[SLOTS + row_tokens :, opm : 2 * opm].astype(BF)
    product_lane = iota((opm, opm * opm), 1)
    unit = iota((opm, opm * opm), 0)
    left_wide = dot(left, flag(product_lane // opm == unit))
    right_wide = dot(right, flag(product_lane % opm == unit))

    def pair_rows(lefts, here):
        products = jnp.concatenate(
            [(lefts[i : i + 1, :] * right_wide).astype(BF) for i in range(PAIR_ROWS)], axis=0
        )
        flat = pair_state[pl.ds(here, PAIR_ROWS)].reshape(PAIR_ROWS * col_tokens, pair_width)
        summed = flat.astype(F32) + dot(products, w_outer[...])
        normed = layer_norm(summed, pair_gain[...]).astype(BF)
        gate = dot(normed, half_gate)
        lift = dot(normed, w_lift[...])
        hidden = (gate * lift * (1.0 + jnp.tanh(gate))).astype(BF)
        result = (summed + dot(hidden, w_drop[...])).astype(BF)
        pair_out[pl.ds(here, PAIR_ROWS)] = result.reshape(PAIR_ROWS, col_tokens, pair_width)

    token_single[...] = jnp.concatenate(
        [added[k * own_tokens : (k + 1) * own_tokens] for k in range(tiles)], axis=1
    ).astype(BF)
    spot = iota((SLOTS, LANES), 0)
    from_before = jnp.where(spot == 0, added[token_rows : token_rows + 1], 0.0)
    from_after = slot_last[...] * added[token_rows + 1 : token_rows + 2]
    back = (slot_back[...] + from_before + from_after).astype(BF)
    lifted = lax.dot_general(
        slot_member[...], back, (((0,), (0,)), ((), ())), preferred_element_type=F32
    )
    atom_out[...] = (updated[...].astype(F32) + lifted).astype(BF)

    copies = []
    for step in range(row_tokens // PAIR_ROWS):
        here = step * PAIR_ROWS
        pair_rows(left_wide[here : here + PAIR_ROWS], here)
        part = pl.ds(here, PAIR_ROWS)
        copies.append(
            pltpu.make_async_copy(pair_out.at[part], pair_far.at[part], leaving.at[step])
        )
        copies[-1].start()
    for copy in copies:
        copy.wait()


def call(kernel, name, operands, outputs, far=(), out_far=(), scratch=()):
    near_spec = pl.BlockSpec(memory_space=pltpu.VMEM)
    far_spec = pl.BlockSpec(memory_space=pltpu.HBM)
    held = sum(math.prod(a.shape) * a.dtype.itemsize for a in operands + outputs)
    return pl.pallas_call(
        kernel,
        out_shape=outputs,
        in_specs=[far_spec] * len(far) + [near_spec] * len(operands),
        out_specs=tuple(far_spec if k in out_far else near_spec for k in range(len(outputs))),
        scratch_shapes=scratch,
        compiler_params=pltpu.CompilerParams(vmem_limit_bytes=min(2 * held + SPARE, MOST)),
        name=name,
    )(*[pltpu.with_memory_space_constraint(a, pltpu.HBM) for a in far], *operands)


def per_device(
    atom_feats,
    key_starts,
    atom_counts,
    atom_gain,
    w_query,
    w_key,
    w_value,
    w_out,
    w_pool,
    w_back,
    pair_state,
    w_left,
    w_right,
    w_outer,
    pair_gain,
    w_gate,
    w_lift,
    w_drop,
):
    rows, width = atom_feats.shape
    devices = lax.axis_size(AXES)
    tokens = atom_counts.shape[0]
    channels = w_pool.shape[1]
    opm = w_left.shape[1]
    own_tokens = tokens // devices
    row_tokens, col_tokens, _ = pair_state.shape
    tiles = channels // LANES
    across = [(i, i + 1) for i in range(1, devices - 1, 2)]
    neighbour = lax.ppermute(atom_feats, AXES, across + [(j, i) for i, j in across])
    sibling = lax.ppermute(atom_feats, AXES, [(i, i ^ 1) for i in range(devices)])

    def held(*shape, dtype=F32):
        return jax.ShapeDtypeStruct(shape, dtype)

    counts_folded = atom_counts.reshape(-1, LANES)
    ready = call(
        ready_kernel,
        "ready",
        (),
        (
            held(rows, width),
            held(rows, 2 * width, dtype=BF),
            held(HEADS * rows, width, dtype=BF),
            held(HEADS * rows, rows),
            held(HEADS * rows, 1),
            held(rows, 2 * rows),
            held(devices * BLOCK, tiles * rows, dtype=BF),
            held(devices * BLOCK, LANES),
            held(SLOTS, rows, dtype=BF),
            held(SLOTS, LANES),
            held(SLOTS, LANES),
            held(SLOTS, LANES),
            held(SLOTS, LANES),
            held(SLOTS + row_tokens + col_tokens, devices * BLOCK, dtype=BF),
            held(1, width),
            held(1, LANES),
            held(width, 2 * width, dtype=BF),
            held(width, width, dtype=BF),
            held(width, channels, dtype=BF),
            held(channels, width, dtype=BF),
            held(LANES, channels, dtype=BF),
        ),
        far=(
            atom_feats,
            key_starts[None],
            atom_counts[None],
            counts_folded,
            atom_gain[None],
            pair_gain[None],
            w_query,
            w_key,
            w_value,
            w_out,
            w_pool,
            w_back,
            w_left.T,
            w_right.T,
        ),
        scratch=(
            pltpu.VMEM((rows, width), BF),
            pltpu.VMEM((1, key_starts.shape[0]), jnp.int32),
            pltpu.VMEM((1, tokens), jnp.int32),
            pltpu.VMEM(counts_folded.shape, jnp.int32),
            pltpu.VMEM((width, width), BF),
            pltpu.VMEM((tokens, LANES), F32),
            pltpu.SemaphoreType.DMA((14,)),
        ),
    )
    (
        own_float,
        keyval,
        stacked,
        scores,
        top,
        far_bias,
        picks,
        row_scale,
        member,
        slot_scale,
        before,
        goes_on,
        last,
        adder,
        atom_gain_kept,
        pair_gain_kept,
        *kept,
    ) = ready
    payload, updated, slot_back = call(
        atom_kernel,
        "atoms",
        (
            neighbour,
            sibling,
            own_float,
            keyval,
            stacked,
            scores,
            top,
            far_bias,
            picks,
            row_scale,
            member,
            slot_scale,
            before,
            goes_on,
            atom_gain_kept,
            *kept,
        ),
        (
            held(devices * BLOCK, LANES, dtype=BF),
            held(rows, width, dtype=BF),
            held(SLOTS, width),
        ),
    )
    arrived = lax.all_to_all(payload.reshape(devices, BLOCK, LANES), AXES, 0, 0)
    opm = w_left.shape[1]
    return call(
        pair_kernel,
        "pairs",
        (
            arrived.reshape(devices * BLOCK, LANES),
            adder,
            updated,
            slot_back,
            last,
            member,
            pair_state,
            w_outer.reshape(opm * opm, -1),
            pair_gain_kept,
            w_gate,
            w_lift,
            w_drop,
        ),
        (
            held(rows, width, dtype=BF),
            held(own_tokens, channels, dtype=BF),
            held(*pair_state.shape, dtype=BF),
        ),
        out_far=(2,),
        scratch=(
            pltpu.VMEM(pair_state.shape, BF),
            pltpu.SemaphoreType.DMA((row_tokens // PAIR_ROWS,)),
        ),
    )


def solution(mesh):
    in_specs = (
        P(("row", "col"), None),
        P(("row", "col")),
        P(),
        P(),
        P(),
        P(),
        P(),
        P(),
        P(),
        P(),
        P("row", "col", None),
        P(),
        P(),
        P(),
        P(),
        P(),
        P(),
        P(),
    )
    out_specs = (P(("row", "col"), None), P(("row", "col"), None), P("row", "col", None))
    return jax.shard_map(
        per_device, mesh=mesh, in_specs=in_specs, out_specs=out_specs, check_vma=False
    )
```

```python
import math

import jax
import jax.numpy as jnp
from jax import lax
from jax.experimental import pallas as pl
from jax.experimental.pallas import tpu as pltpu
from jax.sharding import PartitionSpec as P

HEADS = 4
QB = 32
KW = 128
EPSILON = 1e-05
HALF = KW // 2
FEWEST = 8
LANES = 128
SLOTS = 16
BLOCK = 24
DESTS = 32
PAIR_ROWS = 4
MASKED = -1e30
SPARE = 12 << 20
MOST = 60 << 20
LOG2E = 1.4426950408889634
AXES = ("row", "col")
BF = jnp.bfloat16
F32 = jnp.float32


def layer_norm(values, gain):
    mean_value = jnp.mean(values, axis=-1, keepdims=True)
    centred = values - mean_value
    variance = jnp.mean(centred * centred, axis=-1, keepdims=True)
    return centred * lax.rsqrt(variance + EPSILON) * gain


def dot(a, b):
    return jnp.dot(a, b, preferred_element_type=F32)


def dot_t(a, b):
    return lax.dot_general(a, b, (((1,), (1,)), ((), ())), preferred_element_type=F32)


def iota(shape, axis):
    return lax.broadcasted_iota(jnp.int32, shape, axis)


def flag(mask):
    return jnp.where(mask, 1.0, 0.0).astype(BF)


def place():
    return lax.axis_index("row") * lax.axis_size("col") + lax.axis_index("col")


def repeat(count, step):
    if count <= 8:
        for at in range(count):
            step(at)
    else:

        def body(at, carry):
            step(at)
            return carry

        lax.fori_loop(0, count, body, 0)


def span(at, size):
    if isinstance(at, int):
        return pl.ds(at * size, size)
    return pl.ds(pl.multiple_of(at * size, size), size)


def ready_kernel(
    own_far,
    starts_far,
    counts_far,
    folded_far,
    atom_gain_far,
    pair_gain_far,
    w_query_far,
    w_key_far,
    w_value_far,
    w_out_far,
    w_pool_far,
    w_back_far,
    w_left_far,
    w_right_far,
    own_float,
    keyval,
    stacked,
    scores,
    top,
    far_bias,
    picks,
    row_scale,
    member,
    slot_scale,
    before,
    goes_on,
    last,
    adder,
    atom_gain,
    pair_gain,
    w_kv,
    w_out,
    w_pool,
    w_back,
    w_sides,
    own,
    key_starts,
    counts,
    counts_folded,
    w_query,
    ends,
    arrivals,
):
    rows, width = own.shape
    tokens = counts.shape[1]
    opm = w_left_far.shape[0]
    pairs = (
        (counts_far, counts),
        (folded_far, counts_folded),
        (own_far, own),
        (starts_far, key_starts),
        (atom_gain_far, atom_gain),
        (w_query_far, w_query),
        (w_key_far, w_kv.at[:, :width]),
        (w_value_far, w_kv.at[:, width:]),
        (pair_gain_far, pair_gain),
        (w_out_far, w_out),
        (w_pool_far, w_pool),
        (w_back_far, w_back),
        (w_left_far, w_sides.at[:opm]),
        (w_right_far, w_sides.at[opm : 2 * opm]),
    )
    copies = [pltpu.make_async_copy(a, b, arrivals.at[k]) for k, (a, b) in enumerate(pairs)]
    for copy in copies:
        copy.start()

    tiles = picks.shape[1] // rows
    devices = picks.shape[0] // BLOCK
    atoms = rows * devices
    own_tokens = tokens // devices
    token_rows = own_tokens * tiles
    lead = BLOCK - token_rows
    slots = rows // FEWEST + 1
    position = place()
    first = position * rows
    even = position % 2 == 0
    first_float = first.astype(F32)
    w_sides[2 * opm :, :] = jnp.zeros((LANES - 2 * opm, tiles * LANES), BF)

    for copy in copies[:2]:
        copy.wait()
    counts_wide = jnp.broadcast_to(counts[...].astype(F32), (tiles * rows, tokens)).astype(BF)
    counts_lane = counts_wide[:LANES]
    folded = counts_folded[...].astype(F32).astype(BF)
    upper = flag(iota((LANES, LANES), 0) <= iota((LANES, LANES), 1))
    lower = flag(iota((LANES, LANES), 1) <= iota((LANES, LANES), 0))
    within = dot(folded, upper)
    whole = dot(folded, jnp.ones((LANES, LANES), BF))
    base = jnp.zeros((1, 1), F32)
    passed = jnp.zeros((1, LANES), F32)
    for fold in range(folded.shape[0]):
        ended = within[fold : fold + 1] + passed <= first_float
        base = base + jnp.sum(jnp.where(ended, 1.0, 0.0), axis=1, keepdims=True)
        part = slice(fold * LANES, (fold + 1) * LANES)
        ends[part, :] = passed + dot_t(lower, counts_lane[:, part])
        passed = passed + whole[fold : fold + 1]

    token_lane = iota((SLOTS, tokens), 1).astype(F32)
    slot_token = iota((SLOTS, tokens), 0).astype(F32) + base
    slot_end = dot_t(flag(token_lane <= slot_token), counts_lane)
    slot_start = dot_t(flag(token_lane < slot_token), counts_lane)
    atom_lane = iota((SLOTS, rows), 1).astype(F32) + first_float
    member[...] = flag((atom_lane >= slot_start[:, :rows]) & (atom_lane < slot_end[:, :rows]))
    slot_scale[...] = 1.0 / jnp.maximum(slot_end - slot_start, 1.0)
    last_atom = first_float + (rows - 1)
    is_last = jnp.where((slot_start <= last_atom) & (slot_end > last_atom), 1.0, 0.0)
    last[...] = is_last
    goes_on[...] = is_last * jnp.where(slot_end > first_float + rows, 1.0, 0.0)
    is_first = iota((SLOTS, LANES), 0) == 0
    before[...] = jnp.where(is_first & (slot_start < first_float), 1.0, 0.0)

    def rows_step(at):
        def spread(lanes, axis):
            return iota((DESTS, BLOCK, lanes), axis).reshape(DESTS * BLOCK, lanes)

        here = span(at, DESTS * BLOCK)
        token_at = iota((DESTS * BLOCK, tokens), 1)
        turn = spread(tokens, 1) - lead
        row_token = (spread(tokens, 0) + at * DESTS) * own_tokens + turn % own_tokens
        row_end = dot_t(flag(token_at <= row_token), counts_wide)
        row_start = dot_t(flag(token_at < row_token), counts_wide)
        lanes = tiles * rows
        lane = iota((DESTS * BLOCK, lanes), 1)
        atom = (lane % rows + first).astype(F32)
        turn = spread(lanes, 1) - lead
        tile_fits = (turn >= 0) & (turn // own_tokens == lane // rows)
        picks[here, :] = flag(tile_fits & (atom >= row_start) & (atom < row_end))
        row_scale[here, :] = 1.0 / jnp.maximum(row_end - row_start, 1.0)[:, :LANES]

    repeat(devices // DESTS, rows_step)

    row_tokens = tokens // lax.axis_size("row")
    col_tokens = tokens // lax.axis_size("col")
    first_row = lax.axis_index("row") * row_tokens
    first_col = lax.axis_index("col") * col_tokens

    def adder_step(at):
        here = span(at, LANES)
        spot_lane = iota((1, LANES), 1) + at * LANES
        block = spot_lane // BLOCK
        spot = spot_lane % BLOCK
        edge = (block * rows).astype(F32)
        tally = jnp.zeros((1, LANES), F32)
        for fold in range(tokens // LANES):
            ended = jnp.where(ends[fold * LANES : (fold + 1) * LANES, :] <= edge, 1.0, 0.0)
            tally = tally + jnp.sum(ended, axis=0, keepdims=True)
        token = jnp.where(spot < slots, tally.astype(jnp.int32) + spot, -1)
        line = iota((SLOTS, LANES), 0)
        wanted = jnp.where(
            line == token_rows,
            (position - 1) * BLOCK + slots + 1,
            jnp.where(line == token_rows + 1, (position + 1) * BLOCK + slots, -1),
        )
        fixed = (spot_lane == wanted) | ((line < token_rows) & (spot == line + lead))
        lefts = token == iota((row_tokens, LANES), 0) + first_row
        rights = token == iota((col_tokens, LANES), 0) + first_col
        adder[:SLOTS, here] = flag(fixed)
        adder[SLOTS : SLOTS + row_tokens, here] = flag(lefts)
        adder[SLOTS + row_tokens :, here] = flag(rights)

    repeat(devices * BLOCK // LANES, adder_step)

    for copy in copies[2:8]:
        copy.wait()
    raw = own[...].astype(F32)
    own_float[...] = raw
    normed = layer_norm(raw, atom_gain[...]).astype(BF)
    near = dot(normed, w_kv[...]).astype(BF)
    keyval[...] = near
    query = dot(normed, w_query[...]).astype(BF)
    head_of = iota((1, width), 1) // (width // HEADS)
    heads = jnp.concatenate([query * flag(head_of == h) for h in range(HEADS)], axis=0)
    stacked[...] = heads
    near_index = first + iota((1, rows), 1)
    far_lane = iota((1, 2 * rows), 1)
    is_low = (far_lane < rows) != even
    far_index = first + far_lane % rows + jnp.where(is_low, -rows, rows)
    near_bias, bias = [], []
    for e in range(rows // QB):
        low = key_starts[0:1, e : e + 1]
        seen = (near_index >= low) & (near_index < low + KW)
        near_bias.append(jnp.broadcast_to(jnp.where(seen, 0.0, MASKED), (QB, rows)))
        seen = (far_index >= low) & (far_index < low + KW)
        seen = seen & (far_index >= 0) & (far_index < atoms)
        bias.append(jnp.broadcast_to(jnp.where(seen, 0.0, MASKED), (QB, 2 * rows)))
    far_bias[...] = jnp.concatenate(bias, axis=0)
    raw_scores = dot_t(heads, near[:, :width]) + jnp.concatenate(near_bias * HEADS, axis=0)
    scores[...] = raw_scores
    top[...] = jnp.max(raw_scores, axis=-1, keepdims=True)
    for copy in copies[8:]:
        copy.wait()


def atom_kernel(
    neighbour,
    sibling,
    own_float,
    keyval,
    stacked,
    scores,
    top,
    far_bias,
    picks,
    row_scale,
    member,
    slot_scale,
    before,
    goes_on,
    atom_gain,
    w_kv,
    w_out,
    w_pool,
    w_back,
    w_sides,
    payload,
    updated,
    slot_back,
):
    rows, width = own_float.shape
    tiles = w_pool.shape[1] // LANES
    devices = payload.shape[0] // BLOCK
    slots = rows // FEWEST + 1
    raw = jnp.concatenate([sibling[...], neighbour[...]], axis=0).astype(F32)
    normed = layer_norm(raw, atom_gain[...]).astype(BF)
    far = dot(normed, w_kv[...]).astype(BF)
    far_scores = dot_t(stacked[...], far[:, :width])
    far_scores = far_scores + jnp.concatenate([far_bias[...]] * HEADS, axis=0)
    most = jnp.maximum(top[...], jnp.max(far_scores, axis=-1, keepdims=True))
    scale = (width // HEADS) ** (-0.5) * LOG2E
    raised = jnp.concatenate(
        [
            jnp.exp2((far_scores - most) * scale).astype(BF),
            jnp.exp2((scores[...] - most) * scale).astype(BF),
        ],
        axis=1,
    )
    values = jnp.concatenate([far[:, width:], keyval[:, width:]], axis=0)
    mixed = dot(raised, jnp.concatenate([values, jnp.ones((3 * rows, width), BF)], axis=1))
    head_of = iota((1, width), 1) // (width // HEADS)
    head_mask = [(head_of == h).astype(F32) for h in range(HEADS)]
    total = sum(mixed[h * rows : (h + 1) * rows, :width] * head_mask[h] for h in range(HEADS))
    weight = sum(mixed[h * rows : (h + 1) * rows, width:] * head_mask[h] for h in range(HEADS))
    attended = (total / weight).astype(BF)
    fresh = (own_float[...] + dot(attended, w_out[...])).astype(BF)
    updated[...] = fresh
    feature = jnp.maximum(dot(fresh, w_pool[...]), 0.0).astype(BF)
    feature_tiles = jnp.concatenate(
        [feature[:, k * LANES : (k + 1) * LANES] for k in range(tiles)], axis=0
    )
    slot_single = (
        dot(member[...], feature) * jnp.concatenate([slot_scale[...]] * tiles, axis=1)
    ).astype(BF)
    sides = dot_t(slot_single, w_sides[...])
    backs = dot(slot_single, w_back[...])
    slot_back[...] = backs
    to_before = jnp.sum(backs * before[...], axis=0, keepdims=True)
    to_after = jnp.sum(backs * goes_on[...], axis=0, keepdims=True)
    spot = iota((SLOTS, LANES), 0)
    shared = jnp.where(
        spot < slots,
        sides,
        jnp.where(spot == slots, to_before, jnp.where(spot == slots + 1, to_after, 0.0)),
    )
    shared = jnp.concatenate([shared, jnp.zeros((BLOCK - SLOTS, LANES), F32)], axis=0)

    def send_step(at):
        here = span(at, DESTS * BLOCK)
        singles = dot(picks[here, :], feature_tiles) * row_scale[here, :]
        singles = singles.reshape(DESTS, BLOCK, LANES) + shared[None]
        payload[here, :] = singles.reshape(DESTS * BLOCK, LANES).astype(BF)

    repeat(devices // DESTS, send_step)


def pair_kernel(
    arrived,
    adder,
    updated,
    slot_back,
    slot_last,
    slot_member,
    pair_state,
    w_outer,
    pair_gain,
    w_gate,
    w_lift,
    w_drop,
    atom_out,
    token_single,
    pair_out,
):
    row_tokens, col_tokens, pair_width = pair_state.shape
    own_tokens, channels = token_single.shape
    tiles = channels // LANES
    token_rows = own_tokens * tiles
    opm = math.isqrt(w_outer.shape[0])
    added = dot(adder[...], arrived[...])
    half_gate = w_gate[...] * jnp.asarray(0.5, BF)
    left = added[SLOTS : SLOTS + row_tokens, :opm].astype(BF)
    right = added[SLOTS + row_tokens :, opm : 2 * opm].astype(BF)
    product_lane = iota((opm, opm * opm), 1)
    unit = iota((opm, opm * opm), 0)
    left_wide = dot(left, flag(product_lane // opm == unit))
    right_wide = dot(right, flag(product_lane % opm == unit))

    def pair_rows(lefts, here):
        products = jnp.concatenate(
            [(lefts[i : i + 1, :] * right_wide).astype(BF) for i in range(PAIR_ROWS)], axis=0
        )
        flat = pair_state[pl.ds(here, PAIR_ROWS)].reshape(PAIR_ROWS * col_tokens, pair_width)
        summed = flat.astype(F32) + dot(products, w_outer[...])
        normed = layer_norm(summed, pair_gain[...]).astype(BF)
        gate = dot(normed, half_gate)
        lift = dot(normed, w_lift[...])
        hidden = (gate * lift * (1.0 + jnp.tanh(gate))).astype(BF)
        result = (summed + dot(hidden, w_drop[...])).astype(BF)
        pair_out[pl.ds(here, PAIR_ROWS)] = result.reshape(PAIR_ROWS, col_tokens, pair_width)

    for step in range(row_tokens // PAIR_ROWS):
        here = step * PAIR_ROWS
        pair_rows(left_wide[here : here + PAIR_ROWS], here)

    token_single[...] = jnp.concatenate(
        [added[k * own_tokens : (k + 1) * own_tokens] for k in range(tiles)], axis=1
    ).astype(BF)
    spot = iota((SLOTS, LANES), 0)
    from_before = jnp.where(spot == 0, added[token_rows : token_rows + 1], 0.0)
    from_after = slot_last[...] * added[token_rows + 1 : token_rows + 2]
    back = (slot_back[...] + from_before + from_after).astype(BF)
    lifted = lax.dot_general(
        slot_member[...], back, (((0,), (0,)), ((), ())), preferred_element_type=F32
    )
    atom_out[...] = (updated[...].astype(F32) + lifted).astype(BF)


def call(kernel, name, operands, outputs, far=(), scratch=()):
    near_spec = pl.BlockSpec(memory_space=pltpu.VMEM)
    far_spec = pl.BlockSpec(memory_space=pltpu.HBM)
    held = sum(math.prod(a.shape) * a.dtype.itemsize for a in operands + outputs)
    return pl.pallas_call(
        kernel,
        out_shape=outputs,
        in_specs=[far_spec] * len(far) + [near_spec] * len(operands),
        out_specs=(near_spec,) * len(outputs),
        scratch_shapes=scratch,
        compiler_params=pltpu.CompilerParams(vmem_limit_bytes=min(2 * held + SPARE, MOST)),
        name=name,
    )(*[pltpu.with_memory_space_constraint(a, pltpu.HBM) for a in far], *operands)


def per_device(
    atom_feats,
    key_starts,
    atom_counts,
    atom_gain,
    w_query,
    w_key,
    w_value,
    w_out,
    w_pool,
    w_back,
    pair_state,
    w_left,
    w_right,
    w_outer,
    pair_gain,
    w_gate,
    w_lift,
    w_drop,
):
    rows, width = atom_feats.shape
    devices = lax.axis_size(AXES)
    tokens = atom_counts.shape[0]
    channels = w_pool.shape[1]
    opm = w_left.shape[1]
    own_tokens = tokens // devices
    row_tokens, col_tokens, _ = pair_state.shape
    tiles = channels // LANES
    across = [(i, i + 1) for i in range(1, devices - 1, 2)]
    neighbour = lax.ppermute(atom_feats, AXES, across + [(j, i) for i, j in across])
    sibling = lax.ppermute(atom_feats, AXES, [(i, i ^ 1) for i in range(devices)])

    def held(*shape, dtype=F32):
        return jax.ShapeDtypeStruct(shape, dtype)

    counts_folded = atom_counts.reshape(-1, LANES)
    ready = call(
        ready_kernel,
        "ready",
        (),
        (
            held(rows, width),
            held(rows, 2 * width, dtype=BF),
            held(HEADS * rows, width, dtype=BF),
            held(HEADS * rows, rows),
            held(HEADS * rows, 1),
            held(rows, 2 * rows),
            held(devices * BLOCK, tiles * rows, dtype=BF),
            held(devices * BLOCK, LANES),
            held(SLOTS, rows, dtype=BF),
            held(SLOTS, LANES),
            held(SLOTS, LANES),
            held(SLOTS, LANES),
            held(SLOTS, LANES),
            held(SLOTS + row_tokens + col_tokens, devices * BLOCK, dtype=BF),
            held(1, width),
            held(1, LANES),
            held(width, 2 * width, dtype=BF),
            held(width, width, dtype=BF),
            held(width, channels, dtype=BF),
            held(channels, width, dtype=BF),
            held(LANES, channels, dtype=BF),
        ),
        far=(
            atom_feats,
            key_starts[None],
            atom_counts[None],
            counts_folded,
            atom_gain[None],
            pair_gain[None],
            w_query,
            w_key,
            w_value,
            w_out,
            w_pool,
            w_back,
            w_left.T,
            w_right.T,
        ),
        scratch=(
            pltpu.VMEM((rows, width), BF),
            pltpu.VMEM((1, key_starts.shape[0]), jnp.int32),
            pltpu.VMEM((1, tokens), jnp.int32),
            pltpu.VMEM(counts_folded.shape, jnp.int32),
            pltpu.VMEM((width, width), BF),
            pltpu.VMEM((tokens, LANES), F32),
            pltpu.SemaphoreType.DMA((14,)),
        ),
    )
    (
        own_float,
        keyval,
        stacked,
        scores,
        top,
        far_bias,
        picks,
        row_scale,
        member,
        slot_scale,
        before,
        goes_on,
        last,
        adder,
        atom_gain_kept,
        pair_gain_kept,
        *kept,
    ) = ready
    payload, updated, slot_back = call(
        atom_kernel,
        "atoms",
        (
            neighbour,
            sibling,
            own_float,
            keyval,
            stacked,
            scores,
            top,
            far_bias,
            picks,
            row_scale,
            member,
            slot_scale,
            before,
            goes_on,
            atom_gain_kept,
            *kept,
        ),
        (
            held(devices * BLOCK, LANES, dtype=BF),
            held(rows, width, dtype=BF),
            held(SLOTS, width),
        ),
    )
    arrived = lax.all_to_all(payload.reshape(devices, BLOCK, LANES), AXES, 0, 0)
    opm = w_left.shape[1]
    return call(
        pair_kernel,
        "pairs",
        (
            arrived.reshape(devices * BLOCK, LANES),
            adder,
            updated,
            slot_back,
            last,
            member,
            pair_state,
            w_outer.reshape(opm * opm, -1),
            pair_gain_kept,
            w_gate,
            w_lift,
            w_drop,
        ),
        (
            held(rows, width, dtype=BF),
            held(own_tokens, channels, dtype=BF),
            held(*pair_state.shape, dtype=BF),
        ),
    )


def solution(mesh):
    in_specs = (
        P(("row", "col"), None),
        P(("row", "col")),
        P(),
        P(),
        P(),
        P(),
        P(),
        P(),
        P(),
        P(),
        P("row", "col", None),
        P(),
        P(),
        P(),
        P(),
        P(),
        P(),
        P(),
    )
    out_specs = (P(("row", "col"), None), P(("row", "col"), None), P("row", "col", None))
    return jax.shard_map(
        per_device, mesh=mesh, in_specs=in_specs, out_specs=out_specs, check_vma=False
    )
```

```python
import math

import jax
import jax.numpy as jnp
from jax import lax
from jax.experimental import pallas as pl
from jax.experimental.pallas import tpu as pltpu
from jax.sharding import PartitionSpec as P

HEADS = 4
QB = 32
KW = 128
EPSILON = 1e-05
HALF = KW // 2
FEWEST = 8
LANES = 128
SLOTS = 16
BLOCK = 24
DESTS = 32
PAIR_ROWS = 16
MASKED = -1e30
SPARE = 12 << 20
MOST = 60 << 20
LOG2E = 1.4426950408889634
AXES = ("row", "col")
BF = jnp.bfloat16
F32 = jnp.float32


def layer_norm(values, gain):
    mean_value = jnp.mean(values, axis=-1, keepdims=True)
    centred = values - mean_value
    variance = jnp.mean(centred * centred, axis=-1, keepdims=True)
    return centred * lax.rsqrt(variance + EPSILON) * gain


def dot(a, b):
    return jnp.dot(a, b, preferred_element_type=F32)


def dot_t(a, b):
    return lax.dot_general(a, b, (((1,), (1,)), ((), ())), preferred_element_type=F32)


def iota(shape, axis):
    return lax.broadcasted_iota(jnp.int32, shape, axis)


def flag(mask):
    return jnp.where(mask, 1.0, 0.0).astype(BF)


def place():
    return lax.axis_index("row") * lax.axis_size("col") + lax.axis_index("col")


def repeat(count, step):
    if count <= 8:
        for at in range(count):
            step(at)
    else:

        def body(at, carry):
            step(at)
            return carry

        lax.fori_loop(0, count, body, 0)


def span(at, size):
    if isinstance(at, int):
        return pl.ds(at * size, size)
    return pl.ds(pl.multiple_of(at * size, size), size)


def ready_kernel(
    own_far,
    starts_far,
    counts_far,
    folded_far,
    atom_gain_far,
    pair_gain_far,
    w_query_far,
    w_key_far,
    w_value_far,
    w_out_far,
    w_pool_far,
    w_back_far,
    w_left_far,
    w_right_far,
    w_outer_far,
    own_float,
    keyval,
    stacked,
    scores,
    top,
    far_bias,
    picks,
    row_scale,
    member,
    slot_scale,
    before,
    goes_on,
    last,
    adder,
    atom_gain,
    pair_gain,
    w_kv,
    w_out,
    w_pool,
    w_back,
    w_sides,
    w_outer,
    own,
    key_starts,
    counts,
    counts_folded,
    w_query,
    ends,
    arrivals,
):
    rows, width = own.shape
    tokens = counts.shape[1]
    opm = w_left_far.shape[0]
    pairs = (
        (counts_far, counts),
        (folded_far, counts_folded),
        (own_far, own),
        (starts_far, key_starts),
        (atom_gain_far, atom_gain),
        (w_query_far, w_query),
        (w_key_far, w_kv.at[:, :width]),
        (w_value_far, w_kv.at[:, width:]),
        (pair_gain_far, pair_gain),
        (w_out_far, w_out),
        (w_pool_far, w_pool),
        (w_back_far, w_back),
        (w_left_far, w_sides.at[:opm]),
        (w_right_far, w_sides.at[opm : 2 * opm]),
        (w_outer_far, w_outer.at[:, : w_outer_far.shape[1]]),
    )
    copies = [pltpu.make_async_copy(a, b, arrivals.at[k]) for k, (a, b) in enumerate(pairs)]
    for copy in copies:
        copy.start()

    tiles = picks.shape[1] // rows
    devices = picks.shape[0] // BLOCK
    atoms = rows * devices
    own_tokens = tokens // devices
    token_rows = own_tokens * tiles
    lead = BLOCK - token_rows
    slots = rows // FEWEST + 1
    position = place()
    first = position * rows
    even = position % 2 == 0
    first_float = first.astype(F32)
    w_sides[2 * opm :, :] = jnp.zeros((LANES - 2 * opm, tiles * LANES), BF)

    for copy in copies[:2]:
        copy.wait()
    counts_wide = jnp.broadcast_to(counts[...].astype(F32), (tiles * rows, tokens)).astype(BF)
    counts_lane = counts_wide[:LANES]
    folded = counts_folded[...].astype(F32).astype(BF)
    upper = flag(iota((LANES, LANES), 0) <= iota((LANES, LANES), 1))
    lower = flag(iota((LANES, LANES), 1) <= iota((LANES, LANES), 0))
    within = dot(folded, upper)
    whole = dot(folded, jnp.ones((LANES, LANES), BF))
    base = jnp.zeros((1, 1), F32)
    passed = jnp.zeros((1, LANES), F32)
    for fold in range(folded.shape[0]):
        ended = within[fold : fold + 1] + passed <= first_float
        base = base + jnp.sum(jnp.where(ended, 1.0, 0.0), axis=1, keepdims=True)
        part = slice(fold * LANES, (fold + 1) * LANES)
        ends[part, :] = passed + dot_t(lower, counts_lane[:, part])
        passed = passed + whole[fold : fold + 1]

    token_lane = iota((SLOTS, tokens), 1).astype(F32)
    slot_token = iota((SLOTS, tokens), 0).astype(F32) + base
    slot_end = dot_t(flag(token_lane <= slot_token), counts_lane)
    slot_start = dot_t(flag(token_lane < slot_token), counts_lane)
    atom_lane = iota((SLOTS, rows), 1).astype(F32) + first_float
    member[...] = flag((atom_lane >= slot_start[:, :rows]) & (atom_lane < slot_end[:, :rows]))
    slot_scale[...] = 1.0 / jnp.maximum(slot_end - slot_start, 1.0)
    last_atom = first_float + (rows - 1)
    is_last = jnp.where((slot_start <= last_atom) & (slot_end > last_atom), 1.0, 0.0)
    last[...] = is_last
    goes_on[...] = is_last * jnp.where(slot_end > first_float + rows, 1.0, 0.0)
    is_first = iota((SLOTS, LANES), 0) == 0
    before[...] = jnp.where(is_first & (slot_start < first_float), 1.0, 0.0)

    def rows_step(at):
        def spread(lanes, axis):
            return iota((DESTS, BLOCK, lanes), axis).reshape(DESTS * BLOCK, lanes)

        here = span(at, DESTS * BLOCK)
        token_at = iota((DESTS * BLOCK, tokens), 1)
        turn = spread(tokens, 1) - lead
        row_token = (spread(tokens, 0) + at * DESTS) * own_tokens + turn % own_tokens
        row_end = dot_t(flag(token_at <= row_token), counts_wide)
        row_start = dot_t(flag(token_at < row_token), counts_wide)
        lanes = tiles * rows
        lane = iota((DESTS * BLOCK, lanes), 1)
        atom = (lane % rows + first).astype(F32)
        turn = spread(lanes, 1) - lead
        tile_fits = (turn >= 0) & (turn // own_tokens == lane // rows)
        picks[here, :] = flag(tile_fits & (atom >= row_start) & (atom < row_end))
        row_scale[here, :] = 1.0 / jnp.maximum(row_end - row_start, 1.0)[:, :LANES]

    repeat(devices // DESTS, rows_step)

    row_tokens = tokens // lax.axis_size("row")
    col_tokens = tokens // lax.axis_size("col")
    first_row = lax.axis_index("row") * row_tokens
    first_col = lax.axis_index("col") * col_tokens

    def adder_step(at):
        here = span(at, LANES)
        spot_lane = iota((1, LANES), 1) + at * LANES
        block = spot_lane // BLOCK
        spot = spot_lane % BLOCK
        edge = (block * rows).astype(F32)
        tally = jnp.zeros((1, LANES), F32)
        for fold in range(tokens // LANES):
            ended = jnp.where(ends[fold * LANES : (fold + 1) * LANES, :] <= edge, 1.0, 0.0)
            tally = tally + jnp.sum(ended, axis=0, keepdims=True)
        token = jnp.where(spot < slots, tally.astype(jnp.int32) + spot, -1)
        line = iota((SLOTS, LANES), 0)
        wanted = jnp.where(
            line == token_rows,
            (position - 1) * BLOCK + slots + 1,
            jnp.where(line == token_rows + 1, (position + 1) * BLOCK + slots, -1),
        )
        fixed = (spot_lane == wanted) | ((line < token_rows) & (spot == line + lead))
        lefts = token == iota((row_tokens, LANES), 0) + first_row
        rights = token == iota((col_tokens, LANES), 0) + first_col
        adder[:SLOTS, here] = flag(fixed)
        adder[SLOTS : SLOTS + row_tokens, here] = flag(lefts)
        adder[SLOTS + row_tokens :, here] = flag(rights)

    repeat(devices * BLOCK // LANES, adder_step)

    for copy in copies[2:8]:
        copy.wait()
    raw = own[...].astype(F32)
    own_float[...] = raw
    normed = layer_norm(raw, atom_gain[...]).astype(BF)
    near = dot(normed, w_kv[...]).astype(BF)
    keyval[...] = near
    query = dot(normed, w_query[...]).astype(BF)
    head_of = iota((1, width), 1) // (width // HEADS)
    heads = jnp.concatenate([query * flag(head_of == h) for h in range(HEADS)], axis=0)
    stacked[...] = heads
    near_index = first + iota((1, rows), 1)
    far_lane = iota((1, 2 * rows), 1)
    is_low = (far_lane < rows) != even
    far_index = first + far_lane % rows + jnp.where(is_low, -rows, rows)
    near_bias, bias = [], []
    for e in range(rows // QB):
        low = key_starts[0:1, e : e + 1]
        seen = (near_index >= low) & (near_index < low + KW)
        near_bias.append(jnp.broadcast_to(jnp.where(seen, 0.0, MASKED), (QB, rows)))
        seen = (far_index >= low) & (far_index < low + KW)
        seen = seen & (far_index >= 0) & (far_index < atoms)
        bias.append(jnp.broadcast_to(jnp.where(seen, 0.0, MASKED), (QB, 2 * rows)))
    far_bias[...] = jnp.concatenate(bias, axis=0)
    raw_scores = dot_t(heads, near[:, :width]) + jnp.concatenate(near_bias * HEADS, axis=0)
    scores[...] = raw_scores
    top[...] = jnp.max(raw_scores, axis=-1, keepdims=True)
    for copy in copies[8:]:
        copy.wait()
    pair_width = w_outer_far.shape[1]
    average = jnp.full((pair_width, pair_width), 1.0 / pair_width, F32).astype(BF)
    w_outer[:, pair_width:] = dot(w_outer[:, :pair_width], average).astype(BF)


def atom_kernel(
    neighbour,
    sibling,
    own_float,
    keyval,
    stacked,
    scores,
    top,
    far_bias,
    picks,
    row_scale,
    member,
    slot_scale,
    before,
    goes_on,
    atom_gain,
    w_kv,
    w_out,
    w_pool,
    w_back,
    w_sides,
    payload,
    updated,
    slot_back,
):
    rows, width = own_float.shape
    tiles = w_pool.shape[1] // LANES
    devices = payload.shape[0] // BLOCK
    slots = rows // FEWEST + 1
    raw = jnp.concatenate([sibling[...], neighbour[...]], axis=0).astype(F32)
    normed = layer_norm(raw, atom_gain[...]).astype(BF)
    far = dot(normed, w_kv[...]).astype(BF)
    far_scores = dot_t(stacked[...], far[:, :width])
    far_scores = far_scores + jnp.concatenate([far_bias[...]] * HEADS, axis=0)
    most = jnp.maximum(top[...], jnp.max(far_scores, axis=-1, keepdims=True))
    scale = (width // HEADS) ** (-0.5) * LOG2E
    raised = jnp.concatenate(
        [
            jnp.exp2((far_scores - most) * scale).astype(BF),
            jnp.exp2((scores[...] - most) * scale).astype(BF),
        ],
        axis=1,
    )
    values = jnp.concatenate([far[:, width:], keyval[:, width:]], axis=0)
    mixed = dot(raised, jnp.concatenate([values, jnp.ones((3 * rows, width), BF)], axis=1))
    head_of = iota((1, width), 1) // (width // HEADS)
    head_mask = [(head_of == h).astype(F32) for h in range(HEADS)]
    total = sum(mixed[h * rows : (h + 1) * rows, :width] * head_mask[h] for h in range(HEADS))
    weight = sum(mixed[h * rows : (h + 1) * rows, width:] * head_mask[h] for h in range(HEADS))
    attended = (total / weight).astype(BF)
    fresh = (own_float[...] + dot(attended, w_out[...])).astype(BF)
    updated[...] = fresh
    feature = jnp.maximum(dot(fresh, w_pool[...]), 0.0).astype(BF)
    feature_tiles = jnp.concatenate(
        [feature[:, k * LANES : (k + 1) * LANES] for k in range(tiles)], axis=0
    )
    slot_single = (
        dot(member[...], feature) * jnp.concatenate([slot_scale[...]] * tiles, axis=1)
    ).astype(BF)
    sides = dot_t(slot_single, w_sides[...])
    backs = dot(slot_single, w_back[...])
    slot_back[...] = backs
    to_before = jnp.sum(backs * before[...], axis=0, keepdims=True)
    to_after = jnp.sum(backs * goes_on[...], axis=0, keepdims=True)
    spot = iota((SLOTS, LANES), 0)
    shared = jnp.where(
        spot < slots,
        sides,
        jnp.where(spot == slots, to_before, jnp.where(spot == slots + 1, to_after, 0.0)),
    )
    shared = jnp.concatenate([shared, jnp.zeros((BLOCK - SLOTS, LANES), F32)], axis=0)

    def send_step(at):
        here = span(at, DESTS * BLOCK)
        singles = dot(picks[here, :], feature_tiles) * row_scale[here, :]
        singles = singles.reshape(DESTS, BLOCK, LANES) + shared[None]
        payload[here, :] = singles.reshape(DESTS * BLOCK, LANES).astype(BF)

    repeat(devices // DESTS, send_step)


def pair_kernel(
    arrived,
    adder,
    updated,
    slot_back,
    slot_last,
    slot_member,
    pair_state,
    w_outer,
    pair_gain,
    w_gate,
    w_lift,
    w_drop,
    atom_out,
    token_single,
    pair_out,
):
    row_tokens, col_tokens, pair_width = pair_state.shape
    own_tokens, channels = token_single.shape
    tiles = channels // LANES
    token_rows = own_tokens * tiles
    opm = math.isqrt(w_outer.shape[0])
    added = dot(adder[...], arrived[...])
    half_gate = w_gate[...] * jnp.asarray(0.5, BF)
    left = added[SLOTS : SLOTS + row_tokens, :opm].astype(BF)
    right = added[SLOTS + row_tokens :, opm : 2 * opm].astype(BF)
    product_lane = iota((opm, opm * opm), 1)
    unit = iota((opm, opm * opm), 0)
    left_wide = dot(left, flag(product_lane // opm == unit))
    right_wide = dot(right, flag(product_lane % opm == unit))

    average = jnp.full((pair_width, pair_width), 1.0 / pair_width, F32).astype(BF)

    def pair_rows(lefts, here):
        products = jnp.concatenate(
            [(lefts[i : i + 1, :] * right_wide).astype(BF) for i in range(PAIR_ROWS)], axis=0
        )
        flat = pair_state[pl.ds(here, PAIR_ROWS)].reshape(PAIR_ROWS * col_tokens, pair_width)
        outer = dot(products, w_outer[...])
        summed = flat.astype(F32) + outer[:, :pair_width]
        centred = summed - (dot(flat, average) + outer[:, pair_width:])
        variance = dot((centred * centred).astype(BF), average)
        normed = (centred * lax.rsqrt(variance + EPSILON) * pair_gain[...]).astype(BF)
        gate = dot(normed, half_gate)
        lift = dot(normed, w_lift[...])
        hidden = (gate * lift * (1.0 + jnp.tanh(gate))).astype(BF)
        result = (summed + dot(hidden, w_drop[...])).astype(BF)
        pair_out[pl.ds(here, PAIR_ROWS)] = result.reshape(PAIR_ROWS, col_tokens, pair_width)

    for step in range(row_tokens // PAIR_ROWS):
        here = step * PAIR_ROWS
        pair_rows(left_wide[here : here + PAIR_ROWS], here)

    token_single[...] = jnp.concatenate(
        [added[k * own_tokens : (k + 1) * own_tokens] for k in range(tiles)], axis=1
    ).astype(BF)
    spot = iota((SLOTS, LANES), 0)
    from_before = jnp.where(spot == 0, added[token_rows : token_rows + 1], 0.0)
    from_after = slot_last[...] * added[token_rows + 1 : token_rows + 2]
    back = (slot_back[...] + from_before + from_after).astype(BF)
    lifted = lax.dot_general(
        slot_member[...], back, (((0,), (0,)), ((), ())), preferred_element_type=F32
    )
    atom_out[...] = (updated[...].astype(F32) + lifted).astype(BF)


def call(kernel, name, operands, outputs, far=(), scratch=()):
    near_spec = pl.BlockSpec(memory_space=pltpu.VMEM)
    far_spec = pl.BlockSpec(memory_space=pltpu.HBM)
    held = sum(math.prod(a.shape) * a.dtype.itemsize for a in operands + outputs)
    return pl.pallas_call(
        kernel,
        out_shape=outputs,
        in_specs=[far_spec] * len(far) + [near_spec] * len(operands),
        out_specs=(near_spec,) * len(outputs),
        scratch_shapes=scratch,
        compiler_params=pltpu.CompilerParams(vmem_limit_bytes=min(2 * held + SPARE, MOST)),
        name=name,
    )(*[pltpu.with_memory_space_constraint(a, pltpu.HBM) for a in far], *operands)


def per_device(
    atom_feats,
    key_starts,
    atom_counts,
    atom_gain,
    w_query,
    w_key,
    w_value,
    w_out,
    w_pool,
    w_back,
    pair_state,
    w_left,
    w_right,
    w_outer,
    pair_gain,
    w_gate,
    w_lift,
    w_drop,
):
    rows, width = atom_feats.shape
    devices = lax.axis_size(AXES)
    tokens = atom_counts.shape[0]
    channels = w_pool.shape[1]
    opm = w_left.shape[1]
    own_tokens = tokens // devices
    row_tokens, col_tokens, _ = pair_state.shape
    tiles = channels // LANES
    opm = w_left.shape[1]
    across = [(i, i + 1) for i in range(1, devices - 1, 2)]
    neighbour = lax.ppermute(atom_feats, AXES, across + [(j, i) for i, j in across])
    sibling = lax.ppermute(atom_feats, AXES, [(i, i ^ 1) for i in range(devices)])

    def held(*shape, dtype=F32):
        return jax.ShapeDtypeStruct(shape, dtype)

    counts_folded = atom_counts.reshape(-1, LANES)
    ready = call(
        ready_kernel,
        "ready",
        (),
        (
            held(rows, width),
            held(rows, 2 * width, dtype=BF),
            held(HEADS * rows, width, dtype=BF),
            held(HEADS * rows, rows),
            held(HEADS * rows, 1),
            held(rows, 2 * rows),
            held(devices * BLOCK, tiles * rows, dtype=BF),
            held(devices * BLOCK, LANES),
            held(SLOTS, rows, dtype=BF),
            held(SLOTS, LANES),
            held(SLOTS, LANES),
            held(SLOTS, LANES),
            held(SLOTS, LANES),
            held(SLOTS + row_tokens + col_tokens, devices * BLOCK, dtype=BF),
            held(1, width),
            held(1, LANES),
            held(width, 2 * width, dtype=BF),
            held(width, width, dtype=BF),
            held(width, channels, dtype=BF),
            held(channels, width, dtype=BF),
            held(LANES, channels, dtype=BF),
            held(opm * opm, 2 * w_outer.shape[-1], dtype=BF),
        ),
        far=(
            atom_feats,
            key_starts[None],
            atom_counts[None],
            counts_folded,
            atom_gain[None],
            pair_gain[None],
            w_query,
            w_key,
            w_value,
            w_out,
            w_pool,
            w_back,
            w_left.T,
            w_right.T,
            w_outer.reshape(opm * opm, -1),
        ),
        scratch=(
            pltpu.VMEM((rows, width), BF),
            pltpu.VMEM((1, key_starts.shape[0]), jnp.int32),
            pltpu.VMEM((1, tokens), jnp.int32),
            pltpu.VMEM(counts_folded.shape, jnp.int32),
            pltpu.VMEM((width, width), BF),
            pltpu.VMEM((tokens, LANES), F32),
            pltpu.SemaphoreType.DMA((15,)),
        ),
    )
    (
        own_float,
        keyval,
        stacked,
        scores,
        top,
        far_bias,
        picks,
        row_scale,
        member,
        slot_scale,
        before,
        goes_on,
        last,
        adder,
        atom_gain_kept,
        pair_gain_kept,
        *kept,
        w_outer_kept,
    ) = ready
    payload, updated, slot_back = call(
        atom_kernel,
        "atoms",
        (
            neighbour,
            sibling,
            own_float,
            keyval,
            stacked,
            scores,
            top,
            far_bias,
            picks,
            row_scale,
            member,
            slot_scale,
            before,
            goes_on,
            atom_gain_kept,
            *kept,
        ),
        (
            held(devices * BLOCK, LANES, dtype=BF),
            held(rows, width, dtype=BF),
            held(SLOTS, width),
        ),
    )
    arrived = lax.all_to_all(payload.reshape(devices, BLOCK, LANES), AXES, 0, 0)
    return call(
        pair_kernel,
        "pairs",
        (
            arrived.reshape(devices * BLOCK, LANES),
            adder,
            updated,
            slot_back,
            last,
            member,
            pair_state,
            w_outer_kept,
            pair_gain_kept,
            w_gate,
            w_lift,
            w_drop,
        ),
        (
            held(rows, width, dtype=BF),
            held(own_tokens, channels, dtype=BF),
            held(*pair_state.shape, dtype=BF),
        ),
    )


def solution(mesh):
    in_specs = (
        P(("row", "col"), None),
        P(("row", "col")),
        P(),
        P(),
        P(),
        P(),
        P(),
        P(),
        P(),
        P(),
        P("row", "col", None),
        P(),
        P(),
        P(),
        P(),
        P(),
        P(),
        P(),
    )
    out_specs = (P(("row", "col"), None), P(("row", "col"), None), P("row", "col", None))
    return jax.shard_map(
        per_device, mesh=mesh, in_specs=in_specs, out_specs=out_specs, check_vma=False
    )
```

```python
import math

import jax
import jax.numpy as jnp
from jax import lax
from jax.experimental import pallas as pl
from jax.experimental.pallas import tpu as pltpu
from jax.sharding import PartitionSpec as P

HEADS = 4
QB = 32
KW = 128
EPSILON = 1e-05
HALF = KW // 2
FEWEST = 8
LANES = 128
SLOTS = 16
BLOCK = 24
DESTS = 32
PAIR_ROWS = 16
MASKED = -1e30
SPARE = 12 << 20
MOST = 60 << 20
LOG2E = 1.4426950408889634
AXES = ("row", "col")
BF = jnp.bfloat16
F32 = jnp.float32


def layer_norm(values, gain):
    mean_value = jnp.mean(values, axis=-1, keepdims=True)
    centred = values - mean_value
    variance = jnp.mean(centred * centred, axis=-1, keepdims=True)
    return centred * lax.rsqrt(variance + EPSILON) * gain


def dot(a, b):
    return jnp.dot(a, b, preferred_element_type=F32)


def dot_t(a, b):
    return lax.dot_general(a, b, (((1,), (1,)), ((), ())), preferred_element_type=F32)


def iota(shape, axis):
    return lax.broadcasted_iota(jnp.int32, shape, axis)


def flag(mask):
    return jnp.where(mask, 1.0, 0.0).astype(BF)


def place():
    return lax.axis_index("row") * lax.axis_size("col") + lax.axis_index("col")


def member_at(block, devices):
    return block ^ (devices // 2)


def repeat(count, step):
    if count <= 8:
        for at in range(count):
            step(at)
    else:

        def body(at, carry):
            step(at)
            return carry

        lax.fori_loop(0, count, body, 0)


def span(at, size):
    if isinstance(at, int):
        return pl.ds(at * size, size)
    return pl.ds(pl.multiple_of(at * size, size), size)


def ready_kernel(
    own_far,
    starts_far,
    counts_far,
    folded_far,
    atom_gain_far,
    pair_gain_far,
    w_query_far,
    w_key_far,
    w_value_far,
    w_out_far,
    w_pool_far,
    w_back_far,
    w_left_far,
    w_right_far,
    w_outer_far,
    own_float,
    keyval,
    stacked,
    scores,
    top,
    far_bias,
    picks,
    row_scale,
    member,
    slot_scale,
    before,
    goes_on,
    last,
    adder,
    atom_gain,
    pair_gain,
    w_kv,
    w_out,
    w_pool,
    w_back,
    w_sides,
    w_outer,
    own,
    key_starts,
    counts,
    counts_folded,
    w_query,
    ends,
    arrivals,
):
    rows, width = own.shape
    tokens = counts.shape[1]
    opm = w_left_far.shape[0]
    pairs = (
        (counts_far, counts),
        (folded_far, counts_folded),
        (own_far, own),
        (starts_far, key_starts),
        (atom_gain_far, atom_gain),
        (w_query_far, w_query),
        (w_key_far, w_kv.at[:, :width]),
        (w_value_far, w_kv.at[:, width:]),
        (pair_gain_far, pair_gain),
        (w_out_far, w_out),
        (w_pool_far, w_pool),
        (w_back_far, w_back),
        (w_left_far, w_sides.at[:opm]),
        (w_right_far, w_sides.at[opm : 2 * opm]),
        (w_outer_far, w_outer.at[:, : w_outer_far.shape[1]]),
    )
    copies = [pltpu.make_async_copy(a, b, arrivals.at[k]) for k, (a, b) in enumerate(pairs)]
    for copy in copies:
        copy.start()

    tiles = picks.shape[1] // rows
    devices = picks.shape[0] // BLOCK
    atoms = rows * devices
    own_tokens = tokens // devices
    token_rows = own_tokens * tiles
    lead = BLOCK - token_rows
    slots = rows // FEWEST + 1
    position = place()
    first = position * rows
    even = position % 2 == 0
    first_float = first.astype(F32)
    w_sides[2 * opm :, :] = jnp.zeros((LANES - 2 * opm, tiles * LANES), BF)

    for copy in copies[:2]:
        copy.wait()
    counts_wide = jnp.broadcast_to(counts[...].astype(F32), (tiles * rows, tokens)).astype(BF)
    counts_lane = counts_wide[:LANES]
    folded = counts_folded[...].astype(F32).astype(BF)
    upper = flag(iota((LANES, LANES), 0) <= iota((LANES, LANES), 1))
    lower = flag(iota((LANES, LANES), 1) <= iota((LANES, LANES), 0))
    within = dot(folded, upper)
    whole = dot(folded, jnp.ones((LANES, LANES), BF))
    base = jnp.zeros((1, 1), F32)
    passed = jnp.zeros((1, LANES), F32)
    for fold in range(folded.shape[0]):
        ended = within[fold : fold + 1] + passed <= first_float
        base = base + jnp.sum(jnp.where(ended, 1.0, 0.0), axis=1, keepdims=True)
        part = slice(fold * LANES, (fold + 1) * LANES)
        ends[part, :] = passed + dot_t(lower, counts_lane[:, part])
        passed = passed + whole[fold : fold + 1]

    token_lane = iota((SLOTS, tokens), 1).astype(F32)
    slot_token = iota((SLOTS, tokens), 0).astype(F32) + base
    slot_end = dot_t(flag(token_lane <= slot_token), counts_lane)
    slot_start = dot_t(flag(token_lane < slot_token), counts_lane)
    atom_lane = iota((SLOTS, rows), 1).astype(F32) + first_float
    member[...] = flag((atom_lane >= slot_start[:, :rows]) & (atom_lane < slot_end[:, :rows]))
    slot_scale[...] = 1.0 / jnp.maximum(slot_end - slot_start, 1.0)
    last_atom = first_float + (rows - 1)
    is_last = jnp.where((slot_start <= last_atom) & (slot_end > last_atom), 1.0, 0.0)
    last[...] = is_last
    goes_on[...] = is_last * jnp.where(slot_end > first_float + rows, 1.0, 0.0)
    is_first = iota((SLOTS, LANES), 0) == 0
    before[...] = jnp.where(is_first & (slot_start < first_float), 1.0, 0.0)

    def rows_step(at):
        def spread(lanes, axis):
            return iota((DESTS, BLOCK, lanes), axis).reshape(DESTS * BLOCK, lanes)

        here = span(at, DESTS * BLOCK)
        token_at = iota((DESTS * BLOCK, tokens), 1)
        turn = spread(tokens, 1) - lead
        dest = member_at(spread(tokens, 0) + at * DESTS, devices)
        row_token = dest * own_tokens + turn % own_tokens
        row_end = dot_t(flag(token_at <= row_token), counts_wide)
        row_start = dot_t(flag(token_at < row_token), counts_wide)
        lanes = tiles * rows
        lane = iota((DESTS * BLOCK, lanes), 1)
        atom = (lane % rows + first).astype(F32)
        turn = spread(lanes, 1) - lead
        tile_fits = (turn >= 0) & (turn // own_tokens == lane // rows)
        picks[here, :] = flag(tile_fits & (atom >= row_start) & (atom < row_end))
        row_scale[here, :] = 1.0 / jnp.maximum(row_end - row_start, 1.0)[:, :LANES]

    repeat(devices // DESTS, rows_step)

    row_tokens = tokens // lax.axis_size("row")
    col_tokens = tokens // lax.axis_size("col")
    first_row = lax.axis_index("row") * row_tokens
    first_col = lax.axis_index("col") * col_tokens

    def adder_step(at):
        here = span(at, LANES)
        spot_lane = iota((1, LANES), 1) + at * LANES
        block = member_at(spot_lane // BLOCK, devices)
        spot = spot_lane % BLOCK
        edge = (block * rows).astype(F32)
        tally = jnp.zeros((1, LANES), F32)
        for fold in range(tokens // LANES):
            ended = jnp.where(ends[fold * LANES : (fold + 1) * LANES, :] <= edge, 1.0, 0.0)
            tally = tally + jnp.sum(ended, axis=0, keepdims=True)
        token = jnp.where(spot < slots, tally.astype(jnp.int32) + spot, -1)
        line = iota((SLOTS, LANES), 0)
        wanted = jnp.where(
            line == token_rows,
            (position - 1) * BLOCK + slots + 1,
            jnp.where(line == token_rows + 1, (position + 1) * BLOCK + slots, -1),
        )
        fixed = (block * BLOCK + spot == wanted) | ((line < token_rows) & (spot == line + lead))
        lefts = token == iota((row_tokens, LANES), 0) + first_row
        rights = token == iota((col_tokens, LANES), 0) + first_col
        adder[:SLOTS, here] = flag(fixed)
        adder[SLOTS : SLOTS + row_tokens, here] = flag(lefts)
        adder[SLOTS + row_tokens :, here] = flag(rights)

    repeat(devices * BLOCK // LANES, adder_step)

    for copy in copies[2:8]:
        copy.wait()
    raw = own[...].astype(F32)
    own_float[...] = raw
    normed = layer_norm(raw, atom_gain[...]).astype(BF)
    near = dot(normed, w_kv[...]).astype(BF)
    keyval[...] = near
    query = dot(normed, w_query[...]).astype(BF)
    head_of = iota((1, width), 1) // (width // HEADS)
    heads = jnp.concatenate([query * flag(head_of == h) for h in range(HEADS)], axis=0)
    stacked[...] = heads
    near_index = first + iota((1, rows), 1)
    far_lane = iota((1, 2 * rows), 1)
    is_low = (far_lane < rows) != even
    far_index = first + far_lane % rows + jnp.where(is_low, -rows, rows)
    near_bias, bias = [], []
    for e in range(rows // QB):
        low = key_starts[0:1, e : e + 1]
        seen = (near_index >= low) & (near_index < low + KW)
        near_bias.append(jnp.broadcast_to(jnp.where(seen, 0.0, MASKED), (QB, rows)))
        seen = (far_index >= low) & (far_index < low + KW)
        seen = seen & (far_index >= 0) & (far_index < atoms)
        bias.append(jnp.broadcast_to(jnp.where(seen, 0.0, MASKED), (QB, 2 * rows)))
    far_bias[...] = jnp.concatenate(bias, axis=0)
    raw_scores = dot_t(heads, near[:, :width]) + jnp.concatenate(near_bias * HEADS, axis=0)
    scores[...] = raw_scores
    top[...] = jnp.max(raw_scores, axis=-1, keepdims=True)
    for copy in copies[8:]:
        copy.wait()
    pair_width = w_outer_far.shape[1]
    average = jnp.full((pair_width, pair_width), 1.0 / pair_width, F32).astype(BF)
    w_outer[:, pair_width:] = dot(w_outer[:, :pair_width], average).astype(BF)


def atom_kernel(
    neighbour,
    sibling,
    own_float,
    keyval,
    stacked,
    scores,
    top,
    far_bias,
    picks,
    row_scale,
    member,
    slot_scale,
    before,
    goes_on,
    atom_gain,
    w_kv,
    w_out,
    w_pool,
    w_back,
    w_sides,
    payload,
    updated,
    slot_back,
):
    rows, width = own_float.shape
    tiles = w_pool.shape[1] // LANES
    devices = payload.shape[0] // BLOCK
    slots = rows // FEWEST + 1
    raw = jnp.concatenate([sibling[...], neighbour[...]], axis=0).astype(F32)
    normed = layer_norm(raw, atom_gain[...]).astype(BF)
    far = dot(normed, w_kv[...]).astype(BF)
    far_scores = dot_t(stacked[...], far[:, :width])
    far_scores = far_scores + jnp.concatenate([far_bias[...]] * HEADS, axis=0)
    most = jnp.maximum(top[...], jnp.max(far_scores, axis=-1, keepdims=True))
    scale = (width // HEADS) ** (-0.5) * LOG2E
    raised = jnp.concatenate(
        [
            jnp.exp2((far_scores - most) * scale).astype(BF),
            jnp.exp2((scores[...] - most) * scale).astype(BF),
        ],
        axis=1,
    )
    values = jnp.concatenate([far[:, width:], keyval[:, width:]], axis=0)
    mixed = dot(raised, jnp.concatenate([values, jnp.ones((3 * rows, width), BF)], axis=1))
    head_of = iota((1, width), 1) // (width // HEADS)
    head_mask = [(head_of == h).astype(F32) for h in range(HEADS)]
    total = sum(mixed[h * rows : (h + 1) * rows, :width] * head_mask[h] for h in range(HEADS))
    weight = sum(mixed[h * rows : (h + 1) * rows, width:] * head_mask[h] for h in range(HEADS))
    attended = (total / weight).astype(BF)
    fresh = (own_float[...] + dot(attended, w_out[...])).astype(BF)
    updated[...] = fresh
    feature = jnp.maximum(dot(fresh, w_pool[...]), 0.0).astype(BF)
    feature_tiles = jnp.concatenate(
        [feature[:, k * LANES : (k + 1) * LANES] for k in range(tiles)], axis=0
    )
    slot_single = (
        dot(member[...], feature) * jnp.concatenate([slot_scale[...]] * tiles, axis=1)
    ).astype(BF)
    sides = dot_t(slot_single, w_sides[...])
    backs = dot(slot_single, w_back[...])
    slot_back[...] = backs
    to_before = jnp.sum(backs * before[...], axis=0, keepdims=True)
    to_after = jnp.sum(backs * goes_on[...], axis=0, keepdims=True)
    spot = iota((SLOTS, LANES), 0)
    shared = jnp.where(
        spot < slots,
        sides,
        jnp.where(spot == slots, to_before, jnp.where(spot == slots + 1, to_after, 0.0)),
    )
    shared = jnp.concatenate([shared, jnp.zeros((BLOCK - SLOTS, LANES), F32)], axis=0)

    def send_step(at):
        here = span(at, DESTS * BLOCK)
        singles = dot(picks[here, :], feature_tiles) * row_scale[here, :]
        singles = singles.reshape(DESTS, BLOCK, LANES) + shared[None]
        payload[here, :] = singles.reshape(DESTS * BLOCK, LANES).astype(BF)

    repeat(devices // DESTS, send_step)


def pair_kernel(
    arrived,
    adder,
    updated,
    slot_back,
    slot_last,
    slot_member,
    pair_state,
    w_outer,
    pair_gain,
    w_gate,
    w_lift,
    w_drop,
    atom_out,
    token_single,
    pair_out,
):
    row_tokens, col_tokens, pair_width = pair_state.shape
    own_tokens, channels = token_single.shape
    tiles = channels // LANES
    token_rows = own_tokens * tiles
    opm = math.isqrt(w_outer.shape[0])
    added = dot(adder[...], arrived[...])
    half_gate = w_gate[...] * jnp.asarray(0.5, BF)
    left = added[SLOTS : SLOTS + row_tokens, :opm].astype(BF)
    right = added[SLOTS + row_tokens :, opm : 2 * opm].astype(BF)
    product_lane = iota((opm, opm * opm), 1)
    unit = iota((opm, opm * opm), 0)
    left_wide = dot(left, flag(product_lane // opm == unit))
    right_wide = dot(right, flag(product_lane % opm == unit))

    average = jnp.full((pair_width, pair_width), 1.0 / pair_width, F32).astype(BF)

    def pair_rows(lefts, here):
        products = jnp.concatenate(
            [(lefts[i : i + 1, :] * right_wide).astype(BF) for i in range(PAIR_ROWS)], axis=0
        )
        flat = pair_state[pl.ds(here, PAIR_ROWS)].reshape(PAIR_ROWS * col_tokens, pair_width)
        outer = dot(products, w_outer[...])
        summed = flat.astype(F32) + outer[:, :pair_width]
        centred = summed - (dot(flat, average) + outer[:, pair_width:])
        variance = dot((centred * centred).astype(BF), average)
        normed = (centred * lax.rsqrt(variance + EPSILON) * pair_gain[...]).astype(BF)
        gate = dot(normed, half_gate)
        lift = dot(normed, w_lift[...])
        hidden = (gate * lift * (1.0 + jnp.tanh(gate))).astype(BF)
        result = (summed + dot(hidden, w_drop[...])).astype(BF)
        pair_out[pl.ds(here, PAIR_ROWS)] = result.reshape(PAIR_ROWS, col_tokens, pair_width)

    for step in range(row_tokens // PAIR_ROWS):
        here = step * PAIR_ROWS
        pair_rows(left_wide[here : here + PAIR_ROWS], here)

    token_single[...] = jnp.concatenate(
        [added[k * own_tokens : (k + 1) * own_tokens] for k in range(tiles)], axis=1
    ).astype(BF)
    spot = iota((SLOTS, LANES), 0)
    from_before = jnp.where(spot == 0, added[token_rows : token_rows + 1], 0.0)
    from_after = slot_last[...] * added[token_rows + 1 : token_rows + 2]
    back = (slot_back[...] + from_before + from_after).astype(BF)
    lifted = lax.dot_general(
        slot_member[...], back, (((0,), (0,)), ((), ())), preferred_element_type=F32
    )
    atom_out[...] = (updated[...].astype(F32) + lifted).astype(BF)


def call(kernel, name, operands, outputs, far=(), scratch=()):
    near_spec = pl.BlockSpec(memory_space=pltpu.VMEM)
    far_spec = pl.BlockSpec(memory_space=pltpu.HBM)
    held = sum(math.prod(a.shape) * a.dtype.itemsize for a in operands + outputs)
    return pl.pallas_call(
        kernel,
        out_shape=outputs,
        in_specs=[far_spec] * len(far) + [near_spec] * len(operands),
        out_specs=(near_spec,) * len(outputs),
        scratch_shapes=scratch,
        compiler_params=pltpu.CompilerParams(vmem_limit_bytes=min(2 * held + SPARE, MOST)),
        name=name,
    )(*[pltpu.with_memory_space_constraint(a, pltpu.HBM) for a in far], *operands)


def per_device(
    atom_feats,
    key_starts,
    atom_counts,
    atom_gain,
    w_query,
    w_key,
    w_value,
    w_out,
    w_pool,
    w_back,
    pair_state,
    w_left,
    w_right,
    w_outer,
    pair_gain,
    w_gate,
    w_lift,
    w_drop,
):
    rows, width = atom_feats.shape
    devices = lax.axis_size(AXES)
    tokens = atom_counts.shape[0]
    channels = w_pool.shape[1]
    opm = w_left.shape[1]
    own_tokens = tokens // devices
    row_tokens, col_tokens, _ = pair_state.shape
    tiles = channels // LANES
    opm = w_left.shape[1]
    across = [(i, i + 1) for i in range(1, devices - 1, 2)]
    neighbour = lax.ppermute(atom_feats, AXES, across + [(j, i) for i, j in across])
    sibling = lax.ppermute(atom_feats, AXES, [(i, i ^ 1) for i in range(devices)])

    def held(*shape, dtype=F32):
        return jax.ShapeDtypeStruct(shape, dtype)

    counts_folded = atom_counts.reshape(-1, LANES)
    ready = call(
        ready_kernel,
        "ready",
        (),
        (
            held(rows, width),
            held(rows, 2 * width, dtype=BF),
            held(HEADS * rows, width, dtype=BF),
            held(HEADS * rows, rows),
            held(HEADS * rows, 1),
            held(rows, 2 * rows),
            held(devices * BLOCK, tiles * rows, dtype=BF),
            held(devices * BLOCK, LANES),
            held(SLOTS, rows, dtype=BF),
            held(SLOTS, LANES),
            held(SLOTS, LANES),
            held(SLOTS, LANES),
            held(SLOTS, LANES),
            held(SLOTS + row_tokens + col_tokens, devices * BLOCK, dtype=BF),
            held(1, width),
            held(1, LANES),
            held(width, 2 * width, dtype=BF),
            held(width, width, dtype=BF),
            held(width, channels, dtype=BF),
            held(channels, width, dtype=BF),
            held(LANES, channels, dtype=BF),
            held(opm * opm, 2 * w_outer.shape[-1], dtype=BF),
        ),
        far=(
            atom_feats,
            key_starts[None],
            atom_counts[None],
            counts_folded,
            atom_gain[None],
            pair_gain[None],
            w_query,
            w_key,
            w_value,
            w_out,
            w_pool,
            w_back,
            w_left.T,
            w_right.T,
            w_outer.reshape(opm * opm, -1),
        ),
        scratch=(
            pltpu.VMEM((rows, width), BF),
            pltpu.VMEM((1, key_starts.shape[0]), jnp.int32),
            pltpu.VMEM((1, tokens), jnp.int32),
            pltpu.VMEM(counts_folded.shape, jnp.int32),
            pltpu.VMEM((width, width), BF),
            pltpu.VMEM((tokens, LANES), F32),
            pltpu.SemaphoreType.DMA((15,)),
        ),
    )
    (
        own_float,
        keyval,
        stacked,
        scores,
        top,
        far_bias,
        picks,
        row_scale,
        member,
        slot_scale,
        before,
        goes_on,
        last,
        adder,
        atom_gain_kept,
        pair_gain_kept,
        *kept,
        w_outer_kept,
    ) = ready
    payload, updated, slot_back = call(
        atom_kernel,
        "atoms",
        (
            neighbour,
            sibling,
            own_float,
            keyval,
            stacked,
            scores,
            top,
            far_bias,
            picks,
            row_scale,
            member,
            slot_scale,
            before,
            goes_on,
            atom_gain_kept,
            *kept,
        ),
        (
            held(devices * BLOCK, LANES, dtype=BF),
            held(rows, width, dtype=BF),
            held(SLOTS, width),
        ),
    )
    order = [[member_at(k, devices) for k in range(devices)]]
    arrived = lax.all_to_all(
        payload.reshape(devices, BLOCK, LANES), AXES, 0, 0, axis_index_groups=order
    )
    return call(
        pair_kernel,
        "pairs",
        (
            arrived.reshape(devices * BLOCK, LANES),
            adder,
            updated,
            slot_back,
            last,
            member,
            pair_state,
            w_outer_kept,
            pair_gain_kept,
            w_gate,
            w_lift,
            w_drop,
        ),
        (
            held(rows, width, dtype=BF),
            held(own_tokens, channels, dtype=BF),
            held(*pair_state.shape, dtype=BF),
        ),
    )


def solution(mesh):
    in_specs = (
        P(("row", "col"), None),
        P(("row", "col")),
        P(),
        P(),
        P(),
        P(),
        P(),
        P(),
        P(),
        P(),
        P("row", "col", None),
        P(),
        P(),
        P(),
        P(),
        P(),
        P(),
        P(),
    )
    out_specs = (P(("row", "col"), None), P(("row", "col"), None), P("row", "col", None))
    return jax.shard_map(
        per_device, mesh=mesh, in_specs=in_specs, out_specs=out_specs, check_vma=False
    )
```

```python
import math

import jax
import jax.numpy as jnp
from jax import lax
from jax.experimental import pallas as pl
from jax.experimental.pallas import tpu as pltpu
from jax.sharding import PartitionSpec as P

HEADS = 4
QB = 32
KW = 128
EPSILON = 1e-05
HALF = KW // 2
FEWEST = 8
LANES = 128
SLOTS = 16
BLOCK = 16
SLOT_ROW = 12
DESTS = 32
PAIR_ROWS = 16
MASKED = -1e30
SPARE = 12 << 20
MOST = 60 << 20
LOG2E = 1.4426950408889634
AXES = ("row", "col")
BF = jnp.bfloat16
F32 = jnp.float32


def layer_norm(values, gain):
    mean_value = jnp.mean(values, axis=-1, keepdims=True)
    centred = values - mean_value
    variance = jnp.mean(centred * centred, axis=-1, keepdims=True)
    return centred * lax.rsqrt(variance + EPSILON) * gain


def dot(a, b):
    return jnp.dot(a, b, preferred_element_type=F32)


def dot_t(a, b):
    return lax.dot_general(a, b, (((1,), (1,)), ((), ())), preferred_element_type=F32)


def iota(shape, axis):
    return lax.broadcasted_iota(jnp.int32, shape, axis)


def flag(mask):
    return jnp.where(mask, 1.0, 0.0).astype(BF)


def place():
    return lax.axis_index("row") * lax.axis_size("col") + lax.axis_index("col")


def overlap(base, first_own, own_tokens, slots):
    inner = jnp.minimum(first_own + own_tokens, base + slots) - jnp.maximum(first_own, base)
    return jnp.maximum(inner, 0)


def edge_row(base, first_own, own_tokens, slots):
    last_own = first_own + own_tokens - 1
    last_held = (last_own >= base) & (last_own < base + slots)
    free = jnp.where(last_held, 0, own_tokens - 1)
    whole = overlap(base, first_own, own_tokens, slots) == own_tokens
    return jnp.where(whole, BLOCK - 1, free)


def repeat(count, step):
    if count <= 8:
        for at in range(count):
            step(at)
    else:

        def body(at, carry):
            step(at)
            return carry

        lax.fori_loop(0, count, body, 0)


def span(at, size):
    if isinstance(at, int):
        return pl.ds(at * size, size)
    return pl.ds(pl.multiple_of(at * size, size), size)


def ready_kernel(
    own_far,
    starts_far,
    counts_far,
    folded_far,
    atom_gain_far,
    pair_gain_far,
    w_query_far,
    w_key_far,
    w_value_far,
    w_out_far,
    w_pool_far,
    w_back_far,
    w_left_far,
    w_right_far,
    w_outer_far,
    own_float,
    keyval,
    stacked,
    scores,
    top,
    far_bias,
    picks,
    row_scale,
    selects,
    member,
    slot_scale,
    before,
    goes_on,
    last,
    adder,
    atom_gain,
    pair_gain,
    w_kv,
    w_out,
    w_pool,
    w_back,
    w_sides,
    w_outer,
    own,
    key_starts,
    counts,
    counts_folded,
    w_query,
    ends,
    arrivals,
):
    rows, width = own.shape
    tokens = counts.shape[1]
    opm = w_left_far.shape[0]
    pairs = (
        (counts_far, counts),
        (folded_far, counts_folded),
        (own_far, own),
        (starts_far, key_starts),
        (atom_gain_far, atom_gain),
        (w_query_far, w_query),
        (w_key_far, w_kv.at[:, :width]),
        (w_value_far, w_kv.at[:, width:]),
        (pair_gain_far, pair_gain),
        (w_out_far, w_out),
        (w_pool_far, w_pool),
        (w_back_far, w_back),
        (w_left_far, w_sides.at[:opm]),
        (w_right_far, w_sides.at[opm : 2 * opm]),
        (w_left_far, w_sides.at[2 * LANES - 2 * opm : 2 * LANES - opm]),
        (w_right_far, w_sides.at[2 * LANES - opm :]),
        (w_outer_far, w_outer.at[:, : w_outer_far.shape[1]]),
    )
    copies = [pltpu.make_async_copy(a, b, arrivals.at[k]) for k, (a, b) in enumerate(pairs)]
    for copy in copies:
        copy.start()

    tiles = picks.shape[1] // rows
    devices = picks.shape[0] // BLOCK
    atoms = rows * devices
    own_tokens = tokens // devices
    token_rows = own_tokens * tiles
    slots = rows // FEWEST + 1
    position = place()
    first = position * rows
    even = position % 2 == 0
    first_float = first.astype(F32)
    w_sides[2 * opm : 2 * LANES - 2 * opm, :] = jnp.zeros(
        (2 * LANES - 4 * opm, tiles * LANES), BF
    )

    for copy in copies[:2]:
        copy.wait()
    counts_wide = jnp.broadcast_to(counts[...].astype(F32), (tiles * rows, tokens)).astype(BF)
    counts_lane = counts_wide[:LANES]
    folded = counts_folded[...].astype(F32).astype(BF)
    upper = flag(iota((LANES, LANES), 0) <= iota((LANES, LANES), 1))
    lower = flag(iota((LANES, LANES), 1) <= iota((LANES, LANES), 0))
    within = dot(folded, upper)
    whole = dot(folded, jnp.ones((LANES, LANES), BF))
    base = jnp.zeros((1, 1), F32)
    passed = jnp.zeros((1, LANES), F32)
    for fold in range(folded.shape[0]):
        ended = within[fold : fold + 1] + passed <= first_float
        base = base + jnp.sum(jnp.where(ended, 1.0, 0.0), axis=1, keepdims=True)
        part = slice(fold * LANES, (fold + 1) * LANES)
        ends[part, :] = passed + dot_t(lower, counts_lane[:, part])
        passed = passed + whole[fold : fold + 1]

    base_token = base.astype(jnp.int32)
    token_lane = iota((SLOTS, tokens), 1).astype(F32)
    slot_token = iota((SLOTS, tokens), 0).astype(F32) + base
    slot_end = dot_t(flag(token_lane <= slot_token), counts_lane)
    slot_start = dot_t(flag(token_lane < slot_token), counts_lane)
    atom_lane = iota((SLOTS, rows), 1).astype(F32) + first_float
    member[...] = flag((atom_lane >= slot_start[:, :rows]) & (atom_lane < slot_end[:, :rows]))
    slot_scale[...] = 1.0 / jnp.maximum(slot_end - slot_start, 1.0)
    last_atom = first_float + (rows - 1)
    is_last = jnp.where((slot_start <= last_atom) & (slot_end > last_atom), 1.0, 0.0)
    last[...] = is_last
    goes_on[...] = is_last * jnp.where(slot_end > first_float + rows, 1.0, 0.0)
    is_first = iota((SLOTS, LANES), 0) == 0
    before[...] = jnp.where(is_first & (slot_start < first_float), 1.0, 0.0)

    def rows_step(at):
        def spread(lanes, axis):
            return iota((DESTS, BLOCK, lanes), axis).reshape(DESTS * BLOCK, lanes)

        here = span(at, DESTS * BLOCK)
        token_at = iota((DESTS * BLOCK, tokens), 1)
        turn = spread(tokens, 1) % own_tokens
        row_token = (spread(tokens, 0) + at * DESTS) * own_tokens + turn
        row_end = dot_t(flag(token_at <= row_token), counts_wide)
        row_start = dot_t(flag(token_at < row_token), counts_wide)
        lanes = tiles * rows
        lane = iota((DESTS * BLOCK, lanes), 1)
        atom = (lane % rows + first).astype(F32)
        tile_fits = spread(lanes, 1) // own_tokens == lane // rows
        picks[here, :] = flag(tile_fits & (atom >= row_start) & (atom < row_end))
        row_scale[here, :] = 1.0 / jnp.maximum(row_end - row_start, 1.0)[:, :LANES]
        lanes = 3 * SLOTS
        dest = spread(lanes, 0) + at * DESTS
        spot = spread(lanes, 1)
        kind = iota((DESTS * BLOCK, lanes), 1) // SLOTS
        slot = iota((DESTS * BLOCK, lanes), 1) % SLOTS
        first_own = dest * own_tokens
        shared_tokens = overlap(base_token, first_own, own_tokens, slots)
        token = base_token + slot
        index = jnp.where(token < first_own, slot, slot - shared_tokens)
        mine = (token >= first_own) & (token < first_own + own_tokens)
        room = 2 * (BLOCK - SLOT_ROW)
        target = jnp.where(index < room, SLOT_ROW + index // 2, jnp.where(kind == 0, 0, -1))
        target = jnp.where(index % 2 == kind, target, -1)
        is_slot = (kind < 2) & (slot < slots) & jnp.logical_not(mine) & (spot == target)
        on_edge = spot == edge_row(base_token, first_own, own_tokens, slots)
        beside = jnp.where(slot == 0, position - 1, position + 1)
        is_edge = (kind == 2) & (slot < 2) & on_edge & (dest == beside)
        selects[here, :] = flag(is_slot | is_edge)

    repeat(devices // DESTS, rows_step)

    row_tokens = tokens // lax.axis_size("row")
    col_tokens = tokens // lax.axis_size("col")
    first_row = lax.axis_index("row") * row_tokens
    first_col = lax.axis_index("col") * col_tokens

    def adder_step(at):
        here = span(at, LANES)
        spot_lane = iota((1, LANES), 1) + at * LANES
        block = spot_lane // BLOCK
        spot = spot_lane % BLOCK
        edge = (block * rows).astype(F32)
        tally = jnp.zeros((1, LANES), F32)
        for fold in range(tokens // LANES):
            ended = jnp.where(ends[fold * LANES : (fold + 1) * LANES, :] <= edge, 1.0, 0.0)
            tally = tally + jnp.sum(ended, axis=0, keepdims=True)
        start = tally.astype(jnp.int32)
        first_own = position * own_tokens
        shared_tokens = overlap(start, first_own, own_tokens, slots)

        def token_of(index):
            slot = jnp.where(start + index < first_own, index, index + shared_tokens)
            return jnp.where((index >= 0) & (slot < slots), start + slot, -1)

        in_slots = spot >= SLOT_ROW
        room = 2 * (BLOCK - SLOT_ROW)
        ninth = jnp.where((spot == 0) & (shared_tokens == 0), start + room, -1)
        low_token = jnp.where(in_slots, token_of(2 * (spot - SLOT_ROW)), ninth)
        high_token = jnp.where(in_slots, token_of(2 * (spot - SLOT_ROW) + 1), -1)
        own_token = first_own + spot % own_tokens
        held = (spot < token_rows) & (own_token >= start) & (own_token < start + slots)
        own_token = jnp.where(held, own_token, -1)
        line = iota((SLOTS, LANES), 0)
        side = jnp.where(line == token_rows, position - 1, position + 1)
        on_edge = spot == edge_row(start, first_own, own_tokens, slots)
        is_edge = (line >= token_rows) & (line < token_rows + 2) & on_edge & (block == side)
        lines = [(line < token_rows) & (spot == line) & held | is_edge]
        row_line = iota((row_tokens, LANES), 0) + first_row
        col_line = iota((col_tokens, LANES), 0) + first_col
        for wanted in (row_line, col_line):
            lines += [low_token == wanted, high_token == wanted]
        for tile in range(tiles):
            tile_token = jnp.where(spot // own_tokens == tile, own_token, -1)
            lines += [tile_token == row_line, tile_token == col_line]
        top = 0
        for part in lines:
            adder[top : top + part.shape[0], here] = flag(part)
            top += part.shape[0]

    repeat(devices * BLOCK // LANES, adder_step)

    for copy in copies[2:8]:
        copy.wait()
    raw = own[...].astype(F32)
    own_float[...] = raw
    normed = layer_norm(raw, atom_gain[...]).astype(BF)
    near = dot(normed, w_kv[...]).astype(BF)
    keyval[...] = near
    query = dot(normed, w_query[...]).astype(BF)
    head_of = iota((1, width), 1) // (width // HEADS)
    heads = jnp.concatenate([query * flag(head_of == h) for h in range(HEADS)], axis=0)
    stacked[...] = heads
    near_index = first + iota((1, rows), 1)
    far_lane = iota((1, 2 * rows), 1)
    is_low = (far_lane < rows) != even
    far_index = first + far_lane % rows + jnp.where(is_low, -rows, rows)
    near_bias, bias = [], []
    for e in range(rows // QB):
        low = key_starts[0:1, e : e + 1]
        seen = (near_index >= low) & (near_index < low + KW)
        near_bias.append(jnp.broadcast_to(jnp.where(seen, 0.0, MASKED), (QB, rows)))
        seen = (far_index >= low) & (far_index < low + KW)
        seen = seen & (far_index >= 0) & (far_index < atoms)
        bias.append(jnp.broadcast_to(jnp.where(seen, 0.0, MASKED), (QB, 2 * rows)))
    far_bias[...] = jnp.concatenate(bias, axis=0)
    raw_scores = dot_t(heads, near[:, :width]) + jnp.concatenate(near_bias * HEADS, axis=0)
    scores[...] = raw_scores
    top[...] = jnp.max(raw_scores, axis=-1, keepdims=True)
    for copy in copies[8:]:
        copy.wait()
    pair_width = w_outer_far.shape[1]
    average = jnp.full((pair_width, pair_width), 1.0 / pair_width, F32).astype(BF)
    w_outer[:, pair_width:] = dot(w_outer[:, :pair_width], average).astype(BF)


def atom_kernel(
    neighbour,
    sibling,
    own_float,
    keyval,
    stacked,
    scores,
    top,
    far_bias,
    picks,
    row_scale,
    selects,
    member,
    slot_scale,
    before,
    goes_on,
    atom_gain,
    w_kv,
    w_out,
    w_pool,
    w_back,
    w_sides,
    payload,
    updated,
    slot_back,
):
    rows, width = own_float.shape
    tiles = w_pool.shape[1] // LANES
    devices = payload.shape[0] // BLOCK
    raw = jnp.concatenate([sibling[...], neighbour[...]], axis=0).astype(F32)
    normed = layer_norm(raw, atom_gain[...]).astype(BF)
    far = dot(normed, w_kv[...]).astype(BF)
    far_scores = dot_t(stacked[...], far[:, :width])
    far_scores = far_scores + jnp.concatenate([far_bias[...]] * HEADS, axis=0)
    most = jnp.maximum(top[...], jnp.max(far_scores, axis=-1, keepdims=True))
    scale = (width // HEADS) ** (-0.5) * LOG2E
    raised = jnp.concatenate(
        [
            jnp.exp2((far_scores - most) * scale).astype(BF),
            jnp.exp2((scores[...] - most) * scale).astype(BF),
        ],
        axis=1,
    )
    values = jnp.concatenate([far[:, width:], keyval[:, width:]], axis=0)
    mixed = dot(raised, jnp.concatenate([values, jnp.ones((3 * rows, width), BF)], axis=1))
    head_of = iota((1, width), 1) // (width // HEADS)
    head_mask = [(head_of == h).astype(F32) for h in range(HEADS)]
    total = sum(mixed[h * rows : (h + 1) * rows, :width] * head_mask[h] for h in range(HEADS))
    weight = sum(mixed[h * rows : (h + 1) * rows, width:] * head_mask[h] for h in range(HEADS))
    attended = (total / weight).astype(BF)
    fresh = (own_float[...] + dot(attended, w_out[...])).astype(BF)
    updated[...] = fresh
    feature = jnp.maximum(dot(fresh, w_pool[...]), 0.0).astype(BF)
    feature_tiles = jnp.concatenate(
        [feature[:, k * LANES : (k + 1) * LANES] for k in range(tiles)], axis=0
    )
    slot_single = (
        dot(member[...], feature) * jnp.concatenate([slot_scale[...]] * tiles, axis=1)
    ).astype(BF)
    sides = dot_t(slot_single, w_sides[...]).astype(BF)
    backs = dot(slot_single, w_back[...])
    slot_back[...] = backs
    to_before = jnp.sum(backs * before[...], axis=0, keepdims=True)
    to_after = jnp.sum(backs * goes_on[...], axis=0, keepdims=True)
    spot = iota((SLOTS, LANES), 0)
    edges = jnp.where(spot == 0, to_before, jnp.where(spot == 1, to_after, 0.0)).astype(BF)
    shared = jnp.concatenate([sides[:, :LANES], sides[:, LANES:], edges], axis=0)

    def send_step(at):
        here = span(at, DESTS * BLOCK)
        singles = dot(picks[here, :], feature_tiles) * row_scale[here, :]
        payload[here, :] = (singles + dot(selects[here, :], shared)).astype(BF)

    repeat(devices // DESTS, send_step)


def pair_kernel(
    arrived,
    adder,
    updated,
    slot_back,
    slot_last,
    slot_member,
    pair_state,
    w_outer,
    pair_gain,
    w_gate,
    w_lift,
    w_drop,
    w_sides,
    atom_out,
    token_single,
    pair_out,
):
    row_tokens, col_tokens, pair_width = pair_state.shape
    own_tokens, channels = token_single.shape
    tiles = channels // LANES
    token_rows = own_tokens * tiles
    opm = math.isqrt(w_outer.shape[0])
    added = dot(adder[...], arrived[...])
    half_gate = w_gate[...] * jnp.asarray(0.5, BF)
    parts, top = [], 0
    for height in (SLOTS,) + (row_tokens,) * 2 + (col_tokens,) * 2 + (row_tokens, col_tokens) * tiles:
        parts.append(added[top : top + height])
        top += height
    sums, left_low, left_high, right_low, right_high, *own = parts
    own_left = jnp.concatenate(own[0::2], axis=1).astype(BF)
    own_right = jnp.concatenate(own[1::2], axis=1).astype(BF)
    own_sides = dot_t(jnp.concatenate([own_left, own_right], axis=0), w_sides[:LANES])
    left = left_low[:, :opm] + left_high[:, 2 * opm : 3 * opm] + own_sides[:row_tokens, :opm]
    right = right_low[:, opm : 2 * opm] + right_high[:, 3 * opm : 4 * opm]
    right = right + own_sides[row_tokens:, opm : 2 * opm]
    left, right = left.astype(BF), right.astype(BF)
    product_lane = iota((opm, opm * opm), 1)
    unit = iota((opm, opm * opm), 0)
    left_wide = dot(left, flag(product_lane // opm == unit))
    right_wide = dot(right, flag(product_lane % opm == unit))

    average = jnp.full((pair_width, pair_width), 1.0 / pair_width, F32).astype(BF)

    def pair_rows(lefts, here):
        products = jnp.concatenate(
            [(lefts[i : i + 1, :] * right_wide).astype(BF) for i in range(PAIR_ROWS)], axis=0
        )
        flat = pair_state[pl.ds(here, PAIR_ROWS)].reshape(PAIR_ROWS * col_tokens, pair_width)
        outer = dot(products, w_outer[...])
        summed = flat.astype(F32) + outer[:, :pair_width]
        centred = summed - (dot(flat, average) + outer[:, pair_width:])
        variance = dot((centred * centred).astype(BF), average)
        normed = (centred * lax.rsqrt(variance + EPSILON) * pair_gain[...]).astype(BF)
        gate = dot(normed, half_gate)
        lift = dot(normed, w_lift[...])
        hidden = (gate * lift * (1.0 + jnp.tanh(gate))).astype(BF)
        result = (summed + dot(hidden, w_drop[...])).astype(BF)
        pair_out[pl.ds(here, PAIR_ROWS)] = result.reshape(PAIR_ROWS, col_tokens, pair_width)

    for step in range(row_tokens // PAIR_ROWS):
        here = step * PAIR_ROWS
        pair_rows(left_wide[here : here + PAIR_ROWS], here)

    token_single[...] = jnp.concatenate(
        [sums[k * own_tokens : (k + 1) * own_tokens] for k in range(tiles)], axis=1
    ).astype(BF)
    spot = iota((SLOTS, LANES), 0)
    from_before = jnp.where(spot == 0, sums[token_rows : token_rows + 1], 0.0)
    from_after = slot_last[...] * sums[token_rows + 1 : token_rows + 2]
    back = (slot_back[...] + from_before + from_after).astype(BF)
    lifted = lax.dot_general(
        slot_member[...], back, (((0,), (0,)), ((), ())), preferred_element_type=F32
    )
    atom_out[...] = (updated[...].astype(F32) + lifted).astype(BF)


def call(kernel, name, operands, outputs, far=(), scratch=()):
    near_spec = pl.BlockSpec(memory_space=pltpu.VMEM)
    far_spec = pl.BlockSpec(memory_space=pltpu.HBM)
    held = sum(math.prod(a.shape) * a.dtype.itemsize for a in operands + outputs)
    return pl.pallas_call(
        kernel,
        out_shape=outputs,
        in_specs=[far_spec] * len(far) + [near_spec] * len(operands),
        out_specs=(near_spec,) * len(outputs),
        scratch_shapes=scratch,
        compiler_params=pltpu.CompilerParams(vmem_limit_bytes=min(2 * held + SPARE, MOST)),
        name=name,
    )(*[pltpu.with_memory_space_constraint(a, pltpu.HBM) for a in far], *operands)


def per_device(
    atom_feats,
    key_starts,
    atom_counts,
    atom_gain,
    w_query,
    w_key,
    w_value,
    w_out,
    w_pool,
    w_back,
    pair_state,
    w_left,
    w_right,
    w_outer,
    pair_gain,
    w_gate,
    w_lift,
    w_drop,
):
    rows, width = atom_feats.shape
    devices = lax.axis_size(AXES)
    tokens = atom_counts.shape[0]
    channels = w_pool.shape[1]
    opm = w_left.shape[1]
    own_tokens = tokens // devices
    row_tokens, col_tokens, _ = pair_state.shape
    tiles = channels // LANES
    opm = w_left.shape[1]
    across = [(i, i + 1) for i in range(1, devices - 1, 2)]
    neighbour = lax.ppermute(atom_feats, AXES, across + [(j, i) for i, j in across])
    sibling = lax.ppermute(atom_feats, AXES, [(i, i ^ 1) for i in range(devices)])

    def held(*shape, dtype=F32):
        return jax.ShapeDtypeStruct(shape, dtype)

    counts_folded = atom_counts.reshape(-1, LANES)
    ready = call(
        ready_kernel,
        "ready",
        (),
        (
            held(rows, width),
            held(rows, 2 * width, dtype=BF),
            held(HEADS * rows, width, dtype=BF),
            held(HEADS * rows, rows),
            held(HEADS * rows, 1),
            held(rows, 2 * rows),
            held(devices * BLOCK, tiles * rows, dtype=BF),
            held(devices * BLOCK, LANES),
            held(devices * BLOCK, 3 * SLOTS, dtype=BF),
            held(SLOTS, rows, dtype=BF),
            held(SLOTS, LANES),
            held(SLOTS, LANES),
            held(SLOTS, LANES),
            held(SLOTS, LANES),
            held(
                SLOTS + (2 + tiles) * (row_tokens + col_tokens), devices * BLOCK, dtype=BF
            ),
            held(1, width),
            held(1, LANES),
            held(width, 2 * width, dtype=BF),
            held(width, width, dtype=BF),
            held(width, channels, dtype=BF),
            held(channels, width, dtype=BF),
            held(2 * LANES, channels, dtype=BF),
            held(opm * opm, 2 * w_outer.shape[-1], dtype=BF),
        ),
        far=(
            atom_feats,
            key_starts[None],
            atom_counts[None],
            counts_folded,
            atom_gain[None],
            pair_gain[None],
            w_query,
            w_key,
            w_value,
            w_out,
            w_pool,
            w_back,
            w_left.T,
            w_right.T,
            w_outer.reshape(opm * opm, -1),
        ),
        scratch=(
            pltpu.VMEM((rows, width), BF),
            pltpu.VMEM((1, key_starts.shape[0]), jnp.int32),
            pltpu.VMEM((1, tokens), jnp.int32),
            pltpu.VMEM(counts_folded.shape, jnp.int32),
            pltpu.VMEM((width, width), BF),
            pltpu.VMEM((tokens, LANES), F32),
            pltpu.SemaphoreType.DMA((17,)),
        ),
    )
    (
        own_float,
        keyval,
        stacked,
        scores,
        top,
        far_bias,
        picks,
        row_scale,
        selects,
        member,
        slot_scale,
        before,
        goes_on,
        last,
        adder,
        atom_gain_kept,
        pair_gain_kept,
        *kept,
        w_outer_kept,
    ) = ready
    payload, updated, slot_back = call(
        atom_kernel,
        "atoms",
        (
            neighbour,
            sibling,
            own_float,
            keyval,
            stacked,
            scores,
            top,
            far_bias,
            picks,
            row_scale,
            selects,
            member,
            slot_scale,
            before,
            goes_on,
            atom_gain_kept,
            *kept,
        ),
        (
            held(devices * BLOCK, LANES, dtype=BF),
            held(rows, width, dtype=BF),
            held(SLOTS, width),
        ),
    )
    arrived = lax.all_to_all(payload.reshape(devices, BLOCK, LANES), AXES, 0, 0)
    return call(
        pair_kernel,
        "pairs",
        (
            arrived.reshape(devices * BLOCK, LANES),
            adder,
            updated,
            slot_back,
            last,
            member,
            pair_state,
            w_outer_kept,
            pair_gain_kept,
            w_gate,
            w_lift,
            w_drop,
            kept[-1],
        ),
        (
            held(rows, width, dtype=BF),
            held(own_tokens, channels, dtype=BF),
            held(*pair_state.shape, dtype=BF),
        ),
    )


def solution(mesh):
    in_specs = (
        P(("row", "col"), None),
        P(("row", "col")),
        P(),
        P(),
        P(),
        P(),
        P(),
        P(),
        P(),
        P(),
        P("row", "col", None),
        P(),
        P(),
        P(),
        P(),
        P(),
        P(),
        P(),
    )
    out_specs = (P(("row", "col"), None), P(("row", "col"), None), P("row", "col", None))
    return jax.shard_map(
        per_device, mesh=mesh, in_specs=in_specs, out_specs=out_specs, check_vma=False
    )
```

```python
import math

import jax
import jax.numpy as jnp
from jax import lax
from jax.experimental import pallas as pl
from jax.experimental.pallas import tpu as pltpu
from jax.sharding import PartitionSpec as P

HEADS = 4
QB = 32
KW = 128
EPSILON = 1e-05
HALF = KW // 2
FEWEST = 8
LANES = 128
SLOTS = 16
BLOCK = 16
SLOT_ROW = 12
DESTS = 32
PAIR_ROWS = 16
MASKED = -1e30
SPARE = 12 << 20
MOST = 60 << 20
LOG2E = 1.4426950408889634
AXES = ("row", "col")
BF = jnp.bfloat16
F32 = jnp.float32


def dot(a, b):
    return jnp.dot(a, b, preferred_element_type=F32)


def dot_t(a, b):
    return lax.dot_general(a, b, (((1,), (1,)), ((), ())), preferred_element_type=F32)


def iota(shape, axis):
    return lax.broadcasted_iota(jnp.int32, shape, axis)


def centred_rows(values, gain):
    width = values.shape[1]
    average = jnp.full((width, width), 1.0 / width, F32).astype(BF)
    centred = values.astype(F32) - dot(values, average)
    variance = dot((centred * centred).astype(BF), average)
    return (centred * gain).astype(BF), lax.rsqrt(variance + EPSILON)


def flag(mask):
    return jnp.where(mask, 1.0, 0.0).astype(BF)


def place():
    return lax.axis_index("row") * lax.axis_size("col") + lax.axis_index("col")


def overlap(base, first_own, own_tokens, slots):
    inner = jnp.minimum(first_own + own_tokens, base + slots) - jnp.maximum(first_own, base)
    return jnp.maximum(inner, 0)


def edge_row(base, first_own, own_tokens, slots):
    last_own = first_own + own_tokens - 1
    last_held = (last_own >= base) & (last_own < base + slots)
    free = jnp.where(last_held, 0, own_tokens - 1)
    whole = overlap(base, first_own, own_tokens, slots) == own_tokens
    return jnp.where(whole, BLOCK - 1, free)


def repeat(count, step):
    if count <= 8:
        for at in range(count):
            step(at)
    else:

        def body(at, carry):
            step(at)
            return carry

        lax.fori_loop(0, count, body, 0)


def span(at, size):
    if isinstance(at, int):
        return pl.ds(at * size, size)
    return pl.ds(pl.multiple_of(at * size, size), size)


def ready_kernel(
    own_far,
    starts_far,
    counts_far,
    folded_far,
    atom_gain_far,
    pair_gain_far,
    w_query_far,
    w_key_far,
    w_value_far,
    w_out_far,
    w_pool_far,
    w_back_far,
    w_left_far,
    w_right_far,
    w_outer_far,
    own_float,
    keyval,
    stacked,
    scores,
    top,
    far_bias,
    picks,
    row_scale,
    selects,
    member,
    slot_scale,
    before,
    goes_on,
    last,
    adder,
    atom_gain,
    pair_gain,
    w_kv,
    w_out,
    w_pool,
    w_back,
    w_sides,
    w_outer,
    own,
    key_starts,
    counts,
    counts_folded,
    w_query,
    ends,
    arrivals,
):
    rows, width = own.shape
    tokens = counts.shape[1]
    opm = w_left_far.shape[0]
    pairs = (
        (counts_far, counts),
        (folded_far, counts_folded),
        (own_far, own),
        (starts_far, key_starts),
        (atom_gain_far, atom_gain),
        (w_query_far, w_query),
        (w_key_far, w_kv.at[:, :width]),
        (w_value_far, w_kv.at[:, width:]),
        (pair_gain_far, pair_gain),
        (w_out_far, w_out),
        (w_pool_far, w_pool),
        (w_back_far, w_back),
        (w_left_far, w_sides.at[:opm]),
        (w_right_far, w_sides.at[opm : 2 * opm]),
        (w_left_far, w_sides.at[2 * LANES - 2 * opm : 2 * LANES - opm]),
        (w_right_far, w_sides.at[2 * LANES - opm :]),
        (w_outer_far, w_outer.at[:, : w_outer_far.shape[1]]),
    )
    copies = [pltpu.make_async_copy(a, b, arrivals.at[k]) for k, (a, b) in enumerate(pairs)]
    for copy in copies:
        copy.start()

    tiles = picks.shape[1] // rows
    devices = picks.shape[0] // BLOCK
    atoms = rows * devices
    own_tokens = tokens // devices
    token_rows = own_tokens * tiles
    slots = rows // FEWEST + 1
    position = place()
    first = position * rows
    even = position % 2 == 0
    first_float = first.astype(F32)
    w_sides[2 * opm : 2 * LANES - 2 * opm, :] = jnp.zeros(
        (2 * LANES - 4 * opm, tiles * LANES), BF
    )

    for copy in copies[:8]:
        copy.wait()
    counts_wide = jnp.broadcast_to(counts[...].astype(F32), (tiles * rows, tokens)).astype(BF)
    counts_lane = counts_wide[:LANES]
    folded = counts_folded[...].astype(F32).astype(BF)
    upper = flag(iota((LANES, LANES), 0) <= iota((LANES, LANES), 1))
    lower = flag(iota((LANES, LANES), 1) <= iota((LANES, LANES), 0))
    within = dot(folded, upper)
    whole = dot(folded, jnp.ones((LANES, LANES), BF))
    base = jnp.zeros((1, 1), F32)
    passed = jnp.zeros((1, LANES), F32)
    for fold in range(folded.shape[0]):
        ended = within[fold : fold + 1] + passed <= first_float
        base = base + jnp.sum(jnp.where(ended, 1.0, 0.0), axis=1, keepdims=True)
        part = slice(fold * LANES, (fold + 1) * LANES)
        ends[part, :] = passed + dot_t(lower, counts_lane[:, part])
        passed = passed + whole[fold : fold + 1]

    base_token = base.astype(jnp.int32)
    token_lane = iota((SLOTS, tokens), 1).astype(F32)
    slot_token = iota((SLOTS, tokens), 0).astype(F32) + base
    slot_end = dot_t(flag(token_lane <= slot_token), counts_lane)
    slot_start = dot_t(flag(token_lane < slot_token), counts_lane)
    atom_lane = iota((SLOTS, rows), 1).astype(F32) + first_float
    member[...] = flag((atom_lane >= slot_start[:, :rows]) & (atom_lane < slot_end[:, :rows]))
    slot_scale[...] = 1.0 / jnp.maximum(slot_end - slot_start, 1.0)
    last_atom = first_float + (rows - 1)
    is_last = jnp.where((slot_start <= last_atom) & (slot_end > last_atom), 1.0, 0.0)
    last[...] = is_last
    goes_on[...] = is_last * jnp.where(slot_end > first_float + rows, 1.0, 0.0)
    is_first = iota((SLOTS, LANES), 0) == 0
    before[...] = jnp.where(is_first & (slot_start < first_float), 1.0, 0.0)

    def rows_step(at):
        def spread(lanes, axis):
            return iota((DESTS, BLOCK, lanes), axis).reshape(DESTS * BLOCK, lanes)

        here = span(at, DESTS * BLOCK)
        token_at = iota((DESTS * BLOCK, tokens), 1)
        turn = spread(tokens, 1) % own_tokens
        row_token = (spread(tokens, 0) + at * DESTS) * own_tokens + turn
        row_end = dot_t(flag(token_at <= row_token), counts_wide)
        row_start = dot_t(flag(token_at < row_token), counts_wide)
        lanes = tiles * rows
        lane = iota((DESTS * BLOCK, lanes), 1)
        atom = (lane % rows + first).astype(F32)
        tile_fits = spread(lanes, 1) // own_tokens == lane // rows
        picks[here, :] = flag(tile_fits & (atom >= row_start) & (atom < row_end))
        row_scale[here, :] = 1.0 / jnp.maximum(row_end - row_start, 1.0)[:, :LANES]
        lanes = 3 * SLOTS
        dest = spread(lanes, 0) + at * DESTS
        spot = spread(lanes, 1)
        kind = iota((DESTS * BLOCK, lanes), 1) // SLOTS
        slot = iota((DESTS * BLOCK, lanes), 1) % SLOTS
        first_own = dest * own_tokens
        shared_tokens = overlap(base_token, first_own, own_tokens, slots)
        token = base_token + slot
        index = jnp.where(token < first_own, slot, slot - shared_tokens)
        mine = (token >= first_own) & (token < first_own + own_tokens)
        room = 2 * (BLOCK - SLOT_ROW)
        target = jnp.where(index < room, SLOT_ROW + index // 2, jnp.where(kind == 0, 0, -1))
        target = jnp.where(index % 2 == kind, target, -1)
        is_slot = (kind < 2) & (slot < slots) & jnp.logical_not(mine) & (spot == target)
        on_edge = spot == edge_row(base_token, first_own, own_tokens, slots)
        beside = jnp.where(slot == 0, position - 1, position + 1)
        is_edge = (kind == 2) & (slot < 2) & on_edge & (dest == beside)
        selects[here, :] = flag(is_slot | is_edge)

    repeat(devices // DESTS, rows_step)

    row_tokens = tokens // lax.axis_size("row")
    col_tokens = tokens // lax.axis_size("col")
    first_row = lax.axis_index("row") * row_tokens
    first_col = lax.axis_index("col") * col_tokens

    def adder_step(at):
        here = span(at, LANES)
        spot_lane = iota((1, LANES), 1) + at * LANES
        block = spot_lane // BLOCK
        spot = spot_lane % BLOCK
        edge = (block * rows).astype(F32)
        tally = jnp.zeros((1, LANES), F32)
        for fold in range(tokens // LANES):
            ended = jnp.where(ends[fold * LANES : (fold + 1) * LANES, :] <= edge, 1.0, 0.0)
            tally = tally + jnp.sum(ended, axis=0, keepdims=True)
        start = tally.astype(jnp.int32)
        first_own = position * own_tokens
        shared_tokens = overlap(start, first_own, own_tokens, slots)

        def token_of(index):
            slot = jnp.where(start + index < first_own, index, index + shared_tokens)
            return jnp.where((index >= 0) & (slot < slots), start + slot, -1)

        in_slots = spot >= SLOT_ROW
        room = 2 * (BLOCK - SLOT_ROW)
        ninth = jnp.where((spot == 0) & (shared_tokens == 0), start + room, -1)
        low_token = jnp.where(in_slots, token_of(2 * (spot - SLOT_ROW)), ninth)
        high_token = jnp.where(in_slots, token_of(2 * (spot - SLOT_ROW) + 1), -1)
        own_token = first_own + spot % own_tokens
        held = (spot < token_rows) & (own_token >= start) & (own_token < start + slots)
        own_token = jnp.where(held, own_token, -1)
        line = iota((SLOTS, LANES), 0)
        side = jnp.where(line == token_rows, position - 1, position + 1)
        on_edge = spot == edge_row(start, first_own, own_tokens, slots)
        is_edge = (line >= token_rows) & (line < token_rows + 2) & on_edge & (block == side)
        lines = [(line < token_rows) & (spot == line) & held | is_edge]
        row_line = iota((row_tokens, LANES), 0) + first_row
        col_line = iota((col_tokens, LANES), 0) + first_col
        for wanted in (row_line, col_line):
            lines += [low_token == wanted, high_token == wanted]
        for tile in range(tiles):
            tile_token = jnp.where(spot // own_tokens == tile, own_token, -1)
            lines += [tile_token == row_line, tile_token == col_line]
        top = 0
        for part in lines:
            adder[top : top + part.shape[0], here] = flag(part)
            top += part.shape[0]

    repeat(devices * BLOCK // LANES, adder_step)

    own_float[...] = own[...].astype(F32)
    normed, scaling = centred_rows(own[...], atom_gain[...])
    near = (dot(normed, w_kv[...]) * jnp.concatenate([scaling] * 2, axis=1)).astype(BF)
    keyval[...] = near
    query = (dot(normed, w_query[...]) * scaling).astype(BF)
    head_of = iota((1, width), 1) // (width // HEADS)
    heads = jnp.concatenate([query * flag(head_of == h) for h in range(HEADS)], axis=0)
    stacked[...] = heads
    near_index = first + iota((1, rows), 1)
    far_lane = iota((1, 2 * rows), 1)
    is_low = (far_lane < rows) != even
    far_index = first + far_lane % rows + jnp.where(is_low, -rows, rows)
    near_bias, bias = [], []
    for e in range(rows // QB):
        low = key_starts[0:1, e : e + 1]
        seen = (near_index >= low) & (near_index < low + KW)
        near_bias.append(jnp.broadcast_to(jnp.where(seen, 0.0, MASKED), (QB, rows)))
        seen = (far_index >= low) & (far_index < low + KW)
        seen = seen & (far_index >= 0) & (far_index < atoms)
        bias.append(jnp.broadcast_to(jnp.where(seen, 0.0, MASKED), (QB, 2 * rows)))
    far_bias[...] = jnp.concatenate(bias, axis=0)
    raw_scores = dot_t(heads, near[:, :width]) + jnp.concatenate(near_bias * HEADS, axis=0)
    scores[...] = raw_scores
    top[...] = jnp.max(raw_scores, axis=-1, keepdims=True)
    for copy in copies[8:]:
        copy.wait()
    pair_width = w_outer_far.shape[1]
    average = jnp.full((pair_width, pair_width), 1.0 / pair_width, F32).astype(BF)
    w_outer[:, pair_width:] = dot(w_outer[:, :pair_width], average).astype(BF)


def atom_kernel(
    neighbour,
    sibling,
    own_float,
    keyval,
    stacked,
    scores,
    top,
    far_bias,
    picks,
    row_scale,
    selects,
    member,
    slot_scale,
    before,
    goes_on,
    atom_gain,
    w_kv,
    w_out,
    w_pool,
    w_back,
    w_sides,
    payload,
    updated,
    slot_back,
):
    rows, width = own_float.shape
    tiles = w_pool.shape[1] // LANES
    devices = payload.shape[0] // BLOCK
    raw = jnp.concatenate([sibling[...], neighbour[...]], axis=0)
    normed, scaling = centred_rows(raw, atom_gain[...])
    far = (dot(normed, w_kv[...]) * jnp.concatenate([scaling] * 2, axis=1)).astype(BF)
    far_scores = dot_t(stacked[...], far[:, :width])
    far_scores = far_scores + jnp.concatenate([far_bias[...]] * HEADS, axis=0)
    most = jnp.maximum(top[...], jnp.max(far_scores, axis=-1, keepdims=True))
    scale = (width // HEADS) ** (-0.5) * LOG2E
    raised = jnp.concatenate(
        [
            jnp.exp2((far_scores - most) * scale).astype(BF),
            jnp.exp2((scores[...] - most) * scale).astype(BF),
        ],
        axis=1,
    )
    values = jnp.concatenate([far[:, width:], keyval[:, width:]], axis=0)
    mixed = dot(raised, jnp.concatenate([values, jnp.ones((3 * rows, width), BF)], axis=1))
    head_of = iota((1, width), 1) // (width // HEADS)
    head_mask = [(head_of == h).astype(F32) for h in range(HEADS)]
    total = sum(mixed[h * rows : (h + 1) * rows, :width] * head_mask[h] for h in range(HEADS))
    weight = sum(mixed[h * rows : (h + 1) * rows, width:] * head_mask[h] for h in range(HEADS))
    attended = (total / weight).astype(BF)
    fresh = (own_float[...] + dot(attended, w_out[...])).astype(BF)
    updated[...] = fresh
    feature = jnp.maximum(dot(fresh, w_pool[...]), 0.0).astype(BF)
    feature_tiles = jnp.concatenate(
        [feature[:, k * LANES : (k + 1) * LANES] for k in range(tiles)], axis=0
    )
    slot_single = (
        dot(member[...], feature) * jnp.concatenate([slot_scale[...]] * tiles, axis=1)
    ).astype(BF)
    sides = dot_t(slot_single, w_sides[...]).astype(BF)
    backs = dot(slot_single, w_back[...])
    slot_back[...] = backs
    to_before = jnp.sum(backs * before[...], axis=0, keepdims=True)
    to_after = jnp.sum(backs * goes_on[...], axis=0, keepdims=True)
    spot = iota((SLOTS, LANES), 0)
    edges = jnp.where(spot == 0, to_before, jnp.where(spot == 1, to_after, 0.0)).astype(BF)
    shared = jnp.concatenate([sides[:, :LANES], sides[:, LANES:], edges], axis=0)

    def send_step(at):
        here = span(at, DESTS * BLOCK)
        singles = dot(picks[here, :], feature_tiles) * row_scale[here, :]
        payload[here, :] = (singles + dot(selects[here, :], shared)).astype(BF)

    repeat(devices // DESTS, send_step)


def pair_kernel(
    arrived,
    adder,
    updated,
    slot_back,
    slot_last,
    slot_member,
    pair_state,
    w_outer,
    pair_gain,
    w_gate,
    w_lift,
    w_drop,
    w_sides,
    atom_out,
    token_single,
    pair_out,
):
    row_tokens, col_tokens, pair_width = pair_state.shape
    own_tokens, channels = token_single.shape
    tiles = channels // LANES
    token_rows = own_tokens * tiles
    opm = math.isqrt(w_outer.shape[0])
    added = dot(adder[...], arrived[...])
    half_gate = w_gate[...] * jnp.asarray(0.5, BF)
    parts, top = [], 0
    for height in (SLOTS,) + (row_tokens,) * 2 + (col_tokens,) * 2 + (row_tokens, col_tokens) * tiles:
        parts.append(added[top : top + height])
        top += height
    sums, left_low, left_high, right_low, right_high, *own = parts
    own_left = jnp.concatenate(own[0::2], axis=1).astype(BF)
    own_right = jnp.concatenate(own[1::2], axis=1).astype(BF)
    own_sides = dot_t(jnp.concatenate([own_left, own_right], axis=0), w_sides[:LANES])
    left = left_low[:, :opm] + left_high[:, 2 * opm : 3 * opm] + own_sides[:row_tokens, :opm]
    right = right_low[:, opm : 2 * opm] + right_high[:, 3 * opm : 4 * opm]
    right = right + own_sides[row_tokens:, opm : 2 * opm]
    left, right = left.astype(BF), right.astype(BF)
    product_lane = iota((opm, opm * opm), 1)
    unit = iota((opm, opm * opm), 0)
    left_wide = dot(left, flag(product_lane // opm == unit))
    rights = dot(right, flag(product_lane % opm == unit)).astype(BF)

    average = jnp.full((pair_width, pair_width), 1.0 / pair_width, F32).astype(BF)

    def pair_rows(lefts, here):
        products = []
        for i in range(PAIR_ROWS):
            spread = jnp.broadcast_to(lefts[i : i + 1, :], (SLOTS, lefts.shape[1])).astype(BF)
            products += [
                spread * rights[at : at + SLOTS] for at in range(0, col_tokens, SLOTS)
            ]
        products = jnp.concatenate(products, axis=0)
        flat = pair_state[pl.ds(here, PAIR_ROWS)].reshape(PAIR_ROWS * col_tokens, pair_width)
        outer = dot(products, w_outer[...])
        summed = flat.astype(F32) + outer[:, :pair_width]
        centred = summed - (dot(flat, average) + outer[:, pair_width:])
        variance = dot((centred * centred).astype(BF), average)
        scaling = lax.rsqrt(variance + EPSILON)
        normed = (centred * pair_gain[...]).astype(BF)
        wide = jnp.concatenate([scaling] * (w_lift.shape[1] // pair_width), axis=1)
        gate = dot(normed, half_gate) * wide
        lift = dot(normed, w_lift[...]) * wide
        hidden = (gate * lift * (1.0 + jnp.tanh(gate))).astype(BF)
        result = (summed + dot(hidden, w_drop[...])).astype(BF)
        pair_out[pl.ds(here, PAIR_ROWS)] = result.reshape(PAIR_ROWS, col_tokens, pair_width)

    for step in range(row_tokens // PAIR_ROWS):
        here = step * PAIR_ROWS
        pair_rows(left_wide[here : here + PAIR_ROWS], here)

    token_single[...] = jnp.concatenate(
        [sums[k * own_tokens : (k + 1) * own_tokens] for k in range(tiles)], axis=1
    ).astype(BF)
    spot = iota((SLOTS, LANES), 0)
    from_before = jnp.where(spot == 0, sums[token_rows : token_rows + 1], 0.0)
    from_after = slot_last[...] * sums[token_rows + 1 : token_rows + 2]
    back = (slot_back[...] + from_before + from_after).astype(BF)
    lifted = lax.dot_general(
        slot_member[...], back, (((0,), (0,)), ((), ())), preferred_element_type=F32
    )
    atom_out[...] = (updated[...].astype(F32) + lifted).astype(BF)


def call(kernel, name, operands, outputs, far=(), scratch=()):
    near_spec = pl.BlockSpec(memory_space=pltpu.VMEM)
    far_spec = pl.BlockSpec(memory_space=pltpu.HBM)
    held = sum(math.prod(a.shape) * a.dtype.itemsize for a in operands + outputs)
    return pl.pallas_call(
        kernel,
        out_shape=outputs,
        in_specs=[far_spec] * len(far) + [near_spec] * len(operands),
        out_specs=(near_spec,) * len(outputs),
        scratch_shapes=scratch,
        compiler_params=pltpu.CompilerParams(vmem_limit_bytes=min(2 * held + SPARE, MOST)),
        name=name,
    )(*[pltpu.with_memory_space_constraint(a, pltpu.HBM) for a in far], *operands)


def per_device(
    atom_feats,
    key_starts,
    atom_counts,
    atom_gain,
    w_query,
    w_key,
    w_value,
    w_out,
    w_pool,
    w_back,
    pair_state,
    w_left,
    w_right,
    w_outer,
    pair_gain,
    w_gate,
    w_lift,
    w_drop,
):
    rows, width = atom_feats.shape
    devices = lax.axis_size(AXES)
    tokens = atom_counts.shape[0]
    channels = w_pool.shape[1]
    opm = w_left.shape[1]
    own_tokens = tokens // devices
    row_tokens, col_tokens, _ = pair_state.shape
    tiles = channels // LANES
    opm = w_left.shape[1]
    across = [(i, i + 1) for i in range(1, devices - 1, 2)]
    neighbour = lax.ppermute(atom_feats, AXES, across + [(j, i) for i, j in across])
    sibling = lax.ppermute(atom_feats, AXES, [(i, i ^ 1) for i in range(devices)])

    def held(*shape, dtype=F32):
        return jax.ShapeDtypeStruct(shape, dtype)

    counts_folded = atom_counts.reshape(-1, LANES)
    ready = call(
        ready_kernel,
        "ready",
        (),
        (
            held(rows, width),
            held(rows, 2 * width, dtype=BF),
            held(HEADS * rows, width, dtype=BF),
            held(HEADS * rows, rows),
            held(HEADS * rows, 1),
            held(rows, 2 * rows),
            held(devices * BLOCK, tiles * rows, dtype=BF),
            held(devices * BLOCK, LANES),
            held(devices * BLOCK, 3 * SLOTS, dtype=BF),
            held(SLOTS, rows, dtype=BF),
            held(SLOTS, LANES),
            held(SLOTS, LANES),
            held(SLOTS, LANES),
            held(SLOTS, LANES),
            held(
                SLOTS + (2 + tiles) * (row_tokens + col_tokens), devices * BLOCK, dtype=BF
            ),
            held(1, width),
            held(1, LANES),
            held(width, 2 * width, dtype=BF),
            held(width, width, dtype=BF),
            held(width, channels, dtype=BF),
            held(channels, width, dtype=BF),
            held(2 * LANES, channels, dtype=BF),
            held(opm * opm, 2 * w_outer.shape[-1], dtype=BF),
        ),
        far=(
            atom_feats,
            key_starts[None],
            atom_counts[None],
            counts_folded,
            atom_gain[None],
            pair_gain[None],
            w_query,
            w_key,
            w_value,
            w_out,
            w_pool,
            w_back,
            w_left.T,
            w_right.T,
            w_outer.reshape(opm * opm, -1),
        ),
        scratch=(
            pltpu.VMEM((rows, width), BF),
            pltpu.VMEM((1, key_starts.shape[0]), jnp.int32),
            pltpu.VMEM((1, tokens), jnp.int32),
            pltpu.VMEM(counts_folded.shape, jnp.int32),
            pltpu.VMEM((width, width), BF),
            pltpu.VMEM((tokens, LANES), F32),
            pltpu.SemaphoreType.DMA((17,)),
        ),
    )
    (
        own_float,
        keyval,
        stacked,
        scores,
        top,
        far_bias,
        picks,
        row_scale,
        selects,
        member,
        slot_scale,
        before,
        goes_on,
        last,
        adder,
        atom_gain_kept,
        pair_gain_kept,
        *kept,
        w_outer_kept,
    ) = ready
    payload, updated, slot_back = call(
        atom_kernel,
        "atoms",
        (
            neighbour,
            sibling,
            own_float,
            keyval,
            stacked,
            scores,
            top,
            far_bias,
            picks,
            row_scale,
            selects,
            member,
            slot_scale,
            before,
            goes_on,
            atom_gain_kept,
            *kept,
        ),
        (
            held(devices * BLOCK, LANES, dtype=BF),
            held(rows, width, dtype=BF),
            held(SLOTS, width),
        ),
    )
    arrived = lax.all_to_all(payload.reshape(devices, BLOCK, LANES), AXES, 0, 0)
    return call(
        pair_kernel,
        "pairs",
        (
            arrived.reshape(devices * BLOCK, LANES),
            adder,
            updated,
            slot_back,
            last,
            member,
            pair_state,
            w_outer_kept,
            pair_gain_kept,
            w_gate,
            w_lift,
            w_drop,
            kept[-1],
        ),
        (
            held(rows, width, dtype=BF),
            held(own_tokens, channels, dtype=BF),
            held(*pair_state.shape, dtype=BF),
        ),
    )


def solution(mesh):
    in_specs = (
        P(("row", "col"), None),
        P(("row", "col")),
        P(),
        P(),
        P(),
        P(),
        P(),
        P(),
        P(),
        P(),
        P("row", "col", None),
        P(),
        P(),
        P(),
        P(),
        P(),
        P(),
        P(),
    )
    out_specs = (P(("row", "col"), None), P(("row", "col"), None), P("row", "col", None))
    return jax.shard_map(
        per_device, mesh=mesh, in_specs=in_specs, out_specs=out_specs, check_vma=False
    )
```

```python
import math

import jax
import jax.numpy as jnp
from jax import lax
from jax.experimental import pallas as pl
from jax.experimental.pallas import tpu as pltpu
from jax.sharding import PartitionSpec as P

HEADS = 4
QB = 32
KW = 128
EPSILON = 1e-05
HALF = KW // 2
FEWEST = 8
LANES = 128
SLOTS = 16
BLOCK = 16
SLOT_ROW = 12
DESTS = 32
PAIR_ROWS = 16
GROUP = 8
MASKED = -1e30
SPARE = 12 << 20
MOST = 60 << 20
LOG2E = 1.4426950408889634
AXES = ("row", "col")
BF = jnp.bfloat16
F32 = jnp.float32


def dot(a, b):
    return jnp.dot(a, b, preferred_element_type=F32)


def dot_t(a, b):
    return lax.dot_general(a, b, (((1,), (1,)), ((), ())), preferred_element_type=F32)


def iota(shape, axis):
    return lax.broadcasted_iota(jnp.int32, shape, axis)


def centred_rows(values, gain):
    width = values.shape[1]
    average = jnp.full((width, width), 1.0 / width, F32).astype(BF)
    centred = values.astype(F32) - dot(values, average)
    variance = dot((centred * centred).astype(BF), average)
    return (centred * gain).astype(BF), lax.rsqrt(variance + EPSILON)


def flag(mask):
    return jnp.where(mask, 1.0, 0.0).astype(BF)


def place():
    return lax.axis_index("row") * lax.axis_size("col") + lax.axis_index("col")


def overlap(base, first_own, own_tokens, slots):
    inner = jnp.minimum(first_own + own_tokens, base + slots) - jnp.maximum(first_own, base)
    return jnp.maximum(inner, 0)


def edge_row(base, first_own, own_tokens, slots):
    last_own = first_own + own_tokens - 1
    last_held = (last_own >= base) & (last_own < base + slots)
    free = jnp.where(last_held, 0, own_tokens - 1)
    whole = overlap(base, first_own, own_tokens, slots) == own_tokens
    return jnp.where(whole, BLOCK - 1, free)


def repeat(count, step):
    if count <= 8:
        for at in range(count):
            step(at)
    else:

        def body(at, carry):
            step(at)
            return carry

        lax.fori_loop(0, count, body, 0)


def span(at, size):
    if isinstance(at, int):
        return pl.ds(at * size, size)
    return pl.ds(pl.multiple_of(at * size, size), size)


def ready_kernel(
    own_far,
    starts_far,
    counts_far,
    folded_far,
    atom_gain_far,
    pair_gain_far,
    w_query_far,
    w_key_far,
    w_value_far,
    w_out_far,
    w_pool_far,
    w_back_far,
    w_left_far,
    w_right_far,
    w_outer_far,
    own_float,
    keyval,
    stacked,
    scores,
    top,
    far_bias,
    picks,
    row_scale,
    selects,
    member,
    slot_scale,
    before,
    goes_on,
    last,
    adder,
    atom_gain,
    pair_gain,
    w_kv,
    w_out,
    w_pool,
    w_back,
    w_sides,
    w_outer,
    own,
    key_starts,
    counts,
    counts_folded,
    w_query,
    ends,
    arrivals,
):
    rows, width = own.shape
    tokens = counts.shape[1]
    opm = w_left_far.shape[0]
    pairs = (
        (counts_far, counts),
        (folded_far, counts_folded),
        (own_far, own),
        (starts_far, key_starts),
        (atom_gain_far, atom_gain),
        (w_query_far, w_query),
        (w_key_far, w_kv.at[:, :width]),
        (w_value_far, w_kv.at[:, width:]),
        (pair_gain_far, pair_gain),
        (w_out_far, w_out),
        (w_pool_far, w_pool),
        (w_back_far, w_back),
        (w_left_far, w_sides.at[:opm]),
        (w_right_far, w_sides.at[opm : 2 * opm]),
        (w_left_far, w_sides.at[2 * LANES - 2 * opm : 2 * LANES - opm]),
        (w_right_far, w_sides.at[2 * LANES - opm :]),
        (w_outer_far, w_outer.at[:, : w_outer_far.shape[1]]),
    )
    copies = [pltpu.make_async_copy(a, b, arrivals.at[k]) for k, (a, b) in enumerate(pairs)]
    for copy in copies:
        copy.start()

    tiles = picks.shape[1] // rows
    devices = picks.shape[0] // BLOCK
    atoms = rows * devices
    own_tokens = tokens // devices
    token_rows = own_tokens * tiles
    slots = rows // FEWEST + 1
    position = place()
    first = position * rows
    even = position % 2 == 0
    first_float = first.astype(F32)
    w_sides[2 * opm : 2 * LANES - 2 * opm, :] = jnp.zeros(
        (2 * LANES - 4 * opm, tiles * LANES), BF
    )

    for copy in copies[:8]:
        copy.wait()
    counts_wide = jnp.broadcast_to(counts[...].astype(F32), (tiles * rows, tokens)).astype(BF)
    counts_lane = counts_wide[:LANES]
    folded = counts_folded[...].astype(F32).astype(BF)
    upper = flag(iota((LANES, LANES), 0) <= iota((LANES, LANES), 1))
    lower = flag(iota((LANES, LANES), 1) <= iota((LANES, LANES), 0))
    within = dot(folded, upper)
    whole = dot(folded, jnp.ones((LANES, LANES), BF))
    base = jnp.zeros((1, 1), F32)
    passed = jnp.zeros((1, LANES), F32)
    for fold in range(folded.shape[0]):
        ended = within[fold : fold + 1] + passed <= first_float
        base = base + jnp.sum(jnp.where(ended, 1.0, 0.0), axis=1, keepdims=True)
        part = slice(fold * LANES, (fold + 1) * LANES)
        ends[part, :] = passed + dot_t(lower, counts_lane[:, part])
        passed = passed + whole[fold : fold + 1]

    base_token = base.astype(jnp.int32)
    token_lane = iota((SLOTS, tokens), 1).astype(F32)
    slot_token = iota((SLOTS, tokens), 0).astype(F32) + base
    slot_end = dot_t(flag(token_lane <= slot_token), counts_lane)
    slot_start = dot_t(flag(token_lane < slot_token), counts_lane)
    atom_lane = iota((SLOTS, rows), 1).astype(F32) + first_float
    member[...] = flag((atom_lane >= slot_start[:, :rows]) & (atom_lane < slot_end[:, :rows]))
    slot_scale[...] = 1.0 / jnp.maximum(slot_end - slot_start, 1.0)
    last_atom = first_float + (rows - 1)
    is_last = jnp.where((slot_start <= last_atom) & (slot_end > last_atom), 1.0, 0.0)
    last[...] = is_last
    goes_on[...] = is_last * jnp.where(slot_end > first_float + rows, 1.0, 0.0)
    is_first = iota((SLOTS, LANES), 0) == 0
    before[...] = jnp.where(is_first & (slot_start < first_float), 1.0, 0.0)

    def rows_step(at):
        def spread(lanes, axis):
            return iota((DESTS, BLOCK, lanes), axis).reshape(DESTS * BLOCK, lanes)

        here = span(at, DESTS * BLOCK)
        token_at = iota((DESTS * BLOCK, tokens), 1)
        turn = spread(tokens, 1) % own_tokens
        row_token = (spread(tokens, 0) + at * DESTS) * own_tokens + turn
        row_end = dot_t(flag(token_at <= row_token), counts_wide)
        row_start = dot_t(flag(token_at < row_token), counts_wide)
        lanes = tiles * rows
        lane = iota((DESTS * BLOCK, lanes), 1)
        atom = (lane % rows + first).astype(F32)
        tile_fits = spread(lanes, 1) // own_tokens == lane // rows
        picks[here, :] = flag(tile_fits & (atom >= row_start) & (atom < row_end))
        row_scale[here, :] = 1.0 / jnp.maximum(row_end - row_start, 1.0)[:, :LANES]
        lanes = 3 * SLOTS
        dest = spread(lanes, 0) + at * DESTS
        spot = spread(lanes, 1)
        kind = iota((DESTS * BLOCK, lanes), 1) // SLOTS
        slot = iota((DESTS * BLOCK, lanes), 1) % SLOTS
        first_own = dest * own_tokens
        shared_tokens = overlap(base_token, first_own, own_tokens, slots)
        token = base_token + slot
        index = jnp.where(token < first_own, slot, slot - shared_tokens)
        mine = (token >= first_own) & (token < first_own + own_tokens)
        room = 2 * (BLOCK - SLOT_ROW)
        target = jnp.where(index < room, SLOT_ROW + index // 2, jnp.where(kind == 0, 0, -1))
        target = jnp.where(index % 2 == kind, target, -1)
        is_slot = (kind < 2) & (slot < slots) & jnp.logical_not(mine) & (spot == target)
        on_edge = spot == edge_row(base_token, first_own, own_tokens, slots)
        beside = jnp.where(slot == 0, position - 1, position + 1)
        is_edge = (kind == 2) & (slot < 2) & on_edge & (dest == beside)
        selects[here, :] = flag(is_slot | is_edge)

    repeat(devices // DESTS, rows_step)

    row_tokens = tokens // lax.axis_size("row")
    col_tokens = tokens // lax.axis_size("col")
    first_row = lax.axis_index("row") * row_tokens
    first_col = lax.axis_index("col") * col_tokens

    def adder_step(at):
        here = span(at, LANES)
        spot_lane = iota((1, LANES), 1) + at * LANES
        block = spot_lane // BLOCK
        spot = spot_lane % BLOCK
        edge = (block * rows).astype(F32)
        tally = jnp.zeros((1, LANES), F32)
        for fold in range(tokens // LANES):
            ended = jnp.where(ends[fold * LANES : (fold + 1) * LANES, :] <= edge, 1.0, 0.0)
            tally = tally + jnp.sum(ended, axis=0, keepdims=True)
        start = tally.astype(jnp.int32)
        first_own = position * own_tokens
        shared_tokens = overlap(start, first_own, own_tokens, slots)

        def token_of(index):
            slot = jnp.where(start + index < first_own, index, index + shared_tokens)
            return jnp.where((index >= 0) & (slot < slots), start + slot, -1)

        in_slots = spot >= SLOT_ROW
        room = 2 * (BLOCK - SLOT_ROW)
        ninth = jnp.where((spot == 0) & (shared_tokens == 0), start + room, -1)
        low_token = jnp.where(in_slots, token_of(2 * (spot - SLOT_ROW)), ninth)
        high_token = jnp.where(in_slots, token_of(2 * (spot - SLOT_ROW) + 1), -1)
        own_token = first_own + spot % own_tokens
        held = (spot < token_rows) & (own_token >= start) & (own_token < start + slots)
        own_token = jnp.where(held, own_token, -1)
        line = iota((SLOTS, LANES), 0)
        side = jnp.where(line == token_rows, position - 1, position + 1)
        on_edge = spot == edge_row(start, first_own, own_tokens, slots)
        is_edge = (line >= token_rows) & (line < token_rows + 2) & on_edge & (block == side)
        lines = [(line < token_rows) & (spot == line) & held | is_edge]
        row_line = iota((row_tokens, LANES), 0) + first_row
        col_line = iota((col_tokens, LANES), 0) + first_col
        for wanted in (row_line, col_line):
            lines += [low_token == wanted, high_token == wanted]
        for tile in range(tiles):
            tile_token = jnp.where(spot // own_tokens == tile, own_token, -1)
            lines += [tile_token == row_line, tile_token == col_line]
        top = 0
        for part in lines:
            adder[top : top + part.shape[0], here] = flag(part)
            top += part.shape[0]

    repeat(devices * BLOCK // LANES, adder_step)

    own_float[...] = own[...].astype(F32)
    normed, scaling = centred_rows(own[...], atom_gain[...])
    near = (dot(normed, w_kv[...]) * jnp.concatenate([scaling] * 2, axis=1)).astype(BF)
    keyval[...] = near
    query = (dot(normed, w_query[...]) * scaling).astype(BF)
    head_of = iota((1, width), 1) // (width // HEADS)
    heads = jnp.concatenate([query * flag(head_of == h) for h in range(HEADS)], axis=0)
    stacked[...] = heads
    near_index = first + iota((1, rows), 1)
    far_lane = iota((1, 2 * rows), 1)
    is_low = (far_lane < rows) != even
    far_index = first + far_lane % rows + jnp.where(is_low, -rows, rows)
    near_bias, bias = [], []
    for e in range(rows // QB):
        low = key_starts[0:1, e : e + 1]
        seen = (near_index >= low) & (near_index < low + KW)
        near_bias.append(jnp.broadcast_to(jnp.where(seen, 0.0, MASKED), (QB, rows)))
        seen = (far_index >= low) & (far_index < low + KW)
        seen = seen & (far_index >= 0) & (far_index < atoms)
        bias.append(jnp.broadcast_to(jnp.where(seen, 0.0, MASKED), (QB, 2 * rows)))
    far_bias[...] = jnp.concatenate(bias, axis=0)
    raw_scores = dot_t(heads, near[:, :width]) + jnp.concatenate(near_bias * HEADS, axis=0)
    scores[...] = raw_scores
    top[...] = jnp.max(raw_scores, axis=-1, keepdims=True)
    for copy in copies[8:]:
        copy.wait()
    pair_width = w_outer_far.shape[1]
    average = jnp.full((pair_width, pair_width), 1.0 / pair_width, F32).astype(BF)
    w_outer[:, pair_width:] = dot(w_outer[:, :pair_width], average).astype(BF)


def atom_kernel(
    neighbour,
    sibling,
    own_float,
    keyval,
    stacked,
    scores,
    top,
    far_bias,
    picks,
    row_scale,
    selects,
    member,
    slot_scale,
    before,
    goes_on,
    atom_gain,
    w_kv,
    w_out,
    w_pool,
    w_back,
    w_sides,
    payload,
    updated,
    slot_back,
):
    rows, width = own_float.shape
    tiles = w_pool.shape[1] // LANES
    devices = payload.shape[0] // BLOCK
    raw = jnp.concatenate([sibling[...], neighbour[...]], axis=0)
    normed, scaling = centred_rows(raw, atom_gain[...])
    far = (dot(normed, w_kv[...]) * jnp.concatenate([scaling] * 2, axis=1)).astype(BF)
    far_scores = dot_t(stacked[...], far[:, :width])
    far_scores = far_scores + jnp.concatenate([far_bias[...]] * HEADS, axis=0)
    most = jnp.maximum(top[...], jnp.max(far_scores, axis=-1, keepdims=True))
    scale = (width // HEADS) ** (-0.5) * LOG2E
    raised = jnp.concatenate(
        [
            jnp.exp2((far_scores - most) * scale).astype(BF),
            jnp.exp2((scores[...] - most) * scale).astype(BF),
        ],
        axis=1,
    )
    values = jnp.concatenate([far[:, width:], keyval[:, width:]], axis=0)
    mixed = dot(raised, jnp.concatenate([values, jnp.ones((3 * rows, width), BF)], axis=1))
    head_of = iota((1, width), 1) // (width // HEADS)
    head_mask = [(head_of == h).astype(F32) for h in range(HEADS)]
    total = sum(mixed[h * rows : (h + 1) * rows, :width] * head_mask[h] for h in range(HEADS))
    weight = sum(mixed[h * rows : (h + 1) * rows, width:] * head_mask[h] for h in range(HEADS))
    attended = (total / weight).astype(BF)
    fresh = (own_float[...] + dot(attended, w_out[...])).astype(BF)
    updated[...] = fresh
    feature = jnp.maximum(dot(fresh, w_pool[...]), 0.0).astype(BF)
    feature_tiles = jnp.concatenate(
        [feature[:, k * LANES : (k + 1) * LANES] for k in range(tiles)], axis=0
    )
    slot_single = (
        dot(member[...], feature) * jnp.concatenate([slot_scale[...]] * tiles, axis=1)
    ).astype(BF)
    sides = dot_t(slot_single, w_sides[...]).astype(BF)
    backs = dot(slot_single, w_back[...])
    slot_back[...] = backs
    to_before = jnp.sum(backs * before[...], axis=0, keepdims=True)
    to_after = jnp.sum(backs * goes_on[...], axis=0, keepdims=True)
    spot = iota((SLOTS, LANES), 0)
    edges = jnp.where(spot == 0, to_before, jnp.where(spot == 1, to_after, 0.0)).astype(BF)
    shared = jnp.concatenate([sides[:, :LANES], sides[:, LANES:], edges], axis=0)

    def send_step(at):
        here = span(at, DESTS * BLOCK)
        singles = dot(picks[here, :], feature_tiles) * row_scale[here, :]
        payload[here, :] = (singles + dot(selects[here, :], shared)).astype(BF)

    repeat(devices // DESTS, send_step)


def pair_kernel(
    arrived,
    adder,
    updated,
    slot_back,
    slot_last,
    slot_member,
    pair_state,
    w_outer,
    pair_gain,
    w_gate,
    w_lift,
    w_drop,
    w_sides,
    atom_out,
    token_single,
    pair_out,
):
    row_tokens, col_tokens, pair_width = pair_state.shape
    own_tokens, channels = token_single.shape
    tiles = channels // LANES
    token_rows = own_tokens * tiles
    opm = math.isqrt(w_outer.shape[0])
    added = dot(adder[...], arrived[...])
    half_gate = w_gate[...] * jnp.asarray(0.5, BF)
    parts, top = [], 0
    for height in (SLOTS,) + (row_tokens,) * 2 + (col_tokens,) * 2 + (row_tokens, col_tokens) * tiles:
        parts.append(added[top : top + height])
        top += height
    sums, left_low, left_high, right_low, right_high, *own = parts
    own_left = jnp.concatenate(own[0::2], axis=1).astype(BF)
    own_right = jnp.concatenate(own[1::2], axis=1).astype(BF)
    own_sides = dot_t(jnp.concatenate([own_left, own_right], axis=0), w_sides[:LANES])
    left = left_low[:, :opm] + left_high[:, 2 * opm : 3 * opm] + own_sides[:row_tokens, :opm]
    right = right_low[:, opm : 2 * opm] + right_high[:, 3 * opm : 4 * opm]
    right = right + own_sides[row_tokens:, opm : 2 * opm]
    left, right = left.astype(BF), right.astype(BF)
    depth = GROUP * opm
    unit = flag(iota((opm, depth), 1) % opm == iota((opm, depth), 0))
    corner = jnp.where(iota((GROUP, depth), 1) // opm == iota((GROUP, depth), 0), 1.0, 0.0)

    def spread(rows_of, first, count):
        return jnp.concatenate(
            [
                jnp.broadcast_to(rows_of[k : k + 1, :], (GROUP, depth)) * corner
                for k in range(first, first + count)
            ],
            axis=0,
        ).astype(BF)

    left_wide = dot(left, unit)
    right_blocks = spread(dot(right, unit), 0, col_tokens)
    stages = opm // GROUP
    table = [
        dot(right_blocks, w_outer[g * depth : (g + 1) * depth, :]) for g in range(stages)
    ]
    tables = [
        jnp.concatenate(
            [
                table[g][j * GROUP : (j + 1) * GROUP]
                for j in range(h * GROUP, (h + 1) * GROUP)
                for g in range(stages)
            ],
            axis=0,
        ).astype(BF)
        for h in range(col_tokens // GROUP)
    ]

    def pair_rows(here):
        left_blocks = spread(left_wide, here, PAIR_ROWS)
        terms = [dot(left_blocks, part) for part in tables]
        outer = jnp.concatenate(
            [
                term[i * GROUP : (i + 1) * GROUP]
                for i in range(PAIR_ROWS)
                for term in terms
            ],
            axis=0,
        )
        flat = pair_state[pl.ds(here, PAIR_ROWS)].reshape(PAIR_ROWS * col_tokens, pair_width)
        flat = flat.astype(F32)
        summed = flat + outer[:, :pair_width]
        pair_mean = jnp.mean(flat, axis=-1, keepdims=True)
        centred = summed - (pair_mean + outer[:, pair_width:])
        variance = jnp.mean(centred * centred, axis=-1, keepdims=True)
        scaling = lax.rsqrt(variance + EPSILON)
        normed = (centred * pair_gain[...]).astype(BF)
        gate = dot(normed, half_gate) * scaling
        lift = dot(normed, w_lift[...]) * scaling
        hidden = (gate * lift * (1.0 + jnp.tanh(gate))).astype(BF)
        result = (summed + dot(hidden, w_drop[...])).astype(BF)
        pair_out[pl.ds(here, PAIR_ROWS)] = result.reshape(PAIR_ROWS, col_tokens, pair_width)

    for step in range(row_tokens // PAIR_ROWS):
        here = step * PAIR_ROWS
        pair_rows(here)

    token_single[...] = jnp.concatenate(
        [sums[k * own_tokens : (k + 1) * own_tokens] for k in range(tiles)], axis=1
    ).astype(BF)
    spot = iota((SLOTS, LANES), 0)
    from_before = jnp.where(spot == 0, sums[token_rows : token_rows + 1], 0.0)
    from_after = slot_last[...] * sums[token_rows + 1 : token_rows + 2]
    back = (slot_back[...] + from_before + from_after).astype(BF)
    lifted = lax.dot_general(
        slot_member[...], back, (((0,), (0,)), ((), ())), preferred_element_type=F32
    )
    atom_out[...] = (updated[...].astype(F32) + lifted).astype(BF)


def call(kernel, name, operands, outputs, far=(), scratch=()):
    near_spec = pl.BlockSpec(memory_space=pltpu.VMEM)
    far_spec = pl.BlockSpec(memory_space=pltpu.HBM)
    held = sum(math.prod(a.shape) * a.dtype.itemsize for a in operands + outputs)
    return pl.pallas_call(
        kernel,
        out_shape=outputs,
        in_specs=[far_spec] * len(far) + [near_spec] * len(operands),
        out_specs=(near_spec,) * len(outputs),
        scratch_shapes=scratch,
        compiler_params=pltpu.CompilerParams(vmem_limit_bytes=min(2 * held + SPARE, MOST)),
        name=name,
    )(*[pltpu.with_memory_space_constraint(a, pltpu.HBM) for a in far], *operands)


def per_device(
    atom_feats,
    key_starts,
    atom_counts,
    atom_gain,
    w_query,
    w_key,
    w_value,
    w_out,
    w_pool,
    w_back,
    pair_state,
    w_left,
    w_right,
    w_outer,
    pair_gain,
    w_gate,
    w_lift,
    w_drop,
):
    rows, width = atom_feats.shape
    devices = lax.axis_size(AXES)
    tokens = atom_counts.shape[0]
    channels = w_pool.shape[1]
    opm = w_left.shape[1]
    own_tokens = tokens // devices
    row_tokens, col_tokens, _ = pair_state.shape
    tiles = channels // LANES
    opm = w_left.shape[1]
    across = [(i, i + 1) for i in range(1, devices - 1, 2)]
    neighbour = lax.ppermute(atom_feats, AXES, across + [(j, i) for i, j in across])
    sibling = lax.ppermute(atom_feats, AXES, [(i, i ^ 1) for i in range(devices)])

    def held(*shape, dtype=F32):
        return jax.ShapeDtypeStruct(shape, dtype)

    counts_folded = atom_counts.reshape(-1, LANES)
    ready = call(
        ready_kernel,
        "ready",
        (),
        (
            held(rows, width),
            held(rows, 2 * width, dtype=BF),
            held(HEADS * rows, width, dtype=BF),
            held(HEADS * rows, rows),
            held(HEADS * rows, 1),
            held(rows, 2 * rows),
            held(devices * BLOCK, tiles * rows, dtype=BF),
            held(devices * BLOCK, LANES),
            held(devices * BLOCK, 3 * SLOTS, dtype=BF),
            held(SLOTS, rows, dtype=BF),
            held(SLOTS, LANES),
            held(SLOTS, LANES),
            held(SLOTS, LANES),
            held(SLOTS, LANES),
            held(
                SLOTS + (2 + tiles) * (row_tokens + col_tokens), devices * BLOCK, dtype=BF
            ),
            held(1, width),
            held(1, LANES),
            held(width, 2 * width, dtype=BF),
            held(width, width, dtype=BF),
            held(width, channels, dtype=BF),
            held(channels, width, dtype=BF),
            held(2 * LANES, channels, dtype=BF),
            held(opm * opm, 2 * w_outer.shape[-1], dtype=BF),
        ),
        far=(
            atom_feats,
            key_starts[None],
            atom_counts[None],
            counts_folded,
            atom_gain[None],
            pair_gain[None],
            w_query,
            w_key,
            w_value,
            w_out,
            w_pool,
            w_back,
            w_left.T,
            w_right.T,
            w_outer.reshape(opm * opm, -1),
        ),
        scratch=(
            pltpu.VMEM((rows, width), BF),
            pltpu.VMEM((1, key_starts.shape[0]), jnp.int32),
            pltpu.VMEM((1, tokens), jnp.int32),
            pltpu.VMEM(counts_folded.shape, jnp.int32),
            pltpu.VMEM((width, width), BF),
            pltpu.VMEM((tokens, LANES), F32),
            pltpu.SemaphoreType.DMA((17,)),
        ),
    )
    (
        own_float,
        keyval,
        stacked,
        scores,
        top,
        far_bias,
        picks,
        row_scale,
        selects,
        member,
        slot_scale,
        before,
        goes_on,
        last,
        adder,
        atom_gain_kept,
        pair_gain_kept,
        *kept,
        w_outer_kept,
    ) = ready
    payload, updated, slot_back = call(
        atom_kernel,
        "atoms",
        (
            neighbour,
            sibling,
            own_float,
            keyval,
            stacked,
            scores,
            top,
            far_bias,
            picks,
            row_scale,
            selects,
            member,
            slot_scale,
            before,
            goes_on,
            atom_gain_kept,
            *kept,
        ),
        (
            held(devices * BLOCK, LANES, dtype=BF),
            held(rows, width, dtype=BF),
            held(SLOTS, width),
        ),
    )
    arrived = lax.all_to_all(payload.reshape(devices, BLOCK, LANES), AXES, 0, 0)
    return call(
        pair_kernel,
        "pairs",
        (
            arrived.reshape(devices * BLOCK, LANES),
            adder,
            updated,
            slot_back,
            last,
            member,
            pair_state,
            w_outer_kept,
            pair_gain_kept,
            w_gate,
            w_lift,
            w_drop,
            kept[-1],
        ),
        (
            held(rows, width, dtype=BF),
            held(own_tokens, channels, dtype=BF),
            held(*pair_state.shape, dtype=BF),
        ),
    )


def solution(mesh):
    in_specs = (
        P(("row", "col"), None),
        P(("row", "col")),
        P(),
        P(),
        P(),
        P(),
        P(),
        P(),
        P(),
        P(),
        P("row", "col", None),
        P(),
        P(),
        P(),
        P(),
        P(),
        P(),
        P(),
    )
    out_specs = (P(("row", "col"), None), P(("row", "col"), None), P("row", "col", None))
    return jax.shard_map(
        per_device, mesh=mesh, in_specs=in_specs, out_specs=out_specs, check_vma=False
    )
```

```python
import math

import jax
import jax.numpy as jnp
from jax import lax
from jax.experimental import pallas as pl
from jax.experimental.pallas import tpu as pltpu
from jax.sharding import PartitionSpec as P

HEADS = 4
QB = 32
KW = 128
EPSILON = 1e-05
HALF = KW // 2
FEWEST = 8
LANES = 128
SLOTS = 16
BLOCK = 16
SLOT_ROW = 12
DESTS = 32
PAIR_ROWS = 16
GROUP = 8
MASKED = -1e30
SPARE = 12 << 20
MOST = 60 << 20
LOG2E = 1.4426950408889634
AXES = ("row", "col")
BF = jnp.bfloat16
F32 = jnp.float32


def dot(a, b):
    return jnp.dot(a, b, preferred_element_type=F32)


def dot_t(a, b):
    return lax.dot_general(a, b, (((1,), (1,)), ((), ())), preferred_element_type=F32)


def iota(shape, axis):
    return lax.broadcasted_iota(jnp.int32, shape, axis)


def centred_rows(values, gain):
    width = values.shape[1]
    average = jnp.full((width, width), 1.0 / width, F32).astype(BF)
    centred = values.astype(F32) - dot(values, average)
    variance = dot((centred * centred).astype(BF), average)
    return (centred * gain).astype(BF), lax.rsqrt(variance + EPSILON)


def flag(mask):
    return jnp.where(mask, 1.0, 0.0).astype(BF)


def place():
    return lax.axis_index("row") * lax.axis_size("col") + lax.axis_index("col")


def overlap(base, first_own, own_tokens, slots):
    inner = jnp.minimum(first_own + own_tokens, base + slots) - jnp.maximum(first_own, base)
    return jnp.maximum(inner, 0)


def edge_row(base, first_own, own_tokens, slots):
    last_own = first_own + own_tokens - 1
    last_held = (last_own >= base) & (last_own < base + slots)
    free = jnp.where(last_held, 0, own_tokens - 1)
    whole = overlap(base, first_own, own_tokens, slots) == own_tokens
    return jnp.where(whole, BLOCK - 1, free)


def repeat(count, step):
    if count <= 8:
        for at in range(count):
            step(at)
    else:

        def body(at, carry):
            step(at)
            return carry

        lax.fori_loop(0, count, body, 0)


def span(at, size):
    if isinstance(at, int):
        return pl.ds(at * size, size)
    return pl.ds(pl.multiple_of(at * size, size), size)


def ready_kernel(
    own_far,
    starts_far,
    counts_far,
    folded_far,
    atom_gain_far,
    pair_gain_far,
    w_query_far,
    w_key_far,
    w_value_far,
    w_out_far,
    w_pool_far,
    w_back_far,
    w_left_far,
    w_right_far,
    w_outer_far,
    own_float,
    own_mixed,
    probes,
    scores,
    top,
    far_bias,
    picks,
    row_scale,
    selects,
    member,
    slot_scale,
    before,
    goes_on,
    last,
    adder,
    atom_gain,
    pair_gain,
    w_mixed,
    w_pool,
    w_back,
    w_sides,
    w_outer,
    own,
    key_starts,
    counts,
    counts_folded,
    w_query,
    w_key,
    w_value,
    w_out,
    ends,
    arrivals,
):
    rows, width = own.shape
    tokens = counts.shape[1]
    opm = w_left_far.shape[0]
    pairs = (
        (counts_far, counts),
        (folded_far, counts_folded),
        (own_far, own),
        (starts_far, key_starts),
        (atom_gain_far, atom_gain),
        (w_query_far, w_query),
        (w_key_far, w_key),
        (w_value_far, w_value),
        (w_out_far, w_out),
        (pair_gain_far, pair_gain),
        (w_pool_far, w_pool),
        (w_back_far, w_back),
        (w_left_far, w_sides.at[:opm]),
        (w_right_far, w_sides.at[opm : 2 * opm]),
        (w_left_far, w_sides.at[2 * LANES - 2 * opm : 2 * LANES - opm]),
        (w_right_far, w_sides.at[2 * LANES - opm :]),
        (w_outer_far, w_outer.at[:, : w_outer_far.shape[1]]),
    )
    copies = [pltpu.make_async_copy(a, b, arrivals.at[k]) for k, (a, b) in enumerate(pairs)]
    for copy in copies:
        copy.start()

    tiles = picks.shape[1] // rows
    devices = picks.shape[0] // BLOCK
    atoms = rows * devices
    own_tokens = tokens // devices
    token_rows = own_tokens * tiles
    slots = rows // FEWEST + 1
    position = place()
    first = position * rows
    even = position % 2 == 0
    first_float = first.astype(F32)
    w_sides[2 * opm : 2 * LANES - 2 * opm, :] = jnp.zeros(
        (2 * LANES - 4 * opm, tiles * LANES), BF
    )

    for copy in copies[:9]:
        copy.wait()
    counts_wide = jnp.broadcast_to(counts[...].astype(F32), (tiles * rows, tokens)).astype(BF)
    counts_lane = counts_wide[:LANES]
    folded = counts_folded[...].astype(F32).astype(BF)
    upper = flag(iota((LANES, LANES), 0) <= iota((LANES, LANES), 1))
    lower = flag(iota((LANES, LANES), 1) <= iota((LANES, LANES), 0))
    within = dot(folded, upper)
    whole = dot(folded, jnp.ones((LANES, LANES), BF))
    base = jnp.zeros((1, 1), F32)
    passed = jnp.zeros((1, LANES), F32)
    for fold in range(folded.shape[0]):
        ended = within[fold : fold + 1] + passed <= first_float
        base = base + jnp.sum(jnp.where(ended, 1.0, 0.0), axis=1, keepdims=True)
        part = slice(fold * LANES, (fold + 1) * LANES)
        ends[part, :] = passed + dot_t(lower, counts_lane[:, part])
        passed = passed + whole[fold : fold + 1]

    base_token = base.astype(jnp.int32)
    token_lane = iota((SLOTS, tokens), 1).astype(F32)
    slot_token = iota((SLOTS, tokens), 0).astype(F32) + base
    slot_end = dot_t(flag(token_lane <= slot_token), counts_lane)
    slot_start = dot_t(flag(token_lane < slot_token), counts_lane)
    atom_lane = iota((SLOTS, rows), 1).astype(F32) + first_float
    member[...] = flag((atom_lane >= slot_start[:, :rows]) & (atom_lane < slot_end[:, :rows]))
    slot_scale[...] = 1.0 / jnp.maximum(slot_end - slot_start, 1.0)
    last_atom = first_float + (rows - 1)
    is_last = jnp.where((slot_start <= last_atom) & (slot_end > last_atom), 1.0, 0.0)
    last[...] = is_last
    goes_on[...] = is_last * jnp.where(slot_end > first_float + rows, 1.0, 0.0)
    is_first = iota((SLOTS, LANES), 0) == 0
    before[...] = jnp.where(is_first & (slot_start < first_float), 1.0, 0.0)

    def rows_step(at):
        def spread(lanes, axis):
            return iota((DESTS, BLOCK, lanes), axis).reshape(DESTS * BLOCK, lanes)

        here = span(at, DESTS * BLOCK)
        token_at = iota((1, tokens), 1)
        turn = spread(tokens, 1) % own_tokens
        row_token = (spread(tokens, 0) + at * DESTS) * own_tokens + turn
        row_end = dot_t(flag(token_at <= row_token), counts_wide)
        row_start = dot_t(flag(token_at < row_token), counts_wide)
        lanes = tiles * rows
        lane = iota((1, lanes), 1)
        atom = (lane % rows + first).astype(F32)
        tile_fits = spread(lanes, 1) // own_tokens == lane // rows
        picks[here, :] = flag(tile_fits & (atom >= row_start) & (atom < row_end))
        row_scale[here, :] = 1.0 / jnp.maximum(row_end - row_start, 1.0)[:, :LANES]
        lanes = 3 * SLOTS
        dest = spread(lanes, 0) + at * DESTS
        spot = spread(lanes, 1)
        kind = iota((1, lanes), 1) // SLOTS
        slot = iota((1, lanes), 1) % SLOTS
        first_own = dest * own_tokens
        shared_tokens = overlap(base_token, first_own, own_tokens, slots)
        token = base_token + slot
        index = jnp.where(token < first_own, slot, slot - shared_tokens)
        mine = (token >= first_own) & (token < first_own + own_tokens)
        room = 2 * (BLOCK - SLOT_ROW)
        target = jnp.where(index < room, SLOT_ROW + index // 2, jnp.where(kind == 0, 0, -1))
        target = jnp.where(index % 2 == kind, target, -1)
        is_slot = (kind < 2) & (slot < slots) & jnp.logical_not(mine) & (spot == target)
        on_edge = spot == edge_row(base_token, first_own, own_tokens, slots)
        beside = jnp.where(slot == 0, position - 1, position + 1)
        is_edge = (kind == 2) & (slot < 2) & on_edge & (dest == beside)
        selects[here, :] = flag(is_slot | is_edge)

    repeat(devices // DESTS, rows_step)

    row_tokens = tokens // lax.axis_size("row")
    col_tokens = tokens // lax.axis_size("col")
    first_row = lax.axis_index("row") * row_tokens
    first_col = lax.axis_index("col") * col_tokens

    def adder_step(at):
        here = span(at, LANES)
        spot_lane = iota((1, LANES), 1) + at * LANES
        block = spot_lane // BLOCK
        spot = spot_lane % BLOCK
        edge = (block * rows).astype(F32)
        tally = jnp.zeros((1, LANES), F32)
        for fold in range(tokens // LANES):
            ended = jnp.where(ends[fold * LANES : (fold + 1) * LANES, :] <= edge, 1.0, 0.0)
            tally = tally + jnp.sum(ended, axis=0, keepdims=True)
        start = tally.astype(jnp.int32)
        first_own = position * own_tokens
        shared_tokens = overlap(start, first_own, own_tokens, slots)

        def token_of(index):
            slot = jnp.where(start + index < first_own, index, index + shared_tokens)
            return jnp.where((index >= 0) & (slot < slots), start + slot, -1)

        in_slots = spot >= SLOT_ROW
        room = 2 * (BLOCK - SLOT_ROW)
        ninth = jnp.where((spot == 0) & (shared_tokens == 0), start + room, -1)
        low_token = jnp.where(in_slots, token_of(2 * (spot - SLOT_ROW)), ninth)
        high_token = jnp.where(in_slots, token_of(2 * (spot - SLOT_ROW) + 1), -1)
        own_token = first_own + spot % own_tokens
        held = (spot < token_rows) & (own_token >= start) & (own_token < start + slots)
        own_token = jnp.where(held, own_token, -1)
        line = iota((SLOTS, LANES), 0)
        side = jnp.where(line == token_rows, position - 1, position + 1)
        on_edge = spot == edge_row(start, first_own, own_tokens, slots)
        is_edge = (line >= token_rows) & (line < token_rows + 2) & on_edge & (block == side)
        lines = [(line < token_rows) & (spot == line) & held | is_edge]
        row_line = iota((row_tokens, LANES), 0) + first_row
        col_line = iota((col_tokens, LANES), 0) + first_col
        for wanted in (row_line, col_line):
            lines += [low_token == wanted, high_token == wanted]
        for tile in range(tiles):
            tile_token = jnp.where(spot // own_tokens == tile, own_token, -1)
            lines += [tile_token == row_line, tile_token == col_line]
        top = 0
        for part in lines:
            adder[top : top + part.shape[0], here] = flag(part)
            top += part.shape[0]

    repeat(devices * BLOCK // LANES, adder_step)

    own_float[...] = own[...].astype(F32)
    normed, scaling = centred_rows(own[...], atom_gain[...])
    near = (dot(normed, w_key[...]) * scaling).astype(BF)
    query = (dot(normed, w_query[...]) * scaling).astype(BF)
    head_of = iota((1, width), 1) // (width // HEADS)
    head_mask = [flag(head_of == h) for h in range(HEADS)]
    heads = jnp.concatenate([query * m for m in head_mask], axis=0)
    probes[...] = dot_t(heads, w_key[...]).astype(BF)
    w_mix = jnp.concatenate(
        [dot(w_value[...] * m, w_out[...]).astype(BF) for m in head_mask], axis=1
    )
    w_mixed[...] = w_mix
    own_mixed[...] = (
        dot(normed, w_mix) * jnp.concatenate([scaling] * HEADS, axis=1)
    ).astype(BF)
    near_index = first + iota((1, rows), 1)
    far_lane = iota((1, 2 * rows), 1)
    is_low = (far_lane < rows) != even
    far_index = first + far_lane % rows + jnp.where(is_low, -rows, rows)
    near_bias, bias = [], []
    for e in range(rows // QB):
        low = key_starts[0:1, e : e + 1]
        seen = (near_index >= low) & (near_index < low + KW)
        near_bias.append(jnp.broadcast_to(jnp.where(seen, 0.0, MASKED), (QB, rows)))
        seen = (far_index >= low) & (far_index < low + KW)
        seen = seen & (far_index >= 0) & (far_index < atoms)
        bias.append(jnp.broadcast_to(jnp.where(seen, 0.0, MASKED), (QB, 2 * rows)))
    far_bias[...] = jnp.concatenate(bias, axis=0)
    raw_scores = dot_t(heads, near) + jnp.concatenate(near_bias * HEADS, axis=0)
    scores[...] = raw_scores
    top[...] = jnp.max(raw_scores, axis=-1, keepdims=True)
    for copy in copies[9:]:
        copy.wait()
    pair_width = w_outer_far.shape[1]
    average = jnp.full((pair_width, pair_width), 1.0 / pair_width, F32).astype(BF)
    w_outer[:, pair_width:] = dot(w_outer[:, :pair_width], average).astype(BF)


def atom_kernel(
    neighbour,
    sibling,
    own_float,
    own_mixed,
    probes,
    scores,
    top,
    far_bias,
    picks,
    row_scale,
    selects,
    member,
    slot_scale,
    before,
    goes_on,
    atom_gain,
    w_mixed,
    w_pool,
    w_back,
    w_sides,
    payload,
    updated,
    slot_back,
):
    rows, width = own_float.shape
    tiles = w_pool.shape[1] // LANES
    devices = payload.shape[0] // BLOCK
    raw = jnp.concatenate([sibling[...], neighbour[...]], axis=0)
    average = jnp.full((width, width), 1.0 / width, F32).astype(BF)
    centred = raw.astype(F32) - dot(raw, average)
    squares = (centred * centred).astype(BF)
    normed = (centred * atom_gain[...]).astype(BF)
    scaling = lax.rsqrt(dot(squares, average) + EPSILON)
    scaling_row = lax.rsqrt(dot_t(average[:SLOTS], squares) + EPSILON)[0:1]
    far_mixed = (
        dot(normed, w_mixed[...]) * jnp.concatenate([scaling] * HEADS, axis=1)
    ).astype(BF)
    far_scores = dot_t(probes[...], normed) * scaling_row
    far_scores = far_scores + jnp.concatenate([far_bias[...]] * HEADS, axis=0)
    most = jnp.maximum(top[...], jnp.max(far_scores, axis=-1, keepdims=True))
    scale = (width // HEADS) ** (-0.5) * LOG2E
    raised = jnp.concatenate(
        [
            jnp.exp2((far_scores - most) * scale).astype(BF),
            jnp.exp2((scores[...] - most) * scale).astype(BF),
        ],
        axis=1,
    )
    ones = jnp.ones((3 * rows, width), BF)
    change = own_float[...]
    for h in range(HEADS):
        part = slice(h * width, (h + 1) * width)
        values = jnp.concatenate([far_mixed[:, part], own_mixed[:, part]], axis=0)
        mixed = dot(raised[h * rows : (h + 1) * rows], jnp.concatenate([values, ones], axis=1))
        change = change + mixed[:, :width] / mixed[:, width:]
    fresh = change.astype(BF)
    updated[...] = fresh
    feature = jnp.maximum(dot(fresh, w_pool[...]), 0.0).astype(BF)
    feature_tiles = jnp.concatenate(
        [feature[:, k * LANES : (k + 1) * LANES] for k in range(tiles)], axis=0
    )
    slot_single = (
        dot(member[...], feature) * jnp.concatenate([slot_scale[...]] * tiles, axis=1)
    ).astype(BF)
    sides = dot_t(slot_single, w_sides[...]).astype(BF)
    backs = dot(slot_single, w_back[...])
    slot_back[...] = backs
    to_before = jnp.sum(backs * before[...], axis=0, keepdims=True)
    to_after = jnp.sum(backs * goes_on[...], axis=0, keepdims=True)
    spot = iota((SLOTS, LANES), 0)
    edges = jnp.where(spot == 0, to_before, jnp.where(spot == 1, to_after, 0.0)).astype(BF)
    shared = jnp.concatenate([sides[:, :LANES], sides[:, LANES:], edges], axis=0)

    def send_step(at):
        here = span(at, DESTS * BLOCK)
        singles = dot(picks[here, :], feature_tiles) * row_scale[here, :]
        payload[here, :] = (singles + dot(selects[here, :], shared)).astype(BF)

    repeat(devices // DESTS, send_step)


def pair_kernel(
    arrived,
    adder,
    updated,
    slot_back,
    slot_last,
    slot_member,
    pair_state,
    w_outer,
    pair_gain,
    w_gate,
    w_lift,
    w_drop,
    w_sides,
    atom_out,
    token_single,
    pair_out,
):
    row_tokens, col_tokens, pair_width = pair_state.shape
    own_tokens, channels = token_single.shape
    tiles = channels // LANES
    token_rows = own_tokens * tiles
    opm = math.isqrt(w_outer.shape[0])
    added = dot(adder[...], arrived[...])
    half_gate = w_gate[...] * jnp.asarray(0.5, BF)
    parts, top = [], 0
    for height in (SLOTS,) + (row_tokens,) * 2 + (col_tokens,) * 2 + (row_tokens, col_tokens) * tiles:
        parts.append(added[top : top + height])
        top += height
    sums, left_low, left_high, right_low, right_high, *own = parts
    own_left = jnp.concatenate(own[0::2], axis=1).astype(BF)
    own_right = jnp.concatenate(own[1::2], axis=1).astype(BF)
    own_sides = dot_t(jnp.concatenate([own_left, own_right], axis=0), w_sides[:LANES])
    left = left_low[:, :opm] + left_high[:, 2 * opm : 3 * opm] + own_sides[:row_tokens, :opm]
    right = right_low[:, opm : 2 * opm] + right_high[:, 3 * opm : 4 * opm]
    right = right + own_sides[row_tokens:, opm : 2 * opm]
    left, right = left.astype(BF), right.astype(BF)
    depth = GROUP * opm
    unit = flag(iota((opm, depth), 1) % opm == iota((opm, depth), 0))
    corner = jnp.where(iota((GROUP, depth), 1) // opm == iota((GROUP, depth), 0), 1.0, 0.0)

    def spread(rows_of, first, count):
        return jnp.concatenate(
            [
                jnp.broadcast_to(rows_of[k : k + 1, :], (GROUP, depth)) * corner
                for k in range(first, first + count)
            ],
            axis=0,
        ).astype(BF)

    left_wide = dot(left, unit)
    right_blocks = spread(dot(right, unit), 0, col_tokens)
    stages = opm // GROUP
    table = [
        dot(right_blocks, w_outer[g * depth : (g + 1) * depth, :]) for g in range(stages)
    ]
    tables = [
        jnp.concatenate(
            [
                table[g][j * GROUP : (j + 1) * GROUP]
                for j in range(h * GROUP, (h + 1) * GROUP)
                for g in range(stages)
            ],
            axis=0,
        ).astype(BF)
        for h in range(col_tokens // GROUP)
    ]

    def pair_rows(here):
        left_blocks = spread(left_wide, here, PAIR_ROWS)
        terms = [dot(left_blocks, part) for part in tables]
        outer = jnp.concatenate(
            [
                term[i * GROUP : (i + 1) * GROUP]
                for i in range(PAIR_ROWS)
                for term in terms
            ],
            axis=0,
        )
        flat = pair_state[pl.ds(here, PAIR_ROWS)].reshape(PAIR_ROWS * col_tokens, pair_width)
        flat = flat.astype(F32)
        summed = flat + outer[:, :pair_width]
        pair_mean = jnp.mean(flat, axis=-1, keepdims=True)
        centred = summed - (pair_mean + outer[:, pair_width:])
        variance = jnp.mean(centred * centred, axis=-1, keepdims=True)
        scaling = lax.rsqrt(variance + EPSILON)
        normed = (centred * pair_gain[...]).astype(BF)
        gate = dot(normed, half_gate) * scaling
        lift = dot(normed, w_lift[...]) * scaling
        hidden = (gate * lift * (1.0 + jnp.tanh(gate))).astype(BF)
        result = (summed + dot(hidden, w_drop[...])).astype(BF)
        pair_out[pl.ds(here, PAIR_ROWS)] = result.reshape(PAIR_ROWS, col_tokens, pair_width)

    for step in range(row_tokens // PAIR_ROWS):
        here = step * PAIR_ROWS
        pair_rows(here)

    token_single[...] = jnp.concatenate(
        [sums[k * own_tokens : (k + 1) * own_tokens] for k in range(tiles)], axis=1
    ).astype(BF)
    spot = iota((SLOTS, LANES), 0)
    from_before = jnp.where(spot == 0, sums[token_rows : token_rows + 1], 0.0)
    from_after = slot_last[...] * sums[token_rows + 1 : token_rows + 2]
    back = (slot_back[...] + from_before + from_after).astype(BF)
    lifted = lax.dot_general(
        slot_member[...], back, (((0,), (0,)), ((), ())), preferred_element_type=F32
    )
    atom_out[...] = (updated[...].astype(F32) + lifted).astype(BF)


def call(kernel, name, operands, outputs, far=(), scratch=()):
    near_spec = pl.BlockSpec(memory_space=pltpu.VMEM)
    far_spec = pl.BlockSpec(memory_space=pltpu.HBM)
    held = sum(math.prod(a.shape) * a.dtype.itemsize for a in operands + outputs)
    return pl.pallas_call(
        kernel,
        out_shape=outputs,
        in_specs=[far_spec] * len(far) + [near_spec] * len(operands),
        out_specs=(near_spec,) * len(outputs),
        scratch_shapes=scratch,
        compiler_params=pltpu.CompilerParams(vmem_limit_bytes=min(2 * held + SPARE, MOST)),
        name=name,
    )(*[pltpu.with_memory_space_constraint(a, pltpu.HBM) for a in far], *operands)


def per_device(
    atom_feats,
    key_starts,
    atom_counts,
    atom_gain,
    w_query,
    w_key,
    w_value,
    w_out,
    w_pool,
    w_back,
    pair_state,
    w_left,
    w_right,
    w_outer,
    pair_gain,
    w_gate,
    w_lift,
    w_drop,
):
    rows, width = atom_feats.shape
    devices = lax.axis_size(AXES)
    tokens = atom_counts.shape[0]
    channels = w_pool.shape[1]
    opm = w_left.shape[1]
    own_tokens = tokens // devices
    row_tokens, col_tokens, _ = pair_state.shape
    tiles = channels // LANES
    opm = w_left.shape[1]
    across = [(i, i + 1) for i in range(1, devices - 1, 2)]
    neighbour = lax.ppermute(atom_feats, AXES, across + [(j, i) for i, j in across])
    sibling = lax.ppermute(atom_feats, AXES, [(i, i ^ 1) for i in range(devices)])

    def held(*shape, dtype=F32):
        return jax.ShapeDtypeStruct(shape, dtype)

    counts_folded = atom_counts.reshape(-1, LANES)
    ready = call(
        ready_kernel,
        "ready",
        (),
        (
            held(rows, width),
            held(rows, HEADS * width, dtype=BF),
            held(HEADS * rows, width, dtype=BF),
            held(HEADS * rows, rows),
            held(HEADS * rows, 1),
            held(rows, 2 * rows),
            held(devices * BLOCK, tiles * rows, dtype=BF),
            held(devices * BLOCK, LANES),
            held(devices * BLOCK, 3 * SLOTS, dtype=BF),
            held(SLOTS, rows, dtype=BF),
            held(SLOTS, LANES),
            held(SLOTS, LANES),
            held(SLOTS, LANES),
            held(SLOTS, LANES),
            held(
                SLOTS + (2 + tiles) * (row_tokens + col_tokens), devices * BLOCK, dtype=BF
            ),
            held(1, width),
            held(1, LANES),
            held(width, HEADS * width, dtype=BF),
            held(width, channels, dtype=BF),
            held(channels, width, dtype=BF),
            held(2 * LANES, channels, dtype=BF),
            held(opm * opm, 2 * w_outer.shape[-1], dtype=BF),
        ),
        far=(
            atom_feats,
            key_starts[None],
            atom_counts[None],
            counts_folded,
            atom_gain[None],
            pair_gain[None],
            w_query,
            w_key,
            w_value,
            w_out,
            w_pool,
            w_back,
            w_left.T,
            w_right.T,
            w_outer.reshape(opm * opm, -1),
        ),
        scratch=(
            pltpu.VMEM((rows, width), BF),
            pltpu.VMEM((1, key_starts.shape[0]), jnp.int32),
            pltpu.VMEM((1, tokens), jnp.int32),
            pltpu.VMEM(counts_folded.shape, jnp.int32),
            pltpu.VMEM((width, width), BF),
            pltpu.VMEM((width, width), BF),
            pltpu.VMEM((width, width), BF),
            pltpu.VMEM((width, width), BF),
            pltpu.VMEM((tokens, LANES), F32),
            pltpu.SemaphoreType.DMA((17,)),
        ),
    )
    (
        own_float,
        own_mixed,
        probes,
        scores,
        top,
        far_bias,
        picks,
        row_scale,
        selects,
        member,
        slot_scale,
        before,
        goes_on,
        last,
        adder,
        atom_gain_kept,
        pair_gain_kept,
        *kept,
        w_outer_kept,
    ) = ready
    payload, updated, slot_back = call(
        atom_kernel,
        "atoms",
        (
            neighbour,
            sibling,
            own_float,
            own_mixed,
            probes,
            scores,
            top,
            far_bias,
            picks,
            row_scale,
            selects,
            member,
            slot_scale,
            before,
            goes_on,
            atom_gain_kept,
            *kept,
        ),
        (
            held(devices * BLOCK, LANES, dtype=BF),
            held(rows, width, dtype=BF),
            held(SLOTS, width),
        ),
    )
    arrived = lax.all_to_all(payload.reshape(devices, BLOCK, LANES), AXES, 0, 0)
    return call(
        pair_kernel,
        "pairs",
        (
            arrived.reshape(devices * BLOCK, LANES),
            adder,
            updated,
            slot_back,
            last,
            member,
            pair_state,
            w_outer_kept,
            pair_gain_kept,
            w_gate,
            w_lift,
            w_drop,
            kept[-1],
        ),
        (
            held(rows, width, dtype=BF),
            held(own_tokens, channels, dtype=BF),
            held(*pair_state.shape, dtype=BF),
        ),
    )


def solution(mesh):
    in_specs = (
        P(("row", "col"), None),
        P(("row", "col")),
        P(),
        P(),
        P(),
        P(),
        P(),
        P(),
        P(),
        P(),
        P("row", "col", None),
        P(),
        P(),
        P(),
        P(),
        P(),
        P(),
        P(),
    )
    out_specs = (P(("row", "col"), None), P(("row", "col"), None), P("row", "col", None))
    return jax.shard_map(
        per_device, mesh=mesh, in_specs=in_specs, out_specs=out_specs, check_vma=False
    )
```

```python
import math

import jax
import jax.numpy as jnp
from jax import lax
from jax.experimental import pallas as pl
from jax.experimental.pallas import tpu as pltpu
from jax.sharding import PartitionSpec as P

HEADS = 4
QB = 32
KW = 128
EPSILON = 1e-05
HALF = KW // 2
FEWEST = 8
LANES = 128
SLOTS = 16
BLOCK = 16
SLOT_ROW = 12
DESTS = 32
PAIR_ROWS = 16
GROUP = 8
MASKED = -1e30
SPARE = 12 << 20
MOST = 60 << 20
LOG2E = 1.4426950408889634
AXES = ("row", "col")
BF = jnp.bfloat16
F32 = jnp.float32


def dot(a, b):
    return jnp.dot(a, b, preferred_element_type=F32)


def dot_t(a, b):
    return lax.dot_general(a, b, (((1,), (1,)), ((), ())), preferred_element_type=F32)


def iota(shape, axis):
    return lax.broadcasted_iota(jnp.int32, shape, axis)


def centred_rows(values, gain):
    width = values.shape[1]
    average = jnp.full((width, width), 1.0 / width, F32).astype(BF)
    centred = values.astype(F32) - dot(values, average)
    variance = dot((centred * centred).astype(BF), average)
    return (centred * gain).astype(BF), lax.rsqrt(variance + EPSILON)


def flag(mask):
    return jnp.where(mask, 1.0, 0.0).astype(BF)


def place():
    return lax.axis_index("row") * lax.axis_size("col") + lax.axis_index("col")


def overlap(base, first_own, own_tokens, slots):
    inner = jnp.minimum(first_own + own_tokens, base + slots) - jnp.maximum(first_own, base)
    return jnp.maximum(inner, 0)


def edge_row(base, first_own, own_tokens, slots):
    last_own = first_own + own_tokens - 1
    last_held = (last_own >= base) & (last_own < base + slots)
    free = jnp.where(last_held, 0, own_tokens - 1)
    whole = overlap(base, first_own, own_tokens, slots) == own_tokens
    return jnp.where(whole, BLOCK - 1, free)


def repeat(count, step):
    if count <= 8:
        for at in range(count):
            step(at)
    else:

        def body(at, carry):
            step(at)
            return carry

        lax.fori_loop(0, count, body, 0)


def span(at, size):
    if isinstance(at, int):
        return pl.ds(at * size, size)
    return pl.ds(pl.multiple_of(at * size, size), size)


def ready_kernel(
    own_far,
    starts_far,
    counts_far,
    folded_far,
    atom_gain_far,
    pair_gain_far,
    w_query_far,
    w_key_far,
    w_value_far,
    w_out_far,
    w_pool_far,
    w_back_far,
    w_left_far,
    w_right_far,
    w_outer_far,
    own_float,
    own_mixed,
    probes,
    scores,
    top,
    far_bias,
    route,
    member,
    slot_scale,
    before,
    goes_on,
    last,
    adder,
    own_scale,
    atom_gain,
    pair_gain,
    w_mixed,
    w_pool,
    w_back,
    w_sides,
    w_outer,
    own,
    key_starts,
    counts,
    counts_folded,
    w_query,
    w_key,
    w_value,
    w_out,
    begins,
    ends,
    arrivals,
):
    rows, width = own.shape
    tokens = counts.shape[1]
    opm = w_left_far.shape[0]
    pairs = (
        (counts_far, counts),
        (folded_far, counts_folded),
        (own_far, own),
        (starts_far, key_starts),
        (atom_gain_far, atom_gain),
        (w_query_far, w_query),
        (w_key_far, w_key),
        (w_value_far, w_value),
        (w_out_far, w_out),
        (pair_gain_far, pair_gain),
        (w_pool_far, w_pool),
        (w_back_far, w_back),
        (w_left_far, w_sides.at[:opm]),
        (w_right_far, w_sides.at[opm : 2 * opm]),
        (w_left_far, w_sides.at[2 * LANES - 2 * opm : 2 * LANES - opm]),
        (w_right_far, w_sides.at[2 * LANES - opm :]),
        (w_outer_far, w_outer.at[:, : w_outer_far.shape[1]]),
    )
    copies = [pltpu.make_async_copy(a, b, arrivals.at[k]) for k, (a, b) in enumerate(pairs)]
    for copy in copies:
        copy.start()

    tiles = w_pool.shape[1] // LANES
    devices = route.shape[0] // BLOCK
    atoms = rows * devices
    own_tokens = tokens // devices
    token_rows = own_tokens * tiles
    slots = rows // FEWEST + 1
    position = place()
    first = position * rows
    even = position % 2 == 0
    first_float = first.astype(F32)
    w_sides[2 * opm : 2 * LANES - 2 * opm, :] = jnp.zeros(
        (2 * LANES - 4 * opm, tiles * LANES), BF
    )

    for copy in copies[:9]:
        copy.wait()
    counts_lane = jnp.broadcast_to(counts[...].astype(F32), (LANES, tokens)).astype(BF)
    folded = counts_folded[...].astype(F32).astype(BF)
    upper = flag(iota((LANES, LANES), 0) <= iota((LANES, LANES), 1))
    lower = flag(iota((LANES, LANES), 1) <= iota((LANES, LANES), 0))
    below = flag(iota((LANES, LANES), 1) < iota((LANES, LANES), 0))
    within = dot(folded, upper)
    whole = dot(folded, jnp.ones((LANES, LANES), BF))
    base = jnp.zeros((1, 1), F32)
    passed = jnp.zeros((1, LANES), F32)
    for fold in range(folded.shape[0]):
        ended = within[fold : fold + 1] + passed <= first_float
        base = base + jnp.sum(jnp.where(ended, 1.0, 0.0), axis=1, keepdims=True)
        part = slice(fold * LANES, (fold + 1) * LANES)
        ends[part, :] = passed + dot_t(lower, counts_lane[:, part])
        begins[part, :] = passed + dot_t(below, counts_lane[:, part])
        passed = passed + whole[fold : fold + 1]

    base_token = base.astype(jnp.int32)
    token_lane = iota((SLOTS, tokens), 1).astype(F32)
    slot_token = iota((SLOTS, tokens), 0).astype(F32) + base
    slot_end = dot_t(flag(token_lane <= slot_token), counts_lane)
    slot_start = dot_t(flag(token_lane < slot_token), counts_lane)
    atom_lane = iota((SLOTS, rows), 1).astype(F32) + first_float
    member[...] = flag((atom_lane >= slot_start[:, :rows]) & (atom_lane < slot_end[:, :rows]))
    slot_scale[...] = 1.0 / jnp.maximum(slot_end - slot_start, 1.0)
    last_atom = first_float + (rows - 1)
    is_last = jnp.where((slot_start <= last_atom) & (slot_end > last_atom), 1.0, 0.0)
    last[...] = is_last
    goes_on[...] = is_last * jnp.where(slot_end > first_float + rows, 1.0, 0.0)
    is_first = iota((SLOTS, LANES), 0) == 0
    before[...] = jnp.where(is_first & (slot_start < first_float), 1.0, 0.0)

    lanes = 2 * LANES
    lane = iota((1, lanes), 1)
    atom = (lane % rows + first).astype(F32)
    inside = (atom >= jnp.concatenate([begins[...]] * 2, axis=1)) & (lane < tiles * rows)
    inside = flag(inside & (atom < jnp.concatenate([ends[...]] * 2, axis=1)))
    tile_fits = iota((BLOCK, lanes), 0) // own_tokens == iota((BLOCK, lanes), 1) // rows
    tile_fits = jnp.where(tile_fits, 1.0, 0.0)
    column = iota((1, LANES), 1) - (tiles * rows - LANES)
    kind, slot = column // SLOTS, column % SLOTS
    token = base_token + slot

    def rows_step(at):
        here = span(at, DESTS * BLOCK)
        dest = iota((DESTS, BLOCK, tokens), 0).reshape(DESTS * BLOCK, tokens) + at * DESTS
        turn = iota((DESTS, BLOCK, tokens), 1).reshape(DESTS * BLOCK, tokens) % own_tokens
        picks = dot(flag(iota((1, tokens), 1) == dest * own_tokens + turn), inside)
        picks = picks.reshape(DESTS, BLOCK, lanes) * tile_fits[None]
        picks = picks.reshape(DESTS * BLOCK, lanes)
        dest = iota((DESTS, LANES), 0) + at * DESTS
        first_own = dest * own_tokens
        shared_tokens = overlap(base_token, first_own, own_tokens, slots)
        index = jnp.where(token < first_own, slot, slot - shared_tokens)
        mine = (token >= first_own) & (token < first_own + own_tokens)
        room = 2 * (BLOCK - SLOT_ROW)
        target = jnp.where(index < room, SLOT_ROW + index // 2, jnp.where(kind == 0, 0, -1))
        fits = (index % 2 == kind) & (slot < slots) & jnp.logical_not(mine) & (column >= 0)
        target = jnp.where(fits & (kind < 2), target, -1)
        beside = jnp.where(slot == 0, position - 1, position + 1)
        is_edge = (kind == 2) & (slot < 2) & (dest == beside)
        row = edge_row(base_token, first_own, own_tokens, slots)
        target = jnp.where(is_edge, row, target)
        spot = iota((BLOCK, LANES), 0)
        selects = [
            jnp.where(jnp.broadcast_to(target[d : d + 1], (BLOCK, LANES)) == spot, 1.0, 0.0)
            for d in range(DESTS)
        ]
        high = picks[:, LANES:] + jnp.concatenate(selects, axis=0)
        route[here, :] = jnp.concatenate([picks[:, :LANES], high], axis=1).astype(BF)

    repeat(devices // DESTS, rows_step)

    row_tokens = tokens // lax.axis_size("row")
    col_tokens = tokens // lax.axis_size("col")
    first_row = lax.axis_index("row") * row_tokens
    first_col = lax.axis_index("col") * col_tokens

    def row_counts(height, first_token, cycle):
        token_row = iota((height, tokens), 0) % cycle + first_token
        return dot_t(flag(iota((1, tokens), 1) == token_row), counts_lane)

    owned = [
        row_counts(SLOTS, position * own_tokens, own_tokens),
        row_counts(row_tokens, first_row, row_tokens),
        row_counts(col_tokens, first_col, col_tokens),
    ]
    own_scale[...] = 1.0 / jnp.concatenate(owned, axis=0)

    def adder_step(at):
        here = span(at, LANES)
        spot_lane = iota((1, LANES), 1) + at * LANES
        block = spot_lane // BLOCK
        spot = spot_lane % BLOCK
        edge = (block * rows).astype(F32)
        tally = jnp.zeros((1, LANES), F32)
        for fold in range(tokens // LANES):
            ended = jnp.where(ends[fold * LANES : (fold + 1) * LANES, :] <= edge, 1.0, 0.0)
            tally = tally + jnp.sum(ended, axis=0, keepdims=True)
        start = tally.astype(jnp.int32)
        first_own = position * own_tokens
        shared_tokens = overlap(start, first_own, own_tokens, slots)

        def token_of(index):
            slot = jnp.where(start + index < first_own, index, index + shared_tokens)
            return jnp.where((index >= 0) & (slot < slots), start + slot, -1)

        in_slots = spot >= SLOT_ROW
        room = 2 * (BLOCK - SLOT_ROW)
        ninth = jnp.where((spot == 0) & (shared_tokens == 0), start + room, -1)
        low_token = jnp.where(in_slots, token_of(2 * (spot - SLOT_ROW)), ninth)
        high_token = jnp.where(in_slots, token_of(2 * (spot - SLOT_ROW) + 1), -1)
        own_token = first_own + spot % own_tokens
        held = (spot < token_rows) & (own_token >= start) & (own_token < start + slots)
        own_token = jnp.where(held, own_token, -1)
        line = iota((SLOTS, LANES), 0)
        side = jnp.where(line == token_rows, position - 1, position + 1)
        on_edge = spot == edge_row(start, first_own, own_tokens, slots)
        is_edge = (line >= token_rows) & (line < token_rows + 2) & on_edge & (block == side)
        lines = [(line < token_rows) & (spot == line) & held | is_edge]
        row_line = iota((row_tokens, LANES), 0) + first_row
        col_line = iota((col_tokens, LANES), 0) + first_col
        for wanted in (row_line, col_line):
            lines += [low_token == wanted, high_token == wanted]
        for tile in range(tiles):
            tile_token = jnp.where(spot // own_tokens == tile, own_token, -1)
            lines += [tile_token == row_line, tile_token == col_line]
        top = 0
        for part in lines:
            adder[top : top + part.shape[0], here] = flag(part)
            top += part.shape[0]

    repeat(devices * BLOCK // LANES, adder_step)

    own_float[...] = own[...].astype(F32)
    normed, scaling = centred_rows(own[...], atom_gain[...])
    near = (dot(normed, w_key[...]) * scaling).astype(BF)
    query = (dot(normed, w_query[...]) * scaling).astype(BF)
    head_of = iota((1, width), 1) // (width // HEADS)
    head_mask = [flag(head_of == h) for h in range(HEADS)]
    heads = jnp.concatenate([query * m for m in head_mask], axis=0)
    probes[...] = dot_t(heads, w_key[...]).astype(BF)
    w_mix = jnp.concatenate(
        [dot(w_value[...] * m, w_out[...]).astype(BF) for m in head_mask], axis=1
    )
    w_mixed[...] = w_mix
    own_mixed[...] = (
        dot(normed, w_mix) * jnp.concatenate([scaling] * HEADS, axis=1)
    ).astype(BF)
    near_index = first + iota((1, rows), 1)
    far_lane = iota((1, 2 * rows), 1)
    is_low = (far_lane < rows) != even
    far_index = first + far_lane % rows + jnp.where(is_low, -rows, rows)
    near_bias, bias = [], []
    for e in range(rows // QB):
        low = key_starts[0:1, e : e + 1]
        seen = (near_index >= low) & (near_index < low + KW)
        near_bias.append(jnp.broadcast_to(jnp.where(seen, 0.0, MASKED), (QB, rows)))
        seen = (far_index >= low) & (far_index < low + KW)
        seen = seen & (far_index >= 0) & (far_index < atoms)
        bias.append(jnp.broadcast_to(jnp.where(seen, 0.0, MASKED), (QB, 2 * rows)))
    far_bias[...] = jnp.concatenate(bias, axis=0)
    raw_scores = dot_t(heads, near) + jnp.concatenate(near_bias * HEADS, axis=0)
    scores[...] = raw_scores
    top[...] = jnp.max(raw_scores, axis=-1, keepdims=True)
    for copy in copies[9:]:
        copy.wait()
    pair_width = w_outer_far.shape[1]
    average = jnp.full((pair_width, pair_width), 1.0 / pair_width, F32).astype(BF)
    w_outer[:, pair_width:] = dot(w_outer[:, :pair_width], average).astype(BF)


def atom_kernel(
    neighbour,
    sibling,
    own_float,
    own_mixed,
    probes,
    scores,
    top,
    far_bias,
    route,
    member,
    slot_scale,
    before,
    goes_on,
    atom_gain,
    w_mixed,
    w_pool,
    w_back,
    w_sides,
    payload,
    updated,
    slot_back,
):
    rows, width = own_float.shape
    tiles = w_pool.shape[1] // LANES
    devices = payload.shape[0] // BLOCK
    raw = jnp.concatenate([sibling[...], neighbour[...]], axis=0)
    average = jnp.full((width, width), 1.0 / width, F32).astype(BF)
    centred = raw.astype(F32) - dot(raw, average)
    squares = (centred * centred).astype(BF)
    normed = (centred * atom_gain[...]).astype(BF)
    scaling = lax.rsqrt(dot(squares, average) + EPSILON)
    scaling_row = lax.rsqrt(dot_t(average[:SLOTS], squares) + EPSILON)[0:1]
    far_mixed = (
        dot(normed, w_mixed[...]) * jnp.concatenate([scaling] * HEADS, axis=1)
    ).astype(BF)
    far_scores = dot_t(probes[...], normed) * scaling_row
    far_scores = far_scores + jnp.concatenate([far_bias[...]] * HEADS, axis=0)
    most = jnp.maximum(top[...], jnp.max(far_scores, axis=-1, keepdims=True))
    scale = (width // HEADS) ** (-0.5) * LOG2E
    raised = jnp.concatenate(
        [
            jnp.exp2((far_scores - most) * scale).astype(BF),
            jnp.exp2((scores[...] - most) * scale).astype(BF),
        ],
        axis=1,
    )
    ones = jnp.ones((3 * rows, width), BF)
    change = own_float[...]
    for h in range(HEADS):
        part = slice(h * width, (h + 1) * width)
        values = jnp.concatenate([far_mixed[:, part], own_mixed[:, part]], axis=0)
        mixed = dot(raised[h * rows : (h + 1) * rows], jnp.concatenate([values, ones], axis=1))
        change = change + mixed[:, :width] / mixed[:, width:]
    fresh = change.astype(BF)
    updated[...] = fresh
    feature = jnp.maximum(dot(fresh, w_pool[...]), 0.0).astype(BF)
    feature_tiles = jnp.concatenate(
        [feature[:, k * LANES : (k + 1) * LANES] for k in range(tiles)], axis=0
    )
    slot_single = (
        dot(member[...], feature) * jnp.concatenate([slot_scale[...]] * tiles, axis=1)
    ).astype(BF)
    sides = dot_t(slot_single, w_sides[...]).astype(BF)
    backs = dot(slot_single, w_back[...])
    slot_back[...] = backs
    to_before = jnp.sum(backs * before[...], axis=0, keepdims=True)
    to_after = jnp.sum(backs * goes_on[...], axis=0, keepdims=True)
    spot = iota((SLOTS, LANES), 0)
    edges = jnp.where(spot == 0, to_before, jnp.where(spot == 1, to_after, 0.0)).astype(BF)
    spare = jnp.zeros((2 * LANES - tiles * rows - 3 * SLOTS, LANES), BF)
    source = jnp.concatenate(
        [feature_tiles, sides[:, :LANES], sides[:, LANES:], edges, spare], axis=0
    )

    def send_step(at):
        here = span(at, DESTS * BLOCK)
        payload[here, :] = dot(route[here, :], source).astype(BF)

    repeat(devices // DESTS, send_step)


def pair_kernel(
    arrived,
    adder,
    updated,
    slot_back,
    slot_last,
    slot_member,
    pair_state,
    w_outer,
    pair_gain,
    w_gate,
    w_lift,
    w_drop,
    w_sides,
    own_scale,
    atom_out,
    token_single,
    pair_out,
):
    row_tokens, col_tokens, pair_width = pair_state.shape
    own_tokens, channels = token_single.shape
    tiles = channels // LANES
    token_rows = own_tokens * tiles
    opm = math.isqrt(w_outer.shape[0])
    added = dot(adder[...], arrived[...])
    half_gate = w_gate[...] * jnp.asarray(0.5, BF)
    parts, top = [], 0
    for height in (SLOTS,) + (row_tokens,) * 2 + (col_tokens,) * 2 + (row_tokens, col_tokens) * tiles:
        parts.append(added[top : top + height])
        top += height
    sums, left_low, left_high, right_low, right_high, *own = parts
    owned = own_scale[...]
    row_scale = owned[SLOTS : SLOTS + row_tokens]
    col_scale = owned[SLOTS + row_tokens :]
    own_left = jnp.concatenate([part * row_scale for part in own[0::2]], axis=1).astype(BF)
    own_right = jnp.concatenate([part * col_scale for part in own[1::2]], axis=1).astype(BF)
    own_sides = dot_t(jnp.concatenate([own_left, own_right], axis=0), w_sides[:LANES])
    left = left_low[:, :opm] + left_high[:, 2 * opm : 3 * opm] + own_sides[:row_tokens, :opm]
    right = right_low[:, opm : 2 * opm] + right_high[:, 3 * opm : 4 * opm]
    right = right + own_sides[row_tokens:, opm : 2 * opm]
    left, right = left.astype(BF), right.astype(BF)
    depth = GROUP * opm
    unit = flag(iota((opm, depth), 1) % opm == iota((opm, depth), 0))
    corner = jnp.where(iota((GROUP, depth), 1) // opm == iota((GROUP, depth), 0), 1.0, 0.0)

    def spread(rows_of, first, count):
        return jnp.concatenate(
            [
                jnp.broadcast_to(rows_of[k : k + 1, :], (GROUP, depth)) * corner
                for k in range(first, first + count)
            ],
            axis=0,
        ).astype(BF)

    left_wide = dot(left, unit)
    right_blocks = spread(dot(right, unit), 0, col_tokens)
    stages = opm // GROUP
    table = [
        dot(right_blocks, w_outer[g * depth : (g + 1) * depth, :]) for g in range(stages)
    ]
    tables = [
        jnp.concatenate(
            [
                table[g][j * GROUP : (j + 1) * GROUP]
                for j in range(h * GROUP, (h + 1) * GROUP)
                for g in range(stages)
            ],
            axis=0,
        ).astype(BF)
        for h in range(col_tokens // GROUP)
    ]

    def pair_rows(here):
        left_blocks = spread(left_wide, here, PAIR_ROWS)
        terms = [dot(left_blocks, part) for part in tables]
        outer = jnp.concatenate(
            [
                term[i * GROUP : (i + 1) * GROUP]
                for i in range(PAIR_ROWS)
                for term in terms
            ],
            axis=0,
        )
        flat = pair_state[pl.ds(here, PAIR_ROWS)].reshape(PAIR_ROWS * col_tokens, pair_width)
        flat = flat.astype(F32)
        summed = flat + outer[:, :pair_width]
        pair_mean = jnp.mean(flat, axis=-1, keepdims=True)
        centred = summed - (pair_mean + outer[:, pair_width:])
        variance = jnp.mean(centred * centred, axis=-1, keepdims=True)
        scaling = lax.rsqrt(variance + EPSILON)
        normed = (centred * pair_gain[...]).astype(BF)
        gate = dot(normed, half_gate) * scaling
        lift = dot(normed, w_lift[...]) * scaling
        hidden = (gate * lift * (1.0 + jnp.tanh(gate))).astype(BF)
        result = (summed + dot(hidden, w_drop[...])).astype(BF)
        pair_out[pl.ds(here, PAIR_ROWS)] = result.reshape(PAIR_ROWS, col_tokens, pair_width)

    for step in range(row_tokens // PAIR_ROWS):
        here = step * PAIR_ROWS
        pair_rows(here)

    singles = sums * owned[:SLOTS]
    token_single[...] = jnp.concatenate(
        [singles[k * own_tokens : (k + 1) * own_tokens] for k in range(tiles)], axis=1
    ).astype(BF)
    spot = iota((SLOTS, LANES), 0)
    from_before = jnp.where(spot == 0, sums[token_rows : token_rows + 1], 0.0)
    from_after = slot_last[...] * sums[token_rows + 1 : token_rows + 2]
    back = (slot_back[...] + from_before + from_after).astype(BF)
    lifted = lax.dot_general(
        slot_member[...], back, (((0,), (0,)), ((), ())), preferred_element_type=F32
    )
    atom_out[...] = (updated[...].astype(F32) + lifted).astype(BF)


def call(kernel, name, operands, outputs, far=(), scratch=()):
    near_spec = pl.BlockSpec(memory_space=pltpu.VMEM)
    far_spec = pl.BlockSpec(memory_space=pltpu.HBM)
    held = sum(math.prod(a.shape) * a.dtype.itemsize for a in operands + outputs)
    return pl.pallas_call(
        kernel,
        out_shape=outputs,
        in_specs=[far_spec] * len(far) + [near_spec] * len(operands),
        out_specs=(near_spec,) * len(outputs),
        scratch_shapes=scratch,
        compiler_params=pltpu.CompilerParams(vmem_limit_bytes=min(2 * held + SPARE, MOST)),
        name=name,
    )(*[pltpu.with_memory_space_constraint(a, pltpu.HBM) for a in far], *operands)


def per_device(
    atom_feats,
    key_starts,
    atom_counts,
    atom_gain,
    w_query,
    w_key,
    w_value,
    w_out,
    w_pool,
    w_back,
    pair_state,
    w_left,
    w_right,
    w_outer,
    pair_gain,
    w_gate,
    w_lift,
    w_drop,
):
    rows, width = atom_feats.shape
    devices = lax.axis_size(AXES)
    tokens = atom_counts.shape[0]
    channels = w_pool.shape[1]
    opm = w_left.shape[1]
    own_tokens = tokens // devices
    row_tokens, col_tokens, _ = pair_state.shape
    tiles = channels // LANES
    opm = w_left.shape[1]
    across = [(i, i + 1) for i in range(1, devices - 1, 2)]
    neighbour = lax.ppermute(atom_feats, AXES, across + [(j, i) for i, j in across])
    sibling = lax.ppermute(atom_feats, AXES, [(i, i ^ 1) for i in range(devices)])

    def held(*shape, dtype=F32):
        return jax.ShapeDtypeStruct(shape, dtype)

    counts_folded = atom_counts.reshape(-1, LANES)
    ready = call(
        ready_kernel,
        "ready",
        (),
        (
            held(rows, width),
            held(rows, HEADS * width, dtype=BF),
            held(HEADS * rows, width, dtype=BF),
            held(HEADS * rows, rows),
            held(HEADS * rows, 1),
            held(rows, 2 * rows),
            held(devices * BLOCK, 2 * LANES, dtype=BF),
            held(SLOTS, rows, dtype=BF),
            held(SLOTS, LANES),
            held(SLOTS, LANES),
            held(SLOTS, LANES),
            held(SLOTS, LANES),
            held(
                SLOTS + (2 + tiles) * (row_tokens + col_tokens), devices * BLOCK, dtype=BF
            ),
            held(SLOTS + row_tokens + col_tokens, LANES),
            held(1, width),
            held(1, LANES),
            held(width, HEADS * width, dtype=BF),
            held(width, channels, dtype=BF),
            held(channels, width, dtype=BF),
            held(2 * LANES, channels, dtype=BF),
            held(opm * opm, 2 * w_outer.shape[-1], dtype=BF),
        ),
        far=(
            atom_feats,
            key_starts[None],
            atom_counts[None],
            counts_folded,
            atom_gain[None],
            pair_gain[None],
            w_query,
            w_key,
            w_value,
            w_out,
            w_pool,
            w_back,
            w_left.T,
            w_right.T,
            w_outer.reshape(opm * opm, -1),
        ),
        scratch=(
            pltpu.VMEM((rows, width), BF),
            pltpu.VMEM((1, key_starts.shape[0]), jnp.int32),
            pltpu.VMEM((1, tokens), jnp.int32),
            pltpu.VMEM(counts_folded.shape, jnp.int32),
            pltpu.VMEM((width, width), BF),
            pltpu.VMEM((width, width), BF),
            pltpu.VMEM((width, width), BF),
            pltpu.VMEM((width, width), BF),
            pltpu.VMEM((tokens, LANES), F32),
            pltpu.VMEM((tokens, LANES), F32),
            pltpu.SemaphoreType.DMA((17,)),
        ),
    )
    (
        own_float,
        own_mixed,
        probes,
        scores,
        top,
        far_bias,
        route,
        member,
        slot_scale,
        before,
        goes_on,
        last,
        adder,
        own_scale,
        atom_gain_kept,
        pair_gain_kept,
        *kept,
        w_outer_kept,
    ) = ready
    payload, updated, slot_back = call(
        atom_kernel,
        "atoms",
        (
            neighbour,
            sibling,
            own_float,
            own_mixed,
            probes,
            scores,
            top,
            far_bias,
            route,
            member,
            slot_scale,
            before,
            goes_on,
            atom_gain_kept,
            *kept,
        ),
        (
            held(devices * BLOCK, LANES, dtype=BF),
            held(rows, width, dtype=BF),
            held(SLOTS, width),
        ),
    )
    arrived = lax.all_to_all(payload.reshape(devices, BLOCK, LANES), AXES, 0, 0)
    return call(
        pair_kernel,
        "pairs",
        (
            arrived.reshape(devices * BLOCK, LANES),
            adder,
            updated,
            slot_back,
            last,
            member,
            pair_state,
            w_outer_kept,
            pair_gain_kept,
            w_gate,
            w_lift,
            w_drop,
            kept[-1],
            own_scale,
        ),
        (
            held(rows, width, dtype=BF),
            held(own_tokens, channels, dtype=BF),
            held(*pair_state.shape, dtype=BF),
        ),
    )


def solution(mesh):
    in_specs = (
        P(("row", "col"), None),
        P(("row", "col")),
        P(),
        P(),
        P(),
        P(),
        P(),
        P(),
        P(),
        P(),
        P("row", "col", None),
        P(),
        P(),
        P(),
        P(),
        P(),
        P(),
        P(),
    )
    out_specs = (P(("row", "col"), None), P(("row", "col"), None), P("row", "col", None))
    return jax.shard_map(
        per_device, mesh=mesh, in_specs=in_specs, out_specs=out_specs, check_vma=False
    )
```

```python
import math

import jax
import jax.numpy as jnp
from jax import lax
from jax.experimental import pallas as pl
from jax.experimental.pallas import tpu as pltpu
from jax.sharding import PartitionSpec as P

HEADS = 4
QB = 32
KW = 128
EPSILON = 1e-05
HALF = KW // 2
FEWEST = 8
LANES = 128
SLOTS = 16
BLOCK = 16
SLOT_ROW = 12
DESTS = 32
PAIR_ROWS = 16
GROUP = 8
MASKED = -1e30
SPARE = 12 << 20
MOST = 60 << 20
LOG2E = 1.4426950408889634
AXES = ("row", "col")
BF = jnp.bfloat16
F32 = jnp.float32


def dot(a, b):
    return jnp.dot(a, b, preferred_element_type=F32)


def dot_t(a, b):
    return lax.dot_general(a, b, (((1,), (1,)), ((), ())), preferred_element_type=F32)


def iota(shape, axis):
    return lax.broadcasted_iota(jnp.int32, shape, axis)


def centred_rows(values, gain):
    width = values.shape[1]
    average = jnp.full((width, width), 1.0 / width, F32).astype(BF)
    centred = values.astype(F32) - dot(values, average)
    variance = dot((centred * centred).astype(BF), average)
    return (centred * gain).astype(BF), lax.rsqrt(variance + EPSILON)


def flag(mask):
    return jnp.where(mask, 1.0, 0.0).astype(BF)


def place():
    return lax.axis_index("row") * lax.axis_size("col") + lax.axis_index("col")


def overlap(base, first_own, own_tokens, slots):
    inner = jnp.minimum(first_own + own_tokens, base + slots) - jnp.maximum(first_own, base)
    return jnp.maximum(inner, 0)


def edge_row(base, first_own, own_tokens, slots):
    last_own = first_own + own_tokens - 1
    last_held = (last_own >= base) & (last_own < base + slots)
    free = jnp.where(last_held, 0, own_tokens - 1)
    whole = overlap(base, first_own, own_tokens, slots) == own_tokens
    return jnp.where(whole, BLOCK - 1, free)


def repeat(count, step):
    if count <= 8:
        for at in range(count):
            step(at)
    else:

        def body(at, carry):
            step(at)
            return carry

        lax.fori_loop(0, count, body, 0)


def span(at, size):
    if isinstance(at, int):
        return pl.ds(at * size, size)
    return pl.ds(pl.multiple_of(at * size, size), size)


def ready_kernel(
    own_far,
    starts_far,
    counts_far,
    folded_far,
    atom_gain_far,
    pair_gain_far,
    w_query_far,
    w_key_far,
    w_value_far,
    w_out_far,
    w_pool_far,
    w_back_far,
    w_left_far,
    w_right_far,
    w_outer_far,
    own_float,
    own_mixed,
    probes,
    scores,
    top,
    far_bias,
    route,
    member,
    slot_scale,
    before,
    goes_on,
    last,
    adder,
    own_scale,
    atom_gain,
    pair_gain,
    w_mixed,
    w_pool,
    w_back,
    w_sides,
    w_outer,
    own,
    key_starts,
    counts,
    counts_folded,
    w_query,
    w_key,
    w_value,
    w_out,
    begins,
    ends,
    arrivals,
):
    rows, width = own.shape
    tokens = counts.shape[1]
    opm = w_left_far.shape[0]
    pairs = (
        (counts_far, counts),
        (folded_far, counts_folded),
        (own_far, own),
        (starts_far, key_starts),
        (atom_gain_far, atom_gain),
        (w_query_far, w_query),
        (w_key_far, w_key),
        (w_value_far, w_value),
        (w_out_far, w_out),
        (pair_gain_far, pair_gain),
        (w_pool_far, w_pool),
        (w_back_far, w_back),
        (w_left_far, w_sides.at[:opm]),
        (w_right_far, w_sides.at[opm : 2 * opm]),
        (w_left_far, w_sides.at[2 * LANES - 2 * opm : 2 * LANES - opm]),
        (w_right_far, w_sides.at[2 * LANES - opm :]),
        (w_outer_far, w_outer.at[:, : w_outer_far.shape[1]]),
    )
    copies = [pltpu.make_async_copy(a, b, arrivals.at[k]) for k, (a, b) in enumerate(pairs)]
    for copy in copies:
        copy.start()

    tiles = w_pool.shape[1] // LANES
    devices = route.shape[0] // BLOCK
    atoms = rows * devices
    own_tokens = tokens // devices
    token_rows = own_tokens * tiles
    slots = rows // FEWEST + 1
    position = place()
    first = position * rows
    even = position % 2 == 0
    first_float = first.astype(F32)
    w_sides[2 * opm : 2 * LANES - 2 * opm, :] = jnp.zeros(
        (2 * LANES - 4 * opm, tiles * LANES), BF
    )

    for copy in copies[:9]:
        copy.wait()
    counts_lane = jnp.broadcast_to(counts[...].astype(F32), (LANES, tokens)).astype(BF)
    folded = counts_folded[...].astype(F32).astype(BF)
    upper = flag(iota((LANES, LANES), 0) <= iota((LANES, LANES), 1))
    lower = flag(iota((LANES, LANES), 1) <= iota((LANES, LANES), 0))
    below = flag(iota((LANES, LANES), 1) < iota((LANES, LANES), 0))
    within = dot(folded, upper)
    whole = dot(folded, jnp.ones((LANES, LANES), BF))
    base = jnp.zeros((1, 1), F32)
    passed = jnp.zeros((1, LANES), F32)
    for fold in range(folded.shape[0]):
        ended = within[fold : fold + 1] + passed <= first_float
        base = base + jnp.sum(jnp.where(ended, 1.0, 0.0), axis=1, keepdims=True)
        part = slice(fold * LANES, (fold + 1) * LANES)
        ends[part, :] = passed + dot_t(lower, counts_lane[:, part])
        begins[part, :] = passed + dot_t(below, counts_lane[:, part])
        passed = passed + whole[fold : fold + 1]

    base_token = base.astype(jnp.int32)
    token_lane = iota((SLOTS, tokens), 1).astype(F32)
    slot_token = iota((SLOTS, tokens), 0).astype(F32) + base
    slot_end = dot_t(flag(token_lane <= slot_token), counts_lane)
    slot_start = dot_t(flag(token_lane < slot_token), counts_lane)
    atom_lane = iota((SLOTS, rows), 1).astype(F32) + first_float
    member[...] = flag((atom_lane >= slot_start[:, :rows]) & (atom_lane < slot_end[:, :rows]))
    slot_scale[...] = 1.0 / jnp.maximum(slot_end - slot_start, 1.0)
    last_atom = first_float + (rows - 1)
    is_last = jnp.where((slot_start <= last_atom) & (slot_end > last_atom), 1.0, 0.0)
    last[...] = is_last
    goes_on[...] = is_last * jnp.where(slot_end > first_float + rows, 1.0, 0.0)
    is_first = iota((SLOTS, LANES), 0) == 0
    before[...] = jnp.where(is_first & (slot_start < first_float), 1.0, 0.0)

    lanes = 2 * LANES
    lane = iota((1, lanes), 1)
    atom = (lane % rows + first).astype(F32)
    inside = (atom >= jnp.concatenate([begins[...]] * 2, axis=1)) & (lane < tiles * rows)
    inside = flag(inside & (atom < jnp.concatenate([ends[...]] * 2, axis=1)))
    tile_fits = iota((BLOCK, lanes), 0) // own_tokens == iota((BLOCK, lanes), 1) // rows
    tile_fits = jnp.where(tile_fits, 1.0, 0.0)
    column = iota((1, LANES), 1) - (tiles * rows - LANES)
    kind, slot = column // SLOTS, column % SLOTS
    token = base_token + slot

    def rows_step(at):
        here = span(at, DESTS * BLOCK)
        dest = iota((DESTS, BLOCK, tokens), 0).reshape(DESTS * BLOCK, tokens) + at * DESTS
        turn = iota((DESTS, BLOCK, tokens), 1).reshape(DESTS * BLOCK, tokens) % own_tokens
        picks = dot(flag(iota((1, tokens), 1) == dest * own_tokens + turn), inside)
        picks = picks.reshape(DESTS, BLOCK, lanes) * tile_fits[None]
        picks = picks.reshape(DESTS * BLOCK, lanes)
        dest = iota((DESTS, LANES), 0) + at * DESTS
        first_own = dest * own_tokens
        shared_tokens = overlap(base_token, first_own, own_tokens, slots)
        index = jnp.where(token < first_own, slot, slot - shared_tokens)
        mine = (token >= first_own) & (token < first_own + own_tokens)
        room = 2 * (BLOCK - SLOT_ROW)
        target = jnp.where(index < room, SLOT_ROW + index // 2, jnp.where(kind == 0, 0, -1))
        fits = (index % 2 == kind) & (slot < slots) & jnp.logical_not(mine) & (column >= 0)
        target = jnp.where(fits & (kind < 2), target, -1)
        beside = jnp.where(slot == 0, position - 1, position + 1)
        is_edge = (kind == 2) & (slot < 2) & (dest == beside)
        row = edge_row(base_token, first_own, own_tokens, slots)
        target = jnp.where(is_edge, row, target)
        spot = iota((BLOCK, LANES), 0)
        selects = [
            jnp.where(jnp.broadcast_to(target[d : d + 1], (BLOCK, LANES)) == spot, 1.0, 0.0)
            for d in range(DESTS)
        ]
        high = picks[:, LANES:] + jnp.concatenate(selects, axis=0)
        route[here, :] = jnp.concatenate([picks[:, :LANES], high], axis=1).astype(BF)

    repeat(devices // DESTS, rows_step)

    row_tokens = tokens // lax.axis_size("row")
    col_tokens = tokens // lax.axis_size("col")
    first_row = lax.axis_index("row") * row_tokens
    first_col = lax.axis_index("col") * col_tokens

    def row_counts(height, first_token, cycle):
        token_row = iota((height, tokens), 0) % cycle + first_token
        return dot_t(flag(iota((1, tokens), 1) == token_row), counts_lane)

    owned = [
        row_counts(SLOTS, position * own_tokens, own_tokens),
        row_counts(row_tokens, first_row, row_tokens),
        row_counts(col_tokens, first_col, col_tokens),
    ]
    own_scale[...] = 1.0 / jnp.concatenate(owned, axis=0)

    def adder_step(at):
        here = span(at, LANES)
        spot_lane = iota((1, LANES), 1) + at * LANES
        block = spot_lane // BLOCK
        spot = spot_lane % BLOCK
        edge = (block * rows).astype(F32)
        tally = jnp.zeros((1, LANES), F32)
        for fold in range(tokens // LANES):
            ended = jnp.where(ends[fold * LANES : (fold + 1) * LANES, :] <= edge, 1.0, 0.0)
            tally = tally + jnp.sum(ended, axis=0, keepdims=True)
        start = tally.astype(jnp.int32)
        first_own = position * own_tokens
        shared_tokens = overlap(start, first_own, own_tokens, slots)

        def token_of(index):
            slot = jnp.where(start + index < first_own, index, index + shared_tokens)
            return jnp.where((index >= 0) & (slot < slots), start + slot, -1)

        in_slots = spot >= SLOT_ROW
        room = 2 * (BLOCK - SLOT_ROW)
        ninth = jnp.where((spot == 0) & (shared_tokens == 0), start + room, -1)
        low_token = jnp.where(in_slots, token_of(2 * (spot - SLOT_ROW)), ninth)
        high_token = jnp.where(in_slots, token_of(2 * (spot - SLOT_ROW) + 1), -1)
        own_token = first_own + spot % own_tokens
        held = (spot < token_rows) & (own_token >= start) & (own_token < start + slots)
        own_token = jnp.where(held, own_token, -1)
        line = iota((SLOTS, LANES), 0)
        side = jnp.where(line == token_rows, position - 1, position + 1)
        on_edge = spot == edge_row(start, first_own, own_tokens, slots)
        is_edge = (line >= token_rows) & (line < token_rows + 2) & on_edge & (block == side)
        lines = [(line < token_rows) & (spot == line) & held | is_edge]
        row_line = iota((row_tokens, LANES), 0) + first_row
        col_line = iota((col_tokens, LANES), 0) + first_col
        for wanted in (row_line, col_line):
            lines += [low_token == wanted, high_token == wanted]
        for tile in range(tiles):
            tile_token = jnp.where(spot // own_tokens == tile, own_token, -1)
            lines += [tile_token == row_line, tile_token == col_line]
        top = 0
        for part in lines:
            adder[top : top + part.shape[0], here] = flag(part)
            top += part.shape[0]

    repeat(devices * BLOCK // LANES, adder_step)

    own_float[...] = own[...].astype(F32)
    normed, scaling = centred_rows(own[...], atom_gain[...])
    near = (dot(normed, w_key[...]) * scaling).astype(BF)
    query = (dot(normed, w_query[...]) * scaling).astype(BF)
    head_of = iota((1, width), 1) // (width // HEADS)
    head_mask = [flag(head_of == h) for h in range(HEADS)]
    heads = jnp.concatenate([query * m for m in head_mask], axis=0)
    probes[...] = dot_t(heads, w_key[...]).astype(BF)
    w_mix = jnp.concatenate(
        [dot(w_value[...] * m, w_out[...]).astype(BF) for m in head_mask], axis=1
    )
    w_mixed[...] = w_mix
    own_mixed[...] = (
        dot(normed, w_mix) * jnp.concatenate([scaling] * HEADS, axis=1)
    ).astype(BF)
    near_index = first + iota((1, rows), 1)
    far_lane = iota((1, 2 * rows), 1)
    is_low = (far_lane < rows) != even
    far_index = first + far_lane % rows + jnp.where(is_low, -rows, rows)
    near_bias, bias = [], []
    for e in range(rows // QB):
        low = key_starts[0:1, e : e + 1]
        seen = (near_index >= low) & (near_index < low + KW)
        near_bias.append(jnp.broadcast_to(jnp.where(seen, 0.0, MASKED), (QB, rows)))
        seen = (far_index >= low) & (far_index < low + KW)
        seen = seen & (far_index >= 0) & (far_index < atoms)
        bias.append(jnp.broadcast_to(jnp.where(seen, 0.0, MASKED), (QB, 2 * rows)))
    far_bias[...] = jnp.concatenate(bias, axis=0)
    raw_scores = dot_t(heads, near) + jnp.concatenate(near_bias * HEADS, axis=0)
    scores[...] = raw_scores
    top[...] = jnp.max(raw_scores, axis=-1, keepdims=True)
    for copy in copies[9:]:
        copy.wait()
    pair_width = w_outer_far.shape[1]
    average = jnp.full((pair_width, pair_width), 1.0 / pair_width, F32).astype(BF)
    w_outer[:, pair_width:] = dot(w_outer[:, :pair_width], average).astype(BF)


def atom_kernel(
    neighbour,
    sibling,
    own_float,
    own_mixed,
    probes,
    scores,
    top,
    far_bias,
    route,
    member,
    slot_scale,
    before,
    goes_on,
    atom_gain,
    w_mixed,
    w_pool,
    w_back,
    w_sides,
    payload,
    updated,
    slot_back,
):
    rows, width = own_float.shape
    tiles = w_pool.shape[1] // LANES
    devices = payload.shape[0] // BLOCK
    raw = jnp.concatenate([sibling[...], neighbour[...]], axis=0)
    average = jnp.full((width, width), 1.0 / width, F32).astype(BF)
    centred = raw.astype(F32) - dot(raw, average)
    squares = (centred * centred).astype(BF)
    normed = (centred * atom_gain[...]).astype(BF)
    scaling = lax.rsqrt(dot(squares, average) + EPSILON)
    scaling_row = lax.rsqrt(dot_t(average[:SLOTS], squares) + EPSILON)[0:1]
    far_mixed = (
        dot(normed, w_mixed[...]) * jnp.concatenate([scaling] * HEADS, axis=1)
    ).astype(BF)
    far_scores = dot_t(probes[...], normed) * scaling_row
    far_scores = far_scores + jnp.concatenate([far_bias[...]] * HEADS, axis=0)
    most = jnp.maximum(top[...], jnp.max(far_scores, axis=-1, keepdims=True))
    scale = (width // HEADS) ** (-0.5) * LOG2E
    raised = jnp.concatenate(
        [
            jnp.exp2((far_scores - most) * scale).astype(BF),
            jnp.exp2((scores[...] - most) * scale).astype(BF),
        ],
        axis=1,
    )
    ones = jnp.ones((3 * rows, width), BF)
    change = own_float[...]
    for h in range(HEADS):
        part = slice(h * width, (h + 1) * width)
        values = jnp.concatenate([far_mixed[:, part], own_mixed[:, part]], axis=0)
        mixed = dot(raised[h * rows : (h + 1) * rows], jnp.concatenate([values, ones], axis=1))
        change = change + mixed[:, :width] / mixed[:, width:]
    fresh = change.astype(BF)
    updated[...] = fresh
    feature = jnp.maximum(dot(fresh, w_pool[...]), 0.0).astype(BF)
    feature_tiles = jnp.concatenate(
        [feature[:, k * LANES : (k + 1) * LANES] for k in range(tiles)], axis=0
    )
    slot_single = (
        dot(member[...], feature) * jnp.concatenate([slot_scale[...]] * tiles, axis=1)
    ).astype(BF)
    sides = dot_t(slot_single, w_sides[...]).astype(BF)
    backs = dot(slot_single, w_back[...])
    slot_back[...] = backs
    to_before = jnp.sum(backs * before[...], axis=0, keepdims=True)
    to_after = jnp.sum(backs * goes_on[...], axis=0, keepdims=True)
    spot = iota((SLOTS, LANES), 0)
    edges = jnp.where(spot == 0, to_before, jnp.where(spot == 1, to_after, 0.0)).astype(BF)
    spare = jnp.zeros((2 * LANES - tiles * rows - 3 * SLOTS, LANES), BF)
    source = jnp.concatenate(
        [feature_tiles, sides[:, :LANES], sides[:, LANES:], edges, spare], axis=0
    )

    def send_step(at):
        here = span(at, DESTS * BLOCK)
        payload[here, :] = dot(route[here, :], source).astype(BF)

    repeat(devices // DESTS, send_step)


def pair_kernel(
    arrived,
    adder,
    updated,
    slot_back,
    slot_last,
    slot_member,
    pair_state,
    w_outer,
    pair_gain,
    w_gate,
    w_lift,
    w_drop,
    w_sides,
    own_scale,
    atom_out,
    token_single,
    pair_out,
):
    row_tokens, col_tokens, pair_width = pair_state.shape
    own_tokens, channels = token_single.shape
    tiles = channels // LANES
    token_rows = own_tokens * tiles
    opm = math.isqrt(w_outer.shape[0])
    added = dot(adder[...], arrived[...])
    half_gate = w_gate[...] * jnp.asarray(0.5, BF)
    parts, top = [], 0
    for height in (SLOTS,) + (row_tokens,) * 2 + (col_tokens,) * 2 + (row_tokens, col_tokens) * tiles:
        parts.append(added[top : top + height])
        top += height
    sums, left_low, left_high, right_low, right_high, *own = parts
    owned = own_scale[...]
    row_scale = owned[SLOTS : SLOTS + row_tokens]
    col_scale = owned[SLOTS + row_tokens :]
    own_left = jnp.concatenate([part * row_scale for part in own[0::2]], axis=1).astype(BF)
    own_right = jnp.concatenate([part * col_scale for part in own[1::2]], axis=1).astype(BF)
    own_sides = dot_t(jnp.concatenate([own_left, own_right], axis=0), w_sides[:LANES])
    left = left_low[:, :opm] + left_high[:, 2 * opm : 3 * opm] + own_sides[:row_tokens, :opm]
    right = right_low[:, opm : 2 * opm] + right_high[:, 3 * opm : 4 * opm]
    right = right + own_sides[row_tokens:, opm : 2 * opm]
    depth = GROUP * opm
    corner = jnp.where(iota((GROUP, depth), 1) // opm == iota((GROUP, depth), 0), 1.0, 0.0)

    def spread(rows_of, first, count):
        return jnp.concatenate(
            [
                jnp.broadcast_to(rows_of[k : k + 1, :], (GROUP, depth)) * corner
                for k in range(first, first + count)
            ],
            axis=0,
        ).astype(BF)

    left_wide = jnp.concatenate([left] * GROUP, axis=1)
    right_blocks = spread(jnp.concatenate([right] * GROUP, axis=1), 0, col_tokens)
    stages = opm // GROUP
    table = [
        dot(right_blocks, w_outer[g * depth : (g + 1) * depth, :]) for g in range(stages)
    ]
    tables = [
        jnp.concatenate(
            [
                table[g][j * GROUP : (j + 1) * GROUP]
                for j in range(h * GROUP, (h + 1) * GROUP)
                for g in range(stages)
            ],
            axis=0,
        ).astype(BF)
        for h in range(col_tokens // GROUP)
    ]

    def pair_rows(here):
        left_blocks = spread(left_wide, here, PAIR_ROWS)
        terms = [dot(left_blocks, part) for part in tables]
        outer = jnp.concatenate(
            [
                term[i * GROUP : (i + 1) * GROUP]
                for i in range(PAIR_ROWS)
                for term in terms
            ],
            axis=0,
        )
        flat = pair_state[pl.ds(here, PAIR_ROWS)].reshape(PAIR_ROWS * col_tokens, pair_width)
        flat = flat.astype(F32)
        summed = flat + outer[:, :pair_width]
        pair_mean = jnp.mean(flat, axis=-1, keepdims=True)
        centred = summed - (pair_mean + outer[:, pair_width:])
        variance = jnp.mean(centred * centred, axis=-1, keepdims=True)
        scaling = lax.rsqrt(variance + EPSILON)
        normed = (centred * pair_gain[...]).astype(BF)
        gate = dot(normed, half_gate) * scaling
        lift = dot(normed, w_lift[...])
        hidden = (gate * lift * (1.0 + jnp.tanh(gate))).astype(BF)
        result = (summed + dot(hidden, w_drop[...]) * scaling).astype(BF)
        pair_out[pl.ds(here, PAIR_ROWS)] = result.reshape(PAIR_ROWS, col_tokens, pair_width)

    for step in range(row_tokens // PAIR_ROWS):
        here = step * PAIR_ROWS
        pair_rows(here)

    singles = sums * owned[:SLOTS]
    token_single[...] = jnp.concatenate(
        [singles[k * own_tokens : (k + 1) * own_tokens] for k in range(tiles)], axis=1
    ).astype(BF)
    spot = iota((SLOTS, LANES), 0)
    from_before = jnp.where(spot == 0, sums[token_rows : token_rows + 1], 0.0)
    from_after = slot_last[...] * sums[token_rows + 1 : token_rows + 2]
    back = (slot_back[...] + from_before + from_after).astype(BF)
    lifted = lax.dot_general(
        slot_member[...], back, (((0,), (0,)), ((), ())), preferred_element_type=F32
    )
    atom_out[...] = (updated[...].astype(F32) + lifted).astype(BF)


def call(kernel, name, operands, outputs, far=(), scratch=()):
    near_spec = pl.BlockSpec(memory_space=pltpu.VMEM)
    far_spec = pl.BlockSpec(memory_space=pltpu.HBM)
    held = sum(math.prod(a.shape) * a.dtype.itemsize for a in operands + outputs)
    return pl.pallas_call(
        kernel,
        out_shape=outputs,
        in_specs=[far_spec] * len(far) + [near_spec] * len(operands),
        out_specs=(near_spec,) * len(outputs),
        scratch_shapes=scratch,
        compiler_params=pltpu.CompilerParams(vmem_limit_bytes=min(2 * held + SPARE, MOST)),
        name=name,
    )(*[pltpu.with_memory_space_constraint(a, pltpu.HBM) for a in far], *operands)


def per_device(
    atom_feats,
    key_starts,
    atom_counts,
    atom_gain,
    w_query,
    w_key,
    w_value,
    w_out,
    w_pool,
    w_back,
    pair_state,
    w_left,
    w_right,
    w_outer,
    pair_gain,
    w_gate,
    w_lift,
    w_drop,
):
    rows, width = atom_feats.shape
    devices = lax.axis_size(AXES)
    tokens = atom_counts.shape[0]
    channels = w_pool.shape[1]
    opm = w_left.shape[1]
    own_tokens = tokens // devices
    row_tokens, col_tokens, _ = pair_state.shape
    tiles = channels // LANES
    opm = w_left.shape[1]
    across = [(i, i + 1) for i in range(1, devices - 1, 2)]
    neighbour = lax.ppermute(atom_feats, AXES, across + [(j, i) for i, j in across])
    sibling = lax.ppermute(atom_feats, AXES, [(i, i ^ 1) for i in range(devices)])

    def held(*shape, dtype=F32):
        return jax.ShapeDtypeStruct(shape, dtype)

    counts_folded = atom_counts.reshape(-1, LANES)
    ready = call(
        ready_kernel,
        "ready",
        (),
        (
            held(rows, width),
            held(rows, HEADS * width, dtype=BF),
            held(HEADS * rows, width, dtype=BF),
            held(HEADS * rows, rows),
            held(HEADS * rows, 1),
            held(rows, 2 * rows),
            held(devices * BLOCK, 2 * LANES, dtype=BF),
            held(SLOTS, rows, dtype=BF),
            held(SLOTS, LANES),
            held(SLOTS, LANES),
            held(SLOTS, LANES),
            held(SLOTS, LANES),
            held(
                SLOTS + (2 + tiles) * (row_tokens + col_tokens), devices * BLOCK, dtype=BF
            ),
            held(SLOTS + row_tokens + col_tokens, LANES),
            held(1, width),
            held(1, LANES),
            held(width, HEADS * width, dtype=BF),
            held(width, channels, dtype=BF),
            held(channels, width, dtype=BF),
            held(2 * LANES, channels, dtype=BF),
            held(opm * opm, 2 * w_outer.shape[-1], dtype=BF),
        ),
        far=(
            atom_feats,
            key_starts[None],
            atom_counts[None],
            counts_folded,
            atom_gain[None],
            pair_gain[None],
            w_query,
            w_key,
            w_value,
            w_out,
            w_pool,
            w_back,
            w_left.T,
            w_right.T,
            w_outer.reshape(opm * opm, -1),
        ),
        scratch=(
            pltpu.VMEM((rows, width), BF),
            pltpu.VMEM((1, key_starts.shape[0]), jnp.int32),
            pltpu.VMEM((1, tokens), jnp.int32),
            pltpu.VMEM(counts_folded.shape, jnp.int32),
            pltpu.VMEM((width, width), BF),
            pltpu.VMEM((width, width), BF),
            pltpu.VMEM((width, width), BF),
            pltpu.VMEM((width, width), BF),
            pltpu.VMEM((tokens, LANES), F32),
            pltpu.VMEM((tokens, LANES), F32),
            pltpu.SemaphoreType.DMA((17,)),
        ),
    )
    (
        own_float,
        own_mixed,
        probes,
        scores,
        top,
        far_bias,
        route,
        member,
        slot_scale,
        before,
        goes_on,
        last,
        adder,
        own_scale,
        atom_gain_kept,
        pair_gain_kept,
        *kept,
        w_outer_kept,
    ) = ready
    payload, updated, slot_back = call(
        atom_kernel,
        "atoms",
        (
            neighbour,
            sibling,
            own_float,
            own_mixed,
            probes,
            scores,
            top,
            far_bias,
            route,
            member,
            slot_scale,
            before,
            goes_on,
            atom_gain_kept,
            *kept,
        ),
        (
            held(devices * BLOCK, LANES, dtype=BF),
            held(rows, width, dtype=BF),
            held(SLOTS, width),
        ),
    )
    arrived = lax.all_to_all(payload.reshape(devices, BLOCK, LANES), AXES, 0, 0)
    return call(
        pair_kernel,
        "pairs",
        (
            arrived.reshape(devices * BLOCK, LANES),
            adder,
            updated,
            slot_back,
            last,
            member,
            pair_state,
            w_outer_kept,
            pair_gain_kept,
            w_gate,
            w_lift,
            w_drop,
            kept[-1],
            own_scale,
        ),
        (
            held(rows, width, dtype=BF),
            held(own_tokens, channels, dtype=BF),
            held(*pair_state.shape, dtype=BF),
        ),
    )


def solution(mesh):
    in_specs = (
        P(("row", "col"), None),
        P(("row", "col")),
        P(),
        P(),
        P(),
        P(),
        P(),
        P(),
        P(),
        P(),
        P("row", "col", None),
        P(),
        P(),
        P(),
        P(),
        P(),
        P(),
        P(),
    )
    out_specs = (P(("row", "col"), None), P(("row", "col"), None), P("row", "col", None))
    return jax.shard_map(
        per_device, mesh=mesh, in_specs=in_specs, out_specs=out_specs, check_vma=False
    )
```

```python
import math

import jax
import jax.numpy as jnp
from jax import lax
from jax.experimental import pallas as pl
from jax.experimental.pallas import tpu as pltpu
from jax.sharding import PartitionSpec as P

HEADS = 4
QB = 32
KW = 128
EPSILON = 1e-05
HALF = KW // 2
FEWEST = 8
LANES = 128
SLOTS = 16
BLOCK = 16
SLOT_ROW = 12
DESTS = 32
PAIR_ROWS = 16
GROUP = 8
MASKED = -1e30
SPARE = 12 << 20
MOST = 60 << 20
LOG2E = 1.4426950408889634
AXES = ("row", "col")
BF = jnp.bfloat16
F32 = jnp.float32


def dot(a, b):
    return jnp.dot(a, b, preferred_element_type=F32)


def dot_t(a, b):
    return lax.dot_general(a, b, (((1,), (1,)), ((), ())), preferred_element_type=F32)


def iota(shape, axis):
    return lax.broadcasted_iota(jnp.int32, shape, axis)


def centred_rows(values, gain):
    width = values.shape[1]
    average = jnp.full((width, width), 1.0 / width, F32).astype(BF)
    centred = values.astype(F32) - dot(values, average)
    variance = dot((centred * centred).astype(BF), average)
    return (centred * gain).astype(BF), lax.rsqrt(variance + EPSILON)


def flag(mask):
    return jnp.where(mask, 1.0, 0.0).astype(BF)


def place():
    return lax.axis_index("row") * lax.axis_size("col") + lax.axis_index("col")


def overlap(base, first_own, own_tokens, slots):
    inner = jnp.minimum(first_own + own_tokens, base + slots) - jnp.maximum(first_own, base)
    return jnp.maximum(inner, 0)


def edge_row(base, first_own, own_tokens, slots):
    last_own = first_own + own_tokens - 1
    last_held = (last_own >= base) & (last_own < base + slots)
    free = jnp.where(last_held, 0, own_tokens - 1)
    whole = overlap(base, first_own, own_tokens, slots) == own_tokens
    return jnp.where(whole, BLOCK - 1, free)


def repeat(count, step):
    if count <= 8:
        for at in range(count):
            step(at)
    else:

        def body(at, carry):
            step(at)
            return carry

        lax.fori_loop(0, count, body, 0)


def span(at, size):
    if isinstance(at, int):
        return pl.ds(at * size, size)
    return pl.ds(pl.multiple_of(at * size, size), size)


def ready_kernel(
    own_far,
    starts_far,
    counts_far,
    folded_far,
    atom_gain_far,
    pair_gain_far,
    w_query_far,
    w_key_far,
    w_value_far,
    w_out_far,
    w_pool_far,
    w_back_far,
    w_left_far,
    w_right_far,
    w_outer_far,
    own_float,
    own_mixed,
    probes,
    scores,
    top,
    far_bias,
    route,
    slot_route,
    member,
    slot_scale,
    last,
    adder,
    own_scale,
    atom_gain,
    pair_gain,
    w_mixed,
    w_pool,
    w_back,
    w_sides,
    w_outer,
    own,
    key_starts,
    counts,
    counts_folded,
    w_query,
    w_key,
    w_value,
    w_out,
    begins,
    ends,
    arrivals,
):
    rows, width = own.shape
    tokens = counts.shape[1]
    opm = w_left_far.shape[0]
    pairs = (
        (counts_far, counts),
        (folded_far, counts_folded),
        (own_far, own),
        (starts_far, key_starts),
        (atom_gain_far, atom_gain),
        (w_query_far, w_query),
        (w_key_far, w_key),
        (w_value_far, w_value),
        (w_out_far, w_out),
        (pair_gain_far, pair_gain),
        (w_pool_far, w_pool),
        (w_back_far, w_back),
        (w_left_far, w_sides.at[:opm]),
        (w_right_far, w_sides.at[opm : 2 * opm]),
        (w_left_far, w_sides.at[2 * LANES - 2 * opm : 2 * LANES - opm]),
        (w_right_far, w_sides.at[2 * LANES - opm :]),
        (w_outer_far, w_outer.at[:, : w_outer_far.shape[1]]),
    )
    copies = [pltpu.make_async_copy(a, b, arrivals.at[k]) for k, (a, b) in enumerate(pairs)]
    for copy in copies:
        copy.start()

    tiles = w_pool.shape[1] // LANES
    devices = route.shape[0] // BLOCK
    atoms = rows * devices
    own_tokens = tokens // devices
    token_rows = own_tokens * tiles
    slots = rows // FEWEST + 1
    position = place()
    first = position * rows
    even = position % 2 == 0
    first_float = first.astype(F32)
    w_sides[2 * opm : 2 * LANES - 2 * opm, :] = jnp.zeros(
        (2 * LANES - 4 * opm, tiles * LANES), BF
    )

    for copy in copies[:9]:
        copy.wait()
    counts_lane = jnp.broadcast_to(counts[...].astype(F32), (LANES, tokens)).astype(BF)
    folded = counts_folded[...].astype(F32).astype(BF)
    upper = flag(iota((LANES, LANES), 0) <= iota((LANES, LANES), 1))
    lower = flag(iota((LANES, LANES), 1) <= iota((LANES, LANES), 0))
    below = flag(iota((LANES, LANES), 1) < iota((LANES, LANES), 0))
    within = dot(folded, upper)
    whole = dot(folded, jnp.ones((LANES, LANES), BF))
    base = jnp.zeros((1, 1), F32)
    passed = jnp.zeros((1, LANES), F32)
    for fold in range(folded.shape[0]):
        ended = within[fold : fold + 1] + passed <= first_float
        base = base + jnp.sum(jnp.where(ended, 1.0, 0.0), axis=1, keepdims=True)
        part = slice(fold * LANES, (fold + 1) * LANES)
        ends[part, :] = passed + dot_t(lower, counts_lane[:, part])
        begins[part, :] = passed + dot_t(below, counts_lane[:, part])
        passed = passed + whole[fold : fold + 1]

    base_token = base.astype(jnp.int32)
    token_lane = iota((SLOTS, tokens), 1).astype(F32)
    slot_token = iota((SLOTS, tokens), 0).astype(F32) + base
    slot_end = dot_t(flag(token_lane <= slot_token), counts_lane)
    slot_start = dot_t(flag(token_lane < slot_token), counts_lane)
    atom_lane = iota((SLOTS, rows), 1).astype(F32) + first_float
    member[...] = flag((atom_lane >= slot_start[:, :rows]) & (atom_lane < slot_end[:, :rows]))
    slot_scale[...] = 1.0 / jnp.maximum(slot_end - slot_start, 1.0)
    last_atom = first_float + (rows - 1)
    is_last = jnp.where((slot_start <= last_atom) & (slot_end > last_atom), 1.0, 0.0)
    last[...] = is_last
    goes_on = is_last * jnp.where(slot_end > first_float + rows, 1.0, 0.0)
    carried = jnp.where(slot_start[0:1] < first_float, 1.0, 0.0)

    lanes = 2 * LANES
    lane = iota((1, lanes), 1)
    atom = (lane % rows + first).astype(F32)
    inside = (atom >= jnp.concatenate([begins[...]] * 2, axis=1)) & (lane < tiles * rows)
    inside = flag(inside & (atom < jnp.concatenate([ends[...]] * 2, axis=1)))
    tile_fits = iota((BLOCK, lanes), 0) // own_tokens == iota((BLOCK, lanes), 1) // rows
    tile_fits = jnp.where(tile_fits, 1.0, 0.0)
    twice = jnp.concatenate([slot_start, slot_start], axis=1)
    held_atoms = atom >= twice
    twice = jnp.concatenate([slot_end, slot_end], axis=1)
    held_atoms = jnp.where(held_atoms & (atom < twice), 1.0, 0.0)
    third = lane // rows
    edge_atoms = jnp.concatenate(
        [
            held_atoms[0:1] * jnp.concatenate([carried] * 2, axis=1),
            jnp.sum(held_atoms * jnp.concatenate([goes_on] * 2, axis=1), axis=0, keepdims=True),
            jnp.zeros((SLOTS - 2, lanes), F32),
        ],
        axis=0,
    )
    slot_atoms = jnp.concatenate(
        [
            jnp.where(third == 0, held_atoms, 0.0),
            jnp.where(third == 1, held_atoms, 0.0),
            jnp.where(third == 2, edge_atoms, 0.0),
            jnp.zeros((LANES - 3 * SLOTS, lanes), F32),
        ],
        axis=0,
    ).astype(BF)
    column = iota((1, LANES), 1)
    kind, slot = column // SLOTS, column % SLOTS
    token = base_token + slot

    def rows_step(at):
        here = span(at, DESTS * BLOCK)
        dest = iota((DESTS, BLOCK, tokens), 0).reshape(DESTS * BLOCK, tokens) + at * DESTS
        turn = iota((DESTS, BLOCK, tokens), 1).reshape(DESTS * BLOCK, tokens) % own_tokens
        picks = dot(flag(iota((1, tokens), 1) == dest * own_tokens + turn), inside)
        picks = picks.reshape(DESTS, BLOCK, lanes) * tile_fits[None]
        route[here, :] = picks.reshape(DESTS * BLOCK, lanes).astype(BF)
        dest = iota((DESTS, LANES), 0) + at * DESTS
        first_own = dest * own_tokens
        shared_tokens = overlap(base_token, first_own, own_tokens, slots)
        index = jnp.where(token < first_own, slot, slot - shared_tokens)
        mine = (token >= first_own) & (token < first_own + own_tokens)
        room = 2 * (BLOCK - SLOT_ROW)
        target = jnp.where(index < room, SLOT_ROW + index // 2, jnp.where(kind == 0, 0, -1))
        fits = (index % 2 == kind) & (slot < slots) & jnp.logical_not(mine)
        target = jnp.where(fits & (kind < 2), target, -1)
        beside = jnp.where(slot == 0, position - 1, position + 1)
        is_edge = (kind == 2) & (slot < 2) & (dest == beside)
        row = edge_row(base_token, first_own, own_tokens, slots)
        target = jnp.where(is_edge, row, target)
        spot = iota((BLOCK, LANES), 0)
        selects = [
            jnp.where(jnp.broadcast_to(target[d : d + 1], (BLOCK, LANES)) == spot, 1.0, 0.0)
            for d in range(DESTS)
        ]
        selects = jnp.concatenate(selects, axis=0).astype(BF)
        slot_route[here, :] = dot(selects, slot_atoms).astype(BF)

    repeat(devices // DESTS, rows_step)

    row_tokens = tokens // lax.axis_size("row")
    col_tokens = tokens // lax.axis_size("col")
    first_row = lax.axis_index("row") * row_tokens
    first_col = lax.axis_index("col") * col_tokens

    def row_counts(height, first_token, cycle):
        token_row = iota((height, tokens), 0) % cycle + first_token
        return dot_t(flag(iota((1, tokens), 1) == token_row), counts_lane)

    owned = [
        row_counts(SLOTS, position * own_tokens, own_tokens),
        row_counts(row_tokens, first_row, row_tokens),
        row_counts(col_tokens, first_col, col_tokens),
    ]
    own_scale[...] = 1.0 / jnp.concatenate(owned, axis=0)

    def adder_step(at):
        here = span(at, LANES)
        spot_lane = iota((1, LANES), 1) + at * LANES
        block = spot_lane // BLOCK
        spot = spot_lane % BLOCK
        edge = (block * rows).astype(F32)
        tally = jnp.zeros((1, LANES), F32)
        for fold in range(tokens // LANES):
            ended = jnp.where(ends[fold * LANES : (fold + 1) * LANES, :] <= edge, 1.0, 0.0)
            tally = tally + jnp.sum(ended, axis=0, keepdims=True)
        start = tally.astype(jnp.int32)
        first_own = position * own_tokens
        shared_tokens = overlap(start, first_own, own_tokens, slots)

        def token_of(index):
            slot = jnp.where(start + index < first_own, index, index + shared_tokens)
            return jnp.where((index >= 0) & (slot < slots), start + slot, -1)

        in_slots = spot >= SLOT_ROW
        room = 2 * (BLOCK - SLOT_ROW)
        ninth = jnp.where((spot == 0) & (shared_tokens == 0), start + room, -1)
        low_token = jnp.where(in_slots, token_of(2 * (spot - SLOT_ROW)), ninth)
        high_token = jnp.where(in_slots, token_of(2 * (spot - SLOT_ROW) + 1), -1)
        own_token = first_own + spot % own_tokens
        held = (spot < token_rows) & (own_token >= start) & (own_token < start + slots)
        own_token = jnp.where(held, own_token, -1)
        line = iota((SLOTS, LANES), 0)
        side = jnp.where(line == token_rows, position - 1, position + 1)
        on_edge = spot == edge_row(start, first_own, own_tokens, slots)
        is_edge = (line >= token_rows) & (line < token_rows + 2) & on_edge & (block == side)
        lines = [(line < token_rows) & (spot == line) & held | is_edge]
        row_line = iota((row_tokens, LANES), 0) + first_row
        col_line = iota((col_tokens, LANES), 0) + first_col
        for wanted in (row_line, col_line):
            lines += [low_token == wanted, high_token == wanted]
        for tile in range(tiles):
            tile_token = jnp.where(spot // own_tokens == tile, own_token, -1)
            lines += [tile_token == row_line, tile_token == col_line]
        top = 0
        for part in lines:
            adder[top : top + part.shape[0], here] = flag(part)
            top += part.shape[0]

    repeat(devices * BLOCK // LANES, adder_step)

    own_float[...] = own[...].astype(F32)
    normed, scaling = centred_rows(own[...], atom_gain[...])
    near = (dot(normed, w_key[...]) * scaling).astype(BF)
    query = (dot(normed, w_query[...]) * scaling).astype(BF)
    head_of = iota((1, width), 1) // (width // HEADS)
    head_mask = [flag(head_of == h) for h in range(HEADS)]
    heads = jnp.concatenate([query * m for m in head_mask], axis=0)
    probes[...] = dot_t(heads, w_key[...]).astype(BF)
    w_mix = jnp.concatenate(
        [dot(w_value[...] * m, w_out[...]).astype(BF) for m in head_mask], axis=1
    )
    w_mixed[...] = w_mix
    own_mixed[...] = (
        dot(normed, w_mix) * jnp.concatenate([scaling] * HEADS, axis=1)
    ).astype(BF)
    near_index = first + iota((1, rows), 1)
    far_lane = iota((1, 2 * rows), 1)
    is_low = (far_lane < rows) != even
    far_index = first + far_lane % rows + jnp.where(is_low, -rows, rows)
    near_bias, bias = [], []
    for e in range(rows // QB):
        low = key_starts[0:1, e : e + 1]
        seen = (near_index >= low) & (near_index < low + KW)
        near_bias.append(jnp.broadcast_to(jnp.where(seen, 0.0, MASKED), (QB, rows)))
        seen = (far_index >= low) & (far_index < low + KW)
        seen = seen & (far_index >= 0) & (far_index < atoms)
        bias.append(jnp.broadcast_to(jnp.where(seen, 0.0, MASKED), (QB, 2 * rows)))
    far_bias[...] = jnp.concatenate(bias, axis=0)
    raw_scores = dot_t(heads, near) + jnp.concatenate(near_bias * HEADS, axis=0)
    scores[...] = raw_scores
    top[...] = jnp.max(raw_scores, axis=-1, keepdims=True)
    for copy in copies[9:]:
        copy.wait()
    pair_width = w_outer_far.shape[1]
    average = jnp.full((pair_width, pair_width), 1.0 / pair_width, F32).astype(BF)
    w_outer[:, pair_width:] = dot(w_outer[:, :pair_width], average).astype(BF)


def atom_kernel(
    neighbour,
    sibling,
    own_float,
    own_mixed,
    probes,
    scores,
    top,
    far_bias,
    route,
    slot_route,
    member,
    slot_scale,
    atom_gain,
    w_mixed,
    w_pool,
    w_back,
    w_sides,
    payload,
    updated,
    slot_back,
):
    rows, width = own_float.shape
    tiles = w_pool.shape[1] // LANES
    devices = payload.shape[0] // BLOCK
    raw = jnp.concatenate([sibling[...], neighbour[...]], axis=0)
    average = jnp.full((width, width), 1.0 / width, F32).astype(BF)
    centred = raw.astype(F32) - dot(raw, average)
    squares = (centred * centred).astype(BF)
    normed = (centred * atom_gain[...]).astype(BF)
    scaling = lax.rsqrt(dot(squares, average) + EPSILON)
    scaling_row = lax.rsqrt(dot_t(average[:SLOTS], squares) + EPSILON)[0:1]
    far_mixed = (
        dot(normed, w_mixed[...]) * jnp.concatenate([scaling] * HEADS, axis=1)
    ).astype(BF)
    far_scores = dot_t(probes[...], normed) * scaling_row
    far_scores = far_scores + jnp.concatenate([far_bias[...]] * HEADS, axis=0)
    most = jnp.maximum(top[...], jnp.max(far_scores, axis=-1, keepdims=True))
    scale = (width // HEADS) ** (-0.5) * LOG2E
    raised = jnp.concatenate(
        [
            jnp.exp2((far_scores - most) * scale).astype(BF),
            jnp.exp2((scores[...] - most) * scale).astype(BF),
        ],
        axis=1,
    )
    ones = jnp.ones((3 * rows, width), BF)
    change = own_float[...]
    for h in range(HEADS):
        part = slice(h * width, (h + 1) * width)
        values = jnp.concatenate([far_mixed[:, part], own_mixed[:, part]], axis=0)
        mixed = dot(raised[h * rows : (h + 1) * rows], jnp.concatenate([values, ones], axis=1))
        change = change + mixed[:, :width] / mixed[:, width:]
    fresh = change.astype(BF)
    updated[...] = fresh
    feature = jnp.maximum(dot(fresh, w_pool[...]), 0.0).astype(BF)
    feature_tiles = jnp.concatenate(
        [feature[:, k * LANES : (k + 1) * LANES] for k in range(tiles)], axis=0
    )
    sides = dot_t(feature, w_sides[...]).astype(BF)
    backs = dot(feature, w_back[...]).astype(BF)
    spare = jnp.zeros((2 * LANES - 3 * rows, LANES), BF)
    source = jnp.concatenate([feature_tiles, spare], axis=0)
    slot_source = jnp.concatenate([sides[:, :LANES], sides[:, LANES:], backs, spare], axis=0)

    def send_step(at):
        here = span(at, DESTS * BLOCK)
        singles = dot(route[here, :], source)
        payload[here, :] = (singles + dot(slot_route[here, :], slot_source)).astype(BF)

    repeat(devices // DESTS, send_step)
    slot_back[...] = dot(member[...], backs) * slot_scale[...]


def pair_kernel(
    arrived,
    adder,
    updated,
    slot_back,
    slot_last,
    slot_scale,
    slot_member,
    pair_state,
    w_outer,
    pair_gain,
    w_gate,
    w_lift,
    w_drop,
    w_sides,
    own_scale,
    atom_out,
    token_single,
    pair_out,
):
    row_tokens, col_tokens, pair_width = pair_state.shape
    own_tokens, channels = token_single.shape
    tiles = channels // LANES
    token_rows = own_tokens * tiles
    opm = math.isqrt(w_outer.shape[0])
    added = dot(adder[...], arrived[...])
    half_gate = w_gate[...] * jnp.asarray(0.5, BF)
    parts, top = [], 0
    for height in (SLOTS,) + (row_tokens,) * 2 + (col_tokens,) * 2 + (row_tokens, col_tokens) * tiles:
        parts.append(added[top : top + height])
        top += height
    sums, left_low, left_high, right_low, right_high, *own = parts
    owned = own_scale[...]
    row_scale = owned[SLOTS : SLOTS + row_tokens]
    col_scale = owned[SLOTS + row_tokens :]
    own_left = jnp.concatenate([part * row_scale for part in own[0::2]], axis=1).astype(BF)
    own_right = jnp.concatenate([part * col_scale for part in own[1::2]], axis=1).astype(BF)
    own_sides = dot_t(jnp.concatenate([own_left, own_right], axis=0), w_sides[:LANES])
    left = left_low[:, :opm] + left_high[:, 2 * opm : 3 * opm]
    left = left * row_scale[:, :opm] + own_sides[:row_tokens, :opm]
    right = right_low[:, opm : 2 * opm] + right_high[:, 3 * opm : 4 * opm]
    right = right * col_scale[:, :opm] + own_sides[row_tokens:, opm : 2 * opm]
    depth = GROUP * opm
    corner = jnp.where(iota((GROUP, depth), 1) // opm == iota((GROUP, depth), 0), 1.0, 0.0)

    def spread(rows_of, first, count):
        return jnp.concatenate(
            [
                jnp.broadcast_to(rows_of[k : k + 1, :], (GROUP, depth)) * corner
                for k in range(first, first + count)
            ],
            axis=0,
        ).astype(BF)

    left_wide = jnp.concatenate([left] * GROUP, axis=1)
    right_blocks = spread(jnp.concatenate([right] * GROUP, axis=1), 0, col_tokens)
    stages = opm // GROUP
    table = [
        dot(right_blocks, w_outer[g * depth : (g + 1) * depth, :]) for g in range(stages)
    ]
    tables = [
        jnp.concatenate(
            [
                table[g][j * GROUP : (j + 1) * GROUP]
                for j in range(h * GROUP, (h + 1) * GROUP)
                for g in range(stages)
            ],
            axis=0,
        ).astype(BF)
        for h in range(col_tokens // GROUP)
    ]

    def pair_rows(here):
        left_blocks = spread(left_wide, here, PAIR_ROWS)
        terms = [dot(left_blocks, part) for part in tables]
        outer = jnp.concatenate(
            [
                term[i * GROUP : (i + 1) * GROUP]
                for i in range(PAIR_ROWS)
                for term in terms
            ],
            axis=0,
        )
        flat = pair_state[pl.ds(here, PAIR_ROWS)].reshape(PAIR_ROWS * col_tokens, pair_width)
        flat = flat.astype(F32)
        summed = flat + outer[:, :pair_width]
        pair_mean = jnp.mean(flat, axis=-1, keepdims=True)
        centred = summed - (pair_mean + outer[:, pair_width:])
        variance = jnp.mean(centred * centred, axis=-1, keepdims=True)
        scaling = lax.rsqrt(variance + EPSILON)
        normed = (centred * pair_gain[...]).astype(BF)
        gate = dot(normed, half_gate) * scaling
        lift = dot(normed, w_lift[...])
        hidden = (gate * lift * (1.0 + jnp.tanh(gate))).astype(BF)
        result = (summed + dot(hidden, w_drop[...]) * scaling).astype(BF)
        pair_out[pl.ds(here, PAIR_ROWS)] = result.reshape(PAIR_ROWS, col_tokens, pair_width)

    for step in range(row_tokens // PAIR_ROWS):
        here = step * PAIR_ROWS
        pair_rows(here)

    singles = sums * owned[:SLOTS]
    token_single[...] = jnp.concatenate(
        [singles[k * own_tokens : (k + 1) * own_tokens] for k in range(tiles)], axis=1
    ).astype(BF)
    spot = iota((SLOTS, LANES), 0)
    from_before = jnp.where(spot == 0, sums[token_rows : token_rows + 1], 0.0)
    from_after = slot_last[...] * sums[token_rows + 1 : token_rows + 2]
    back = (slot_back[...] + (from_before + from_after) * slot_scale[...]).astype(BF)
    lifted = lax.dot_general(
        slot_member[...], back, (((0,), (0,)), ((), ())), preferred_element_type=F32
    )
    atom_out[...] = (updated[...].astype(F32) + lifted).astype(BF)


def call(kernel, name, operands, outputs, far=(), scratch=()):
    near_spec = pl.BlockSpec(memory_space=pltpu.VMEM)
    far_spec = pl.BlockSpec(memory_space=pltpu.HBM)
    held = sum(math.prod(a.shape) * a.dtype.itemsize for a in operands + outputs)
    return pl.pallas_call(
        kernel,
        out_shape=outputs,
        in_specs=[far_spec] * len(far) + [near_spec] * len(operands),
        out_specs=(near_spec,) * len(outputs),
        scratch_shapes=scratch,
        compiler_params=pltpu.CompilerParams(vmem_limit_bytes=min(2 * held + SPARE, MOST)),
        name=name,
    )(*[pltpu.with_memory_space_constraint(a, pltpu.HBM) for a in far], *operands)


def per_device(
    atom_feats,
    key_starts,
    atom_counts,
    atom_gain,
    w_query,
    w_key,
    w_value,
    w_out,
    w_pool,
    w_back,
    pair_state,
    w_left,
    w_right,
    w_outer,
    pair_gain,
    w_gate,
    w_lift,
    w_drop,
):
    rows, width = atom_feats.shape
    devices = lax.axis_size(AXES)
    tokens = atom_counts.shape[0]
    channels = w_pool.shape[1]
    opm = w_left.shape[1]
    own_tokens = tokens // devices
    row_tokens, col_tokens, _ = pair_state.shape
    tiles = channels // LANES
    opm = w_left.shape[1]
    across = [(i, i + 1) for i in range(1, devices - 1, 2)]
    neighbour = lax.ppermute(atom_feats, AXES, across + [(j, i) for i, j in across])
    sibling = lax.ppermute(atom_feats, AXES, [(i, i ^ 1) for i in range(devices)])

    def held(*shape, dtype=F32):
        return jax.ShapeDtypeStruct(shape, dtype)

    counts_folded = atom_counts.reshape(-1, LANES)
    ready = call(
        ready_kernel,
        "ready",
        (),
        (
            held(rows, width),
            held(rows, HEADS * width, dtype=BF),
            held(HEADS * rows, width, dtype=BF),
            held(HEADS * rows, rows),
            held(HEADS * rows, 1),
            held(rows, 2 * rows),
            held(devices * BLOCK, 2 * LANES, dtype=BF),
            held(devices * BLOCK, 2 * LANES, dtype=BF),
            held(SLOTS, rows, dtype=BF),
            held(SLOTS, LANES),
            held(SLOTS, LANES),
            held(
                SLOTS + (2 + tiles) * (row_tokens + col_tokens), devices * BLOCK, dtype=BF
            ),
            held(SLOTS + row_tokens + col_tokens, LANES),
            held(1, width),
            held(1, LANES),
            held(width, HEADS * width, dtype=BF),
            held(width, channels, dtype=BF),
            held(channels, width, dtype=BF),
            held(2 * LANES, channels, dtype=BF),
            held(opm * opm, 2 * w_outer.shape[-1], dtype=BF),
        ),
        far=(
            atom_feats,
            key_starts[None],
            atom_counts[None],
            counts_folded,
            atom_gain[None],
            pair_gain[None],
            w_query,
            w_key,
            w_value,
            w_out,
            w_pool,
            w_back,
            w_left.T,
            w_right.T,
            w_outer.reshape(opm * opm, -1),
        ),
        scratch=(
            pltpu.VMEM((rows, width), BF),
            pltpu.VMEM((1, key_starts.shape[0]), jnp.int32),
            pltpu.VMEM((1, tokens), jnp.int32),
            pltpu.VMEM(counts_folded.shape, jnp.int32),
            pltpu.VMEM((width, width), BF),
            pltpu.VMEM((width, width), BF),
            pltpu.VMEM((width, width), BF),
            pltpu.VMEM((width, width), BF),
            pltpu.VMEM((tokens, LANES), F32),
            pltpu.VMEM((tokens, LANES), F32),
            pltpu.SemaphoreType.DMA((17,)),
        ),
    )
    (
        own_float,
        own_mixed,
        probes,
        scores,
        top,
        far_bias,
        route,
        slot_route,
        member,
        slot_scale,
        last,
        adder,
        own_scale,
        atom_gain_kept,
        pair_gain_kept,
        *kept,
        w_outer_kept,
    ) = ready
    payload, updated, slot_back = call(
        atom_kernel,
        "atoms",
        (
            neighbour,
            sibling,
            own_float,
            own_mixed,
            probes,
            scores,
            top,
            far_bias,
            route,
            slot_route,
            member,
            slot_scale,
            atom_gain_kept,
            *kept,
        ),
        (
            held(devices * BLOCK, LANES, dtype=BF),
            held(rows, width, dtype=BF),
            held(SLOTS, width),
        ),
    )
    arrived = lax.all_to_all(payload.reshape(devices, BLOCK, LANES), AXES, 0, 0)
    return call(
        pair_kernel,
        "pairs",
        (
            arrived.reshape(devices * BLOCK, LANES),
            adder,
            updated,
            slot_back,
            last,
            slot_scale,
            member,
            pair_state,
            w_outer_kept,
            pair_gain_kept,
            w_gate,
            w_lift,
            w_drop,
            kept[-1],
            own_scale,
        ),
        (
            held(rows, width, dtype=BF),
            held(own_tokens, channels, dtype=BF),
            held(*pair_state.shape, dtype=BF),
        ),
    )


def solution(mesh):
    in_specs = (
        P(("row", "col"), None),
        P(("row", "col")),
        P(),
        P(),
        P(),
        P(),
        P(),
        P(),
        P(),
        P(),
        P("row", "col", None),
        P(),
        P(),
        P(),
        P(),
        P(),
        P(),
        P(),
    )
    out_specs = (P(("row", "col"), None), P(("row", "col"), None), P("row", "col", None))
    return jax.shard_map(
        per_device, mesh=mesh, in_specs=in_specs, out_specs=out_specs, check_vma=False
    )
```

```python
import math

import jax
import jax.numpy as jnp
from jax import lax
from jax.experimental import pallas as pl
from jax.experimental.pallas import tpu as pltpu
from jax.sharding import PartitionSpec as P

HEADS = 4
QB = 32
KW = 128
EPSILON = 1e-05
HALF = KW // 2
FEWEST = 8
LANES = 128
SLOTS = 16
BLOCK = 16
SLOT_ROW = 12
DESTS = 32
PAIR_ROWS = 16
GROUP = 8
MASKED = -1e30
SPARE = 12 << 20
MOST = 60 << 20
LOG2E = 1.4426950408889634
AXES = ("row", "col")
BF = jnp.bfloat16
F32 = jnp.float32


def dot(a, b):
    return jnp.dot(a, b, preferred_element_type=F32)


def dot_t(a, b):
    return lax.dot_general(a, b, (((1,), (1,)), ((), ())), preferred_element_type=F32)


def iota(shape, axis):
    return lax.broadcasted_iota(jnp.int32, shape, axis)


def centred_rows(values, gain):
    width = values.shape[1]
    average = jnp.full((width, width), 1.0 / width, F32).astype(BF)
    centred = values.astype(F32) - dot(values, average)
    variance = dot((centred * centred).astype(BF), average)
    return (centred * gain).astype(BF), lax.rsqrt(variance + EPSILON)


def flag(mask):
    return jnp.where(mask, 1.0, 0.0).astype(BF)


def place():
    return lax.axis_index("row") * lax.axis_size("col") + lax.axis_index("col")


def overlap(base, first_own, own_tokens, slots):
    inner = jnp.minimum(first_own + own_tokens, base + slots) - jnp.maximum(first_own, base)
    return jnp.maximum(inner, 0)


def edge_row(base, first_own, own_tokens, slots):
    last_own = first_own + own_tokens - 1
    last_held = (last_own >= base) & (last_own < base + slots)
    free = jnp.where(last_held, 0, own_tokens - 1)
    whole = overlap(base, first_own, own_tokens, slots) == own_tokens
    return jnp.where(whole, BLOCK - 1, free)


def repeat(count, step):
    if count <= 8:
        for at in range(count):
            step(at)
    else:

        def body(at, carry):
            step(at)
            return carry

        lax.fori_loop(0, count, body, 0)


def span(at, size):
    if isinstance(at, int):
        return pl.ds(at * size, size)
    return pl.ds(pl.multiple_of(at * size, size), size)


def ready_kernel(
    own_far,
    starts_far,
    counts_far,
    folded_far,
    atom_gain_far,
    pair_gain_far,
    w_query_far,
    w_key_far,
    w_value_far,
    w_out_far,
    w_pool_far,
    w_back_far,
    w_left_far,
    w_right_far,
    w_outer_far,
    own_float,
    probes,
    own_part,
    top,
    far_bias,
    route,
    member,
    slot_scale,
    before,
    goes_on,
    last,
    adder,
    own_scale,
    atom_gain,
    pair_gain,
    w_mixed,
    w_pool,
    w_back,
    w_sides,
    w_outer,
    own,
    key_starts,
    counts,
    counts_folded,
    w_query,
    w_key,
    w_value,
    w_out,
    begins,
    ends,
    arrivals,
):
    rows, width = own.shape
    tokens = counts.shape[1]
    opm = w_left_far.shape[0]
    pairs = (
        (counts_far, counts),
        (folded_far, counts_folded),
        (own_far, own),
        (starts_far, key_starts),
        (atom_gain_far, atom_gain),
        (w_query_far, w_query),
        (w_key_far, w_key),
        (w_value_far, w_value),
        (w_out_far, w_out),
        (pair_gain_far, pair_gain),
        (w_pool_far, w_pool),
        (w_back_far, w_back),
        (w_left_far, w_sides.at[:opm]),
        (w_right_far, w_sides.at[opm : 2 * opm]),
        (w_left_far, w_sides.at[2 * LANES - 2 * opm : 2 * LANES - opm]),
        (w_right_far, w_sides.at[2 * LANES - opm :]),
        (w_outer_far, w_outer.at[:, : w_outer_far.shape[1]]),
    )
    copies = [pltpu.make_async_copy(a, b, arrivals.at[k]) for k, (a, b) in enumerate(pairs)]
    for copy in copies:
        copy.start()

    tiles = w_pool.shape[1] // LANES
    devices = route.shape[0] // BLOCK
    atoms = rows * devices
    own_tokens = tokens // devices
    token_rows = own_tokens * tiles
    slots = rows // FEWEST + 1
    position = place()
    first = position * rows
    even = position % 2 == 0
    first_float = first.astype(F32)
    w_sides[2 * opm : 2 * LANES - 2 * opm, :] = jnp.zeros(
        (2 * LANES - 4 * opm, tiles * LANES), BF
    )

    for copy in copies[:9]:
        copy.wait()
    counts_lane = jnp.broadcast_to(counts[...].astype(F32), (LANES, tokens)).astype(BF)
    folded = counts_folded[...].astype(F32).astype(BF)
    upper = flag(iota((LANES, LANES), 0) <= iota((LANES, LANES), 1))
    lower = flag(iota((LANES, LANES), 1) <= iota((LANES, LANES), 0))
    below = flag(iota((LANES, LANES), 1) < iota((LANES, LANES), 0))
    within = dot(folded, upper)
    whole = dot(folded, jnp.ones((LANES, LANES), BF))
    base = jnp.zeros((1, 1), F32)
    passed = jnp.zeros((1, LANES), F32)
    for fold in range(folded.shape[0]):
        ended = within[fold : fold + 1] + passed <= first_float
        base = base + jnp.sum(jnp.where(ended, 1.0, 0.0), axis=1, keepdims=True)
        part = slice(fold * LANES, (fold + 1) * LANES)
        ends[part, :] = passed + dot_t(lower, counts_lane[:, part])
        begins[part, :] = passed + dot_t(below, counts_lane[:, part])
        passed = passed + whole[fold : fold + 1]

    base_token = base.astype(jnp.int32)
    token_lane = iota((SLOTS, tokens), 1).astype(F32)
    slot_token = iota((SLOTS, tokens), 0).astype(F32) + base
    slot_end = dot_t(flag(token_lane <= slot_token), counts_lane)
    slot_start = dot_t(flag(token_lane < slot_token), counts_lane)
    atom_lane = iota((SLOTS, rows), 1).astype(F32) + first_float
    member[...] = flag((atom_lane >= slot_start[:, :rows]) & (atom_lane < slot_end[:, :rows]))
    slot_scale[...] = 1.0 / jnp.maximum(slot_end - slot_start, 1.0)
    last_atom = first_float + (rows - 1)
    is_last = jnp.where((slot_start <= last_atom) & (slot_end > last_atom), 1.0, 0.0)
    last[...] = is_last
    goes_on[...] = is_last * jnp.where(slot_end > first_float + rows, 1.0, 0.0)
    is_first = iota((SLOTS, LANES), 0) == 0
    before[...] = jnp.where(is_first & (slot_start < first_float), 1.0, 0.0)

    lanes = 2 * LANES
    lane = iota((1, lanes), 1)
    atom = (lane % rows + first).astype(F32)
    inside = (atom >= jnp.concatenate([begins[...]] * 2, axis=1)) & (lane < tiles * rows)
    inside = flag(inside & (atom < jnp.concatenate([ends[...]] * 2, axis=1)))
    tile_fits = iota((BLOCK, lanes), 0) // own_tokens == iota((BLOCK, lanes), 1) // rows
    tile_fits = jnp.where(tile_fits, 1.0, 0.0)
    column = iota((1, LANES), 1) - (tiles * rows - LANES)
    kind, slot = column // SLOTS, column % SLOTS
    token = base_token + slot

    def rows_step(at):
        here = span(at, DESTS * BLOCK)
        dest = iota((DESTS, BLOCK, tokens), 0).reshape(DESTS * BLOCK, tokens) + at * DESTS
        turn = iota((DESTS, BLOCK, tokens), 1).reshape(DESTS * BLOCK, tokens) % own_tokens
        picks = dot(flag(iota((1, tokens), 1) == dest * own_tokens + turn), inside)
        picks = picks.reshape(DESTS, BLOCK, lanes) * tile_fits[None]
        picks = picks.reshape(DESTS * BLOCK, lanes)
        dest = iota((DESTS, LANES), 0) + at * DESTS
        first_own = dest * own_tokens
        shared_tokens = overlap(base_token, first_own, own_tokens, slots)
        index = jnp.where(token < first_own, slot, slot - shared_tokens)
        mine = (token >= first_own) & (token < first_own + own_tokens)
        room = 2 * (BLOCK - SLOT_ROW)
        target = jnp.where(index < room, SLOT_ROW + index // 2, jnp.where(kind == 0, 0, -1))
        fits = (index % 2 == kind) & (slot < slots) & jnp.logical_not(mine) & (column >= 0)
        target = jnp.where(fits & (kind < 2), target, -1)
        beside = jnp.where(slot == 0, position - 1, position + 1)
        is_edge = (kind == 2) & (slot < 2) & (dest == beside)
        row = edge_row(base_token, first_own, own_tokens, slots)
        target = jnp.where(is_edge, row, target)
        spot = iota((BLOCK, LANES), 0)
        selects = [
            jnp.where(jnp.broadcast_to(target[d : d + 1], (BLOCK, LANES)) == spot, 1.0, 0.0)
            for d in range(DESTS)
        ]
        high = picks[:, LANES:] + jnp.concatenate(selects, axis=0)
        route[here, :] = jnp.concatenate([picks[:, :LANES], high], axis=1).astype(BF)

    repeat(devices // DESTS, rows_step)

    row_tokens = tokens // lax.axis_size("row")
    col_tokens = tokens // lax.axis_size("col")
    first_row = lax.axis_index("row") * row_tokens
    first_col = lax.axis_index("col") * col_tokens

    def row_counts(height, first_token, cycle):
        token_row = iota((height, tokens), 0) % cycle + first_token
        return dot_t(flag(iota((1, tokens), 1) == token_row), counts_lane)

    owned = [
        row_counts(SLOTS, position * own_tokens, own_tokens),
        row_counts(row_tokens, first_row, row_tokens),
        row_counts(col_tokens, first_col, col_tokens),
    ]
    own_scale[...] = 1.0 / jnp.concatenate(owned, axis=0)

    def adder_step(at):
        here = span(at, LANES)
        spot_lane = iota((1, LANES), 1) + at * LANES
        block = spot_lane // BLOCK
        spot = spot_lane % BLOCK
        edge = (block * rows).astype(F32)
        tally = jnp.zeros((1, LANES), F32)
        for fold in range(tokens // LANES):
            ended = jnp.where(ends[fold * LANES : (fold + 1) * LANES, :] <= edge, 1.0, 0.0)
            tally = tally + jnp.sum(ended, axis=0, keepdims=True)
        start = tally.astype(jnp.int32)
        first_own = position * own_tokens
        shared_tokens = overlap(start, first_own, own_tokens, slots)

        def token_of(index):
            slot = jnp.where(start + index < first_own, index, index + shared_tokens)
            return jnp.where((index >= 0) & (slot < slots), start + slot, -1)

        in_slots = spot >= SLOT_ROW
        room = 2 * (BLOCK - SLOT_ROW)
        ninth = jnp.where((spot == 0) & (shared_tokens == 0), start + room, -1)
        low_token = jnp.where(in_slots, token_of(2 * (spot - SLOT_ROW)), ninth)
        high_token = jnp.where(in_slots, token_of(2 * (spot - SLOT_ROW) + 1), -1)
        own_token = first_own + spot % own_tokens
        held = (spot < token_rows) & (own_token >= start) & (own_token < start + slots)
        own_token = jnp.where(held, own_token, -1)
        line = iota((SLOTS, LANES), 0)
        side = jnp.where(line == token_rows, position - 1, position + 1)
        on_edge = spot == edge_row(start, first_own, own_tokens, slots)
        is_edge = (line >= token_rows) & (line < token_rows + 2) & on_edge & (block == side)
        lines = [(line < token_rows) & (spot == line) & held | is_edge]
        row_line = iota((row_tokens, LANES), 0) + first_row
        col_line = iota((col_tokens, LANES), 0) + first_col
        for wanted in (row_line, col_line):
            lines += [low_token == wanted, high_token == wanted]
        for tile in range(tiles):
            tile_token = jnp.where(spot // own_tokens == tile, own_token, -1)
            lines += [tile_token == row_line, tile_token == col_line]
        top = 0
        for part in lines:
            adder[top : top + part.shape[0], here] = flag(part)
            top += part.shape[0]

    repeat(devices * BLOCK // LANES, adder_step)

    own_float[...] = own[...].astype(F32)
    normed, scaling = centred_rows(own[...], atom_gain[...])
    near = (dot(normed, w_key[...]) * scaling).astype(BF)
    query = (dot(normed, w_query[...]) * scaling).astype(BF)
    head_of = iota((1, width), 1) // (width // HEADS)
    head_mask = [flag(head_of == h) for h in range(HEADS)]
    heads = jnp.concatenate([query * m for m in head_mask], axis=0)
    probes[...] = dot_t(heads, w_key[...]).astype(BF)
    w_mix = jnp.concatenate(
        [dot(w_value[...] * m, w_out[...]).astype(BF) for m in head_mask], axis=1
    )
    w_mixed[...] = w_mix
    own_mixed = (
        dot(normed, w_mix) * jnp.concatenate([scaling] * HEADS, axis=1)
    ).astype(BF)
    near_index = first + iota((1, rows), 1)
    far_lane = iota((1, 2 * rows), 1)
    is_low = (far_lane < rows) != even
    far_index = first + far_lane % rows + jnp.where(is_low, -rows, rows)
    near_bias, bias = [], []
    for e in range(rows // QB):
        low = key_starts[0:1, e : e + 1]
        seen = (near_index >= low) & (near_index < low + KW)
        near_bias.append(jnp.broadcast_to(jnp.where(seen, 0.0, MASKED), (QB, rows)))
        seen = (far_index >= low) & (far_index < low + KW)
        seen = seen & (far_index >= 0) & (far_index < atoms)
        bias.append(jnp.broadcast_to(jnp.where(seen, 0.0, MASKED), (QB, 2 * rows)))
    far_bias[...] = jnp.concatenate(bias, axis=0)
    raw_scores = dot_t(heads, near) + jnp.concatenate(near_bias * HEADS, axis=0)
    most = jnp.max(raw_scores, axis=-1, keepdims=True)
    top[...] = most
    raised = jnp.exp2((raw_scores - most) * ((width // HEADS) ** (-0.5) * LOG2E)).astype(BF)
    ones = jnp.ones((rows, width), BF)
    for h in range(HEADS):
        part = slice(h * rows, (h + 1) * rows)
        values = jnp.concatenate([own_mixed[:, h * width : (h + 1) * width], ones], axis=1)
        own_part[part, :] = dot(raised[part], values)
    for copy in copies[9:]:
        copy.wait()
    pair_width = w_outer_far.shape[1]
    average = jnp.full((pair_width, pair_width), 1.0 / pair_width, F32).astype(BF)
    w_outer[:, pair_width:] = dot(w_outer[:, :pair_width], average).astype(BF)


def atom_kernel(
    neighbour,
    sibling,
    own_float,
    probes,
    own_part,
    top,
    far_bias,
    route,
    member,
    slot_scale,
    before,
    goes_on,
    atom_gain,
    w_mixed,
    w_pool,
    w_back,
    w_sides,
    payload,
    updated,
    slot_back,
):
    rows, width = own_float.shape
    tiles = w_pool.shape[1] // LANES
    devices = payload.shape[0] // BLOCK
    raw = jnp.concatenate([sibling[...], neighbour[...]], axis=0)
    average = jnp.full((width, width), 1.0 / width, F32).astype(BF)
    centred = raw.astype(F32) - dot(raw, average)
    squares = (centred * centred).astype(BF)
    normed = (centred * atom_gain[...]).astype(BF)
    scaling = lax.rsqrt(dot(squares, average) + EPSILON)
    scaling_row = lax.rsqrt(dot_t(average[:SLOTS], squares) + EPSILON)[0:1]
    far_mixed = (
        dot(normed, w_mixed[...]) * jnp.concatenate([scaling] * HEADS, axis=1)
    ).astype(BF)
    far_scores = dot_t(probes[...], normed) * scaling_row
    far_scores = far_scores + jnp.concatenate([far_bias[...]] * HEADS, axis=0)
    most = jnp.maximum(top[...], jnp.max(far_scores, axis=-1, keepdims=True))
    scale = (width // HEADS) ** (-0.5) * LOG2E
    raised = jnp.exp2((far_scores - most) * scale).astype(BF)
    shrink = jnp.exp2((top[...] - most) * scale)
    ones = jnp.ones((2 * rows, width), BF)
    change = own_float[...]
    for h in range(HEADS):
        part = slice(h * rows, (h + 1) * rows)
        values = jnp.concatenate([far_mixed[:, h * width : (h + 1) * width], ones], axis=1)
        mixed = dot(raised[part], values) + own_part[part, :] * shrink[part]
        change = change + mixed[:, :width] / mixed[:, width:]
    fresh = change.astype(BF)
    updated[...] = fresh
    feature = jnp.maximum(dot(fresh, w_pool[...]), 0.0).astype(BF)
    feature_tiles = jnp.concatenate(
        [feature[:, k * LANES : (k + 1) * LANES] for k in range(tiles)], axis=0
    )
    slot_single = (
        dot(member[...], feature) * jnp.concatenate([slot_scale[...]] * tiles, axis=1)
    ).astype(BF)
    sides = dot_t(slot_single, w_sides[...]).astype(BF)
    backs = dot(slot_single, w_back[...])
    slot_back[...] = backs
    to_before = jnp.sum(backs * before[...], axis=0, keepdims=True)
    to_after = jnp.sum(backs * goes_on[...], axis=0, keepdims=True)
    spot = iota((SLOTS, LANES), 0)
    edges = jnp.where(spot == 0, to_before, jnp.where(spot == 1, to_after, 0.0)).astype(BF)
    spare = jnp.zeros((2 * LANES - tiles * rows - 3 * SLOTS, LANES), BF)
    source = jnp.concatenate(
        [feature_tiles, sides[:, :LANES], sides[:, LANES:], edges, spare], axis=0
    )

    def send_step(at):
        here = span(at, DESTS * BLOCK)
        payload[here, :] = dot(route[here, :], source).astype(BF)

    repeat(devices // DESTS, send_step)


def pair_kernel(
    arrived,
    adder,
    updated,
    slot_back,
    slot_last,
    slot_member,
    pair_state,
    w_outer,
    pair_gain,
    w_gate,
    w_lift,
    w_drop,
    w_sides,
    own_scale,
    atom_out,
    token_single,
    pair_out,
):
    row_tokens, col_tokens, pair_width = pair_state.shape
    own_tokens, channels = token_single.shape
    tiles = channels // LANES
    token_rows = own_tokens * tiles
    opm = math.isqrt(w_outer.shape[0])
    added = dot(adder[...], arrived[...])
    half_gate = w_gate[...] * jnp.asarray(0.5, BF)
    parts, top = [], 0
    for height in (SLOTS,) + (row_tokens,) * 2 + (col_tokens,) * 2 + (row_tokens, col_tokens) * tiles:
        parts.append(added[top : top + height])
        top += height
    sums, left_low, left_high, right_low, right_high, *own = parts
    owned = own_scale[...]
    row_scale = owned[SLOTS : SLOTS + row_tokens]
    col_scale = owned[SLOTS + row_tokens :]
    own_left = jnp.concatenate([part * row_scale for part in own[0::2]], axis=1).astype(BF)
    own_right = jnp.concatenate([part * col_scale for part in own[1::2]], axis=1).astype(BF)
    own_sides = dot_t(jnp.concatenate([own_left, own_right], axis=0), w_sides[:LANES])
    left = left_low[:, :opm] + left_high[:, 2 * opm : 3 * opm] + own_sides[:row_tokens, :opm]
    right = right_low[:, opm : 2 * opm] + right_high[:, 3 * opm : 4 * opm]
    right = right + own_sides[row_tokens:, opm : 2 * opm]
    depth = GROUP * opm
    corner = jnp.where(iota((GROUP, depth), 1) // opm == iota((GROUP, depth), 0), 1.0, 0.0)

    def spread(rows_of, first, count):
        return jnp.concatenate(
            [
                jnp.broadcast_to(rows_of[k : k + 1, :], (GROUP, depth)) * corner
                for k in range(first, first + count)
            ],
            axis=0,
        ).astype(BF)

    left_wide = jnp.concatenate([left] * GROUP, axis=1)
    right_blocks = spread(jnp.concatenate([right] * GROUP, axis=1), 0, col_tokens)
    stages = opm // GROUP
    table = [
        dot(right_blocks, w_outer[g * depth : (g + 1) * depth, :]) for g in range(stages)
    ]
    tables = [
        jnp.concatenate(
            [
                table[g][j * GROUP : (j + 1) * GROUP]
                for j in range(h * GROUP, (h + 1) * GROUP)
                for g in range(stages)
            ],
            axis=0,
        ).astype(BF)
        for h in range(col_tokens // GROUP)
    ]

    def pair_rows(here):
        left_blocks = spread(left_wide, here, PAIR_ROWS)
        terms = [dot(left_blocks, part) for part in tables]
        outer = jnp.concatenate(
            [
                term[i * GROUP : (i + 1) * GROUP]
                for i in range(PAIR_ROWS)
                for term in terms
            ],
            axis=0,
        )
        flat = pair_state[pl.ds(here, PAIR_ROWS)].reshape(PAIR_ROWS * col_tokens, pair_width)
        flat = flat.astype(F32)
        summed = flat + outer[:, :pair_width]
        pair_mean = jnp.mean(flat, axis=-1, keepdims=True)
        centred = summed - (pair_mean + outer[:, pair_width:])
        variance = jnp.mean(centred * centred, axis=-1, keepdims=True)
        scaling = lax.rsqrt(variance + EPSILON)
        normed = (centred * pair_gain[...]).astype(BF)
        gate = dot(normed, half_gate) * scaling
        lift = dot(normed, w_lift[...])
        hidden = (gate * lift * (1.0 + jnp.tanh(gate))).astype(BF)
        result = (summed + dot(hidden, w_drop[...]) * scaling).astype(BF)
        pair_out[pl.ds(here, PAIR_ROWS)] = result.reshape(PAIR_ROWS, col_tokens, pair_width)

    for step in range(row_tokens // PAIR_ROWS):
        here = step * PAIR_ROWS
        pair_rows(here)

    singles = sums * owned[:SLOTS]
    token_single[...] = jnp.concatenate(
        [singles[k * own_tokens : (k + 1) * own_tokens] for k in range(tiles)], axis=1
    ).astype(BF)
    spot = iota((SLOTS, LANES), 0)
    from_before = jnp.where(spot == 0, sums[token_rows : token_rows + 1], 0.0)
    from_after = slot_last[...] * sums[token_rows + 1 : token_rows + 2]
    back = (slot_back[...] + from_before + from_after).astype(BF)
    lifted = lax.dot_general(
        slot_member[...], back, (((0,), (0,)), ((), ())), preferred_element_type=F32
    )
    atom_out[...] = (updated[...].astype(F32) + lifted).astype(BF)


def call(kernel, name, operands, outputs, far=(), scratch=()):
    near_spec = pl.BlockSpec(memory_space=pltpu.VMEM)
    far_spec = pl.BlockSpec(memory_space=pltpu.HBM)
    held = sum(math.prod(a.shape) * a.dtype.itemsize for a in operands + outputs)
    return pl.pallas_call(
        kernel,
        out_shape=outputs,
        in_specs=[far_spec] * len(far) + [near_spec] * len(operands),
        out_specs=(near_spec,) * len(outputs),
        scratch_shapes=scratch,
        compiler_params=pltpu.CompilerParams(vmem_limit_bytes=min(2 * held + SPARE, MOST)),
        name=name,
    )(*[pltpu.with_memory_space_constraint(a, pltpu.HBM) for a in far], *operands)


def per_device(
    atom_feats,
    key_starts,
    atom_counts,
    atom_gain,
    w_query,
    w_key,
    w_value,
    w_out,
    w_pool,
    w_back,
    pair_state,
    w_left,
    w_right,
    w_outer,
    pair_gain,
    w_gate,
    w_lift,
    w_drop,
):
    rows, width = atom_feats.shape
    devices = lax.axis_size(AXES)
    tokens = atom_counts.shape[0]
    channels = w_pool.shape[1]
    opm = w_left.shape[1]
    own_tokens = tokens // devices
    row_tokens, col_tokens, _ = pair_state.shape
    tiles = channels // LANES
    opm = w_left.shape[1]
    across = [(i, i + 1) for i in range(1, devices - 1, 2)]
    neighbour = lax.ppermute(atom_feats, AXES, across + [(j, i) for i, j in across])
    sibling = lax.ppermute(atom_feats, AXES, [(i, i ^ 1) for i in range(devices)])

    def held(*shape, dtype=F32):
        return jax.ShapeDtypeStruct(shape, dtype)

    counts_folded = atom_counts.reshape(-1, LANES)
    ready = call(
        ready_kernel,
        "ready",
        (),
        (
            held(rows, width),
            held(HEADS * rows, width, dtype=BF),
            held(HEADS * rows, 2 * width),
            held(HEADS * rows, 1),
            held(rows, 2 * rows),
            held(devices * BLOCK, 2 * LANES, dtype=BF),
            held(SLOTS, rows, dtype=BF),
            held(SLOTS, LANES),
            held(SLOTS, LANES),
            held(SLOTS, LANES),
            held(SLOTS, LANES),
            held(
                SLOTS + (2 + tiles) * (row_tokens + col_tokens), devices * BLOCK, dtype=BF
            ),
            held(SLOTS + row_tokens + col_tokens, LANES),
            held(1, width),
            held(1, LANES),
            held(width, HEADS * width, dtype=BF),
            held(width, channels, dtype=BF),
            held(channels, width, dtype=BF),
            held(2 * LANES, channels, dtype=BF),
            held(opm * opm, 2 * w_outer.shape[-1], dtype=BF),
        ),
        far=(
            atom_feats,
            key_starts[None],
            atom_counts[None],
            counts_folded,
            atom_gain[None],
            pair_gain[None],
            w_query,
            w_key,
            w_value,
            w_out,
            w_pool,
            w_back,
            w_left.T,
            w_right.T,
            w_outer.reshape(opm * opm, -1),
        ),
        scratch=(
            pltpu.VMEM((rows, width), BF),
            pltpu.VMEM((1, key_starts.shape[0]), jnp.int32),
            pltpu.VMEM((1, tokens), jnp.int32),
            pltpu.VMEM(counts_folded.shape, jnp.int32),
            pltpu.VMEM((width, width), BF),
            pltpu.VMEM((width, width), BF),
            pltpu.VMEM((width, width), BF),
            pltpu.VMEM((width, width), BF),
            pltpu.VMEM((tokens, LANES), F32),
            pltpu.VMEM((tokens, LANES), F32),
            pltpu.SemaphoreType.DMA((17,)),
        ),
    )
    (
        own_float,
        probes,
        own_part,
        top,
        far_bias,
        route,
        member,
        slot_scale,
        before,
        goes_on,
        last,
        adder,
        own_scale,
        atom_gain_kept,
        pair_gain_kept,
        *kept,
        w_outer_kept,
    ) = ready
    payload, updated, slot_back = call(
        atom_kernel,
        "atoms",
        (
            neighbour,
            sibling,
            own_float,
            probes,
            own_part,
            top,
            far_bias,
            route,
            member,
            slot_scale,
            before,
            goes_on,
            atom_gain_kept,
            *kept,
        ),
        (
            held(devices * BLOCK, LANES, dtype=BF),
            held(rows, width, dtype=BF),
            held(SLOTS, width),
        ),
    )
    arrived = lax.all_to_all(payload.reshape(devices, BLOCK, LANES), AXES, 0, 0)
    return call(
        pair_kernel,
        "pairs",
        (
            arrived.reshape(devices * BLOCK, LANES),
            adder,
            updated,
            slot_back,
            last,
            member,
            pair_state,
            w_outer_kept,
            pair_gain_kept,
            w_gate,
            w_lift,
            w_drop,
            kept[-1],
            own_scale,
        ),
        (
            held(rows, width, dtype=BF),
            held(own_tokens, channels, dtype=BF),
            held(*pair_state.shape, dtype=BF),
        ),
    )


def solution(mesh):
    in_specs = (
        P(("row", "col"), None),
        P(("row", "col")),
        P(),
        P(),
        P(),
        P(),
        P(),
        P(),
        P(),
        P(),
        P("row", "col", None),
        P(),
        P(),
        P(),
        P(),
        P(),
        P(),
        P(),
    )
    out_specs = (P(("row", "col"), None), P(("row", "col"), None), P("row", "col", None))
    return jax.shard_map(
        per_device, mesh=mesh, in_specs=in_specs, out_specs=out_specs, check_vma=False
    )
```

```python
import math

import jax
import jax.numpy as jnp
from jax import lax
from jax.experimental import pallas as pl
from jax.experimental.pallas import tpu as pltpu
from jax.sharding import PartitionSpec as P

HEADS = 4
QB = 32
KW = 128
EPSILON = 1e-05
HALF = KW // 2
FEWEST = 8
LANES = 128
SLOTS = 16
BLOCK = 16
SLOT_ROW = 12
DESTS = 32
PAIR_ROWS = 16
GROUP = 8
MASKED = -1e30
SPARE = 12 << 20
MOST = 60 << 20
LOG2E = 1.4426950408889634
AXES = ("row", "col")
BF = jnp.bfloat16
F32 = jnp.float32


def dot(a, b):
    return jnp.dot(a, b, preferred_element_type=F32)


def dot_t(a, b):
    return lax.dot_general(a, b, (((1,), (1,)), ((), ())), preferred_element_type=F32)


def iota(shape, axis):
    return lax.broadcasted_iota(jnp.int32, shape, axis)


def centred_rows(values, gain):
    width = values.shape[1]
    average = jnp.full((width, width), 1.0 / width, F32).astype(BF)
    centred = values.astype(F32) - dot(values, average)
    variance = dot((centred * centred).astype(BF), average)
    return (centred * gain).astype(BF), lax.rsqrt(variance + EPSILON)


def flag(mask):
    return jnp.where(mask, 1.0, 0.0).astype(BF)


def place():
    return lax.axis_index("row") * lax.axis_size("col") + lax.axis_index("col")


def overlap(base, first_own, own_tokens, slots):
    inner = jnp.minimum(first_own + own_tokens, base + slots) - jnp.maximum(first_own, base)
    return jnp.maximum(inner, 0)


def edge_row(base, first_own, own_tokens, slots):
    last_own = first_own + own_tokens - 1
    last_held = (last_own >= base) & (last_own < base + slots)
    free = jnp.where(last_held, 0, own_tokens - 1)
    whole = overlap(base, first_own, own_tokens, slots) == own_tokens
    return jnp.where(whole, BLOCK - 1, free)


def repeat(count, step):
    if count <= 8:
        for at in range(count):
            step(at)
    else:

        def body(at, carry):
            step(at)
            return carry

        lax.fori_loop(0, count, body, 0)


def span(at, size):
    if isinstance(at, int):
        return pl.ds(at * size, size)
    return pl.ds(pl.multiple_of(at * size, size), size)


def ready_kernel(
    own_far,
    starts_far,
    counts_far,
    folded_far,
    atom_gain_far,
    pair_gain_far,
    w_query_far,
    w_key_far,
    w_value_far,
    w_out_far,
    w_pool_far,
    w_back_far,
    w_left_far,
    w_right_far,
    w_outer_far,
    own_float,
    own_mixed,
    probes,
    scores,
    top,
    far_bias,
    route,
    member,
    slot_scale,
    before,
    goes_on,
    last,
    adder,
    own_scale,
    atom_gain,
    pair_gain,
    w_mixed,
    w_pool,
    w_back,
    w_turned,
    w_outer,
    own,
    key_starts,
    counts,
    counts_folded,
    w_query,
    w_key,
    w_value,
    w_out,
    w_sides,
    begins,
    ends,
    arrivals,
):
    rows, width = own.shape
    tokens = counts.shape[1]
    opm = w_left_far.shape[0]
    pairs = (
        (counts_far, counts),
        (folded_far, counts_folded),
        (own_far, own),
        (starts_far, key_starts),
        (atom_gain_far, atom_gain),
        (w_query_far, w_query),
        (w_key_far, w_key),
        (w_value_far, w_value),
        (w_out_far, w_out),
        (pair_gain_far, pair_gain),
        (w_pool_far, w_pool),
        (w_back_far, w_back),
        (w_left_far, w_sides.at[:opm]),
        (w_right_far, w_sides.at[opm : 2 * opm]),
        (w_left_far, w_sides.at[2 * LANES - 2 * opm : 2 * LANES - opm]),
        (w_right_far, w_sides.at[2 * LANES - opm :]),
        (w_outer_far, w_outer.at[:, : w_outer_far.shape[1]]),
    )
    copies = [pltpu.make_async_copy(a, b, arrivals.at[k]) for k, (a, b) in enumerate(pairs)]
    for copy in copies:
        copy.start()

    tiles = w_pool.shape[1] // LANES
    devices = route.shape[0] // BLOCK
    atoms = rows * devices
    own_tokens = tokens // devices
    token_rows = own_tokens * tiles
    slots = rows // FEWEST + 1
    position = place()
    first = position * rows
    even = position % 2 == 0
    first_float = first.astype(F32)
    w_sides[2 * opm : 2 * LANES - 2 * opm, :] = jnp.zeros(
        (2 * LANES - 4 * opm, tiles * LANES), BF
    )

    for copy in copies[:9]:
        copy.wait()
    counts_lane = jnp.broadcast_to(counts[...].astype(F32), (LANES, tokens)).astype(BF)
    folded = counts_folded[...].astype(F32).astype(BF)
    upper = flag(iota((LANES, LANES), 0) <= iota((LANES, LANES), 1))
    lower = flag(iota((LANES, LANES), 1) <= iota((LANES, LANES), 0))
    below = flag(iota((LANES, LANES), 1) < iota((LANES, LANES), 0))
    within = dot(folded, upper)
    whole = dot(folded, jnp.ones((LANES, LANES), BF))
    base = jnp.zeros((1, 1), F32)
    passed = jnp.zeros((1, LANES), F32)
    for fold in range(folded.shape[0]):
        ended = within[fold : fold + 1] + passed <= first_float
        base = base + jnp.sum(jnp.where(ended, 1.0, 0.0), axis=1, keepdims=True)
        part = slice(fold * LANES, (fold + 1) * LANES)
        ends[part, :] = passed + dot_t(lower, counts_lane[:, part])
        begins[part, :] = passed + dot_t(below, counts_lane[:, part])
        passed = passed + whole[fold : fold + 1]

    base_token = base.astype(jnp.int32)
    token_lane = iota((SLOTS, tokens), 1).astype(F32)
    slot_token = iota((SLOTS, tokens), 0).astype(F32) + base
    slot_end = dot_t(flag(token_lane <= slot_token), counts_lane)
    slot_start = dot_t(flag(token_lane < slot_token), counts_lane)
    atom_lane = iota((SLOTS, rows), 1).astype(F32) + first_float
    member[...] = flag((atom_lane >= slot_start[:, :rows]) & (atom_lane < slot_end[:, :rows]))
    slot_scale[...] = 1.0 / jnp.maximum(slot_end - slot_start, 1.0)
    last_atom = first_float + (rows - 1)
    is_last = jnp.where((slot_start <= last_atom) & (slot_end > last_atom), 1.0, 0.0)
    last[...] = is_last
    goes_on[...] = is_last * jnp.where(slot_end > first_float + rows, 1.0, 0.0)
    is_first = iota((SLOTS, LANES), 0) == 0
    before[...] = jnp.where(is_first & (slot_start < first_float), 1.0, 0.0)

    lanes = 2 * LANES
    lane = iota((1, lanes), 1)
    atom = (lane % rows + first).astype(F32)
    inside = (atom >= jnp.concatenate([begins[...]] * 2, axis=1)) & (lane < tiles * rows)
    inside = flag(inside & (atom < jnp.concatenate([ends[...]] * 2, axis=1)))
    tile_fits = iota((BLOCK, lanes), 0) // own_tokens == iota((BLOCK, lanes), 1) // rows
    tile_fits = jnp.where(tile_fits, 1.0, 0.0)
    column = iota((1, LANES), 1) - (tiles * rows - LANES)
    kind, slot = column // SLOTS, column % SLOTS
    token = base_token + slot

    def rows_step(at):
        here = span(at, DESTS * BLOCK)
        dest = iota((DESTS, BLOCK, tokens), 0).reshape(DESTS * BLOCK, tokens) + at * DESTS
        turn = iota((DESTS, BLOCK, tokens), 1).reshape(DESTS * BLOCK, tokens) % own_tokens
        picks = dot(flag(iota((1, tokens), 1) == dest * own_tokens + turn), inside)
        picks = picks.reshape(DESTS, BLOCK, lanes) * tile_fits[None]
        picks = picks.reshape(DESTS * BLOCK, lanes)
        dest = iota((DESTS, LANES), 0) + at * DESTS
        first_own = dest * own_tokens
        shared_tokens = overlap(base_token, first_own, own_tokens, slots)
        index = jnp.where(token < first_own, slot, slot - shared_tokens)
        mine = (token >= first_own) & (token < first_own + own_tokens)
        room = 2 * (BLOCK - SLOT_ROW)
        target = jnp.where(index < room, SLOT_ROW + index // 2, jnp.where(kind == 0, 0, -1))
        fits = (index % 2 == kind) & (slot < slots) & jnp.logical_not(mine) & (column >= 0)
        target = jnp.where(fits & (kind < 2), target, -1)
        beside = jnp.where(slot == 0, position - 1, position + 1)
        is_edge = (kind == 2) & (slot < 2) & (dest == beside)
        row = edge_row(base_token, first_own, own_tokens, slots)
        target = jnp.where(is_edge, row, target)
        spot = iota((BLOCK, LANES), 0)
        selects = [
            jnp.where(jnp.broadcast_to(target[d : d + 1], (BLOCK, LANES)) == spot, 1.0, 0.0)
            for d in range(DESTS)
        ]
        high = picks[:, LANES:] + jnp.concatenate(selects, axis=0)
        route[here, :] = jnp.concatenate([picks[:, :LANES], high], axis=1).astype(BF)

    repeat(devices // DESTS, rows_step)

    row_tokens = tokens // lax.axis_size("row")
    col_tokens = tokens // lax.axis_size("col")
    first_row = lax.axis_index("row") * row_tokens
    first_col = lax.axis_index("col") * col_tokens

    def row_counts(height, first_token, cycle):
        token_row = iota((height, tokens), 0) % cycle + first_token
        return dot_t(flag(iota((1, tokens), 1) == token_row), counts_lane)

    owned = [
        row_counts(SLOTS, position * own_tokens, own_tokens),
        row_counts(row_tokens, first_row, row_tokens),
        row_counts(col_tokens, first_col, col_tokens),
    ]
    own_scale[...] = 1.0 / jnp.concatenate(owned, axis=0)

    def adder_step(at):
        here = span(at, LANES)
        spot_lane = iota((1, LANES), 1) + at * LANES
        block = spot_lane // BLOCK
        spot = spot_lane % BLOCK
        edge = (block * rows).astype(F32)
        tally = jnp.zeros((1, LANES), F32)
        for fold in range(tokens // LANES):
            ended = jnp.where(ends[fold * LANES : (fold + 1) * LANES, :] <= edge, 1.0, 0.0)
            tally = tally + jnp.sum(ended, axis=0, keepdims=True)
        start = tally.astype(jnp.int32)
        first_own = position * own_tokens
        shared_tokens = overlap(start, first_own, own_tokens, slots)

        def token_of(index):
            slot = jnp.where(start + index < first_own, index, index + shared_tokens)
            return jnp.where((index >= 0) & (slot < slots), start + slot, -1)

        in_slots = spot >= SLOT_ROW
        room = 2 * (BLOCK - SLOT_ROW)
        ninth = jnp.where((spot == 0) & (shared_tokens == 0), start + room, -1)
        low_token = jnp.where(in_slots, token_of(2 * (spot - SLOT_ROW)), ninth)
        high_token = jnp.where(in_slots, token_of(2 * (spot - SLOT_ROW) + 1), -1)
        own_token = first_own + spot % own_tokens
        held = (spot < token_rows) & (own_token >= start) & (own_token < start + slots)
        own_token = jnp.where(held, own_token, -1)
        line = iota((SLOTS, LANES), 0)
        side = jnp.where(line == token_rows, position - 1, position + 1)
        on_edge = spot == edge_row(start, first_own, own_tokens, slots)
        is_edge = (line >= token_rows) & (line < token_rows + 2) & on_edge & (block == side)
        lines = [(line < token_rows) & (spot == line) & held | is_edge]
        row_line = iota((row_tokens, LANES), 0) + first_row
        col_line = iota((col_tokens, LANES), 0) + first_col
        for wanted in (row_line, col_line):
            lines += [low_token == wanted, high_token == wanted]
        for tile in range(tiles):
            tile_token = jnp.where(spot // own_tokens == tile, own_token, -1)
            lines += [tile_token == row_line, tile_token == col_line]
        top = 0
        for part in lines:
            adder[top : top + part.shape[0], here] = flag(part)
            top += part.shape[0]

    repeat(devices * BLOCK // LANES, adder_step)

    own_float[...] = own[...].astype(F32)
    normed, scaling = centred_rows(own[...], atom_gain[...])
    near = (dot(normed, w_key[...]) * scaling).astype(BF)
    query = (dot(normed, w_query[...]) * scaling).astype(BF)
    head_of = iota((1, width), 1) // (width // HEADS)
    head_mask = [flag(head_of == h) for h in range(HEADS)]
    heads = jnp.concatenate([query * m for m in head_mask], axis=0)
    probes[...] = dot_t(heads, w_key[...]).astype(BF)
    w_mix = jnp.concatenate(
        [dot(w_value[...] * m, w_out[...]).astype(BF) for m in head_mask], axis=1
    )
    w_mixed[...] = w_mix
    own_mixed[...] = (
        dot(normed, w_mix) * jnp.concatenate([scaling] * HEADS, axis=1)
    ).astype(BF)
    near_index = first + iota((1, rows), 1)
    far_lane = iota((1, 2 * rows), 1)
    is_low = (far_lane < rows) != even
    far_index = first + far_lane % rows + jnp.where(is_low, -rows, rows)
    near_bias, bias = [], []
    for e in range(rows // QB):
        low = key_starts[0:1, e : e + 1]
        seen = (near_index >= low) & (near_index < low + KW)
        near_bias.append(jnp.broadcast_to(jnp.where(seen, 0.0, MASKED), (QB, rows)))
        seen = (far_index >= low) & (far_index < low + KW)
        seen = seen & (far_index >= 0) & (far_index < atoms)
        bias.append(jnp.broadcast_to(jnp.where(seen, 0.0, MASKED), (QB, 2 * rows)))
    far_bias[...] = jnp.concatenate(bias, axis=0)
    raw_scores = dot_t(heads, near) + jnp.concatenate(near_bias * HEADS, axis=0)
    scores[...] = raw_scores
    top[...] = jnp.max(raw_scores, axis=-1, keepdims=True)
    for copy in copies[9:]:
        copy.wait()
    channels = tiles * LANES
    same = flag(iota((channels, channels), 0) == iota((channels, channels), 1))
    w_turned[...] = dot_t(same, w_sides[...]).astype(BF)
    pair_width = w_outer_far.shape[1]
    average = jnp.full((pair_width, pair_width), 1.0 / pair_width, F32).astype(BF)
    w_outer[:, pair_width:] = dot(w_outer[:, :pair_width], average).astype(BF)


def atom_kernel(
    neighbour,
    sibling,
    own_float,
    own_mixed,
    probes,
    scores,
    top,
    far_bias,
    route,
    member,
    slot_scale,
    before,
    goes_on,
    atom_gain,
    w_mixed,
    w_pool,
    w_back,
    w_sides,
    payload,
    updated,
    slot_back,
):
    rows, width = own_float.shape
    tiles = w_pool.shape[1] // LANES
    devices = payload.shape[0] // BLOCK
    raw = jnp.concatenate([sibling[...], neighbour[...]], axis=0)
    average = jnp.full((width, width), 1.0 / width, F32).astype(BF)
    centred = raw.astype(F32) - dot(raw, average)
    squares = (centred * centred).astype(BF)
    normed = (centred * atom_gain[...]).astype(BF)
    scaling = lax.rsqrt(dot(squares, average) + EPSILON)
    scaling_row = lax.rsqrt(dot_t(average[:SLOTS], squares) + EPSILON)[0:1]
    far_mixed = (
        dot(normed, w_mixed[...]) * jnp.concatenate([scaling] * HEADS, axis=1)
    ).astype(BF)
    far_scores = dot_t(probes[...], normed) * scaling_row
    far_scores = far_scores + jnp.concatenate([far_bias[...]] * HEADS, axis=0)
    most = jnp.maximum(top[...], jnp.max(far_scores, axis=-1, keepdims=True))
    scale = (width // HEADS) ** (-0.5) * LOG2E
    raised = jnp.concatenate(
        [
            jnp.exp2((far_scores - most) * scale).astype(BF),
            jnp.exp2((scores[...] - most) * scale).astype(BF),
        ],
        axis=1,
    )
    ones = jnp.ones((3 * rows, width), BF)
    change = own_float[...]
    for h in range(HEADS):
        part = slice(h * width, (h + 1) * width)
        values = jnp.concatenate([far_mixed[:, part], own_mixed[:, part]], axis=0)
        mixed = dot(raised[h * rows : (h + 1) * rows], jnp.concatenate([values, ones], axis=1))
        change = change + mixed[:, :width] / mixed[:, width:]
    fresh = change.astype(BF)
    updated[...] = fresh
    feature = jnp.maximum(dot(fresh, w_pool[...]), 0.0).astype(BF)
    feature_tiles = jnp.concatenate(
        [feature[:, k * LANES : (k + 1) * LANES] for k in range(tiles)], axis=0
    )
    slot_single = (
        dot(member[...], feature) * jnp.concatenate([slot_scale[...]] * tiles, axis=1)
    ).astype(BF)
    sides = dot(slot_single, w_sides[...]).astype(BF)
    backs = dot(slot_single, w_back[...])
    slot_back[...] = backs
    to_before = jnp.sum(backs * before[...], axis=0, keepdims=True)
    to_after = jnp.sum(backs * goes_on[...], axis=0, keepdims=True)
    spot = iota((SLOTS, LANES), 0)
    edges = jnp.where(spot == 0, to_before, jnp.where(spot == 1, to_after, 0.0)).astype(BF)
    spare = jnp.zeros((2 * LANES - tiles * rows - 3 * SLOTS, LANES), BF)
    source = jnp.concatenate(
        [feature_tiles, sides[:, :LANES], sides[:, LANES:], edges, spare], axis=0
    )

    def send_step(at):
        here = span(at, DESTS * BLOCK)
        payload[here, :] = dot(route[here, :], source).astype(BF)

    repeat(devices // DESTS, send_step)


def pair_kernel(
    arrived,
    adder,
    updated,
    slot_back,
    slot_last,
    slot_member,
    pair_state,
    w_outer,
    pair_gain,
    w_gate,
    w_lift,
    w_drop,
    w_sides,
    own_scale,
    atom_out,
    token_single,
    pair_out,
):
    row_tokens, col_tokens, pair_width = pair_state.shape
    own_tokens, channels = token_single.shape
    tiles = channels // LANES
    token_rows = own_tokens * tiles
    opm = math.isqrt(w_outer.shape[0])
    added = dot(adder[...], arrived[...])
    half_gate = w_gate[...] * jnp.asarray(0.5, BF)
    parts, top = [], 0
    for height in (SLOTS,) + (row_tokens,) * 2 + (col_tokens,) * 2 + (row_tokens, col_tokens) * tiles:
        parts.append(added[top : top + height])
        top += height
    sums, left_low, left_high, right_low, right_high, *own = parts
    owned = own_scale[...]
    row_scale = owned[SLOTS : SLOTS + row_tokens]
    col_scale = owned[SLOTS + row_tokens :]
    own_left = jnp.concatenate([part * row_scale for part in own[0::2]], axis=1).astype(BF)
    own_right = jnp.concatenate([part * col_scale for part in own[1::2]], axis=1).astype(BF)
    own_sides = dot(jnp.concatenate([own_left, own_right], axis=0), w_sides[:, :LANES])
    left = left_low[:, :opm] + left_high[:, 2 * opm : 3 * opm] + own_sides[:row_tokens, :opm]
    right = right_low[:, opm : 2 * opm] + right_high[:, 3 * opm : 4 * opm]
    right = right + own_sides[row_tokens:, opm : 2 * opm]
    depth = GROUP * opm
    corner = jnp.where(iota((GROUP, depth), 1) // opm == iota((GROUP, depth), 0), 1.0, 0.0)

    def spread(rows_of, first, count):
        return jnp.concatenate(
            [
                jnp.broadcast_to(rows_of[k : k + 1, :], (GROUP, depth)) * corner
                for k in range(first, first + count)
            ],
            axis=0,
        ).astype(BF)

    left_wide = jnp.concatenate([left] * GROUP, axis=1)
    right_blocks = spread(jnp.concatenate([right] * GROUP, axis=1), 0, col_tokens)
    stages = opm // GROUP
    table = [
        dot(right_blocks, w_outer[g * depth : (g + 1) * depth, :]) for g in range(stages)
    ]
    tables = [
        jnp.concatenate(
            [
                table[g][j * GROUP : (j + 1) * GROUP]
                for j in range(h * GROUP, (h + 1) * GROUP)
                for g in range(stages)
            ],
            axis=0,
        ).astype(BF)
        for h in range(col_tokens // GROUP)
    ]

    def pair_rows(here):
        left_blocks = spread(left_wide, here, PAIR_ROWS)
        terms = [dot(left_blocks, part) for part in tables]
        outer = jnp.concatenate(
            [
                term[i * GROUP : (i + 1) * GROUP]
                for i in range(PAIR_ROWS)
                for term in terms
            ],
            axis=0,
        )
        flat = pair_state[pl.ds(here, PAIR_ROWS)].reshape(PAIR_ROWS * col_tokens, pair_width)
        flat = flat.astype(F32)
        summed = flat + outer[:, :pair_width]
        pair_mean = jnp.mean(flat, axis=-1, keepdims=True)
        centred = summed - (pair_mean + outer[:, pair_width:])
        variance = jnp.mean(centred * centred, axis=-1, keepdims=True)
        scaling = lax.rsqrt(variance + EPSILON)
        normed = (centred * pair_gain[...]).astype(BF)
        gate = dot(normed, half_gate) * scaling
        lift = dot(normed, w_lift[...])
        hidden = (gate * lift * (1.0 + jnp.tanh(gate))).astype(BF)
        result = (summed + dot(hidden, w_drop[...]) * scaling).astype(BF)
        pair_out[pl.ds(here, PAIR_ROWS)] = result.reshape(PAIR_ROWS, col_tokens, pair_width)

    for step in range(row_tokens // PAIR_ROWS):
        here = step * PAIR_ROWS
        pair_rows(here)

    singles = sums * owned[:SLOTS]
    token_single[...] = jnp.concatenate(
        [singles[k * own_tokens : (k + 1) * own_tokens] for k in range(tiles)], axis=1
    ).astype(BF)
    spot = iota((SLOTS, LANES), 0)
    from_before = jnp.where(spot == 0, sums[token_rows : token_rows + 1], 0.0)
    from_after = slot_last[...] * sums[token_rows + 1 : token_rows + 2]
    back = (slot_back[...] + from_before + from_after).astype(BF)
    lifted = lax.dot_general(
        slot_member[...], back, (((0,), (0,)), ((), ())), preferred_element_type=F32
    )
    atom_out[...] = (updated[...].astype(F32) + lifted).astype(BF)


def call(kernel, name, operands, outputs, far=(), scratch=()):
    near_spec = pl.BlockSpec(memory_space=pltpu.VMEM)
    far_spec = pl.BlockSpec(memory_space=pltpu.HBM)
    held = sum(math.prod(a.shape) * a.dtype.itemsize for a in operands + outputs)
    return pl.pallas_call(
        kernel,
        out_shape=outputs,
        in_specs=[far_spec] * len(far) + [near_spec] * len(operands),
        out_specs=(near_spec,) * len(outputs),
        scratch_shapes=scratch,
        compiler_params=pltpu.CompilerParams(vmem_limit_bytes=min(2 * held + SPARE, MOST)),
        name=name,
    )(*[pltpu.with_memory_space_constraint(a, pltpu.HBM) for a in far], *operands)


def per_device(
    atom_feats,
    key_starts,
    atom_counts,
    atom_gain,
    w_query,
    w_key,
    w_value,
    w_out,
    w_pool,
    w_back,
    pair_state,
    w_left,
    w_right,
    w_outer,
    pair_gain,
    w_gate,
    w_lift,
    w_drop,
):
    rows, width = atom_feats.shape
    devices = lax.axis_size(AXES)
    tokens = atom_counts.shape[0]
    channels = w_pool.shape[1]
    opm = w_left.shape[1]
    own_tokens = tokens // devices
    row_tokens, col_tokens, _ = pair_state.shape
    tiles = channels // LANES
    opm = w_left.shape[1]
    across = [(i, i + 1) for i in range(1, devices - 1, 2)]
    neighbour = lax.ppermute(atom_feats, AXES, across + [(j, i) for i, j in across])
    sibling = lax.ppermute(atom_feats, AXES, [(i, i ^ 1) for i in range(devices)])

    def held(*shape, dtype=F32):
        return jax.ShapeDtypeStruct(shape, dtype)

    counts_folded = atom_counts.reshape(-1, LANES)
    ready = call(
        ready_kernel,
        "ready",
        (),
        (
            held(rows, width),
            held(rows, HEADS * width, dtype=BF),
            held(HEADS * rows, width, dtype=BF),
            held(HEADS * rows, rows),
            held(HEADS * rows, 1),
            held(rows, 2 * rows),
            held(devices * BLOCK, 2 * LANES, dtype=BF),
            held(SLOTS, rows, dtype=BF),
            held(SLOTS, LANES),
            held(SLOTS, LANES),
            held(SLOTS, LANES),
            held(SLOTS, LANES),
            held(
                SLOTS + (2 + tiles) * (row_tokens + col_tokens), devices * BLOCK, dtype=BF
            ),
            held(SLOTS + row_tokens + col_tokens, LANES),
            held(1, width),
            held(1, LANES),
            held(width, HEADS * width, dtype=BF),
            held(width, channels, dtype=BF),
            held(channels, width, dtype=BF),
            held(channels, 2 * LANES, dtype=BF),
            held(opm * opm, 2 * w_outer.shape[-1], dtype=BF),
        ),
        far=(
            atom_feats,
            key_starts[None],
            atom_counts[None],
            counts_folded,
            atom_gain[None],
            pair_gain[None],
            w_query,
            w_key,
            w_value,
            w_out,
            w_pool,
            w_back,
            w_left.T,
            w_right.T,
            w_outer.reshape(opm * opm, -1),
        ),
        scratch=(
            pltpu.VMEM((rows, width), BF),
            pltpu.VMEM((1, key_starts.shape[0]), jnp.int32),
            pltpu.VMEM((1, tokens), jnp.int32),
            pltpu.VMEM(counts_folded.shape, jnp.int32),
            pltpu.VMEM((width, width), BF),
            pltpu.VMEM((width, width), BF),
            pltpu.VMEM((width, width), BF),
            pltpu.VMEM((width, width), BF),
            pltpu.VMEM((2 * LANES, channels), BF),
            pltpu.VMEM((tokens, LANES), F32),
            pltpu.VMEM((tokens, LANES), F32),
            pltpu.SemaphoreType.DMA((17,)),
        ),
    )
    (
        own_float,
        own_mixed,
        probes,
        scores,
        top,
        far_bias,
        route,
        member,
        slot_scale,
        before,
        goes_on,
        last,
        adder,
        own_scale,
        atom_gain_kept,
        pair_gain_kept,
        *kept,
        w_outer_kept,
    ) = ready
    payload, updated, slot_back = call(
        atom_kernel,
        "atoms",
        (
            neighbour,
            sibling,
            own_float,
            own_mixed,
            probes,
            scores,
            top,
            far_bias,
            route,
            member,
            slot_scale,
            before,
            goes_on,
            atom_gain_kept,
            *kept,
        ),
        (
            held(devices * BLOCK, LANES, dtype=BF),
            held(rows, width, dtype=BF),
            held(SLOTS, width),
        ),
    )
    arrived = lax.all_to_all(payload.reshape(devices, BLOCK, LANES), AXES, 0, 0)
    return call(
        pair_kernel,
        "pairs",
        (
            arrived.reshape(devices * BLOCK, LANES),
            adder,
            updated,
            slot_back,
            last,
            member,
            pair_state,
            w_outer_kept,
            pair_gain_kept,
            w_gate,
            w_lift,
            w_drop,
            kept[-1],
            own_scale,
        ),
        (
            held(rows, width, dtype=BF),
            held(own_tokens, channels, dtype=BF),
            held(*pair_state.shape, dtype=BF),
        ),
    )


def solution(mesh):
    in_specs = (
        P(("row", "col"), None),
        P(("row", "col")),
        P(),
        P(),
        P(),
        P(),
        P(),
        P(),
        P(),
        P(),
        P("row", "col", None),
        P(),
        P(),
        P(),
        P(),
        P(),
        P(),
        P(),
    )
    out_specs = (P(("row", "col"), None), P(("row", "col"), None), P("row", "col", None))
    return jax.shard_map(
        per_device, mesh=mesh, in_specs=in_specs, out_specs=out_specs, check_vma=False
    )
```

```python
import math

import jax
import jax.numpy as jnp
from jax import lax
from jax.experimental import pallas as pl
from jax.experimental.pallas import tpu as pltpu
from jax.sharding import PartitionSpec as P

HEADS = 4
QB = 32
KW = 128
EPSILON = 1e-05
HALF = KW // 2
FEWEST = 8
LANES = 128
SLOTS = 16
BLOCK = 16
SLOT_ROW = 12
DESTS = 32
PAIR_ROWS = 16
GROUP = 8
MASKED = -1e30
SPARE = 12 << 20
MOST = 60 << 20
LOG2E = 1.4426950408889634
AXES = ("row", "col")
BF = jnp.bfloat16
F32 = jnp.float32


def dot(a, b):
    return jnp.dot(a, b, preferred_element_type=F32)


def dot_t(a, b):
    return lax.dot_general(a, b, (((1,), (1,)), ((), ())), preferred_element_type=F32)


def iota(shape, axis):
    return lax.broadcasted_iota(jnp.int32, shape, axis)


def centred_rows(values, gain):
    width = values.shape[1]
    average = jnp.full((width, width), 1.0 / width, F32).astype(BF)
    centred = values.astype(F32) - dot(values, average)
    variance = dot((centred * centred).astype(BF), average)
    return (centred * gain).astype(BF), lax.rsqrt(variance + EPSILON)


def flag(mask):
    return jnp.where(mask, 1.0, 0.0).astype(BF)


def place():
    return lax.axis_index("row") * lax.axis_size("col") + lax.axis_index("col")


def overlap(base, first_own, own_tokens, slots):
    inner = jnp.minimum(first_own + own_tokens, base + slots) - jnp.maximum(first_own, base)
    return jnp.maximum(inner, 0)


def edge_row(base, first_own, own_tokens, slots):
    last_own = first_own + own_tokens - 1
    last_held = (last_own >= base) & (last_own < base + slots)
    free = jnp.where(last_held, 0, own_tokens - 1)
    whole = overlap(base, first_own, own_tokens, slots) == own_tokens
    return jnp.where(whole, BLOCK - 1, free)


def repeat(count, step):
    if count <= 8:
        for at in range(count):
            step(at)
    else:

        def body(at, carry):
            step(at)
            return carry

        lax.fori_loop(0, count, body, 0)


def span(at, size):
    if isinstance(at, int):
        return pl.ds(at * size, size)
    return pl.ds(pl.multiple_of(at * size, size), size)


def ready_kernel(
    own_far,
    starts_far,
    counts_far,
    folded_far,
    atom_gain_far,
    pair_gain_far,
    w_query_far,
    w_key_far,
    w_value_far,
    w_out_far,
    w_pool_far,
    w_back_far,
    w_left_far,
    w_right_far,
    w_outer_far,
    own_float,
    own_mixed,
    probes,
    scores,
    top,
    far_bias,
    route,
    member,
    slot_scale,
    before,
    goes_on,
    last,
    adder,
    own_scale,
    atom_gain,
    pair_gain,
    w_mixed,
    w_pool,
    w_back,
    w_sides,
    w_outer,
    own,
    key_starts,
    counts,
    counts_folded,
    w_query,
    w_key,
    w_value,
    w_out,
    begins,
    ends,
    arrivals,
):
    rows, width = own.shape
    tokens = counts.shape[1]
    opm = w_left_far.shape[0]
    pairs = (
        (counts_far, counts),
        (folded_far, counts_folded),
        (own_far, own),
        (starts_far, key_starts),
        (atom_gain_far, atom_gain),
        (w_query_far, w_query),
        (w_key_far, w_key),
        (w_value_far, w_value),
        (w_out_far, w_out),
        (pair_gain_far, pair_gain),
        (w_pool_far, w_pool),
        (w_back_far, w_back),
        (w_left_far, w_sides.at[:opm]),
        (w_right_far, w_sides.at[opm : 2 * opm]),
        (w_left_far, w_sides.at[2 * LANES - 2 * opm : 2 * LANES - opm]),
        (w_right_far, w_sides.at[2 * LANES - opm :]),
        (w_outer_far, w_outer.at[:, : w_outer_far.shape[1]]),
    )
    copies = [pltpu.make_async_copy(a, b, arrivals.at[k]) for k, (a, b) in enumerate(pairs)]
    for copy in copies:
        copy.start()

    tiles = w_pool.shape[1] // LANES
    devices = route.shape[0] // BLOCK
    atoms = rows * devices
    own_tokens = tokens // devices
    token_rows = own_tokens * tiles
    slots = rows // FEWEST + 1
    position = place()
    first = position * rows
    even = position % 2 == 0
    first_float = first.astype(F32)
    w_sides[2 * opm : 2 * LANES - 2 * opm, :] = jnp.zeros(
        (2 * LANES - 4 * opm, tiles * LANES), BF
    )

    for copy in copies[:9]:
        copy.wait()
    counts_lane = jnp.broadcast_to(counts[...].astype(F32), (LANES, tokens)).astype(BF)
    folded = counts_folded[...].astype(F32).astype(BF)
    upper = flag(iota((LANES, LANES), 0) <= iota((LANES, LANES), 1))
    lower = flag(iota((LANES, LANES), 1) <= iota((LANES, LANES), 0))
    below = flag(iota((LANES, LANES), 1) < iota((LANES, LANES), 0))
    within = dot(folded, upper)
    whole = dot(folded, jnp.ones((LANES, LANES), BF))
    base = jnp.zeros((1, 1), F32)
    passed = jnp.zeros((1, LANES), F32)
    for fold in range(folded.shape[0]):
        ended = within[fold : fold + 1] + passed <= first_float
        base = base + jnp.sum(jnp.where(ended, 1.0, 0.0), axis=1, keepdims=True)
        part = slice(fold * LANES, (fold + 1) * LANES)
        ends[part, :] = passed + dot_t(lower, counts_lane[:, part])
        begins[part, :] = passed + dot_t(below, counts_lane[:, part])
        passed = passed + whole[fold : fold + 1]

    base_token = base.astype(jnp.int32)
    token_lane = iota((SLOTS, tokens), 1).astype(F32)
    slot_token = iota((SLOTS, tokens), 0).astype(F32) + base
    slot_end = dot_t(flag(token_lane <= slot_token), counts_lane)
    slot_start = dot_t(flag(token_lane < slot_token), counts_lane)
    atom_lane = iota((SLOTS, rows), 1).astype(F32) + first_float
    member[...] = flag((atom_lane >= slot_start[:, :rows]) & (atom_lane < slot_end[:, :rows]))
    slot_scale[...] = 1.0 / jnp.maximum(slot_end - slot_start, 1.0)
    last_atom = first_float + (rows - 1)
    is_last = jnp.where((slot_start <= last_atom) & (slot_end > last_atom), 1.0, 0.0)
    last[...] = is_last
    goes_on[...] = is_last * jnp.where(slot_end > first_float + rows, 1.0, 0.0)
    is_first = iota((SLOTS, LANES), 0) == 0
    before[...] = jnp.where(is_first & (slot_start < first_float), 1.0, 0.0)

    lanes = 2 * LANES
    lane = iota((1, lanes), 1)
    atom = (lane % rows + first).astype(F32)
    inside = (atom >= jnp.concatenate([begins[...]] * 2, axis=1)) & (lane < tiles * rows)
    inside = flag(inside & (atom < jnp.concatenate([ends[...]] * 2, axis=1)))
    tile_fits = iota((BLOCK, lanes), 0) // own_tokens == iota((BLOCK, lanes), 1) // rows
    tile_fits = jnp.where(tile_fits, 1.0, 0.0)
    column = iota((1, LANES), 1) - (tiles * rows - LANES)
    kind, slot = column // SLOTS, column % SLOTS
    token = base_token + slot

    def rows_step(at):
        here = span(at, DESTS * BLOCK)
        dest = iota((DESTS, BLOCK, tokens), 0).reshape(DESTS * BLOCK, tokens) + at * DESTS
        turn = iota((DESTS, BLOCK, tokens), 1).reshape(DESTS * BLOCK, tokens) % own_tokens
        picks = dot(flag(iota((1, tokens), 1) == dest * own_tokens + turn), inside)
        picks = picks.reshape(DESTS, BLOCK, lanes) * tile_fits[None]
        picks = picks.reshape(DESTS * BLOCK, lanes)
        dest = iota((DESTS, LANES), 0) + at * DESTS
        first_own = dest * own_tokens
        shared_tokens = overlap(base_token, first_own, own_tokens, slots)
        index = jnp.where(token < first_own, slot, slot - shared_tokens)
        mine = (token >= first_own) & (token < first_own + own_tokens)
        room = 2 * (BLOCK - SLOT_ROW)
        target = jnp.where(index < room, SLOT_ROW + index // 2, jnp.where(kind == 0, 0, -1))
        fits = (index % 2 == kind) & (slot < slots) & jnp.logical_not(mine) & (column >= 0)
        target = jnp.where(fits & (kind < 2), target, -1)
        beside = jnp.where(slot == 0, position - 1, position + 1)
        is_edge = (kind == 2) & (slot < 2) & (dest == beside)
        row = edge_row(base_token, first_own, own_tokens, slots)
        target = jnp.where(is_edge, row, target)
        spot = iota((BLOCK, LANES), 0)
        selects = [
            jnp.where(jnp.broadcast_to(target[d : d + 1], (BLOCK, LANES)) == spot, 1.0, 0.0)
            for d in range(DESTS)
        ]
        high = picks[:, LANES:] + jnp.concatenate(selects, axis=0)
        route[here, :] = jnp.concatenate([picks[:, :LANES], high], axis=1).astype(BF)

    repeat(devices // DESTS, rows_step)

    row_tokens = tokens // lax.axis_size("row")
    col_tokens = tokens // lax.axis_size("col")
    first_row = lax.axis_index("row") * row_tokens
    first_col = lax.axis_index("col") * col_tokens

    def row_counts(height, first_token, cycle):
        token_row = iota((height, tokens), 0) % cycle + first_token
        return dot_t(flag(iota((1, tokens), 1) == token_row), counts_lane)

    owned = [
        row_counts(SLOTS, position * own_tokens, own_tokens),
        row_counts(row_tokens, first_row, row_tokens),
        row_counts(col_tokens, first_col, col_tokens),
    ]
    own_scale[...] = 1.0 / jnp.concatenate(owned, axis=0)

    def adder_step(at):
        here = span(at, LANES)
        spot_lane = iota((1, LANES), 1) + at * LANES
        block = spot_lane // BLOCK
        spot = spot_lane % BLOCK
        edge = (block * rows).astype(F32)
        tally = jnp.zeros((1, LANES), F32)
        for fold in range(tokens // LANES):
            ended = jnp.where(ends[fold * LANES : (fold + 1) * LANES, :] <= edge, 1.0, 0.0)
            tally = tally + jnp.sum(ended, axis=0, keepdims=True)
        start = tally.astype(jnp.int32)
        first_own = position * own_tokens
        shared_tokens = overlap(start, first_own, own_tokens, slots)

        def token_of(index):
            slot = jnp.where(start + index < first_own, index, index + shared_tokens)
            return jnp.where((index >= 0) & (slot < slots), start + slot, -1)

        in_slots = spot >= SLOT_ROW
        room = 2 * (BLOCK - SLOT_ROW)
        ninth = jnp.where((spot == 0) & (shared_tokens == 0), start + room, -1)
        low_token = jnp.where(in_slots, token_of(2 * (spot - SLOT_ROW)), ninth)
        high_token = jnp.where(in_slots, token_of(2 * (spot - SLOT_ROW) + 1), -1)
        own_token = first_own + spot % own_tokens
        held = (spot < token_rows) & (own_token >= start) & (own_token < start + slots)
        own_token = jnp.where(held, own_token, -1)
        line = iota((SLOTS, LANES), 0)
        side = jnp.where(line == token_rows, position - 1, position + 1)
        on_edge = spot == edge_row(start, first_own, own_tokens, slots)
        is_edge = (line >= token_rows) & (line < token_rows + 2) & on_edge & (block == side)
        lines = [(line < token_rows) & (spot == line) & held | is_edge]
        row_line = iota((row_tokens, LANES), 0) + first_row
        col_line = iota((col_tokens, LANES), 0) + first_col
        for wanted in (row_line, col_line):
            lines += [low_token == wanted, high_token == wanted]
        for tile in range(tiles):
            tile_token = jnp.where(spot // own_tokens == tile, own_token, -1)
            lines += [tile_token == row_line, tile_token == col_line]
        top = 0
        for part in lines:
            adder[top : top + part.shape[0], here] = flag(part)
            top += part.shape[0]

    repeat(devices * BLOCK // LANES, adder_step)

    own_float[...] = own[...].astype(F32)
    normed, scaling = centred_rows(own[...], atom_gain[...])
    near = (dot(normed, w_key[...]) * scaling).astype(BF)
    query = (dot(normed, w_query[...]) * scaling).astype(BF)
    head_of = iota((1, width), 1) // (width // HEADS)
    head_mask = [flag(head_of == h) for h in range(HEADS)]
    heads = jnp.concatenate([query * m for m in head_mask], axis=0)
    probes[...] = dot_t(heads, w_key[...]).astype(BF)
    w_mix = jnp.concatenate(
        [dot(w_value[...] * m, w_out[...]).astype(BF) for m in head_mask], axis=1
    )
    w_mixed[...] = w_mix
    own_mixed[...] = (
        dot(normed, w_mix) * jnp.concatenate([scaling] * HEADS, axis=1)
    ).astype(BF)
    near_index = first + iota((1, rows), 1)
    far_lane = iota((1, 2 * rows), 1)
    is_low = (far_lane < rows) != even
    far_index = first + far_lane % rows + jnp.where(is_low, -rows, rows)
    near_bias, bias = [], []
    for e in range(rows // QB):
        low = key_starts[0:1, e : e + 1]
        seen = (near_index >= low) & (near_index < low + KW)
        near_bias.append(jnp.broadcast_to(jnp.where(seen, 0.0, MASKED), (QB, rows)))
        seen = (far_index >= low) & (far_index < low + KW)
        seen = seen & (far_index >= 0) & (far_index < atoms)
        bias.append(jnp.broadcast_to(jnp.where(seen, 0.0, MASKED), (QB, 2 * rows)))
    far_bias[...] = jnp.concatenate(bias, axis=0)
    raw_scores = dot_t(heads, near) + jnp.concatenate(near_bias * HEADS, axis=0)
    scores[...] = raw_scores
    top[...] = jnp.max(raw_scores, axis=-1, keepdims=True)
    for copy in copies[9:]:
        copy.wait()
    pair_width = w_outer_far.shape[1]
    average = jnp.full((pair_width, pair_width), 1.0 / pair_width, F32).astype(BF)
    w_outer[:, pair_width:] = dot(w_outer[:, :pair_width], average).astype(BF)


def atom_kernel(
    neighbour,
    sibling,
    own_float,
    own_mixed,
    probes,
    scores,
    top,
    far_bias,
    route,
    member,
    slot_scale,
    before,
    goes_on,
    atom_gain,
    w_mixed,
    w_pool,
    w_back,
    w_sides,
    payload,
    updated,
    slot_back,
):
    rows, width = own_float.shape
    tiles = w_pool.shape[1] // LANES
    devices = payload.shape[0] // BLOCK
    raw = jnp.concatenate([sibling[...], neighbour[...]], axis=0)
    average = jnp.full((width, width), 1.0 / width, F32).astype(BF)
    centred = raw.astype(F32) - dot(raw, average)
    squares = (centred * centred).astype(BF)
    normed = (centred * atom_gain[...]).astype(BF)
    scaling = lax.rsqrt(dot(squares, average) + EPSILON)
    scaling_row = lax.rsqrt(dot_t(average[:SLOTS], squares) + EPSILON)[0:1]
    far_mixed = (
        dot(normed, w_mixed[...]) * jnp.concatenate([scaling] * HEADS, axis=1)
    ).astype(BF)
    far_scores = dot_t(probes[...], normed) * scaling_row
    far_scores = far_scores + jnp.concatenate([far_bias[...]] * HEADS, axis=0)
    most = jnp.maximum(top[...], jnp.max(far_scores, axis=-1, keepdims=True))
    scale = (width // HEADS) ** (-0.5) * LOG2E
    raised = jnp.concatenate(
        [
            jnp.exp2((far_scores - most) * scale).astype(BF),
            jnp.exp2((scores[...] - most) * scale).astype(BF),
        ],
        axis=1,
    )
    ones = jnp.ones((3 * rows, width), BF)
    change = own_float[...]
    for h in range(HEADS):
        part = slice(h * width, (h + 1) * width)
        values = jnp.concatenate([far_mixed[:, part], own_mixed[:, part]], axis=0)
        mixed = dot(raised[h * rows : (h + 1) * rows], jnp.concatenate([values, ones], axis=1))
        change = change + mixed[:, :width] / mixed[:, width:]
    fresh = change.astype(BF)
    updated[...] = fresh
    feature = jnp.maximum(dot(fresh, w_pool[...]), 0.0).astype(BF)
    feature_tiles = jnp.concatenate(
        [feature[:, k * LANES : (k + 1) * LANES] for k in range(tiles)], axis=0
    )
    slot_single = (
        dot(member[...], feature) * jnp.concatenate([slot_scale[...]] * tiles, axis=1)
    ).astype(BF)
    sides = dot_t(slot_single, w_sides[...]).astype(BF)
    backs = dot(slot_single, w_back[...])
    slot_back[...] = backs
    to_before = jnp.sum(backs * before[...], axis=0, keepdims=True)
    to_after = jnp.sum(backs * goes_on[...], axis=0, keepdims=True)
    spot = iota((SLOTS, LANES), 0)
    edges = jnp.where(spot == 0, to_before, jnp.where(spot == 1, to_after, 0.0)).astype(BF)
    ahead = tiles * rows - LANES
    spare = jnp.zeros((LANES - ahead, LANES), BF)
    source = jnp.concatenate([feature_tiles, spare], axis=0)
    spare = jnp.zeros((LANES - ahead - 3 * SLOTS, LANES), BF)
    slot_source = jnp.concatenate(
        [jnp.zeros((ahead, LANES), BF), sides[:, :LANES], sides[:, LANES:], edges, spare], axis=0
    )

    def send_step(at):
        here = span(at, DESTS * BLOCK)
        singles = dot(route[here, :], source)
        payload[here, :] = (singles + dot(route[here, LANES:], slot_source)).astype(BF)

    repeat(devices // DESTS, send_step)


def pair_kernel(
    arrived,
    adder,
    updated,
    slot_back,
    slot_last,
    slot_member,
    pair_state,
    w_outer,
    pair_gain,
    w_gate,
    w_lift,
    w_drop,
    w_sides,
    own_scale,
    atom_out,
    token_single,
    pair_out,
):
    row_tokens, col_tokens, pair_width = pair_state.shape
    own_tokens, channels = token_single.shape
    tiles = channels // LANES
    token_rows = own_tokens * tiles
    opm = math.isqrt(w_outer.shape[0])
    added = dot(adder[...], arrived[...])
    half_gate = w_gate[...] * jnp.asarray(0.5, BF)
    parts, top = [], 0
    for height in (SLOTS,) + (row_tokens,) * 2 + (col_tokens,) * 2 + (row_tokens, col_tokens) * tiles:
        parts.append(added[top : top + height])
        top += height
    sums, left_low, left_high, right_low, right_high, *own = parts
    owned = own_scale[...]
    row_scale = owned[SLOTS : SLOTS + row_tokens]
    col_scale = owned[SLOTS + row_tokens :]
    own_left = jnp.concatenate([part * row_scale for part in own[0::2]], axis=1).astype(BF)
    own_right = jnp.concatenate([part * col_scale for part in own[1::2]], axis=1).astype(BF)
    own_sides = dot_t(jnp.concatenate([own_left, own_right], axis=0), w_sides[:LANES])
    left = left_low[:, :opm] + left_high[:, 2 * opm : 3 * opm] + own_sides[:row_tokens, :opm]
    right = right_low[:, opm : 2 * opm] + right_high[:, 3 * opm : 4 * opm]
    right = right + own_sides[row_tokens:, opm : 2 * opm]
    depth = GROUP * opm
    corner = jnp.where(iota((GROUP, depth), 1) // opm == iota((GROUP, depth), 0), 1.0, 0.0)

    def spread(rows_of, first, count):
        return jnp.concatenate(
            [
                jnp.broadcast_to(rows_of[k : k + 1, :], (GROUP, depth)) * corner
                for k in range(first, first + count)
            ],
            axis=0,
        ).astype(BF)

    left_wide = jnp.concatenate([left] * GROUP, axis=1)
    right_blocks = spread(jnp.concatenate([right] * GROUP, axis=1), 0, col_tokens)
    stages = opm // GROUP
    table = [
        dot(right_blocks, w_outer[g * depth : (g + 1) * depth, :]) for g in range(stages)
    ]
    tables = [
        jnp.concatenate(
            [
                table[g][j * GROUP : (j + 1) * GROUP]
                for j in range(h * GROUP, (h + 1) * GROUP)
                for g in range(stages)
            ],
            axis=0,
        ).astype(BF)
        for h in range(col_tokens // GROUP)
    ]

    def pair_rows(here):
        left_blocks = spread(left_wide, here, PAIR_ROWS)
        terms = [dot(left_blocks, part) for part in tables]
        outer = jnp.concatenate(
            [
                term[i * GROUP : (i + 1) * GROUP]
                for i in range(PAIR_ROWS)
                for term in terms
            ],
            axis=0,
        )
        flat = pair_state[pl.ds(here, PAIR_ROWS)].reshape(PAIR_ROWS * col_tokens, pair_width)
        flat = flat.astype(F32)
        summed = flat + outer[:, :pair_width]
        pair_mean = jnp.mean(flat, axis=-1, keepdims=True)
        centred = summed - (pair_mean + outer[:, pair_width:])
        variance = jnp.mean(centred * centred, axis=-1, keepdims=True)
        scaling = lax.rsqrt(variance + EPSILON)
        normed = (centred * pair_gain[...]).astype(BF)
        gate = dot(normed, half_gate) * scaling
        lift = dot(normed, w_lift[...])
        hidden = (gate * lift * (1.0 + jnp.tanh(gate))).astype(BF)
        result = (summed + dot(hidden, w_drop[...]) * scaling).astype(BF)
        pair_out[pl.ds(here, PAIR_ROWS)] = result.reshape(PAIR_ROWS, col_tokens, pair_width)

    for step in range(row_tokens // PAIR_ROWS):
        here = step * PAIR_ROWS
        pair_rows(here)

    singles = sums * owned[:SLOTS]
    token_single[...] = jnp.concatenate(
        [singles[k * own_tokens : (k + 1) * own_tokens] for k in range(tiles)], axis=1
    ).astype(BF)
    spot = iota((SLOTS, LANES), 0)
    from_before = jnp.where(spot == 0, sums[token_rows : token_rows + 1], 0.0)
    from_after = slot_last[...] * sums[token_rows + 1 : token_rows + 2]
    back = (slot_back[...] + from_before + from_after).astype(BF)
    lifted = lax.dot_general(
        slot_member[...], back, (((0,), (0,)), ((), ())), preferred_element_type=F32
    )
    atom_out[...] = (updated[...].astype(F32) + lifted).astype(BF)


def call(kernel, name, operands, outputs, far=(), scratch=()):
    near_spec = pl.BlockSpec(memory_space=pltpu.VMEM)
    far_spec = pl.BlockSpec(memory_space=pltpu.HBM)
    held = sum(math.prod(a.shape) * a.dtype.itemsize for a in operands + outputs)
    return pl.pallas_call(
        kernel,
        out_shape=outputs,
        in_specs=[far_spec] * len(far) + [near_spec] * len(operands),
        out_specs=(near_spec,) * len(outputs),
        scratch_shapes=scratch,
        compiler_params=pltpu.CompilerParams(vmem_limit_bytes=min(2 * held + SPARE, MOST)),
        name=name,
    )(*[pltpu.with_memory_space_constraint(a, pltpu.HBM) for a in far], *operands)


def per_device(
    atom_feats,
    key_starts,
    atom_counts,
    atom_gain,
    w_query,
    w_key,
    w_value,
    w_out,
    w_pool,
    w_back,
    pair_state,
    w_left,
    w_right,
    w_outer,
    pair_gain,
    w_gate,
    w_lift,
    w_drop,
):
    rows, width = atom_feats.shape
    devices = lax.axis_size(AXES)
    tokens = atom_counts.shape[0]
    channels = w_pool.shape[1]
    opm = w_left.shape[1]
    own_tokens = tokens // devices
    row_tokens, col_tokens, _ = pair_state.shape
    tiles = channels // LANES
    opm = w_left.shape[1]
    across = [(i, i + 1) for i in range(1, devices - 1, 2)]
    neighbour = lax.ppermute(atom_feats, AXES, across + [(j, i) for i, j in across])
    sibling = lax.ppermute(atom_feats, AXES, [(i, i ^ 1) for i in range(devices)])

    def held(*shape, dtype=F32):
        return jax.ShapeDtypeStruct(shape, dtype)

    counts_folded = atom_counts.reshape(-1, LANES)
    ready = call(
        ready_kernel,
        "ready",
        (),
        (
            held(rows, width),
            held(rows, HEADS * width, dtype=BF),
            held(HEADS * rows, width, dtype=BF),
            held(HEADS * rows, rows),
            held(HEADS * rows, 1),
            held(rows, 2 * rows),
            held(devices * BLOCK, 2 * LANES, dtype=BF),
            held(SLOTS, rows, dtype=BF),
            held(SLOTS, LANES),
            held(SLOTS, LANES),
            held(SLOTS, LANES),
            held(SLOTS, LANES),
            held(
                SLOTS + (2 + tiles) * (row_tokens + col_tokens), devices * BLOCK, dtype=BF
            ),
            held(SLOTS + row_tokens + col_tokens, LANES),
            held(1, width),
            held(1, LANES),
            held(width, HEADS * width, dtype=BF),
            held(width, channels, dtype=BF),
            held(channels, width, dtype=BF),
            held(2 * LANES, channels, dtype=BF),
            held(opm * opm, 2 * w_outer.shape[-1], dtype=BF),
        ),
        far=(
            atom_feats,
            key_starts[None],
            atom_counts[None],
            counts_folded,
            atom_gain[None],
            pair_gain[None],
            w_query,
            w_key,
            w_value,
            w_out,
            w_pool,
            w_back,
            w_left.T,
            w_right.T,
            w_outer.reshape(opm * opm, -1),
        ),
        scratch=(
            pltpu.VMEM((rows, width), BF),
            pltpu.VMEM((1, key_starts.shape[0]), jnp.int32),
            pltpu.VMEM((1, tokens), jnp.int32),
            pltpu.VMEM(counts_folded.shape, jnp.int32),
            pltpu.VMEM((width, width), BF),
            pltpu.VMEM((width, width), BF),
            pltpu.VMEM((width, width), BF),
            pltpu.VMEM((width, width), BF),
            pltpu.VMEM((tokens, LANES), F32),
            pltpu.VMEM((tokens, LANES), F32),
            pltpu.SemaphoreType.DMA((17,)),
        ),
    )
    (
        own_float,
        own_mixed,
        probes,
        scores,
        top,
        far_bias,
        route,
        member,
        slot_scale,
        before,
        goes_on,
        last,
        adder,
        own_scale,
        atom_gain_kept,
        pair_gain_kept,
        *kept,
        w_outer_kept,
    ) = ready
    payload, updated, slot_back = call(
        atom_kernel,
        "atoms",
        (
            neighbour,
            sibling,
            own_float,
            own_mixed,
            probes,
            scores,
            top,
            far_bias,
            route,
            member,
            slot_scale,
            before,
            goes_on,
            atom_gain_kept,
            *kept,
        ),
        (
            held(devices * BLOCK, LANES, dtype=BF),
            held(rows, width, dtype=BF),
            held(SLOTS, width),
        ),
    )
    arrived = lax.all_to_all(payload.reshape(devices, BLOCK, LANES), AXES, 0, 0)
    return call(
        pair_kernel,
        "pairs",
        (
            arrived.reshape(devices * BLOCK, LANES),
            adder,
            updated,
            slot_back,
            last,
            member,
            pair_state,
            w_outer_kept,
            pair_gain_kept,
            w_gate,
            w_lift,
            w_drop,
            kept[-1],
            own_scale,
        ),
        (
            held(rows, width, dtype=BF),
            held(own_tokens, channels, dtype=BF),
            held(*pair_state.shape, dtype=BF),
        ),
    )


def solution(mesh):
    in_specs = (
        P(("row", "col"), None),
        P(("row", "col")),
        P(),
        P(),
        P(),
        P(),
        P(),
        P(),
        P(),
        P(),
        P("row", "col", None),
        P(),
        P(),
        P(),
        P(),
        P(),
        P(),
        P(),
    )
    out_specs = (P(("row", "col"), None), P(("row", "col"), None), P("row", "col", None))
    return jax.shard_map(
        per_device, mesh=mesh, in_specs=in_specs, out_specs=out_specs, check_vma=False
    )
```
